32 devices in a mesh: dp: 4 (over y, x), seq: 8 (over z, core).
Axes of the slice: x: 2, y: 2, z: 4, core: 2. Of those that a mesh axis runs over, the one named last changes fastest.
Arguments:
- inputs: bfloat16 [8, 2048, 512], P('dp', 'seq'), may hold values from -6 to 6
- w_qkv: bfloat16 [512, 1536], P(('dp', 'seq')), may hold values from -0.25 to 0.25
- bias_qv: bfloat16 [2, 512], P(None, ('dp', 'seq')), may hold values from -1.796875 to 1.796875
- w_out: bfloat16 [512, 512], P(('dp', 'seq')), may hold values from -1 to 1
- bias_out: bfloat16 [512], P(('dp', 'seq')), may hold values from -1.796875 to 1.796875
- w_in: bfloat16 [512, 2048], P(('dp', 'seq')), may hold values from -0.25 to 0.25
- bias_in: bfloat16 [2048], P(('dp', 'seq')), may hold values from -1.796875 to 1.796875
- w_back: bfloat16 [2048, 512], P(('dp', 'seq')), may hold values from -0.1875 to 0.1875
- bias_back: bfloat16 [512], P(('dp', 'seq')), may hold values from -1.796875 to 1.796875
- alphas: float32 [2], replicated, may hold values from 0.2 to 0.4
- cotangent: bfloat16 [8, 2048, 512], P('dp', 'seq'), may hold values from -6 to 6
Outputs:
- outputs: bfloat16 [8, 2048, 512], P('dp', 'seq')
- grad_inputs: bfloat16 [8, 2048, 512], P('dp', 'seq')
- grad_w_qkv: float32 [512, 1536], P(('dp', 'seq'))
- grad_bias_qv: float32 [2, 512], P(None, ('dp', 'seq'))
- grad_w_out: float32 [512, 512], P(('dp', 'seq'))
- grad_bias_out: float32 [512], P(('dp', 'seq'))
- grad_w_in: float32 [512, 2048], P(('dp', 'seq'))
- grad_bias_in: float32 [2048], P(('dp', 'seq'))
- grad_w_back: float32 [2048, 512], P(('dp', 'seq'))
- grad_bias_back: float32 [512], P(('dp', 'seq'))
- grad_alphas: float32 [2], replicated
The draws below stay inside these ranges and needn't reach their ends.
All inputs are finite; a program needn't handle non-finite values.
Results may differ from the reference program's by a relative error of at most 0.038.
Values may be sent and summed in bfloat16 or wider, within the bound.
No kernel may reach another device: no remote copies, remote signals or barrier semaphores. Data moves between devices by JAX's collectives and lax.ppermute only.
A program may use at most 128 MiB of HBM per device.

```python
import math
import jax
import jax.numpy as jnp
from jax import lax

D = 512
HEADS = 8
HEAD_DIM = 64
FF = 2048
BLOCK = 256
SEQS = 8
LENGTH = 2048


def block_levels(stream_key, extent, cuts, smallest, high):
    def one(dim, parts):
        draws = jax.random.uniform(jax.random.fold_in(jax.random.fold_in(stream_key, 6), dim), (parts,), jnp.float32, smallest / len(cuts), high / len(cuts))
        return jnp.repeat(jnp.exp(draws), extent[dim] // parts).reshape((-1,) + (1,) * (len(extent) - dim - 1))

    level = one(*cuts[0])
    for cut in cuts[1:]:
        level = level * one(*cut)
    return level


def normal_values(own_key, shape, spread, reach, cuts=(), kind=jnp.bfloat16):
    factor_of = block_levels(own_key, shape, cuts, -0.22, 0.18) if cuts else 1.0
    array = jax.random.normal(own_key, shape, jnp.float32) * spread * factor_of
    return jnp.minimum(jnp.maximum(array, -reach), reach).astype(kind)


def setup_inputs(seed: int = 0) -> dict:
    streams_of = jax.random.split(jax.random.key(seed), 12)
    return {
        "inputs": normal_values(streams_of[0], (SEQS, LENGTH, D), 1.0, 6.0, ((0, 4), (1, 8))),
        "w_qkv": normal_values(streams_of[1], (D, 3 * D), D ** -0.5, 0.25, ((0, 32),)),
        "bias_qv": normal_values(streams_of[2], (2, D), 0.3, 1.796875, ((1, 32),)),
        "w_out": normal_values(streams_of[3], (D, D), (D // 16) ** -0.5, 1.0, ((0, 32),)),
        "bias_out": normal_values(streams_of[4], (D,), 0.3, 1.796875, ((0, 32),)),
        "w_in": normal_values(streams_of[5], (D, FF), D ** -0.5, 0.25, ((0, 32),)),
        "bias_in": normal_values(streams_of[6], (FF,), 0.3, 1.796875, ((0, 32),)),
        "w_back": normal_values(streams_of[7], (FF, D), (FF // 2) ** -0.5, 0.1875, ((0, 32),)),
        "bias_back": normal_values(streams_of[8], (D,), 0.3, 1.796875, ((0, 32),)),
        "alphas": jnp.clip(jax.random.uniform(streams_of[9], (2,), jnp.float32, 0.2, 0.4), 0.2, 0.4),
        "cotangent": normal_values(streams_of[10], (SEQS, LENGTH, D), 1.0, 6.0, ((0, 4), (1, 8))),
    }


@jax.custom_vjp
def low(v):
    return lax.optimization_barrier(v.astype(jnp.bfloat16)).astype(jnp.float32)

@jax.custom_vjp
def low_back(v):
    return v

def low_keep(v):
    return (low(v), None)

def low_pass(kept, grad):
    return (grad,)

def back_keep(v):
    return (v, None)

def back_low(kept, grad):
    return (low(grad),)
low.defvjp(low_keep, low_pass)
low_back.defvjp(back_keep, back_low)
HIGH = lax.Precision.HIGHEST

def smooth_gate(values):
    return jax.nn.gelu(values, approximate=True)

def attend_sequence(queries, keys, values):
    length = queries.shape[0]
    qrows = min(512, length)
    scale = 1.0 / math.sqrt(HEAD_DIM)
    key_block = jnp.arange(length, dtype=jnp.int32) // BLOCK

    def one_block(index):
        qblk = lax.dynamic_slice_in_dim(queries, index * qrows, qrows, 0)
        scores = jnp.einsum('qhd,khd->hqk', qblk, keys, precision=HIGH) * scale
        scores = low_back(scores)
        query_block = (index * qrows + jnp.arange(qrows, dtype=jnp.int32)) // BLOCK
        allowed = key_block[None, :] <= query_block[:, None]
        scores = jnp.where(allowed[None], scores, -1e+30)
        shifted = scores - lax.optimization_barrier(jnp.max(scores, axis=-1, keepdims=True))
        weights = jnp.where(allowed[None], jnp.exp(shifted), 0.0)
        probs = weights / lax.optimization_barrier(jnp.sum(weights, axis=-1, keepdims=True))
        return jnp.einsum('hqk,khd->qhd', low(probs), values, precision=HIGH)
    blocks = lax.map(jax.checkpoint(one_block), jnp.arange(length // qrows, dtype=jnp.int32))
    return blocks.reshape(length, D)

def forward(inputs, w_qkv, bias_qv, w_out, bias_out, w_in, bias_in, w_back, bias_back, alphas):
    qkv_bias = jnp.concatenate([bias_qv[0], jnp.zeros((D,), jnp.float32), bias_qv[1]])

    def one_sequence(rows):
        qkv = jnp.dot(rows, w_qkv, precision=HIGH) + qkv_bias
        qkv = low_back(low(qkv))
        length = rows.shape[0]
        queries = qkv[:, :D].reshape(length, HEADS, HEAD_DIM)
        keys = qkv[:, D:2 * D].reshape(length, HEADS, HEAD_DIM)
        values = qkv[:, 2 * D:].reshape(length, HEADS, HEAD_DIM)
        mixed = attend_sequence(queries, keys, values)
        mixed = low_back(low(mixed))
        attn = low_back(jnp.dot(mixed, w_out, precision=HIGH) + bias_out)
        first = rows + alphas[0] * attn
        hidden = low(first)
        pre = low_back(jnp.dot(hidden, w_in, precision=HIGH) + bias_in)
        gated = low_back(low(smooth_gate(pre)))
        branch = low_back(jnp.dot(gated, w_back, precision=HIGH) + bias_back)
        return first + alphas[1] * branch
    return lax.map(one_sequence, inputs)

def reference(inputs, w_qkv, bias_qv, w_out, bias_out, w_in, bias_in, w_back, bias_back, alphas, cotangent):
    params = [inputs, w_qkv, bias_qv, w_out, bias_out, w_in, bias_in, w_back, bias_back, alphas]
    params = [p.astype(jnp.float32) for p in params]
    result, pull = jax.vjp(forward, *params)
    grads = pull(cotangent.astype(jnp.float32))
    return (result.astype(jnp.bfloat16), grads[0].astype(jnp.bfloat16), grads[1], grads[2], grads[3], grads[4], grads[5], grads[6], grads[7], grads[8], grads[9])
```

```python
import functools
import math

import jax
import jax.numpy as jnp
from jax import lax
from jax.experimental import pallas as pl
from jax.experimental.pallas import tpu as pltpu
from jax.sharding import Mesh, PartitionSpec as P

D = 512
HEADS = 8
HEAD_DIM = 64
FF = 2048
BLOCK = 256
HALF = D // 2
CORE_HEADS = HEADS // 2
SLABS = FF // D
BF = jnp.bfloat16
F32 = jnp.float32
MESH_AXES = ("a", "b", "z", "c")
VMEM = pl.BlockSpec(memory_space=pltpu.VMEM)
SMEM = pl.BlockSpec(memory_space=pltpu.SMEM)
ANY = pl.BlockSpec(memory_space=pl.ANY)
GELU_C = math.sqrt(2.0 / math.pi)


def dot(left, right):
    return jnp.dot(left, right, preferred_element_type=F32)


def ndot(left, right):
    return lax.dot_general(left, right, (((1,), (1,)), ((), ())), preferred_element_type=F32)


def tdot(left, right):
    return lax.dot_general(left, right, (((0,), (0,)), ((), ())), preferred_element_type=F32)


def flip(block):
    return block.astype(F32).T.astype(BF)


def query_blocks(z, c, nz):
    half = nz // 2
    k = lax.rem(z, half)

    def first(parity):
        return jnp.where(lax.rem(k, 2) == parity, k, nz - 1 - k)

    mine, other = first(c), first(1 - c)
    return (mine, mine + nz, other, other + nz)


def attend_kernel(nz, n1, n2, *refs):
    ids = refs[0]
    xo = refs[1 : 1 + nz]
    xs = refs[1 + nz : 1 + 2 * nz]
    pieces = refs[1 + 2 * nz : 1 + 2 * nz + 2 * n1 * n2]
    bias_q, bias_v = refs[1 + 2 * nz + 2 * n1 * n2 : 3 + 2 * nz + 2 * n1 * n2]
    (xall, wq, kn, vn, qn, ot, lse, o_mine, o_send, x_mine) = refs[
        3 + 2 * nz + 2 * n1 * n2 : 13 + 2 * nz + 2 * n1 * n2
    ]
    vt, qz, m_s, l_s, acc_s = refs[13 + 2 * nz + 2 * n1 * n2 :]
    z, c, a, b = ids[0], ids[1], ids[2], ids[3]
    for r in range(nz):
        src = lax.rem(z - r + nz, nz)
        xall[2 * src + c] = xo[r][...]
        xall[2 * src + 1 - c] = xs[r][...]
    i = 0
    for h in range(2):
        for ra in range(n1):
            for rb in range(n2):
                dp = lax.rem(a - ra + n1, n1) * n2 + lax.rem(b - rb + n2, n2)
                wq[2 * dp + h] = pieces[i][...]
                i += 1
    weights = wq.shape[0] * wq.shape[1]
    w_all = wq[...].reshape(weights, 3 * HALF)
    w_q, w_kv = w_all[:, :HALF], w_all[:, HALF:]

    def project(block, unused):
        kv = dot(xall[block], w_kv)
        kn[block] = kv[:, :HALF].astype(BF)
        value = kv[:, HALF:] + bias_v[...]
        vn[block] = value.astype(BF)
        vt[block] = value.T.astype(BF)
        return unused

    lax.fori_loop(0, 2 * nz, project, 0)
    blocks = query_blocks(z, c, nz)
    rows = lax.broadcasted_iota(jnp.int32, (HALF, BLOCK), 0) // HEAD_DIM
    for i, block in enumerate(blocks):
        xq = xall[block]
        if i < 2:
            x_mine[i] = xq
        q = ((dot(xq, w_q) + bias_q[...]).astype(BF).astype(F32) * (1.0 / math.sqrt(HEAD_DIM))).astype(BF)
        qn[i] = q
        qt = q.astype(F32).T
        for h in range(CORE_HEADS):
            qz[h] = jnp.where(rows == h, qt, 0.0).astype(BF)
        m_s[...] = jnp.full_like(m_s, -1e30)
        l_s[...] = jnp.zeros_like(l_s)
        acc_s[...] = jnp.zeros_like(acc_s)

        def step(kb, unused):
            keys = kn[kb]
            for h in range(CORE_HEADS):
                head = slice(h * HEAD_DIM, (h + 1) * HEAD_DIM)
                s = dot(keys, qz[h])
                old = m_s[h]
                new = jnp.maximum(old, jnp.max(s, axis=0, keepdims=True))
                p = jnp.exp(s - new)
                shrink = jnp.exp(old - new)
                m_s[h] = new
                l_s[h] = l_s[h] * shrink + jnp.sum(p, axis=0, keepdims=True)
                acc_s[head, :] = acc_s[head, :] * shrink + dot(vt[kb, head, :], p.astype(BF))
            return unused

        lax.fori_loop(0, block + 1, step, 0)
        for h in range(CORE_HEADS):
            head = slice(h * HEAD_DIM, (h + 1) * HEAD_DIM)
            total = l_s[h]
            lse[i, h : h + 1, :] = m_s[h] + jnp.log(total)
            acc_s[head, :] = acc_s[head, :] / total
        o = acc_s[...]
        ot[i] = o
        target = o_mine if i < 2 else o_send
        target[i % 2] = o.T.astype(BF)


def ffn_kernel(n1, n2, *refs):
    npieces = 2 * n1 * n2
    ids, alphas, o_mine, o_recv, x_mine, cot_a, cot_b, bo, bi, bb = refs[:10]
    pieces = refs[10 : 10 + 2 * npieces]
    (out, dx1, d_mine, d_send, g_keep, g_send, gb_o, gb_i, gb_b, ga) = refs[
        10 + 2 * npieces : 20 + 2 * npieces
    ]
    w, wo_s, wi_s, wb_s, mixed, h_s, r_s, dpre_s, dff_s, dattn_s, g_s, sems = refs[20 + 2 * npieces :]
    c, a, b, group = ids[1], ids[2], ids[3], ids[4]
    copies = []
    i = 0
    for h in range(2):
        for ra in range(n1):
            for rb in range(n2):
                dp = lax.rem(a - ra + n1, n1) * n2 + lax.rem(b - rb + n2, n2)
                for own in range(2):
                    copies.append(
                        pltpu.make_async_copy(
                            pieces[own * npieces + i],
                            w.at[c if own == 0 else 1 - c, 2 * dp + h],
                            sems.at[own * npieces + i],
                        )
                    )
                i += 1
    for copy in copies:
        copy.start()
    mixed[c] = o_mine[...].reshape(2 * BLOCK, HALF)
    mixed[1 - c] = o_recv[...].reshape(2 * BLOCK, HALF)
    for copy in copies:
        copy.wait()
    ndp = n1 * n2
    rd = D // ndp
    for half in range(2):
        lanes = slice(half * HALF, (half + 1) * HALF)
        whole = w[half].reshape(ndp, 9 * rd, HALF)
        wb_s[:, lanes] = whole[:, : 4 * rd].reshape(FF, HALF)
        for s in range(SLABS):
            wi_s[s, :, lanes] = whole[:, (4 + s) * rd : (5 + s) * rd].reshape(D, HALF)
        wo_s[:, lanes] = whole[:, 8 * rd :].reshape(D, HALF)
    alpha_attn, alpha_ffn = alphas[0], alphas[1]

    def tile(t, sums):
        rows = pl.ds(pl.multiple_of(t * BLOCK, BLOCK), BLOCK)
        ob0, ob1 = mixed[0, rows, :], mixed[1, rows, :]
        attn = dot(ob0, wo_s[:HALF, :]) + dot(ob1, wo_s[HALF:, :]) + bo[...]
        x1 = x_mine[t].astype(F32) + alpha_attn * attn
        hidden = x1.astype(BF)
        h_s[rows, :] = hidden
        dy = jnp.where(t == group, cot_a[...], cot_b[...]).astype(F32)
        dff = (alpha_ffn * dy).astype(BF)
        dff_s[rows, :] = dff
        ff = jnp.zeros((BLOCK, D), F32) + bb[...]
        dx = dy
        for s in range(SLABS):
            lanes = slice(s * D, (s + 1) * D)
            pre = dot(hidden, wi_s[s]) + bi[:, lanes]
            square = pre * pre
            t_ = jnp.tanh(GELU_C * pre * (1.0 + 0.044715 * square))
            half_up = 0.5 * (1.0 + t_)
            r = (pre * half_up).astype(BF)
            slope = half_up + 0.5 * pre * (1.0 - t_ * t_) * (GELU_C * (1.0 + 3.0 * 0.044715 * square))
            r_s[rows, lanes] = r
            ff = ff + dot(r, wb_s[lanes, :])
            dr = ndot(dff, wb_s[lanes, :]).astype(BF).astype(F32)
            dpre = (dr * slope).astype(BF)
            dpre_s[rows, lanes] = dpre
            dx = dx + ndot(dpre, wi_s[s])
        out[t] = (x1 + alpha_ffn * ff).astype(BF)
        dx1[t] = dx
        dattn = (alpha_attn * dx).astype(BF)
        dattn_s[rows, :] = dattn
        d_mixed = ndot(dattn, wo_s[...]).astype(BF)
        d_mine[t] = jnp.where(c == 0, d_mixed[:, :HALF], d_mixed[:, HALF:])
        d_send[t] = jnp.where(c == 0, d_mixed[:, HALF:], d_mixed[:, :HALF])
        return (sums[0] + jnp.sum(dx * attn, axis=0, keepdims=True), sums[1] + jnp.sum(dy * ff, axis=0, keepdims=True))

    zero = jnp.zeros((1, D), F32)
    sum_attn, sum_ffn = lax.fori_loop(0, 2, tile, (zero, zero))
    ga[...] = jnp.concatenate([sum_attn, sum_ffn], axis=0)
    dff, dattn, hidden = dff_s[...], dattn_s[...], h_s[...]
    gb_o[...] = jnp.sum(dattn.astype(F32), axis=0, keepdims=True)
    gb_b[...] = jnp.sum(dff.astype(F32), axis=0, keepdims=True)
    ht = flip(hidden)

    def put(first, value):
        count = value.shape[0] // ndp
        for half in range(2):
            part = value[:, half * HALF : (half + 1) * HALF].astype(BF).reshape(ndp, count, HALF)
            g_s[half, :, first : first + count, :] = part

    for s in range(SLABS):
        lanes = slice(s * D, (s + 1) * D)
        dpre = dpre_s[:, lanes]
        gb_i[:, lanes] = jnp.sum(dpre.astype(F32), axis=0, keepdims=True)
        put((4 + s) * rd, dot(ht, dpre))
        g_back = dot(flip(r_s[:, lanes]), dff)
        per = ndp // SLABS if ndp >= SLABS else 1
        count = 4 * rd
        for half in range(2):
            part = g_back[:, half * HALF : (half + 1) * HALF].astype(BF).reshape(per, count, HALF)
            g_s[half, s * per : (s + 1) * per, :count, :] = part
    both = jnp.concatenate([mixed[0], mixed[1]], axis=1)
    put(8 * rd, dot(flip(both), dattn))
    done = [
        pltpu.make_async_copy(g_s.at[c], g_keep, sems.at[0]),
        pltpu.make_async_copy(g_s.at[1 - c], g_send, sems.at[1]),
    ]
    for copy in done:
        copy.start()
    for copy in done:
        copy.wait()


def back_kernel(nz, *refs):
    (ids, xall, wq, kn, vn, qn, ot, lse, d_mine, d_recv, dx1) = refs[:11]
    dx_keep, dx_send, dw, gb = refs[11:15]
    kt, qz, qzt, oz, ozt, dk_s, dv_s, dq_s, dqkv, dxs = refs[15:]
    z, c = ids[0], ids[1]
    scale = 1.0 / math.sqrt(HEAD_DIM)
    dk_s[...] = jnp.zeros_like(dk_s)
    dv_s[...] = jnp.zeros_like(dv_s)
    dqkv[...] = jnp.zeros_like(dqkv)

    def turn(block, unused):
        kt[block] = flip(kn[block])
        return unused

    lax.fori_loop(0, 2 * nz, turn, 0)
    rows = lax.broadcasted_iota(jnp.int32, (HALF, BLOCK), 0) // HEAD_DIM
    lanes = lax.broadcasted_iota(jnp.int32, (BLOCK, HALF), 1) // HEAD_DIM
    blocks = query_blocks(z, c, nz)
    gq = jnp.zeros((1, HALF), F32)
    for i, block in enumerate(blocks):
        q = qn[i].astype(F32)
        d_o = (d_mine[i] if i < 2 else d_recv[i - 2]).astype(F32)
        qt, dot_ = q.T, d_o.T
        product = dot_ * ot[i]
        deltas = []
        for h in range(CORE_HEADS):
            head = slice(h * HEAD_DIM, (h + 1) * HEAD_DIM)
            deltas.append(jnp.sum(product[head], axis=0, keepdims=True))
            qz[h] = jnp.where(lanes == h, q, 0.0).astype(BF)
            oz[h] = jnp.where(lanes == h, d_o, 0.0).astype(BF)
            qzt[h] = jnp.where(rows == h, qt, 0.0).astype(BF)
            ozt[h] = jnp.where(rows == h, dot_, 0.0).astype(BF)
        dq_s[...] = jnp.zeros_like(dq_s)

        def step(kb, unused):
            keys, values = kn[kb], vn[kb]
            dk = dk_s[kb]
            dv = dv_s[kb]
            for h in range(CORE_HEADS):
                head = slice(h * HEAD_DIM, (h + 1) * HEAD_DIM)
                p = jnp.exp(dot(keys, qzt[h]) - lse[i, h : h + 1, :])
                dp = dot(values, ozt[h])
                ds = (p * (dp - deltas[h])).astype(BF)
                dv = dv + dot(p.astype(BF), oz[h])
                dk = dk + dot(ds, qz[h])
                dq_s[head, :] = dq_s[head, :] + dot(kt[kb, head, :], ds)
            dk_s[kb] = dk
            dv_s[kb] = dv
            return unused

        lax.fori_loop(0, block + 1, step, 0)
        dq = (dq_s[...] * scale).T.astype(BF)
        gq = gq + jnp.sum(dq.astype(F32), axis=0, keepdims=True)
        dqkv[block, :, :HALF] = dq

    w_all = wq[...].reshape(D, 3 * HALF)

    def finish(block, gv):
        dv = dv_s[block].astype(BF)
        dqkv[block, :, HALF : 2 * HALF] = dk_s[block].astype(BF)
        dqkv[block, :, 2 * HALF :] = dv
        dxs[block] = ndot(dqkv[block], w_all)
        return gv + jnp.sum(dv.astype(F32), axis=0, keepdims=True)

    gv = lax.fori_loop(0, 2 * nz, finish, jnp.zeros((1, HALF), F32))
    gb[...] = jnp.concatenate([gq, gv], axis=0)
    for i in range(2):
        dxs[blocks[i]] = dxs[blocks[i]] + dx1[i]
    for s in range(nz):
        dx_keep[s] = dxs[2 * s + c].astype(BF)
        dx_send[s] = dxs[2 * s + 1 - c].astype(BF)
    total = jnp.zeros((D, 3 * HALF), F32)
    acc = dot(flip(xall[0]), dqkv[0])
    for block in range(1, 2 * nz):
        acc = acc + dot(flip(xall[block]), dqkv[block])
    dw[...] = (total + acc).astype(BF)


def shape(dims, kind):
    return jax.ShapeDtypeStruct(dims, kind)


def cost(flops, size, trans=0):
    return pl.CostEstimate(flops=int(flops), bytes_accessed=int(size), transcendentals=int(trans))


def make_body(n1, n2, nz):
    ndp = n1 * n2
    nsh = ndp * nz * 2
    rs = D // nsh
    rd = D // ndp
    half = nz // 2
    swap = [(0, 1), (1, 0)]

    def turn(count, by):
        return [(s, (s + by) % count) for s in range(count)]

    def place(k, c):
        return (k if k % 2 == c else nz - 1 - k) // 2

    near, far = [], []
    for k in range(half):
        for c in range(2):
            src = place(k, c)
            near += [(2 * src + c, 2 * k + c), (2 * (half + src) + c, 2 * (half + k) + c)]
            far += [(2 * (half + src) + c, 2 * k + c), (2 * src + c, 2 * (half + k) + c)]
    near_back = [(d, s) for s, d in near]
    far_back = [(d, s) for s, d in far]

    def pick(array, index, axis=0):
        return lax.dynamic_index_in_dim(array, index, axis, keepdims=False)

    def body(inputs, w_qkv, bias_qv, w_out, bias_out, w_in, bias_in, w_back, bias_back, alphas, cotangent):
        z, c = lax.axis_index("z"), lax.axis_index("c")
        a, b = lax.axis_index("a"), lax.axis_index("b")
        group = z // half
        ids = jnp.stack([z, c, a, b, group]).astype(jnp.int32)

        def by_core(own, other):
            return jnp.where(c == 0, jnp.stack([own, other]), jnp.stack([other, own]))

        def along_z(piece):
            parts = [piece] + [lax.ppermute(piece, "z", turn(nz, r)) for r in range(1, nz)]
            ring = jnp.stack(parts[::-1] + parts[::-1])
            return lax.dynamic_slice_in_dim(ring, nz - 1 - z, nz, 0)

        def along_dp(rows):
            cut = rows.shape[0] // 2
            first, second = rows[:cut], rows[cut:]
            f1 = [first] + [lax.ppermute(first, "b", turn(n2, r)) for r in range(1, n2)]
            s1 = [second] + [lax.ppermute(second, "a", turn(n1, r)) for r in range(1, n1)]
            parts = []
            for ra in range(n1):
                for rb in range(n2):
                    parts.append(f1[rb] if ra == 0 else lax.ppermute(f1[rb], "a", turn(n1, ra)))
            for ra in range(n1):
                for rb in range(n2):
                    parts.append(s1[ra] if rb == 0 else lax.ppermute(s1[ra], "b", turn(n2, rb)))
            return parts

        def scatter_dp(whole):
            w5 = whole.reshape((n1, n2) + whole.shape[1:])
            first, second = w5[:, :, 0], w5[:, :, 1]

            def over(part, name, count, me, axis):
                got = [
                    lax.ppermute(pick(part, lax.rem(me + r, count), axis), name, turn(count, r))
                    for r in range(1, count)
                ]
                total = pick(part, me, axis).astype(F32)
                for g in got:
                    total = total + g.astype(F32)
                return total.astype(BF)

            first = over(first, "b", n2, b, 1)
            second = over(second, "a", n1, a, 0)
            first = over(first, "a", n1, a, 0)
            second = over(second, "b", n2, b, 0)
            return first, second

        def scatter_z(parts):
            got = [
                lax.ppermute(pick(parts, lax.rem(z + r, nz)), "z", turn(nz, r)) for r in range(1, nz)
            ]
            total = pick(parts, z).astype(F32)
            for g in got:
                total = total + g.astype(F32)
            return total

        wq_cut = w_qkv.reshape(rs, 3, 2, HALF)
        wq_own = pick(wq_cut, c, 2).reshape(rs, 3 * HALF)
        wq_give = pick(wq_cut, 1 - c, 2).reshape(rs, 3 * HALF)
        wq_chip = by_core(wq_own, lax.ppermute(wq_give, "c", swap)).reshape(2 * rs, 3 * HALF)
        wq_pieces = along_dp(along_z(wq_chip).reshape(rd, 3 * HALF))

        x_own = [pick(inputs, group)] + [
            lax.ppermute(pick(inputs, lax.rem(z + r, nz) // half), "z", turn(nz, r)) for r in range(1, nz)
        ]
        x_other = [lax.ppermute(part, "c", swap) for part in x_own]

        def columns(which):
            back = pick(w_back.reshape(4 * rs, 2, HALF), which, 1)
            win = pick(w_in.reshape(rs, SLABS, 2, HALF), which, 2)
            win = jnp.transpose(win, (1, 0, 2)).reshape(SLABS * rs, HALF)
            return jnp.concatenate([back, win, pick(w_out.reshape(rs, 2, HALF), which, 1)], axis=0)

        wf_chip = by_core(columns(c), lax.ppermute(columns(1 - c), "c", swap))
        wf = along_z(wf_chip)
        wf = jnp.concatenate(
            [wf[:, :, : 4 * rs].reshape(4 * rd, HALF)]
            + [wf[:, :, (4 + s) * rs : (5 + s) * rs].reshape(rd, HALF) for s in range(SLABS)]
            + [wf[:, :, 8 * rs :].reshape(rd, HALF)],
            axis=0,
        )
        wf_pieces = along_dp(wf)
        wf_others = [lax.ppermute(part, "c", swap) for part in wf_pieces]

        small = jnp.concatenate([bias_qv[0], bias_qv[1], bias_out, bias_back, bias_in])
        small = lax.all_to_all(
            jnp.broadcast_to(small[None], (nsh, 8 * rs)), MESH_AXES, 0, 0, tiled=True
        ).astype(F32)
        bias_q = pick(small[:, :rs].reshape(2, 1, HALF), c)
        bias_v = pick(small[:, rs : 2 * rs].reshape(2, 1, HALF), c)
        bo = small[:, 2 * rs : 3 * rs].reshape(1, D)
        bb = small[:, 3 * rs : 4 * rs].reshape(1, D)
        bi = small[:, 4 * rs :].reshape(1, FF)

        cot_a = lax.ppermute(pick(cotangent, group), ("z", "c"), near)
        cot_b = lax.ppermute(pick(cotangent, 1 - group), ("z", "c"), far)

        nb = 2 * nz
        pairs = (2 * nb + 2) * CORE_HEADS * BLOCK * BLOCK
        (xall, wq, kn, vn, qn, ot, lse, o_mine, o_send, x_mine) = pl.pallas_call(
            functools.partial(attend_kernel, nz, n1, n2),
            out_shape=(
                shape((nb, BLOCK, D), BF),
                shape((2 * ndp, rd // 2, 3 * HALF), BF),
                shape((nb, BLOCK, HALF), BF),
                shape((nb, BLOCK, HALF), BF),
                shape((4, BLOCK, HALF), BF),
                shape((4, HALF, BLOCK), F32),
                shape((4, CORE_HEADS, BLOCK), F32),
                shape((2, BLOCK, HALF), BF),
                shape((2, BLOCK, HALF), BF),
                shape((2, BLOCK, D), BF),
            ),
            in_specs=[SMEM] + [VMEM] * (2 * nz + 2 * ndp + 2),
            out_specs=(VMEM,) * 10,
            scratch_shapes=[
                pltpu.VMEM((nb, HALF, BLOCK), BF),
                pltpu.VMEM((CORE_HEADS, HALF, BLOCK), BF),
                pltpu.VMEM((CORE_HEADS, 1, BLOCK), F32),
                pltpu.VMEM((CORE_HEADS, 1, BLOCK), F32),
                pltpu.VMEM((HALF, BLOCK), F32),
            ],
            compiler_params=pltpu.CompilerParams(vmem_limit_bytes=40 * 2**20),
            cost_estimate=cost(16 * pairs * HALF // 4, 8 * 2**20, pairs),
            name="attend",
        )(ids, *x_own, *x_other, *wq_pieces, bias_q, bias_v)
        o_recv = lax.ppermute(o_send, "c", swap)

        npieces = 2 * ndp
        nh = 9 * rd // 2
        (out, dx1, d_mine, d_send, g_keep, g_send, gb_o, gb_i, gb_b, ga) = pl.pallas_call(
            functools.partial(ffn_kernel, n1, n2),
            out_shape=(
                shape((2, BLOCK, D), BF),
                shape((2, BLOCK, D), F32),
                shape((2, BLOCK, HALF), BF),
                shape((2, BLOCK, HALF), BF),
                shape((ndp, 9 * rd, HALF), BF),
                shape((ndp, 9 * rd, HALF), BF),
                shape((1, D), F32),
                shape((1, FF), F32),
                shape((1, D), F32),
                shape((2, D), F32),
            ),
            in_specs=[SMEM, SMEM] + [VMEM] * 8 + [ANY] * (2 * npieces),
            out_specs=(VMEM,) * 4 + (ANY, ANY) + (VMEM,) * 4,
            scratch_shapes=[
                pltpu.VMEM((2, 2 * ndp, nh, HALF), BF),
                pltpu.VMEM((D, D), BF),
                pltpu.VMEM((SLABS, D, D), BF),
                pltpu.VMEM((FF, D), BF),
                pltpu.VMEM((2, 2 * BLOCK, HALF), BF),
                pltpu.VMEM((2 * BLOCK, D), BF),
                pltpu.VMEM((2 * BLOCK, FF), BF),
                pltpu.VMEM((2 * BLOCK, FF), BF),
                pltpu.VMEM((2 * BLOCK, D), BF),
                pltpu.VMEM((2 * BLOCK, D), BF),
                pltpu.VMEM((2, ndp, 9 * rd, HALF), BF),
                pltpu.SemaphoreType.DMA((2 * npieces,)),
            ],
            compiler_params=pltpu.CompilerParams(vmem_limit_bytes=48 * 2**20),
            cost_estimate=cost(6 * 2 * BLOCK * 9 * D * HALF * 2, 20 * 2**20, 2 * BLOCK * FF),
            name="ffn",
        )(ids, alphas, o_mine, o_recv, x_mine, cot_a, cot_b, bo, bi, bb, *wf_pieces, *wf_others)
        d_recv = lax.ppermute(d_send, "c", swap)

        out_a = lax.ppermute(pick(out, group), ("z", "c"), near_back)
        out_b = lax.ppermute(pick(out, 1 - group), ("z", "c"), far_back)
        outputs = jnp.where(group == 0, jnp.stack([out_a, out_b]), jnp.stack([out_b, out_a]))

        g_all = (g_keep.astype(F32) + lax.ppermute(g_send, "c", swap).astype(F32)).astype(BF)
        g_first, g_second = scatter_dp(g_all.reshape(ndp, 2, nh, HALF))
        g_dp = jnp.concatenate([g_first, g_second], axis=0)
        g_z = jnp.concatenate(
            [g_dp[: 4 * rd].reshape(nz, 2, 4 * rs, HALF)]
            + [g_dp[(4 + s) * rd : (5 + s) * rd].reshape(nz, 2, rs, HALF) for s in range(SLABS)]
            + [g_dp[8 * rd :].reshape(nz, 2, rs, HALF)],
            axis=2,
        )
        g_mine = scatter_z(g_z)
        g_own = pick(g_mine, c)
        g_other = lax.ppermute(pick(g_mine, 1 - c).astype(BF), "c", swap).astype(F32)
        g_whole = by_core(g_own, g_other)
        grad_w_back = jnp.transpose(g_whole[:, : 4 * rs], (1, 0, 2)).reshape(4 * rs, D)
        grad_w_in = jnp.transpose(
            g_whole[:, 4 * rs : 8 * rs].reshape(2, SLABS, rs, HALF), (2, 1, 0, 3)
        ).reshape(rs, FF)
        grad_w_out = jnp.transpose(g_whole[:, 8 * rs :], (1, 0, 2)).reshape(rs, D)

        dx_keep, dx_send, dw, gb = pl.pallas_call(
            functools.partial(back_kernel, nz),
            out_shape=(
                shape((nz, BLOCK, D), BF),
                shape((nz, BLOCK, D), BF),
                shape((D, 3 * HALF), BF),
                shape((2, HALF), F32),
            ),
            in_specs=[SMEM] + [VMEM] * 10,
            out_specs=(VMEM,) * 4,
            scratch_shapes=[
                pltpu.VMEM((nb, HALF, BLOCK), BF),
                pltpu.VMEM((CORE_HEADS, BLOCK, HALF), BF),
                pltpu.VMEM((CORE_HEADS, HALF, BLOCK), BF),
                pltpu.VMEM((CORE_HEADS, BLOCK, HALF), BF),
                pltpu.VMEM((CORE_HEADS, HALF, BLOCK), BF),
                pltpu.VMEM((nb, BLOCK, HALF), F32),
                pltpu.VMEM((nb, BLOCK, HALF), F32),
                pltpu.VMEM((HALF, BLOCK), F32),
                pltpu.VMEM((nb, BLOCK, 3 * HALF), BF),
                pltpu.VMEM((nb, BLOCK, D), F32),
            ],
            compiler_params=pltpu.CompilerParams(vmem_limit_bytes=56 * 2**20),
            cost_estimate=cost(40 * pairs * HALF // 4, 12 * 2**20, pairs),
            name="back",
        )(ids, xall, wq, kn, vn, qn, ot, lse, d_mine, d_recv, dx1)

        dx = (dx_keep.astype(F32) + lax.ppermute(dx_send, "c", swap).astype(F32)).astype(BF)
        parts = [pick(dx, z)] + [
            lax.ppermute(pick(dx, lax.rem(z + r, nz)), "z", turn(nz, r)) for r in range(1, nz)
        ]
        grads = []
        for which in range(2):
            total = jnp.zeros((BLOCK, D), F32)
            for r, part in enumerate(parts):
                source = lax.rem(z - r + nz, nz) // half
                total = total + jnp.where(source == which, part.astype(F32), 0.0)
            grads.append(total.astype(BF))
        grad_inputs = jnp.stack(grads)

        first, second = scatter_dp(dw.reshape(ndp, 2, rd // 2, 3 * HALF))
        dw_z = jnp.concatenate([first, second], axis=0).reshape(nz, 2, rs, 3 * HALF)
        dw_mine = scatter_z(dw_z)
        dw_own = pick(dw_mine, c)
        dw_other = lax.ppermute(pick(dw_mine, 1 - c).astype(BF), "c", swap).astype(F32)
        grad_w_qkv = jnp.transpose(
            by_core(dw_own, dw_other).reshape(2, rs, 3, HALF), (1, 2, 0, 3)
        ).reshape(rs, 3 * D)

        at = jnp.arange(2, dtype=jnp.int32)[:, None] == c
        gq = jnp.where(at, gb[0][None], 0.0).reshape(nsh, rs)
        gv = jnp.where(at, gb[1][None], 0.0).reshape(nsh, rs)
        gate = jnp.broadcast_to(jnp.sum(ga, axis=1)[None], (nsh, 2))
        packed = jnp.concatenate(
            [gq, gv, gb_o.reshape(nsh, rs), gb_b.reshape(nsh, rs), gb_i.reshape(nsh, 4 * rs), gate], axis=1
        )
        packed = jnp.sum(lax.all_to_all(packed, MESH_AXES, 0, 0, tiled=True), axis=0)
        grad_bias_qv = packed[: 2 * rs].reshape(2, rs)
        return (
            outputs,
            grad_inputs,
            grad_w_qkv,
            grad_bias_qv,
            grad_w_out,
            packed[2 * rs : 3 * rs],
            grad_w_in,
            packed[4 * rs : 8 * rs],
            grad_w_back,
            packed[3 * rs : 4 * rs],
            packed[8 * rs :],
        )

    return body


def solution(mesh):
    ndp, nseq = mesh.devices.shape
    n1 = math.isqrt(ndp)
    n2 = ndp // n1
    nz = nseq // 2
    fine = Mesh(mesh.devices.reshape(n1, n2, nz, 2), MESH_AXES)
    dp, seq = ("a", "b"), ("z", "c")
    rows = P(dp, seq, None)
    both = dp + seq
    return jax.shard_map(
        make_body(n1, n2, nz),
        mesh=fine,
        in_specs=(
            rows,
            P(both, None),
            P(None, both),
            P(both, None),
            P(both),
            P(both, None),
            P(both),
            P(both, None),
            P(both),
            P(),
            rows,
        ),
        out_specs=(
            rows,
            rows,
            P(both, None),
            P(None, both),
            P(both, None),
            P(both),
            P(both, None),
            P(both),
            P(both, None),
            P(both),
            P(),
        ),
        check_vma=False,
    )
```

```python
import functools
import math

import jax
import jax.numpy as jnp
from jax import lax
from jax.experimental import pallas as pl
from jax.experimental.pallas import tpu as pltpu
from jax.sharding import Mesh, PartitionSpec as P

D = 512
HEADS = 8
HEAD_DIM = 64
FF = 2048
BLOCK = 256
HALF = D // 2
CORE_HEADS = HEADS // 2
SLABS = FF // D
BF = jnp.bfloat16
F32 = jnp.float32
MESH_AXES = ("a", "b", "z", "c")
VMEM = pl.BlockSpec(memory_space=pltpu.VMEM)
SMEM = pl.BlockSpec(memory_space=pltpu.SMEM)
ANY = pl.BlockSpec(memory_space=pl.ANY)
HBM = pl.BlockSpec(memory_space=pltpu.HBM)
WQ = 3 * HALF + 128
GELU_C = math.sqrt(2.0 / math.pi)


def dot(left, right):
    return jnp.dot(left, right, preferred_element_type=F32)


def ndot(left, right):
    return lax.dot_general(left, right, (((1,), (1,)), ((), ())), preferred_element_type=F32)


def tdot(left, right):
    return lax.dot_general(left, right, (((0,), (0,)), ((), ())), preferred_element_type=F32)


def flip(block):
    return block.astype(F32).T.astype(BF)


def query_blocks(z, c, nz):
    half = nz // 2
    k = lax.rem(z, half)

    def first(parity):
        return jnp.where(lax.rem(k, 2) == parity, k, nz - 1 - k)

    mine, other = first(c), first(1 - c)
    return (mine, mine + nz, other, other + nz)


def moves(sems, pairs):
    copies = [pltpu.make_async_copy(src, dst, sems.at[i]) for i, (src, dst) in enumerate(pairs)]
    for copy in copies:
        copy.start()
    return copies


def wait(copies):
    for copy in copies:
        copy.wait()


def over_keys(block, chunk):
    pairs = (block + 1) // 2

    def step(i, unused):
        chunk(2 * i, 2)
        return unused

    lax.fori_loop(0, pairs, step, 0)

    @pl.when(lax.rem(block, 2) == 0)
    def _():
        chunk(block, 1)


def attend_blocks(blocks, kn, vt, qn, ot, lse, o, scratch):
    qz, s_s, m_s, l_s, acc_s = scratch
    rows = lax.broadcasted_iota(jnp.int32, (HALF, BLOCK), 0) // HEAD_DIM
    for i, block in enumerate(blocks):
        qt = qn[i].astype(F32).T
        for h in range(CORE_HEADS):
            qz[h] = jnp.where(rows == h, qt, 0.0).astype(BF)
        m_s[...] = jnp.full_like(m_s, -1e30)
        l_s[...] = jnp.zeros_like(l_s)
        acc_s[...] = jnp.zeros_like(acc_s)

        def chunk(first, count):
            keys = kn[pl.ds(first, count)].reshape(count * BLOCK, HALF)
            for h in range(CORE_HEADS):
                s_s[h, : count * BLOCK] = dot(keys, qz[h])
            for h in range(CORE_HEADS):
                head = slice(h * HEAD_DIM, (h + 1) * HEAD_DIM)
                s = s_s[h, : count * BLOCK]
                old = m_s[h]
                new = jnp.maximum(old, jnp.max(s, axis=0, keepdims=True))
                p = jnp.exp(s - new)
                shrink = jnp.exp(old - new)
                m_s[h] = new
                l_s[h] = l_s[h] * shrink + jnp.sum(p, axis=0, keepdims=True)
                p = p.astype(BF)
                acc = acc_s[head, :] * shrink
                for j in range(count):
                    acc = acc + dot(vt[first + j, head, :], p[j * BLOCK : (j + 1) * BLOCK])
                acc_s[head, :] = acc

        over_keys(block, chunk)
        for h in range(CORE_HEADS):
            head = slice(h * HEAD_DIM, (h + 1) * HEAD_DIM)
            total = l_s[h]
            lse[i, h : h + 1, :] = m_s[h] + jnp.log(total)
            acc_s[head, :] = acc_s[head, :] / total
        value = acc_s[...]
        ot[i] = value
        o[i] = value.T.astype(BF)


def first_kernel(nz, ndp, rr, ids, xo, xs, wa, wb, *refs):
    (kn_out, vn_out, vt_out, qm_out, qo_out, ot_out, lse, o_out, bo, bb, bi) = refs[:11]
    xall, wq, kn, vn, vt, q_mine, q_other, ot, o, spread = refs[11:21]
    scratch, sems = refs[21:26], refs[26]
    z, c = ids[0], ids[1]
    weights = moves(
        sems,
        [(wa.at[dp], wq.at[2 * dp]) for dp in range(ndp)] + [(wb.at[dp], wq.at[2 * dp + 1]) for dp in range(ndp)],
    )
    rows_in = moves(
        sems.at[pl.ds(2 * ndp, 2 * nz)],
        [(xo.at[s], xall.at[2 * s + c]) for s in range(nz)]
        + [(xs.at[s], xall.at[2 * s + 1 - c]) for s in range(nz)],
    )
    wait(weights)
    bias = wq[:, :, 3 * HALF :].reshape(D, 128).astype(F32)
    turned = bias.T
    bo[...] = turned[2:3]
    bb[...] = turned[3:4]
    lanes = lax.broadcasted_iota(jnp.int32, (D // rr, rr, 128), 2)
    for s in range(SLABS):
        spread[:, s] = jnp.where(lanes == 4 + s, bias.reshape(D // rr, rr, 128), 0.0)
    bi[...] = jnp.sum(spread[...].reshape(FF, 128).T[4:8], axis=0, keepdims=True)
    bias_q = jnp.where(c == 0, turned[0:1, :HALF], turned[0:1, HALF:])
    bias_v = jnp.where(c == 0, turned[1:2, :HALF], turned[1:2, HALF:])
    w_q = wq[:, :, :HALF].reshape(D, HALF)
    w_kv = wq[:, :, HALF : 3 * HALF].reshape(D, 2 * HALF)
    wait(rows_in)

    def project(block, unused):
        kv = dot(xall[block], w_kv)
        kn[block] = kv[:, :HALF].astype(BF)
        value = kv[:, HALF:] + bias_v
        vn[block] = value.astype(BF)
        vt[block] = value.T.astype(BF)
        return unused

    lax.fori_loop(0, 2 * nz, project, 0)
    blocks = query_blocks(z, c, nz)
    for i, block in enumerate(blocks):
        q = (dot(xall[block], w_q) + bias_q).astype(BF).astype(F32) * (1.0 / math.sqrt(HEAD_DIM))
        (q_mine if i < 2 else q_other)[i % 2] = q.astype(BF)
    out = moves(
        sems, [(kn, kn_out), (vn, vn_out), (vt, vt_out), (q_mine, qm_out), (q_other, qo_out)]
    )
    attend_blocks(blocks[2:], kn, vt, q_other, ot, lse, o, scratch)
    out += moves(sems.at[pl.ds(5, 2)], [(ot, ot_out), (o, o_out)])
    wait(out)


def second_kernel(nz, ids, kn_in, vt_in, q_in, ot_out, lse, o_out, kn, vt, qn, ot, o, *rest):
    scratch, sems = rest[:5], rest[5]
    wait(moves(sems, [(kn_in, kn), (vt_in, vt), (q_in, qn)]))
    blocks = query_blocks(ids[0], ids[1], nz)
    attend_blocks(blocks[:2], kn, vt, qn, ot, lse, o, scratch)
    wait(moves(sems, [(ot, ot_out), (o, o_out)]))


def ffn_kernel(nz, ndp, parts, *refs):
    ids, alphas, o_mine, o_recv, xo, cot_a, cot_b, bo, bi, bb = refs[:10]
    pieces = refs[10:14]
    (out_o, dx1_o, d_mine_o, d_send_o, g_keep, g_send, gb_o, gb_i, gb_b, ga) = refs[14:24]
    w, wo_s, wi_s, wb_s, mixed, x_s, cot, h_s, r_s, dpre_s, dff_s, dattn_s, g_s = refs[24:37]
    out, dx1, d_both, sems = refs[37:]
    c, group = ids[1], ids[4]
    copies = []
    for i in range(4):
        for dp in range(ndp):
            copies.append((pieces[i].at[dp], w.at[c if i < 2 else 1 - c, 2 * dp + i % 2]))
    weights = moves(sems, copies)
    mine = query_blocks(ids[0], c, nz)
    acts = moves(
        sems.at[pl.ds(4 * ndp, 6)],
        [
            (o_mine, mixed.at[c]),
            (o_recv, mixed.at[1 - c]),
            (xo.at[mine[0] // 2], x_s.at[0]),
            (xo.at[mine[1] // 2], x_s.at[1]),
            (cot_a, cot.at[group]),
            (cot_b, cot.at[1 - group]),
        ],
    )
    wait(weights)
    count = ndp * parts
    rd = D // count
    for half in range(2):
        lanes = slice(half * HALF, (half + 1) * HALF)
        whole = w[half].reshape(count, 9 * rd, HALF)
        wo_s[:, lanes] = whole[:, 8 * rd :].reshape(D, HALF)
        for s in range(SLABS):
            wi_s[s, :, lanes] = whole[:, (4 + s) * rd : (5 + s) * rd].reshape(D, HALF)
        wb_s[:, lanes] = whole[:, : 4 * rd].reshape(FF, HALF)
    wait(acts)
    alpha_attn, alpha_ffn = alphas[0], alphas[1]

    def tile(t, sums):
        rows = pl.ds(pl.multiple_of(t * BLOCK, BLOCK), BLOCK)
        attn = dot(mixed[0, t], wo_s[:HALF, :]) + dot(mixed[1, t], wo_s[HALF:, :]) + bo[...]
        x1 = x_s[t].astype(F32) + alpha_attn * attn
        hidden = x1.astype(BF)
        h_s[rows, :] = hidden
        dy = cot[t].astype(F32)
        dff = (alpha_ffn * dy).astype(BF)
        dff_s[rows, :] = dff
        ff = jnp.zeros((BLOCK, D), F32) + bb[...]
        dx = dy
        for s in range(SLABS):
            lanes = slice(s * D, (s + 1) * D)
            pre = dot(hidden, wi_s[s]) + bi[:, lanes]
            square = pre * pre
            t_ = jnp.tanh(GELU_C * pre * (1.0 + 0.044715 * square))
            half_up = 0.5 * (1.0 + t_)
            r = (pre * half_up).astype(BF)
            slope = half_up + 0.5 * pre * (1.0 - t_ * t_) * (GELU_C * (1.0 + 3.0 * 0.044715 * square))
            r_s[rows, lanes] = r
            ff = ff + dot(r, wb_s[lanes, :])
            dr = ndot(dff, wb_s[lanes, :]).astype(BF).astype(F32)
            dpre = (dr * slope).astype(BF)
            dpre_s[rows, lanes] = dpre
            dx = dx + ndot(dpre, wi_s[s])
        out[t] = (x1 + alpha_ffn * ff).astype(BF)
        dx1[t] = dx
        dattn = (alpha_attn * dx).astype(BF)
        dattn_s[rows, :] = dattn
        d_both[0, t] = ndot(dattn, wo_s[:HALF, :]).astype(BF)
        d_both[1, t] = ndot(dattn, wo_s[HALF:, :]).astype(BF)
        return (sums[0] + jnp.sum(dx * attn, axis=0, keepdims=True), sums[1] + jnp.sum(dy * ff, axis=0, keepdims=True))

    zero = jnp.zeros((1, D), F32)
    sum_attn, sum_ffn = lax.fori_loop(0, 2, tile, (zero, zero))
    done = moves(
        sems, [(d_both.at[c], d_mine_o), (d_both.at[1 - c], d_send_o), (out, out_o), (dx1, dx1_o)]
    )
    ga[...] = jnp.concatenate([sum_attn, sum_ffn], axis=0)
    dff, dattn, hidden = dff_s[...], dattn_s[...], h_s[...]
    gb_o[...] = jnp.sum(dattn.astype(F32), axis=0, keepdims=True)
    gb_b[...] = jnp.sum(dff.astype(F32), axis=0, keepdims=True)
    ht = flip(hidden)

    def put(first, value):
        size = value.shape[0] // count
        for half in range(2):
            part = value[:, half * HALF : (half + 1) * HALF].astype(BF).reshape(count, size, HALF)
            g_s[half, :, first : first + size, :] = part

    per = count // SLABS
    for s in range(SLABS):
        lanes = slice(s * D, (s + 1) * D)
        dpre = dpre_s[:, lanes]
        gb_i[:, lanes] = jnp.sum(dpre.astype(F32), axis=0, keepdims=True)
        put((4 + s) * rd, dot(ht, dpre))
        g_back = dot(flip(r_s[:, lanes]), dff)
        for half in range(2):
            part = g_back[:, half * HALF : (half + 1) * HALF].astype(BF).reshape(per, 4 * rd, HALF)
            g_s[half, s * per : (s + 1) * per, : 4 * rd, :] = part
    both = jnp.concatenate([mixed[0].reshape(2 * BLOCK, HALF), mixed[1].reshape(2 * BLOCK, HALF)], axis=1)
    put(8 * rd, dot(flip(both), dattn))
    done += moves(sems.at[pl.ds(4, 2)], [(g_s.at[c], g_keep), (g_s.at[1 - c], g_send)])
    wait(done)


def back_blocks(blocks, kn, vn, kt, q_in, d_in, ot, lse, dk_s, dv_s, dq_out, scratch):
    qz, qzt, oz, ozt, dq_s, p_s, dp_s = scratch
    rows = lax.broadcasted_iota(jnp.int32, (HALF, BLOCK), 0) // HEAD_DIM
    lanes = lax.broadcasted_iota(jnp.int32, (BLOCK, HALF), 1) // HEAD_DIM
    gq = jnp.zeros((1, HALF), F32)
    for i, block in enumerate(blocks):
        q, d_o = q_in[i].astype(F32), d_in[i].astype(F32)
        qt, dot_ = q.T, d_o.T
        product = dot_ * ot[i]
        deltas = []
        for h in range(CORE_HEADS):
            head = slice(h * HEAD_DIM, (h + 1) * HEAD_DIM)
            deltas.append(jnp.sum(product[head], axis=0, keepdims=True))
            qz[h] = jnp.where(lanes == h, q, 0.0).astype(BF)
            oz[h] = jnp.where(lanes == h, d_o, 0.0).astype(BF)
            qzt[h] = jnp.where(rows == h, qt, 0.0).astype(BF)
            ozt[h] = jnp.where(rows == h, dot_, 0.0).astype(BF)
        dq_s[...] = jnp.zeros_like(dq_s)

        def chunk(first, count):
            size = count * BLOCK
            keys = kn[pl.ds(first, count)].reshape(size, HALF)
            values = vn[pl.ds(first, count)].reshape(size, HALF)
            for h in range(CORE_HEADS):
                p_s[h, :size] = dot(keys, qzt[h])
                dp_s[h, :size] = dot(values, ozt[h])
            dk = dk_s[pl.ds(first, count)].reshape(size, HALF)
            dv = dv_s[pl.ds(first, count)].reshape(size, HALF)
            for h in range(CORE_HEADS):
                head = slice(h * HEAD_DIM, (h + 1) * HEAD_DIM)
                p = jnp.exp(p_s[h, :size] - lse[i, h : h + 1, :])
                ds = (p * (dp_s[h, :size] - deltas[h])).astype(BF)
                dv = dv + dot(p.astype(BF), oz[h])
                dk = dk + dot(ds, qz[h])
                dq = dq_s[head, :]
                for j in range(count):
                    dq = dq + dot(kt[first + j, head, :], ds[j * BLOCK : (j + 1) * BLOCK])
                dq_s[head, :] = dq
            dk_s[pl.ds(first, count)] = dk.reshape(count, BLOCK, HALF)
            dv_s[pl.ds(first, count)] = dv.reshape(count, BLOCK, HALF)

        over_keys(block, chunk)
        dq = (dq_s[...] * (1.0 / math.sqrt(HEAD_DIM))).T.astype(BF)
        gq = gq + jnp.sum(dq.astype(F32), axis=0, keepdims=True)
        dq_out[i] = dq
    return gq


def back_first(nz, ids, kn_in, vn_in, q_in, ot_in, lse, d_in, dk_out, dv_out, dq_out, gq_out, *refs):
    kn, vn, kt, qn, ot, d_o, dk_s, dv_s, dq_all = refs[:9]
    scratch, sems = refs[9:16], refs[16]
    loads = moves(sems, [(kn_in, kn), (vn_in, vn), (q_in, qn), (ot_in, ot), (d_in, d_o)])
    dk_s[...] = jnp.zeros_like(dk_s)
    dv_s[...] = jnp.zeros_like(dv_s)
    wait(loads)
    for block in range(2 * nz):
        kt[block] = flip(kn[block])
    blocks = query_blocks(ids[0], ids[1], nz)
    gq_out[...] = back_blocks(blocks[:2], kn, vn, kt, qn, d_o, ot, lse, dk_s, dv_s, dq_all, scratch)
    wait(moves(sems, [(dk_s, dk_out), (dv_s, dv_out), (dq_all, dq_out)]))


def back_second(nz, ndp, rs, rr, *refs):
    (ids, xo, xs, wa, wb, kn_in, vn_in, q_in, ot_in, lse, d_in, dk_in, dv_in, dq_in, gq_in, dx1_in) = refs[:16]
    (gb_o, gb_i, gb_b, ga, dx_keep, dx_send, dw_out) = refs[16:23]
    (xall, wq, kn, vn, kt, qn, ot, d_o, dk_s, dv_s, dq_mine, dq_other, dx1, dqkv, dxs, dw, spread) = refs[23:40]
    scratch, sems = refs[40:47], refs[47]
    z, c = ids[0], ids[1]
    loads = moves(
        sems,
        [(kn_in, kn), (vn_in, vn), (q_in, qn), (ot_in, ot), (d_in, d_o), (dk_in, dk_s), (dv_in, dv_s), (dq_in, dq_mine), (dx1_in, dx1)],
    )
    late = moves(
        sems.at[pl.ds(9, 2 * ndp + 2 * nz)],
        [(wa.at[dp], wq.at[2 * dp]) for dp in range(ndp)]
        + [(wb.at[dp], wq.at[2 * dp + 1]) for dp in range(ndp)]
        + [(xo.at[s], xall.at[2 * s + c]) for s in range(nz)]
        + [(xs.at[s], xall.at[2 * s + 1 - c]) for s in range(nz)],
    )
    dqkv[:, :, :HALF] = jnp.zeros((2 * nz, BLOCK, HALF), BF)
    wait(loads)
    for block in range(2 * nz):
        kt[block] = flip(kn[block])
    blocks = query_blocks(z, c, nz)
    gq = gq_in[...] + back_blocks(blocks[2:], kn, vn, kt, qn, d_o, ot, lse, dk_s, dv_s, dq_other, scratch)
    for i in range(2):
        dqkv[blocks[i], :, :HALF] = dq_mine[i]
        dqkv[blocks[2 + i], :, :HALF] = dq_other[i]
    wait(late)
    w_all = wq[:, :, : 3 * HALF].reshape(D, 3 * HALF)

    def finish(block, gv):
        dv = dv_s[block].astype(BF)
        dqkv[block, :, HALF : 2 * HALF] = dk_s[block].astype(BF)
        dqkv[block, :, 2 * HALF :] = dv
        dxs[block] = ndot(dqkv[block], w_all)
        return gv + jnp.sum(dv.astype(F32), axis=0, keepdims=True)

    gv = lax.fori_loop(0, 2 * nz, finish, jnp.zeros((1, HALF), F32))
    for i in range(2):
        dxs[blocks[i]] = dxs[blocks[i]] + dx1[i]
    for s in range(nz):
        dx_keep[s] = dxs[2 * s + c].astype(BF)
        dx_send[s] = dxs[2 * s + 1 - c].astype(BF)
    acc = dot(flip(xall[0]), dqkv[0])
    for block in range(1, 2 * nz):
        acc = acc + dot(flip(xall[block]), dqkv[block])
    dw[:, : 3 * HALF] = acc.astype(BF)
    nothing = jnp.zeros((1, HALF), F32)
    own = [jnp.concatenate([jnp.where(c == 0, g, nothing), jnp.where(c == 0, nothing, g)], axis=1) for g in (gq, gv)]
    tile = jnp.concatenate(own + [gb_o[...], gb_b[...], jnp.zeros((124, D), F32)], axis=0).T
    spread[...] = jnp.broadcast_to(gb_i[...], (128, FF)).T.reshape(D // rr, SLABS, rr, 128)
    lanes = lax.broadcasted_iota(jnp.int32, (D // rr, rr, 128), 2)
    tile = tile.reshape(D // rr, rr, 128)
    for s in range(SLABS):
        tile = jnp.where(lanes == 4 + s, spread[:, s], tile)
    tile = tile.reshape(D, 128)
    if rs >= 16:
        me = ids[2]
        lane = lax.broadcasted_iota(jnp.int32, (D, 128), 1) - 8 - 6 * (me // rs)
        mine = lax.rem(lax.broadcasted_iota(jnp.int32, (D, 128), 0), rs) == lax.rem(me, rs)
        gates = jnp.sum(ga[...], axis=1, keepdims=True)
        for which in range(2):
            rest = gates[which : which + 1]
            for i in range(3):
                high = rest.astype(BF).astype(F32)
                tile = jnp.where(mine & (lane == 2 * i + which), high, tile)
                rest = rest - high
    dw[:, 3 * HALF :] = tile.astype(BF)
    wait(moves(sems, [(dw, dw_out)]))


def shape(dims, kind):
    return jax.ShapeDtypeStruct(dims, kind)


def cost(flops, size, trans=0):
    return pl.CostEstimate(flops=int(flops), bytes_accessed=int(size), transcendentals=int(trans))


def after(array, *others):
    return lax.optimization_barrier((array,) + others)[0]


def make_body(n1, n2, nz):
    ndp = n1 * n2
    nsh = ndp * nz * 2
    rs = D // nsh
    rd = D // ndp
    half = nz // 2
    parts = 2 * nz if rs % 16 == 0 else 1
    rr = rd // parts
    swap = [(0, 1), (1, 0)]

    def bits(count):
        return [1 << i for i in range(count.bit_length() - 1)]

    def place(k, c):
        return (k if k % 2 == c else nz - 1 - k) // 2

    near, far = [], []
    for k in range(half):
        for c in range(2):
            src = place(k, c)
            near += [(2 * src + c, 2 * k + c), (2 * (half + src) + c, 2 * (half + k) + c)]
            far += [(2 * (half + src) + c, 2 * k + c), (2 * src + c, 2 * (half + k) + c)]
    near_back = [(d, s) for s, d in near]
    far_back = [(d, s) for s, d in far]

    def pick(array, index, axis=0):
        return lax.dynamic_index_in_dim(array, index, axis, keepdims=False)

    def by_bit(bit, own, other, axis=0):
        return jnp.where(bit == 0, jnp.stack([own, other], axis), jnp.stack([other, own], axis))

    def exchange(array, name, count, bit):
        return lax.ppermute(array, name, [(s, s ^ bit) for s in range(count)])

    def gather(array, name, count, lead=0):
        me = lax.axis_index(name)
        for i, bit in enumerate(reversed(bits(count))):
            array = by_bit((me // bit) % 2, array, exchange(array, name, count, bit), lead + i)
        dims = array.shape
        return array.reshape(dims[:lead] + (count,) + dims[lead + len(bits(count)) :])

    def scatter(array, name, count, lead=0, last=BF):
        me = lax.axis_index(name)
        steps = bits(count)
        dims = array.shape
        array = array.reshape(dims[:lead] + (2,) * len(steps) + dims[lead + 1 :])
        for i, bit in enumerate(steps):
            axis = lead + len(steps) - 1 - i
            mine = (me // bit) % 2
            got = exchange(pick(array, 1 - mine, axis).astype(BF), name, count, bit)
            array = pick(array, mine, axis).astype(F32) + got.astype(F32)
            array = array.astype(last if i == len(steps) - 1 else BF)
        return array

    def gather_dp_1(rows):
        cut = rows.shape[0] // 2
        return gather(rows[:cut], "b", n2), gather(rows[cut:], "a", n1)

    def gather_dp_2(first, second):
        dims = (ndp,) + first.shape[1:]
        return gather(first, "a", n1).reshape(dims), gather(second, "b", n2, 1).reshape(dims)

    def scatter_dp_1(whole):
        w5 = whole.reshape((n1, n2) + whole.shape[1:])
        return scatter(w5[:, :, 0], "b", n2, 1), scatter(w5[:, :, 1], "a", n1)

    def scatter_dp_2(first, second):
        return jnp.concatenate([scatter(first, "a", n1), scatter(second, "b", n2)], axis=0)

    def body(inputs, w_qkv, bias_qv, w_out, bias_out, w_in, bias_in, w_back, bias_back, alphas, cotangent):
        z, c = lax.axis_index("z"), lax.axis_index("c")
        group = z // half
        device = ((lax.axis_index("a") * n2 + lax.axis_index("b")) * nz + z) * 2 + c
        ids = jnp.stack([z, c, device, z, group]).astype(jnp.int32)

        xo = by_bit(group, pick(inputs, group), exchange(pick(inputs, 1 - group), "z", nz, half))
        for i, bit in enumerate(reversed(bits(half))):
            xo = by_bit((z // bit) % 2, xo, exchange(xo, "z", nz, bit), 1 + i)
        xo = xo.reshape(nz, BLOCK, D)
        xs = lax.ppermute(xo, "c", swap)

        def heads(which):
            return jnp.concatenate(
                [lax.dynamic_slice_in_dim(w_qkv, i * D + which * HALF, HALF, 1) for i in range(3)] + [tile], axis=1
            )

        tile = jnp.stack([bias_qv[0], bias_qv[1], bias_out, bias_back] + [bias_in[i * rs : (i + 1) * rs] for i in range(SLABS)])
        tile = jnp.pad(tile.T, ((0, 0), (0, 120)))
        wq_chip = by_bit(c, heads(c), lax.ppermute(heads(1 - c), "c", swap)).reshape(2 * rs, WQ)
        wq_dp = gather(wq_chip, "z", nz).reshape(rd, WQ)
        if parts == 1:
            hidden_bias = wq_dp[:, 3 * HALF + 4 : 3 * HALF + 8].reshape(2 * nz, rs, SLABS)
            hidden_bias = jnp.transpose(hidden_bias, (0, 2, 1)).reshape(SLABS, rd).T
            wq_dp = jnp.concatenate(
                [wq_dp[:, : 3 * HALF + 4], hidden_bias, wq_dp[:, 3 * HALF + 8 :]], axis=1
            )
        wq_a1, wq_b1 = gather_dp_1(wq_dp)
        wq_a, wq_b = gather_dp_2(wq_a1, wq_b1)

        def columns(which):
            def cut(array, first):
                return lax.dynamic_slice_in_dim(array, first + which * HALF, HALF, 1)

            return jnp.concatenate([cut(w_back, 0)] + [cut(w_in, s * D) for s in range(SLABS)] + [cut(w_out, 0)], axis=0)

        wf_chip = by_bit(c, columns(c), lax.ppermute(columns(1 - c), "c", swap))
        wf = gather(wf_chip, "z", nz)
        if parts == 1:
            wf = jnp.concatenate(
                [wf[:, :, : 4 * rs].reshape(4 * rd, HALF)]
                + [wf[:, :, (4 + s) * rs : (5 + s) * rs].reshape(rd, HALF) for s in range(SLABS)]
                + [wf[:, :, 8 * rs :].reshape(rd, HALF)],
                axis=0,
            )
        wf_a1, wf_b1 = gather_dp_1(after(wf.reshape(9 * rd, HALF), wq_a1, wq_b1))
        wf_a1, wf_b1 = lax.optimization_barrier((wf_a1, wf_b1, wq_a, wq_b))[:2]
        wf_a, wf_b = gather_dp_2(wf_a1, wf_b1)

        cot = after(cotangent, xo)
        cot_a = lax.ppermute(pick(cot, group), ("z", "c"), near)
        cot_b = lax.ppermute(pick(cot, 1 - group), ("z", "c"), far)

        nb = 2 * nz
        pairs = (nb + 1) * CORE_HEADS * BLOCK * BLOCK
        heads_t = pltpu.VMEM((CORE_HEADS, HALF, BLOCK), BF)
        scores = pltpu.VMEM((CORE_HEADS, 2 * BLOCK, BLOCK), F32)
        scratch = [
            heads_t,
            scores,
            pltpu.VMEM((CORE_HEADS, 1, BLOCK), F32),
            pltpu.VMEM((CORE_HEADS, 1, BLOCK), F32),
            pltpu.VMEM((HALF, BLOCK), F32),
        ]
        natural, turned = (nb, BLOCK, HALF), (nb, HALF, BLOCK)
        two, two_t = (2, BLOCK, HALF), (2, HALF, BLOCK)
        two_lse = (2, CORE_HEADS, BLOCK)
        wq_shape = (2 * ndp, rd // 2, WQ)
        xo_1, xs_1, wq_a1_, wq_b1_, _, _ = lax.optimization_barrier((xo, xs, wq_a, wq_b, wf_a1, wf_b1))
        (kn, vn, vt, q_mine, q_other, ot_other, lse_other, o_send, bo, bb, bi) = pl.pallas_call(
            functools.partial(first_kernel, nz, ndp, rr),
            out_shape=(
                shape(natural, BF),
                shape(natural, BF),
                shape(turned, BF),
                shape(two, BF),
                shape(two, BF),
                shape(two_t, F32),
                shape(two_lse, F32),
                shape(two, BF),
                shape((1, D), F32),
                shape((1, D), F32),
                shape((1, FF), F32),
            ),
            in_specs=[SMEM] + [ANY] * 4,
            out_specs=(HBM,) * 6 + (VMEM, HBM) + (VMEM,) * 3,
            scratch_shapes=[
                pltpu.VMEM((nb, BLOCK, D), BF),
                pltpu.VMEM(wq_shape, BF),
                pltpu.VMEM(natural, BF),
                pltpu.VMEM(natural, BF),
                pltpu.VMEM(turned, BF),
                pltpu.VMEM(two, BF),
                pltpu.VMEM(two, BF),
                pltpu.VMEM(two_t, F32),
                pltpu.VMEM(two, BF),
                pltpu.VMEM((D // rr, SLABS, rr, 128), F32),
            ]
            + scratch
            + [pltpu.SemaphoreType.DMA((2 * ndp + 2 * nz,))],
            compiler_params=pltpu.CompilerParams(vmem_limit_bytes=(20 if nz == 4 else 40) * 2**20),
            cost_estimate=cost(4 * pairs * HALF, 8 * 2**20, pairs),
            name="first",
        )(ids, xo_1, xs_1, wq_a1_, wq_b1_)
        o_recv = lax.ppermute(o_send, "c", swap)
        q_mine_2, wf_a, wf_b = lax.optimization_barrier((q_mine, wf_a, wf_b))
        wf_c, wf_d = lax.ppermute(wf_a, "c", swap), lax.ppermute(wf_b, "c", swap)
        ot_mine, lse_mine, o_mine = pl.pallas_call(
            functools.partial(second_kernel, nz),
            out_shape=(shape(two_t, F32), shape(two_lse, F32), shape(two, BF)),
            in_specs=[SMEM] + [HBM] * 3,
            out_specs=(HBM, VMEM, HBM),
            scratch_shapes=[
                pltpu.VMEM(natural, BF),
                pltpu.VMEM(turned, BF),
                pltpu.VMEM(two, BF),
                pltpu.VMEM(two_t, F32),
                pltpu.VMEM(two, BF),
            ]
            + scratch
            + [pltpu.SemaphoreType.DMA((3,))],
            compiler_params=pltpu.CompilerParams(vmem_limit_bytes=16 * 2**20),
            cost_estimate=cost(4 * pairs * HALF, 4 * 2**20, pairs),
            name="second",
        )(ids, kn, vt, q_mine_2)

        nh = 9 * rd // 2
        grouped = (ndp * parts, 9 * rd // parts, HALF)
        (out, dx1, d_mine, d_send, g_keep, g_send, gb_o, gb_i, gb_b, ga) = pl.pallas_call(
            functools.partial(ffn_kernel, nz, ndp, parts),
            out_shape=(
                shape((2, BLOCK, D), BF),
                shape((2, BLOCK, D), F32),
                shape(two, BF),
                shape(two, BF),
                shape(grouped, BF),
                shape(grouped, BF),
                shape((1, D), F32),
                shape((1, FF), F32),
                shape((1, D), F32),
                shape((2, D), F32),
            ),
            in_specs=[SMEM, SMEM] + [ANY] * 5 + [VMEM] * 3 + [ANY] * 4,
            out_specs=(HBM,) * 6 + (VMEM,) * 4,
            scratch_shapes=[
                pltpu.VMEM((2, 2 * ndp, nh, HALF), BF),
                pltpu.VMEM((D, D), BF),
                pltpu.VMEM((SLABS, D, D), BF),
                pltpu.VMEM((FF, D), BF),
                pltpu.VMEM((2, 2, BLOCK, HALF), BF),
                pltpu.VMEM((2, BLOCK, D), BF),
                pltpu.VMEM((2, BLOCK, D), BF),
                pltpu.VMEM((2 * BLOCK, D), BF),
                pltpu.VMEM((2 * BLOCK, FF), BF),
                pltpu.VMEM((2 * BLOCK, FF), BF),
                pltpu.VMEM((2 * BLOCK, D), BF),
                pltpu.VMEM((2 * BLOCK, D), BF),
                pltpu.VMEM((2,) + grouped, BF),
                pltpu.VMEM((2, BLOCK, D), BF),
                pltpu.VMEM((2, BLOCK, D), F32),
                pltpu.VMEM((2, 2, BLOCK, HALF), BF),
                pltpu.SemaphoreType.DMA((4 * ndp + 6,)),
            ],
            compiler_params=pltpu.CompilerParams(vmem_limit_bytes=36 * 2**20),
            cost_estimate=cost(6 * 2 * BLOCK * 9 * D * HALF * 2, 20 * 2**20, 2 * BLOCK * FF),
            name="ffn",
        )(ids, alphas, o_mine, o_recv, xo, cot_a, cot_b, bo, bi, bb, wf_a, wf_b, wf_c, wf_d)
        d_recv = lax.ppermute(d_send, "c", swap)

        out_a = lax.ppermute(pick(out, group), ("z", "c"), near_back)
        out_b = lax.ppermute(pick(out, 1 - group), ("z", "c"), far_back)
        outputs = by_bit(group, out_a, out_b)

        back_scratch = [
            pltpu.VMEM((CORE_HEADS, BLOCK, HALF), BF),
            heads_t,
            pltpu.VMEM((CORE_HEADS, BLOCK, HALF), BF),
            heads_t,
            pltpu.VMEM((HALF, BLOCK), F32),
            scores,
            scores,
        ]
        dk, dv, dq_mine, gq = pl.pallas_call(
            functools.partial(back_first, nz),
            out_shape=(shape(natural, F32), shape(natural, F32), shape(two, BF), shape((1, HALF), F32)),
            in_specs=[SMEM] + [HBM] * 4 + [VMEM, HBM],
            out_specs=(HBM,) * 3 + (VMEM,),
            scratch_shapes=[
                pltpu.VMEM(natural, BF),
                pltpu.VMEM(natural, BF),
                pltpu.VMEM(turned, BF),
                pltpu.VMEM(two, BF),
                pltpu.VMEM(two_t, F32),
                pltpu.VMEM(two, BF),
                pltpu.VMEM(natural, F32),
                pltpu.VMEM(natural, F32),
                pltpu.VMEM(two, BF),
            ]
            + back_scratch
            + [pltpu.SemaphoreType.DMA((5,))],
            compiler_params=pltpu.CompilerParams(vmem_limit_bytes=(24 if nz == 4 else 40) * 2**20),
            cost_estimate=cost(10 * pairs * HALF, 10 * 2**20, pairs),
            name="back_first",
        )(ids, kn, vn, q_mine, ot_mine, lse_mine, d_mine)

        g_all = (g_keep.astype(F32) + lax.ppermute(g_send, "c", swap).astype(F32)).astype(BF)
        g_a1, g_b1 = scatter_dp_1(g_all.reshape(ndp, 2, nh, HALF))
        g_dp = scatter_dp_2(g_a1, g_b1)
        if parts == 1:
            g_dp = jnp.concatenate(
                [g_dp[: 4 * rd].reshape(nz, 2, 4 * rs, HALF)]
                + [g_dp[(4 + s) * rd : (5 + s) * rd].reshape(nz, 2, rs, HALF) for s in range(SLABS)]
                + [g_dp[8 * rd :].reshape(nz, 2, rs, HALF)],
                axis=2,
            )
        g_mine = scatter(g_dp.reshape(nz, 2, 9 * rs, HALF), "z", nz, 0, F32)
        g_own = pick(g_mine, c)
        g_other = lax.ppermute(pick(g_mine, 1 - c).astype(BF), "c", swap).astype(F32)
        g_whole = by_bit(c, g_own, g_other)
        grad_w_back = jnp.transpose(g_whole[:, : 4 * rs], (1, 0, 2)).reshape(4 * rs, D)
        grad_w_in = jnp.transpose(
            g_whole[:, 4 * rs : 8 * rs].reshape(2, SLABS, rs, HALF), (2, 1, 0, 3)
        ).reshape(rs, FF)
        grad_w_out = jnp.transpose(g_whole[:, 8 * rs :], (1, 0, 2)).reshape(rs, D)

        d_recv, _ = lax.optimization_barrier((d_recv, g_all))
        dx_keep, dx_send, dw = pl.pallas_call(
            functools.partial(back_second, nz, ndp, rs, rr),
            out_shape=(shape((nz, BLOCK, D), BF), shape((nz, BLOCK, D), BF), shape((D, WQ), BF)),
            in_specs=[SMEM] + [HBM] * 8 + [VMEM] + [HBM] * 4 + [VMEM, HBM] + [VMEM] * 4,
            out_specs=(VMEM, VMEM, HBM),
            scratch_shapes=[
                pltpu.VMEM((nb, BLOCK, D), BF),
                pltpu.VMEM(wq_shape, BF),
                pltpu.VMEM(natural, BF),
                pltpu.VMEM(natural, BF),
                pltpu.VMEM(turned, BF),
                pltpu.VMEM(two, BF),
                pltpu.VMEM(two_t, F32),
                pltpu.VMEM(two, BF),
                pltpu.VMEM(natural, F32),
                pltpu.VMEM(natural, F32),
                pltpu.VMEM(two, BF),
                pltpu.VMEM(two, BF),
                pltpu.VMEM((2, BLOCK, D), F32),
                pltpu.VMEM((nb, BLOCK, 3 * HALF), BF),
                pltpu.VMEM((nb, BLOCK, D), F32),
                pltpu.VMEM((D, WQ), BF),
                pltpu.VMEM((D // rr, SLABS, rr, 128), F32),
            ]
            + back_scratch
            + [pltpu.SemaphoreType.DMA((9 + 2 * ndp + 2 * nz,))],
            compiler_params=pltpu.CompilerParams(vmem_limit_bytes=(40 if nz == 4 else 60) * 2**20),
            cost_estimate=cost(12 * pairs * HALF, 12 * 2**20, pairs),
            name="back_second",
        )(
            ids, xo, xs, wq_a, wq_b, kn, vn, q_other, ot_other, lse_other, d_recv, dk, dv, dq_mine, gq, dx1,
            gb_o, gb_i, gb_b, ga,
        )

        dx_sum = (dx_keep.astype(F32) + lax.ppermute(dx_send, "c", swap).astype(F32)).astype(BF)
        dx = dx_sum
        dx = dx.reshape((2,) * len(bits(nz)) + (BLOCK, D))
        for bit in bits(half):
            axis = dx.ndim - 3
            mine = (z // bit) % 2
            got = exchange(pick(dx, 1 - mine, axis), "z", nz, bit)
            dx = (pick(dx, mine, axis).astype(F32) + got.astype(F32)).astype(BF)
        grad_inputs = by_bit(group, pick(dx, group), exchange(pick(dx, 1 - group), "z", nz, half))

        dw = after(dw, dx_sum)
        dw_dp = scatter_dp_2(*scatter_dp_1(dw.reshape(ndp, 2, rd // 2, WQ)))
        if parts == 1:
            hidden_bias = dw_dp[:, 3 * HALF + 4 : 3 * HALF + 8].T.reshape(2 * nz, SLABS, rs)
            hidden_bias = jnp.transpose(hidden_bias, (0, 2, 1)).reshape(rd, SLABS)
            dw_dp = jnp.concatenate(
                [dw_dp[:, : 3 * HALF + 4], hidden_bias, dw_dp[:, 3 * HALF + 8 :]], axis=1
            )
        dw_mine = scatter(dw_dp.reshape(nz, 2, rs, WQ), "z", nz, 0, F32)
        dw_own = pick(dw_mine, c)
        dw_other = lax.ppermute(pick(dw_mine, 1 - c).astype(BF), "c", swap).astype(F32)
        first, second = jnp.where(c == 0, dw_own, dw_other), jnp.where(c == 0, dw_other, dw_own)
        grad_w_qkv = jnp.concatenate(
            [half_[:, i * HALF : (i + 1) * HALF] for i in range(3) for half_ in (first, second)], axis=1
        )
        sums = (dw_own + dw_other)[:, 3 * HALF :]
        by_row = sums[:, :8].T
        if rs >= 16:
            lane = jnp.arange(128, dtype=jnp.int32)
            grad_alphas = jnp.stack(
                [jnp.sum(jnp.where((lane >= 8) & (lane % 2 == which), sums, 0.0)) for which in range(2)]
            )
        else:
            grad_alphas = lax.psum(jnp.sum(ga, axis=1), MESH_AXES)
        return (
            outputs,
            grad_inputs,
            grad_w_qkv,
            by_row[:2],
            grad_w_out,
            by_row[2],
            grad_w_in,
            by_row[4:].reshape(SLABS * rs),
            grad_w_back,
            by_row[3],
            grad_alphas,
        )

    return body


def solution(mesh):
    ndp, nseq = mesh.devices.shape
    n1 = math.isqrt(ndp)
    n2 = ndp // n1
    nz = nseq // 2
    fine = Mesh(mesh.devices.reshape(n1, n2, nz, 2), MESH_AXES)
    dp, seq = ("a", "b"), ("z", "c")
    rows = P(dp, seq, None)
    both = dp + seq
    return jax.shard_map(
        make_body(n1, n2, nz),
        mesh=fine,
        in_specs=(
            rows,
            P(both, None),
            P(None, both),
            P(both, None),
            P(both),
            P(both, None),
            P(both),
            P(both, None),
            P(both),
            P(),
            rows,
        ),
        out_specs=(
            rows,
            rows,
            P(both, None),
            P(None, both),
            P(both, None),
            P(both),
            P(both, None),
            P(both),
            P(both, None),
            P(both),
            P(),
        ),
        check_vma=False,
    )
```

```python
import functools
import math

import jax
import jax.numpy as jnp
from jax import lax
from jax.experimental import pallas as pl
from jax.experimental.pallas import tpu as pltpu
from jax.sharding import Mesh, PartitionSpec as P

D = 512
HEADS = 8
HEAD_DIM = 64
FF = 2048
BLOCK = 256
HALF = D // 2
CORE_HEADS = HEADS // 2
SLABS = FF // D
BF = jnp.bfloat16
F32 = jnp.float32
MESH_AXES = ("a", "b", "z", "c")
VMEM = pl.BlockSpec(memory_space=pltpu.VMEM)
SMEM = pl.BlockSpec(memory_space=pltpu.SMEM)
ANY = pl.BlockSpec(memory_space=pl.ANY)
WQ = 3 * HALF + 128
GELU_C = math.sqrt(2.0 / math.pi)


def dot(left, right):
    return jnp.dot(left, right, preferred_element_type=F32)


def ndot(left, right):
    return lax.dot_general(left, right, (((1,), (1,)), ((), ())), preferred_element_type=F32)


def flip(block):
    return block.astype(F32).T.astype(BF)


def query_blocks(z, c, nz):
    near, far = 2 * z, 2 * (nz - 1 - z)
    return (near + c, far + c, near + 1 - c, far + 1 - c)


def over_keys(block, chunk):
    def step(i, unused):
        chunk(2 * i, 2)
        return unused

    lax.fori_loop(0, (block + 1) // 2, step, 0)

    @pl.when(lax.rem(block, 2) == 0)
    def _():
        chunk(block, 1)


def attend_blocks(blocks, kn, vt, qn, ot, lse, o, scratch):
    qz, s_s, m_s, l_s, acc_s = scratch
    rows = lax.broadcasted_iota(jnp.int32, (HALF, BLOCK), 0) // HEAD_DIM
    for i, block in enumerate(blocks):
        qt = qn[i].astype(F32).T
        for h in range(CORE_HEADS):
            qz[h] = jnp.where(rows == h, qt, 0.0).astype(BF)
        m_s[...] = jnp.full_like(m_s, -1e30)
        l_s[...] = jnp.zeros_like(l_s)
        acc_s[...] = jnp.zeros_like(acc_s)

        def chunk(first, count):
            keys = kn[pl.ds(first, count)].reshape(count * BLOCK, HALF)
            for h in range(CORE_HEADS):
                s_s[h, : count * BLOCK] = dot(keys, qz[h])
            for h in range(CORE_HEADS):
                head = slice(h * HEAD_DIM, (h + 1) * HEAD_DIM)
                s = s_s[h, : count * BLOCK]
                old = m_s[h]
                new = jnp.maximum(old, jnp.max(s, axis=0, keepdims=True))
                p = jnp.exp(s - new)
                shrink = jnp.exp(old - new)
                m_s[h] = new
                l_s[h] = l_s[h] * shrink + jnp.sum(p, axis=0, keepdims=True)
                p = p.astype(BF)
                acc = acc_s[head, :] * shrink
                for j in range(count):
                    acc = acc + dot(vt[first + j, head, :], p[j * BLOCK : (j + 1) * BLOCK])
                acc_s[head, :] = acc

        over_keys(block, chunk)
        for h in range(CORE_HEADS):
            head = slice(h * HEAD_DIM, (h + 1) * HEAD_DIM)
            total = l_s[h]
            lse[i, h : h + 1, :] = m_s[h] + jnp.log(total)
            acc_s[head, :] = acc_s[head, :] / total
        value = acc_s[...]
        ot[i] = value
        o[i] = value.T.astype(BF)


def moves(sems, pairs):
    copies = [pltpu.make_async_copy(src, dst, sems.at[i]) for i, (src, dst) in enumerate(pairs)]
    for copy in copies:
        copy.start()
    return copies


def wait(copies):
    for copy in copies:
        copy.wait()


def pack_kernel(rs, ids, ins, outs, *refs):
    w_qkv, w_back, w_in, w_out, bias_qv, bias_out, bias_back, bias_in = refs[:8]
    tile, sems = refs[8], refs[9]
    group = ids[4]
    loads = moves(sems, [(ins[i], refs[i]) for i in range(8)])
    rows = moves(
        sems.at[pl.ds(8, 4)],
        [(ins[8 + i].at[which], outs[3 + 2 * i + j]) for i in range(2) for j, which in enumerate((1 - group, group))],
    )
    wait(loads)
    tile[...] = jnp.zeros_like(tile)
    tile[0:2, :rs] = bias_qv[...].astype(F32)
    tile[2:3, :rs] = bias_out[...].astype(F32)
    tile[3:4, :rs] = bias_back[...].astype(F32)
    for i in range(SLABS):
        tile[4 + i : 5 + i, :rs] = bias_in[:, i * rs : (i + 1) * rs].astype(F32)
    turned = tile[...].T[:rs].astype(BF)
    q_keep, f_keep, give = outs[:3]

    def cut(ref, first, core):
        return ref[:, pl.ds(pl.multiple_of(first + core * HALF, HALF), HALF)]

    for i in range(3):
        q_keep[:, i * HALF : (i + 1) * HALF] = cut(w_qkv, i * D, ids[1])
        give[(9 + i) * rs : (10 + i) * rs] = cut(w_qkv, i * D, 1 - ids[1])
    q_keep[:, 3 * HALF :] = turned
    give[12 * rs :, :128] = turned
    give[12 * rs :, 128:] = jnp.zeros((rs, 128), BF)
    for f_out, core in ((f_keep, ids[1]), (give, 1 - ids[1])):
        f_out[: 4 * rs] = cut(w_back, 0, core)
        for i in range(SLABS):
            f_out[(4 + i) * rs : (5 + i) * rs] = cut(w_in, i * D, core)
        f_out[8 * rs : 9 * rs] = cut(w_out, 0, core)
    wait(rows)


def core_kernel(rs, ids, ins, outs):
    q_keep, f_keep, got = ins
    wq, wf = outs
    c = ids[1]
    wq[c] = q_keep[...]
    wf[c] = f_keep[...]
    wf[1 - c] = got[: 9 * rs]
    for i in range(3):
        wq[1 - c, :, i * HALF : (i + 1) * HALF] = got[(9 + i) * rs : (10 + i) * rs]
    wq[1 - c, :, 3 * HALF :] = got[12 * rs :, :128]


def my_bit(ids, where):
    index, bit = where
    return lax.rem(lax.shift_right_logical(ids[index], bit), 2)


def join(ids, own, got, outs, where, post=1):
    mine = my_bit(ids, where)
    pre = own.shape[0] // post
    for p in range(pre):
        out = outs[p * len(outs) // pre]
        at = 2 * p - 2 * pre // len(outs) * (p * len(outs) // pre)
        for q in range(post):
            out[(at + mine) * post + q] = own[p * post + q]
            out[(at + 1 - mine) * post + q] = got[p * post + q]


def first_kernel(nz, ndp, n2, rr, ids, ins, outs, spread, *scratch):
    xo, xs = ins[:2]
    wq_pieces = ins[2:4]
    xall, wq, kn, vn, kt, vt, q_mine, q_other, ot, lse, o, bo, bb, bi = outs
    z, c = ids[0], ids[1]
    for s in range(nz):
        xall[2 * s + c] = xo[s]
        xall[2 * s + 1 - c] = xs[s]
    for far, piece in enumerate(wq_pieces):
        bit = lax.rem(ids[3], 2)
        for j in range(piece.shape[0]):
            wq[(2 * (j // n2) + (1 - bit if far else bit)) * n2 + j % n2] = piece[j]
    bias = wq[:, :, 3 * HALF :].reshape(D, 128).astype(F32)
    turned = bias.T
    bo[...] = turned[2:3]
    bb[...] = turned[3:4]
    lanes = lax.broadcasted_iota(jnp.int32, (D // rr, rr, 128), 2)
    for s in range(SLABS):
        spread[:, s] = jnp.where(lanes == 4 + s, bias.reshape(D // rr, rr, 128), 0.0)
    bi[...] = jnp.sum(spread[...].reshape(FF, 128).T[4:8], axis=0, keepdims=True)
    bias_q = jnp.where(c == 0, turned[0:1, :HALF], turned[0:1, HALF:])
    bias_v = jnp.where(c == 0, turned[1:2, :HALF], turned[1:2, HALF:])
    w_q = wq[:, :, :HALF].reshape(D, HALF)
    w_kv = wq[:, :, HALF : 3 * HALF].reshape(D, 2 * HALF)

    def project(block, unused):
        kv = dot(xall[block], w_kv)
        key = kv[:, :HALF]
        kn[block] = key.astype(BF)
        kt[block] = key.T.astype(BF)
        value = kv[:, HALF:] + bias_v
        vn[block] = value.astype(BF)
        vt[block] = value.T.astype(BF)
        return unused

    lax.fori_loop(0, 2 * nz, project, 0)
    blocks = query_blocks(z, c, nz)
    for i, block in enumerate(blocks):
        q = (dot(xall[block], w_q) + bias_q).astype(BF).astype(F32) * (1.0 / math.sqrt(HEAD_DIM))
        (q_mine if i < 2 else q_other)[i % 2] = q.astype(BF)
    attend_blocks(blocks[2:], kn, vt, q_other, ot, lse, o, scratch)


def place_dp(ids, pieces, ndp, n2, put):
    for i, piece in enumerate(pieces):
        far, half = i // 2, i % 2
        for j in range(ndp // 2):
            if half == 0:
                bit = lax.rem(ids[3], 2)
                dp = (2 * (j // n2) + (1 - bit if far else bit)) * n2 + j % n2
            else:
                bit = lax.rem(ids[5], 2)
                dp = j // (n2 // 2) * n2 + 2 * (j % (n2 // 2)) + (1 - bit if far else bit)
            put(dp, half, piece(j) if callable(piece) else piece[j])


def second_kernel(nz, ids, ins, outs, *scratch):
    kn, vt, qn = ins
    ot, lse, o = outs
    blocks = query_blocks(ids[0], ids[1], nz)
    attend_blocks(blocks[:2], kn, vt, qn, ot, lse, o, scratch)


def ffn_kernel(nz, ndp, n2, parts, ids, ins, outs, *refs):
    alphas, o_mine, got, xall, cot_a, cot_b, bo, bi, bb = ins[:9]
    pieces = ins[9:13]
    rows = pieces[0].shape[1]

    def received(i):
        return lambda j: got[pl.ds(2 * BLOCK + (i * (ndp // 2) + j) * rows, rows)]

    (out_near, out_far, dx1, d_mine, g_keep, give, gb_o, gb_i, gb_b, ga) = outs
    w, wo_s, wi_s, wb_s, mixed, h_s, r_s, dpre_s, dff_s, dattn_s = refs
    c = ids[1]
    for core in range(2):
        own = pieces if core == 0 else [received(i) for i in range(4)]
        which = c if core == 0 else 1 - c

        def put(dp, half, value):
            w[which, 2 * dp + half] = value

        place_dp(ids, own, ndp, n2, put)
    count = ndp * parts
    rd = D // count
    for half in range(2):
        lanes = slice(half * HALF, (half + 1) * HALF)
        whole = w[half].reshape(count, 9 * rd, HALF)
        wo_s[:, lanes] = whole[:, 8 * rd :].reshape(D, HALF)
        for s in range(SLABS):
            wi_s[s, :, lanes] = whole[:, (4 + s) * rd : (5 + s) * rd].reshape(D, HALF)
        wb_s[:, lanes] = whole[:, : 4 * rd].reshape(FF, HALF)
    mixed[c] = o_mine[...]
    mixed[1 - c] = got[: 2 * BLOCK].reshape(2, BLOCK, HALF)
    alpha_attn, alpha_ffn = alphas[0], alphas[1]
    mine = query_blocks(ids[0], c, nz)

    def tile(t, sums):
        rows = pl.ds(pl.multiple_of(t * BLOCK, BLOCK), BLOCK)
        attn = dot(mixed[0, t], wo_s[:HALF, :]) + dot(mixed[1, t], wo_s[HALF:, :]) + bo[...]
        x1 = xall[jnp.where(t == 0, mine[0], mine[1])].astype(F32) + alpha_attn * attn
        hidden = x1.astype(BF)
        h_s[rows, :] = hidden
        dy = jnp.where(t == 0, cot_a[...], cot_b[...]).astype(F32)
        dff = (alpha_ffn * dy).astype(BF)
        dff_s[rows, :] = dff
        ff = jnp.zeros((BLOCK, D), F32) + bb[...]
        dx = dy
        for s in range(SLABS):
            lanes = slice(s * D, (s + 1) * D)
            pre = dot(hidden, wi_s[s]) + bi[:, lanes]
            square = pre * pre
            t_ = jnp.tanh(GELU_C * pre * (1.0 + 0.044715 * square))
            half_up = 0.5 * (1.0 + t_)
            r = (pre * half_up).astype(BF)
            slope = half_up + 0.5 * pre * (1.0 - t_ * t_) * (GELU_C * (1.0 + 3.0 * 0.044715 * square))
            r_s[rows, lanes] = r
            ff = ff + dot(r, wb_s[lanes, :])
            dr = ndot(dff, wb_s[lanes, :]).astype(BF).astype(F32)
            dpre = (dr * slope).astype(BF)
            dpre_s[rows, lanes] = dpre
            dx = dx + ndot(dpre, wi_s[s])
        out = (x1 + alpha_ffn * ff).astype(BF)

        @pl.when(t == 0)
        def _():
            out_near[...] = out

        @pl.when(t == 1)
        def _():
            out_far[...] = out

        dx1[t] = dx
        dattn = (alpha_attn * dx).astype(BF)
        dattn_s[rows, :] = dattn
        d_mine[rows, :] = ndot(dattn, wo_s[pl.ds(pl.multiple_of(c * HALF, HALF), HALF), :]).astype(BF)
        give[rows, :] = ndot(dattn, wo_s[pl.ds(pl.multiple_of((1 - c) * HALF, HALF), HALF), :]).astype(BF)
        return (sums[0] + jnp.sum(dx * attn, axis=0, keepdims=True), sums[1] + jnp.sum(dy * ff, axis=0, keepdims=True))

    zero = jnp.zeros((1, D), F32)
    sum_attn, sum_ffn = lax.fori_loop(0, 2, tile, (zero, zero))
    ga[...] = jnp.concatenate([sum_attn, sum_ffn], axis=0)
    gb_o[...] = jnp.sum(dattn_s[...].astype(F32), axis=0, keepdims=True)
    gb_b[...] = jnp.sum(dff_s[...].astype(F32), axis=0, keepdims=True)
    for s in range(SLABS):
        lanes = slice(s * D, (s + 1) * D)
        gb_i[:, lanes] = jnp.sum(dpre_s[:, lanes].astype(F32), axis=0, keepdims=True)
    both = jnp.concatenate([mixed[0].reshape(2 * BLOCK, HALF), mixed[1].reshape(2 * BLOCK, HALF)], axis=1)
    ht, bt = flip(h_s[...]), flip(both)
    per = count // SLABS

    for core in (c, 1 - c):

        def columns(ref, first):
            return ref[:, pl.ds(pl.multiple_of(first + core * HALF, HALF), HALF)]

        def put(group, first, value):
            if core is c:
                g_keep[group, first : first + value.shape[0], :] = value
            else:
                row = 2 * BLOCK + group * 9 * rd + first
                give[row : row + value.shape[0], :] = value

        dff = columns(dff_s, 0)
        g_out = dot(bt, columns(dattn_s, 0)).astype(BF)
        for i in range(count):
            put(i, 8 * rd, g_out[i * rd : (i + 1) * rd])
        for s in range(SLABS):
            lanes = slice(s * D, (s + 1) * D)
            g_in = dot(ht, columns(dpre_s, s * D)).astype(BF)
            for i in range(count):
                put(i, (4 + s) * rd, g_in[i * rd : (i + 1) * rd])
            g_back = dot(flip(r_s[:, lanes]), dff).astype(BF)
            for i in range(per):
                put(s * per + i, 0, g_back[4 * i * rd : 4 * (i + 1) * rd])


def back_blocks(blocks, kn, vn, kt, q_in, d_in, ot, lse, dk_s, dv_s, dq_out, scratch):
    qz, qzt, oz, ozt, dq_s, p_s, dp_s = scratch
    rows = lax.broadcasted_iota(jnp.int32, (HALF, BLOCK), 0) // HEAD_DIM
    lanes = lax.broadcasted_iota(jnp.int32, (BLOCK, HALF), 1) // HEAD_DIM
    gq = jnp.zeros((1, HALF), F32)
    for i, block in enumerate(blocks):
        q, d_o = q_in[i].astype(F32), d_in[i * BLOCK : (i + 1) * BLOCK].astype(F32)
        qt, dot_ = q.T, d_o.T
        product = dot_ * ot[i]
        deltas = []
        for h in range(CORE_HEADS):
            head = slice(h * HEAD_DIM, (h + 1) * HEAD_DIM)
            deltas.append(jnp.sum(product[head], axis=0, keepdims=True))
            qz[h] = jnp.where(lanes == h, q, 0.0).astype(BF)
            oz[h] = jnp.where(lanes == h, d_o, 0.0).astype(BF)
            qzt[h] = jnp.where(rows == h, qt, 0.0).astype(BF)
            ozt[h] = jnp.where(rows == h, dot_, 0.0).astype(BF)
        dq_s[...] = jnp.zeros_like(dq_s)

        def chunk(first, count):
            size = count * BLOCK
            keys = kn[pl.ds(first, count)].reshape(size, HALF)
            values = vn[pl.ds(first, count)].reshape(size, HALF)
            for h in range(CORE_HEADS):
                p_s[h, :size] = dot(keys, qzt[h])
                dp_s[h, :size] = dot(values, ozt[h])
            dk = dk_s[pl.ds(first, count)].reshape(size, HALF)
            dv = dv_s[pl.ds(first, count)].reshape(size, HALF)
            for h in range(CORE_HEADS):
                head = slice(h * HEAD_DIM, (h + 1) * HEAD_DIM)
                p = jnp.exp(p_s[h, :size] - lse[i, h : h + 1, :])
                ds = (p * (dp_s[h, :size] - deltas[h])).astype(BF)
                dv = dv + dot(p.astype(BF), oz[h])
                dk = dk + dot(ds, qz[h])
                dq = dq_s[head, :]
                for j in range(count):
                    dq = dq + dot(kt[first + j, head, :], ds[j * BLOCK : (j + 1) * BLOCK])
                dq_s[head, :] = dq
            dk_s[pl.ds(first, count)] = dk.reshape(count, BLOCK, HALF)
            dv_s[pl.ds(first, count)] = dv.reshape(count, BLOCK, HALF)

        over_keys(block, chunk)
        dq = (dq_s[...] * (1.0 / math.sqrt(HEAD_DIM))).T.astype(BF)
        gq = gq + jnp.sum(dq.astype(F32), axis=0, keepdims=True)
        dq_out[i] = dq
    return gq


def back_kernel(nz, which, ids, ins, outs, *scratch):
    kn, vn, kt, qn, ot, lse, d_o = ins[:7]
    dk, dv, dq, gq = outs
    if which == 0:
        dk[...] = jnp.zeros_like(dk)
        dv[...] = jnp.zeros_like(dv)
    blocks = query_blocks(ids[0], ids[1], nz)[2 * which : 2 * which + 2]
    gq[...] = back_blocks(blocks, kn, vn, kt, qn, d_o, ot, lse, dk, dv, dq, scratch)


def dx_kernel(nz, ids, ins, outs, dxs):
    wq, dk, dv, dq_mine, dq_other, dx1 = ins
    dx_keep, dqkv, *dx_send = outs
    z, c = ids[0], ids[1]
    dqkv[:, :, :HALF] = jnp.zeros((2 * nz, BLOCK, HALF), BF)
    blocks = query_blocks(z, c, nz)
    for i in range(2):
        dqkv[blocks[i], :, :HALF] = dq_mine[i]
        dqkv[blocks[2 + i], :, :HALF] = dq_other[i]
    w_all = wq[:, :, : 3 * HALF].reshape(D, 3 * HALF)

    def finish(block, unused):
        dqkv[block, :, HALF : 2 * HALF] = dk[block].astype(BF)
        dqkv[block, :, 2 * HALF :] = dv[block].astype(BF)
        dxs[block] = ndot(dqkv[block], w_all)
        return unused

    lax.fori_loop(0, 2 * nz, finish, 0)
    for i in range(2):
        dxs[blocks[i]] = dxs[blocks[i]] + dx1[i]
    half = nz // 2
    for p in range(half):
        chip = ids[4] * half + p
        for i, at in ((p, chip), (half + p, nz - 1 - chip)):
            dx_keep[i] = dxs[2 * at + c].astype(BF)
            dx_send[i][...] = dxs[2 * at + 1 - c].astype(BF)


def dw_kernel(nz, rs, rr, ids, ins, outs, spread):
    xall, dqkv, gq_mine, gq_other, gb_o, gb_i, gb_b, ga = ins
    (dw,) = outs
    c = ids[1]
    gv = jnp.zeros((1, HALF), F32)
    acc = None
    for block in range(2 * nz):
        term = dot(flip(xall[block]), dqkv[block])
        acc = term if block == 0 else acc + term
        gv = gv + jnp.sum(dqkv[block, :, 2 * HALF :].astype(F32), axis=0, keepdims=True)
    gq = gq_mine[...] + gq_other[...]
    nothing = jnp.zeros((1, HALF), F32)
    own = [jnp.concatenate([jnp.where(c == 0, g, nothing), jnp.where(c == 0, nothing, g)], axis=1) for g in (gq, gv)]
    tile = jnp.concatenate(own + [gb_o[...], gb_b[...], jnp.zeros((124, D), F32)], axis=0).T
    spread[...] = jnp.broadcast_to(gb_i[...], (128, FF)).T.reshape(D // rr, SLABS, rr, 128)
    lanes = lax.broadcasted_iota(jnp.int32, (D // rr, rr, 128), 2)
    tile = tile.reshape(D // rr, rr, 128)
    for s in range(SLABS):
        tile = jnp.where(lanes == 4 + s, spread[:, s], tile)
    tile = tile.reshape(D, 128)
    if rs >= 16:
        me = ids[2]
        lane = lax.broadcasted_iota(jnp.int32, (D, 128), 1) - 8 - 6 * (me // rs)
        mine = lax.rem(lax.broadcasted_iota(jnp.int32, (D, 128), 0), rs) == lax.rem(me, rs)
        gates = jnp.sum(ga[...], axis=1, keepdims=True)
        for which in range(2):
            rest = gates[which : which + 1]
            for i in range(3):
                high = rest.astype(BF).astype(F32)
                tile = jnp.where(mine & (lane == 2 * i + which), high, tile)
                rest = rest - high
    rows = dw.shape[1]
    dw[:, :, : 3 * HALF] = acc.astype(BF).reshape(D // rows, rows, 3 * HALF)
    dw[:, :, 3 * HALF :] = tile.astype(BF).reshape(D // rows, rows, 128)


def sum_kernel(plans, ids, ins, outs):
    outs = list(outs)
    for numbers, size, where, pre, post, stride, first, flat in plans:

        def total(static, dynamic):
            source = static * stride // size
            index = (static + dynamic) * stride + first - source * size
            refs = [ins[number] for number in numbers[source]]
            value = refs[0][index]
            if len(refs) == 2 and flat is None:
                value = value.astype(F32) + refs[1][index].astype(F32)
            elif len(refs) == 2:
                rows = value.shape[0]
                start = pl.multiple_of(flat + index * rows, 16)
                value = value.astype(F32) + refs[1][pl.ds(start, rows), :].astype(F32)
            return value

        if where is None:
            out = outs.pop(0)
            for index in range(out.shape[0]):
                out[index] = total(index, 0).astype(out.dtype)
            continue
        keep, send = outs.pop(0), outs.pop(0)
        mine = my_bit(ids, where)
        for p in range(pre):
            for q in range(post):
                keep[p * post + q] = total(2 * p * post + q, mine * post).astype(keep.dtype)
                send[p * post + q] = total(2 * p * post + q, (1 - mine) * post).astype(send.dtype)


def grads_kernel(rs, ids, ins, outs):
    own, other = ins
    w_back, w_in, w_out = outs
    for ref, core in ((own, ids[1]), (other, 1 - ids[1])):

        def lanes(first):
            return pl.ds(pl.multiple_of(first + core * HALF, HALF), HALF)

        value = ref[0].astype(F32)
        w_back[:, lanes(0)] = value[: 4 * rs]
        for s in range(SLABS):
            w_in[:, lanes(s * D)] = value[(4 + s) * rs : (5 + s) * rs]
        w_out[:, lanes(0)] = value[8 * rs :]


def last_kernel(rs, ids, ins, outs):
    own, other = ins
    w_qkv, gb_qv, gb_o, gb_i, gb_b, gates = outs
    for ref, core in ((own, ids[1]), (other, 1 - ids[1])):
        value = ref[0].astype(F32)
        for i in range(3):
            lanes = pl.ds(pl.multiple_of(i * D + core * HALF, HALF), HALF)
            w_qkv[:, lanes] = value[:, i * HALF : (i + 1) * HALF]
    sums = own[0, :, 3 * HALF :] + other[0, :, 3 * HALF :].astype(F32)
    lane = lax.broadcasted_iota(jnp.int32, (1, 128), 1)
    column = jnp.sum(sums, axis=0, keepdims=True)
    for which in range(2):
        used = (lane >= 8) & (lax.rem(lane, 2) == which)
        gates[:, which : which + 1] = jnp.sum(jnp.where(used, column, 0.0), axis=1, keepdims=True)
    by_row = jnp.concatenate([sums, jnp.zeros((128 - rs, 128), F32)], axis=0).T
    gb_qv[...] = by_row[:2, :rs]
    gb_o[...] = by_row[2:3, :rs]
    gb_b[...] = by_row[3:4, :rs]
    for s in range(SLABS):
        gb_i[:, s * rs : (s + 1) * rs] = by_row[4 + s : 5 + s, :rs]


def shape(dims, kind):
    return jax.ShapeDtypeStruct(dims, kind)


def vmem(dims, kind):
    return pltpu.VMEM(dims, kind)


def in_hbm(array):
    return pltpu.with_memory_space_constraint(array, pltpu.HBM)


def cost(megabytes):
    return pl.CostEstimate(flops=0, bytes_accessed=megabytes * 2**20, transcendentals=0)


def call(
    name, kernel, ids, ins, outs, after=(), scratch=(), limit=12, weight=0, where=None, aliases=None, out=VMEM
):
    count, waits = len(ins), len(after)

    def run(*refs):
        given, rest = refs[1 : 1 + count], refs[1 + count + waits :]
        kernel(refs[0], given, rest[: len(outs)], *rest[len(outs) :])

    return pl.pallas_call(
        run,
        out_shape=tuple(outs),
        in_specs=[SMEM] + (where or [VMEM] * count) + [ANY] * waits,
        out_specs=out if isinstance(out, tuple) else (out,) * len(outs),
        scratch_shapes=list(scratch),
        compiler_params=pltpu.CompilerParams(vmem_limit_bytes=limit * 2**20),
        cost_estimate=cost(weight),
        input_output_aliases=aliases or {},
        name=name,
    )(ids, *ins, *after)


def pack_call(ids, rs, ins):
    return call(
        "pack",
        functools.partial(pack_kernel, rs),
        ids,
        [in_hbm(array) for array in ins],
        [vmem((rs, WQ), BF), vmem((9 * rs, HALF), BF), vmem((13 * rs, HALF), BF)] + [vmem((BLOCK, D), BF)] * 4,
        scratch=[pltpu.VMEM(array.shape, BF) for array in ins[:8]]
        + [pltpu.VMEM((128, 128), F32), pltpu.SemaphoreType.DMA((12,))],
        where=[ANY] * 10,
    )


def join_call(name, ids, jobs, after=(), extra=None, extra_ins=(), extra_outs=(), cuts=None):
    ins, outs, spans = [], [], []
    for (own, got, _, _), cut in zip(jobs, cuts or [1] * len(jobs)):
        ins += [own, got]
        spans.append(slice(len(outs), len(outs) + cut))
        outs += [vmem((2 * own.shape[0] // cut,) + own.shape[1:], own.dtype)] * cut
    number = len(outs)

    def kernel(ids_ref, given, results):
        for i, (_, _, where, post) in enumerate(jobs):
            join(ids_ref, given[2 * i], given[2 * i + 1], results[spans[i]], where, post)
        if extra is not None:
            extra(ids_ref, given[2 * len(jobs) :], results[number:])

    return call(name, kernel, ids, ins + list(extra_ins), outs + list(extra_outs), after)


def sum_call(name, ids, jobs, after=(), last=BF, flat=None):
    ins, outs, plans = [], [], []

    def number(array):
        for i, other in enumerate(ins):
            if other is array:
                return i
        ins.append(array)
        return len(ins) - 1

    for sources, where, pre, post, stride, first in jobs:
        numbers = [tuple(number(array) for array in pair if array is not None) for pair in sources]
        tail = sources[0][0].shape[1:]
        size = sources[0][0].shape[0]
        plans.append((numbers, size, where, pre, post, stride, first, flat))
        if where is None:
            outs.append(vmem((size * len(sources) // stride,) + tail, last))
        else:
            outs += [vmem((pre * post,) + tail, last), vmem((pre * post,) + tail, BF)]
    return call(name, functools.partial(sum_kernel, plans), ids, ins, outs, after)


def make_body(n1, n2, nz):
    ndp = n1 * n2
    nsh = ndp * nz * 2
    rs = D // nsh
    rd = D // ndp
    half = nz // 2
    parts = 2 * nz if rs % 16 == 0 else 1
    rr = rd // parts
    nh = 9 * rd // 2
    swap = [(0, 1), (1, 0)]
    bits_a, bits_b, bits_z = (count.bit_length() - 1 for count in (n1, n2, nz))
    counts = {"a": n1, "b": n2, "z": nz}
    slot = {"a": 3, "b": 5, "z": 0}

    def to_mirror(array):
        return lax.ppermute(array, "z", [(s, nz - 1 - s) for s in range(nz)])

    def exchange(array, name, bit):
        return lax.ppermute(array, name, [(s, s ^ (1 << bit)) for s in range(counts[name])])

    def to_other(array):
        return lax.ppermute(array, "c", swap)

    def body(inputs, w_qkv, bias_qv, w_out, bias_out, w_in, bias_in, w_back, bias_back, alphas, cotangent):
        z, c = lax.axis_index("z"), lax.axis_index("c")
        a, b = lax.axis_index("a"), lax.axis_index("b")
        device = ((a * n2 + b) * nz + z) * 2 + c
        ids = jnp.stack([z, c, device, a, z // half, b]).astype(jnp.int32)

        latest = []

        def hand_on(ids_ref, given, results):
            for source, target in zip(given, results):
                target[...] = source[...]

        def step(name, jobs, extra=(), cuts=None, others=()):
            result = join_call(
                name, ids, jobs, latest + list(others), hand_on, extra, [vmem(e.shape, e.dtype) for e in extra], cuts
            )
            latest[:] = [result[0]]
            return result


        q_keep, f_keep, give, x_give, x_keep, cot_give, cot_a = pack_call(
            ids, rs,
            [w_qkv, w_back, w_in, w_out, bias_qv, bias_out[None], bias_back[None], bias_in[None], inputs, cotangent],
        )
        wq, wf = call(
            "core", functools.partial(core_kernel, rs), ids, [q_keep, f_keep, to_other(give)],
            [vmem((2, rs, WQ), BF), vmem((2, 9 * rs, HALF), BF)],
        )
        latest[:] = [wq]
        wq, wf = wq.reshape(1, 2 * rs, WQ), wf.reshape(1, 2 * 9 * rs, HALF)
        wf = wf.reshape(2 * 9 * rs, HALF)
        q_got = exchange(wq, "z", bits_z - 1)
        wf_parts = [(wf, 0)]
        for i in reversed(range(bits_z)):
            wf_parts += [(exchange(part, "z", i), place | (1 << i)) for part, place in wf_parts]
        for i in reversed(range(2, bits_z)):
            (wq,) = step("q_z", [(wq, q_got, (0, i), 1)])
            q_got = exchange(wq, "z", i - 1)
        wq, x_give = step("q_z", [(wq, q_got, (0, 1), 1)], [x_give])
        q_got = exchange(wq, "z", 0)
        x_far = to_mirror(x_give)
        cot_b = to_mirror(cot_give)
        wq, x_keep = step("q_z", [(wq, q_got, (0, 0), 1)], [x_keep])
        wq = wq.reshape(rd, WQ)
        if parts == 1:
            hidden_bias = wq[:, 3 * HALF + 4 : 3 * HALF + 8].reshape(2 * nz, rs, SLABS)
            hidden_bias = jnp.transpose(hidden_bias, (0, 2, 1)).reshape(SLABS, rd).T
            wq = jnp.concatenate([wq[:, : 3 * HALF + 4], hidden_bias, wq[:, 3 * HALF + 8 :]], axis=1)
        wq = wq[None]
        for i in reversed(range(1, bits_b)):
            q_got = exchange(wq, "b", i)
            (wq,) = step("q_b", [(wq, q_got, (5, i), 1)])
        q_got = exchange(wq, "b", 0)

        own = x_keep[None]
        own_got = exchange(own, "z", max(bits_z - 2, 0))
        (far_rows,) = call("x_far", hand_on, ids, [x_far], [vmem((BLOCK, D), BF)], latest)
        latest[:] = [far_rows]
        far_rows = far_rows[None]
        for i in reversed(range(1, bits_z - 1)):
            far_got = exchange(far_rows, "z", i)
            own, far_rows = step("x_z", [(own, own_got, (0, i), 1), (far_rows, far_got, (0, i), 1)])
            own_got = exchange(own, "z", i - 1)
        far_got = exchange(far_rows, "z", 0)

        def in_place(ids_ref, given, results):
            for group in range(2):

                @pl.when(ids_ref[4] == group)
                def _():
                    for ref, (_, place) in zip(given, wf_parts):
                        at = lax.rem(lax.bitwise_xor(ids_ref[0], place), half)
                        results[group ^ (place // half)][at] = ref[...]

        halves = vmem((half, 2 * 9 * rs, HALF), BF)
        wq, first, second = join_call(
            "mid", ids, [(wq, q_got, (5, 0), 1)], latest + [own_got], in_place, [part for part, _ in wf_parts],
            [halves, halves],
        )
        latest[:] = [wq]
        if parts == 1:
            wf = jnp.concatenate([first, second], axis=0).reshape(nz, 2, 9 * rs, HALF)
            wf = jnp.concatenate(
                [wf[:, :, : 4 * rs].reshape(4 * rd, HALF)]
                + [wf[:, :, (4 + s) * rs : (5 + s) * rs].reshape(rd, HALF) for s in range(SLABS)]
                + [wf[:, :, 8 * rs :].reshape(rd, HALF)],
                axis=0,
            )
            first, second = wf[:nh], wf[nh:]
        first, second = first.reshape(1, nh, HALF), second.reshape(1, nh, HALF)
        for i in reversed(range(1, bits_a)):
            q_got = exchange(wq, "a", i)
            (wq,) = step("q_a", [(wq, q_got, (3, i), n2)])
        wq_pieces = [wq, exchange(wq, "a", 0)]
        for i in reversed(range(bits_b)):
            got = exchange(first, "b", i), exchange(second, "a", i)
            first, second = step(
                "f_dp", [(first, got[0], (5, i), 1), (second, got[1], (3, i), 1)], others=[wq_pieces[1]]
            )
        for i in reversed(range(1, bits_a)):
            got = exchange(first, "a", i), exchange(second, "b", i)
            first, second = step("f_dp", [(first, got[0], (3, i), n2), (second, got[1], (5, i), 1)])
        wf_pieces = [first, second, exchange(first, "a", 0), exchange(second, "b", 0)]

        def rows_of_all(ids_ref, given, results):
            own_ref, own_got_ref, far_ref, far_got_ref = given
            (xo_ref,) = results
            base, mine = ids_ref[4] * half, my_bit(ids_ref, (0, 0))
            for p in range(half // 2):
                for own_part, far_part, at in (
                    (own_ref, far_ref, base + 2 * p + mine),
                    (own_got_ref, far_got_ref, base + 2 * p + 1 - mine),
                ):
                    xo_ref[at] = own_part[p]
                    xo_ref[nz - 1 - at] = far_part[p]

        (xo,) = call("x_all", rows_of_all, ids, [own, own_got, far_rows, far_got], [vmem((nz, BLOCK, D), BF)], latest)
        latest[:] = [xo]
        xs = to_other(xo)

        nb = 2 * nz
        heads_t = pltpu.VMEM((CORE_HEADS, HALF, BLOCK), BF)
        scores = pltpu.VMEM((CORE_HEADS, 2 * BLOCK, BLOCK), F32)
        scratch = [
            heads_t,
            scores,
            pltpu.VMEM((CORE_HEADS, 1, BLOCK), F32),
            pltpu.VMEM((CORE_HEADS, 1, BLOCK), F32),
            pltpu.VMEM((HALF, BLOCK), F32),
        ]
        natural, turned = (nb, BLOCK, HALF), (nb, HALF, BLOCK)
        two, two_t = (2, BLOCK, HALF), (2, HALF, BLOCK)
        two_lse = (2, CORE_HEADS, BLOCK)
        spread = pltpu.VMEM((D // rr, SLABS, rr, 128), F32)
        (xall, wq, kn, vn, kt, vt, q_mine, q_other, ot_other, lse_other, o_send, bo, bb, bi) = call(
            "first",
            functools.partial(first_kernel, nz, ndp, n2, rr),
            ids,
            [xo, xs, *wq_pieces],
            [
                vmem((nb, BLOCK, D), BF),
                vmem((ndp, rd, WQ), BF),
                vmem(natural, BF),
                vmem(natural, BF),
                vmem(turned, BF),
                vmem(turned, BF),
                vmem(two, BF),
                vmem(two, BF),
                vmem(two_t, F32),
                vmem(two_lse, F32),
                vmem(two, BF),
                vmem((1, D), F32),
                vmem((1, D), F32),
                vmem((1, FF), F32),
            ],
            latest,
            [spread] + scratch,
            limit=16,
        )

        def give_kernel(ids_ref, given, results):
            row = 0
            for part in given:
                for i in range(part.shape[0]):
                    results[0][row : row + part.shape[1]] = part[i]
                    row += part.shape[1]

        (give,) = call(
            "give", give_kernel, ids, [o_send, *wf_pieces], [vmem((2 * BLOCK + 2 * ndp * nh, HALF), BF)],
            [cot_b], limit=16,
        )
        ffn_got = to_other(give)
        ot_mine, lse_mine, o_mine = call(
            "second",
            functools.partial(second_kernel, nz),
            ids,
            [kn, vt, q_mine],
            [vmem(two_t, F32), vmem(two_lse, F32), vmem(two, BF)],
            (),
            scratch,
        )

        grouped = (ndp * parts, 9 * rd // parts, HALF)
        (out_near, out_far, dx1, d_mine, g_keep, give, gb_o, gb_i, gb_b, ga) = call(
            "ffn",
            functools.partial(ffn_kernel, nz, ndp, n2, parts),
            ids,
            [alphas, o_mine, ffn_got, xall, cot_a, cot_b, bo, bi, bb, *wf_pieces],
            [
                vmem((BLOCK, D), BF),
                vmem((BLOCK, D), BF),
                vmem((2, BLOCK, D), F32),
                vmem((2 * BLOCK, HALF), BF),
                vmem(grouped, BF),
                vmem((2 * BLOCK + ndp * 9 * rd, HALF), BF),
                vmem((1, D), F32),
                vmem((1, FF), F32),
                vmem((1, D), F32),
                vmem((2, D), F32),
            ],
            scratch=[
                pltpu.VMEM((2, 2 * ndp, nh, HALF), BF),
                pltpu.VMEM((D, D), BF),
                pltpu.VMEM((SLABS, D, D), BF),
                pltpu.VMEM((FF, D), BF),
                pltpu.VMEM((2, 2, BLOCK, HALF), BF),
                pltpu.VMEM((2 * BLOCK, D), BF),
                pltpu.VMEM((2 * BLOCK, FF), BF),
                pltpu.VMEM((2 * BLOCK, FF), BF),
                pltpu.VMEM((2 * BLOCK, D), BF),
                pltpu.VMEM((2 * BLOCK, D), BF),
            ],
            limit=28,
            where=[SMEM] + [VMEM] * 12,
        )
        back_got = to_other(give)
        out_b = to_mirror(out_far)

        back_scratch = [
            pltpu.VMEM((CORE_HEADS, BLOCK, HALF), BF),
            heads_t,
            pltpu.VMEM((CORE_HEADS, BLOCK, HALF), BF),
            heads_t,
            pltpu.VMEM((HALF, BLOCK), F32),
            scores,
            scores,
        ]
        back_out = [vmem(natural, F32), vmem(natural, F32), vmem(two, BF), vmem((1, HALF), F32)]
        dk, dv, dq_mine, gq_mine = call(
            "back_first",
            functools.partial(back_kernel, nz, 0),
            ids,
            [kn, vn, kt, q_mine, ot_mine, lse_mine, d_mine],
            back_out,
            scratch=back_scratch,
            limit=16,
        )

        latest[:] = [gq_mine]
        done = {}

        def along(axis, count, pre, post):
            return [(axis, i, pre * (count >> (i + 1)), post) for i in range(count.bit_length() - 1)]

        def dp_scatter(name, kept, got, rows, columns, flat=None):
            axes = (along("b", n2, n1, 1) + along("a", n1, 1, 1), along("a", n1, 1, n2) + along("b", n2, 1, 1))
            whole = (kept.reshape(2 * ndp, rows, columns), got)
            state = [(whole, 2, 0), (whole, 2, 1)]
            for i in range(len(axes[0])):
                steps = axes[0][i], axes[1][i]
                result = sum_call(
                    name,
                    ids,
                    [
                        ([pair], (slot[axis], bit), pre, post, stride, first)
                        for (pair, stride, first), (axis, bit, pre, post) in zip(state, steps)
                    ],
                    latest,
                    flat=flat if i == 0 else None,
                )
                latest[:] = [result[0]]
                state = [
                    ((result[2 * j], exchange(result[2 * j + 1], steps[j][0], steps[j][1])), 1, 0) for j in range(2)
                ]
                yield
            return [pair for pair, _, _ in state]

        def z_scatter(name, sources):
            for _, i, pre, _ in along("z", nz, 1, 1):
                kept, send = sum_call(name, ids, [(sources, (slot["z"], i), pre, 1, 1, 0)], latest)
                latest[:] = [kept]
                sources = [(kept, exchange(send, "z", i))]
                yield
            rows, columns = kept.shape[1] // 2, kept.shape[2]
            sources = [tuple(array.reshape(2, rows, columns) for array in sources[0])]
            keep, send = sum_call(name, ids, [(sources, (1, 0), 1, 1, 1, 0)], latest, F32)
            latest[:] = [keep]
            return keep, to_other(send)

        def whole_dp(name, sources):
            return [part[0] for part in sum_call(name, ids, [([pair], None, 0, 0, 1, 0) for pair in sources], latest)]

        def g_chain():
            sources = yield from dp_scatter("g_dp", g_keep, back_got, nh, HALF, 2 * BLOCK)
            if parts == 1:
                g_dp = jnp.concatenate(whole_dp("g_dp", sources), axis=0)
                g_dp = jnp.concatenate(
                    [g_dp[: 4 * rd].reshape(nz, 2, 4 * rs, HALF)]
                    + [g_dp[(4 + s) * rd : (5 + s) * rd].reshape(nz, 2, rs, HALF) for s in range(SLABS)]
                    + [g_dp[8 * rd :].reshape(nz, 2, rs, HALF)],
                    axis=2,
                )
                sources = [(g_dp.reshape(nz, 2 * 9 * rs, HALF), None)]
            else:
                sources = [tuple(array.reshape(half, 2 * 9 * rs, HALF) for array in pair) for pair in sources]
            keep, got = yield from z_scatter("g_z", sources)
            yield
            done["g"] = call(
                "g_last", functools.partial(grads_kernel, rs), ids, [keep, got],
                [shape((4 * rs, D), F32), shape((rs, FF), F32), shape((rs, D), F32)], latest,
            )
            latest[:] = [done["g"][2]]

        g_steps = g_chain()
        next(g_steps)
        dk, dv, dq_other, gq_other = call(
            "back_second",
            functools.partial(back_kernel, nz, 1),
            ids,
            [kn, vn, kt, q_other, ot_other, lse_other, back_got, dk, dv],
            back_out,
            latest,
            back_scratch,
            limit=16,
            aliases={8: 0, 9: 1},
        )
        def out_kernel(ids_ref, given, results, sems):
            group = ids_ref[4]
            copies = moves(sems, [(given[0], results[0].at[group]), (given[1], results[0].at[1 - group])])
            results[1][...] = jnp.zeros_like(results[1])
            wait(copies)

        def to_rows(name, own, got):
            rows, token = call(
                name, out_kernel, ids, [own, got], [pltpu.HBM((2, BLOCK, D), BF), vmem((8, 128), F32)], latest,
                [pltpu.SemaphoreType.DMA((2,))], where=[ANY, ANY],
                out=(pl.BlockSpec(memory_space=pltpu.HBM), VMEM),
            )
            latest[:] = [token]
            return rows

        latest[:] = [gq_other]
        outputs = to_rows("outputs", out_near, out_b)
        next(g_steps)
        dx_keep, dqkv, *dx_send = call(
            "dx",
            functools.partial(dx_kernel, nz),
            ids,
            [wq, dk, dv, dq_mine, dq_other, dx1],
            [vmem((nz, BLOCK, D), BF), vmem((nb, BLOCK, 3 * HALF), BF)] + [vmem((BLOCK, D), BF)] * nz,
            latest,
            [pltpu.VMEM((nb, BLOCK, D), F32)],
        )
        dx_got = [to_other(part) for part in dx_send]
        latest[:] = [dx_keep]
        next(g_steps)
        (dw,) = call(
            "dw",
            functools.partial(dw_kernel, nz, rs, rr),
            ids,
            [xall, dqkv, gq_mine, gq_other, gb_o, gb_i, gb_b, ga],
            [vmem((2 * ndp, rd // 2, WQ), BF)],
            latest,
            [spread],
        )

        latest[:] = [dw]

        def dx_chain():
            def first_sums(ids_ref, given, results):
                mine = my_bit(ids_ref, (0, 0))
                kept, got = given[0], given[1:]
                for p in range(half):
                    for bit, target in ((mine, results[0]), (1 - mine, results[1])):
                        received = jnp.where(bit == 0, got[2 * p][...], got[2 * p + 1][...]).astype(F32)
                        target[p] = (kept[2 * p + bit].astype(F32) + received).astype(BF)

            kept, send = call(
                "dx_z", first_sums, ids, [dx_keep, *dx_got], [vmem((half, BLOCK, D), BF)] * 2, latest
            )
            latest[:] = [kept]
            got = exchange(send, "z", 0)
            yield
            for i in range(1, bits_z - 1):
                kept, send = sum_call("dx_z", ids, [([(kept, got)], (0, i), nz >> (i + 1), 1, 1, 0)], latest)
                latest[:] = [kept]
                got = exchange(send, "z", i)
                yield
            near, far = sum_call("dx_z", ids, [([(kept, got)], (0, 30), 1, 1, 1, 0)], latest)
            latest[:] = [near]
            got = to_mirror(far.reshape(BLOCK, D))
            yield
            done["inputs"] = to_rows("dx_last", near.reshape(BLOCK, D), got)

        def dw_chain():
            sources = yield from dp_scatter("w_dp", dw, None, rd // 2, WQ)
            if parts == 1:
                dw_dp = jnp.concatenate(whole_dp("w_dp", sources), axis=0)
                hidden_bias = dw_dp[:, 3 * HALF + 4 : 3 * HALF + 8].T.reshape(2 * nz, SLABS, rs)
                hidden_bias = jnp.transpose(hidden_bias, (0, 2, 1)).reshape(rd, SLABS)
                dw_dp = jnp.concatenate([dw_dp[:, : 3 * HALF + 4], hidden_bias, dw_dp[:, 3 * HALF + 8 :]], axis=1)
                sources = [(dw_dp.reshape(nz, 2 * rs, WQ), None)]
            else:
                sources = [tuple(array.reshape(half, 2 * rs, WQ) for array in pair) for pair in sources]
            keep, got = yield from z_scatter("w_z", sources)
            yield
            done["w"] = call(
                "w_last", functools.partial(last_kernel, rs), ids, [keep, got],
                [shape((rs, 3 * D), F32), shape((2, rs), F32), shape((1, rs), F32), shape((1, SLABS * rs), F32)]
                + [shape((1, rs), F32), shape((1, 2), F32)],
                latest,
            )
            latest[:] = [done["w"][0]]

        steps = {"x": dx_chain(), "g": g_steps, "w": dw_chain()}
        for name in "xwwxgwgwxwgw" + "xgw" * bits_z:
            next(steps[name], 0)
        gb_qv, gb_out, gb_in, gb_back, grad_alphas = done["w"][1:]
        if rs < 16:
            grad_alphas = lax.psum(jnp.sum(ga, axis=1), MESH_AXES)
        return (
            outputs,
            done["inputs"],
            done["w"][0],
            gb_qv,
            done["g"][2],
            gb_out.reshape(rs),
            done["g"][1],
            gb_in.reshape(SLABS * rs),
            done["g"][0],
            gb_back.reshape(rs),
            grad_alphas.reshape(2),
        )

    return body


def solution(mesh):
    ndp, nseq = mesh.devices.shape
    n1 = math.isqrt(ndp)
    n2 = ndp // n1
    nz = nseq // 2
    fine = Mesh(mesh.devices.reshape(n1, n2, nz, 2), MESH_AXES)
    dp, seq = ("a", "b"), ("z", "c")
    rows = P(dp, seq, None)
    both = dp + seq
    return jax.shard_map(
        make_body(n1, n2, nz),
        mesh=fine,
        in_specs=(
            rows,
            P(both, None),
            P(None, both),
            P(both, None),
            P(both),
            P(both, None),
            P(both),
            P(both, None),
            P(both),
            P(),
            rows,
        ),
        out_specs=(
            rows,
            rows,
            P(both, None),
            P(None, both),
            P(both, None),
            P(both),
            P(both, None),
            P(both),
            P(both, None),
            P(both),
            P(),
        ),
        check_vma=False,
    )
```

```python
import functools
import math

import jax
import jax.numpy as jnp
from jax import lax
from jax.experimental import pallas as pl
from jax.experimental.pallas import tpu as pltpu
from jax.sharding import Mesh, PartitionSpec as P

D = 512
HEADS = 8
HEAD_DIM = 64
FF = 2048
BLOCK = 256
HALF = D // 2
CORE_HEADS = HEADS // 2
SLABS = FF // D
BF = jnp.bfloat16
F32 = jnp.float32
MESH_AXES = ("a", "b", "z", "c")
VMEM = pl.BlockSpec(memory_space=pltpu.VMEM)
SMEM = pl.BlockSpec(memory_space=pltpu.SMEM)
ANY = pl.BlockSpec(memory_space=pl.ANY)
WQ = 3 * HALF + 128
GELU_C = math.sqrt(2.0 / math.pi)


def dot(left, right):
    return jnp.dot(left, right, preferred_element_type=F32)


def ndot(left, right):
    return lax.dot_general(left, right, (((1,), (1,)), ((), ())), preferred_element_type=F32)


def flip(block):
    return block.astype(F32).T.astype(BF)


def query_blocks(z, c, nz):
    near, far = 2 * z, 2 * (nz - 1 - z)
    return (near + c, far + c, near + 1 - c, far + 1 - c)


def over_keys(block, chunk):
    def step(i, unused):
        chunk(2 * i, 2)
        return unused

    lax.fori_loop(0, (block + 1) // 2, step, 0)

    @pl.when(lax.rem(block, 2) == 0)
    def _():
        chunk(block, 1)


def attend_blocks(blocks, kn, vt, qn, ot, lse, o, scratch):
    qz, s_s, m_s, l_s, acc_s = scratch
    rows = lax.broadcasted_iota(jnp.int32, (HALF, BLOCK), 0) // HEAD_DIM
    for i, block in enumerate(blocks):
        qt = qn[i].astype(F32).T
        for h in range(CORE_HEADS):
            qz[h] = jnp.where(rows == h, qt, 0.0).astype(BF)
        m_s[...] = jnp.full_like(m_s, -1e30)
        l_s[...] = jnp.zeros_like(l_s)
        acc_s[...] = jnp.zeros_like(acc_s)

        def chunk(first, count):
            keys = kn[pl.ds(first, count)].reshape(count * BLOCK, HALF)
            for h in range(CORE_HEADS):
                s_s[h, : count * BLOCK] = dot(keys, qz[h])
            for h in range(CORE_HEADS):
                head = slice(h * HEAD_DIM, (h + 1) * HEAD_DIM)
                s = s_s[h, : count * BLOCK]
                old = m_s[h]
                new = jnp.maximum(old, jnp.max(s, axis=0, keepdims=True))
                p = jnp.exp(s - new)
                shrink = jnp.exp(old - new)
                m_s[h] = new
                l_s[h] = l_s[h] * shrink + jnp.sum(p, axis=0, keepdims=True)
                p = p.astype(BF)
                acc = acc_s[head, :] * shrink
                for j in range(count):
                    acc = acc + dot(vt[first + j, head, :], p[j * BLOCK : (j + 1) * BLOCK])
                acc_s[head, :] = acc

        over_keys(block, chunk)
        for h in range(CORE_HEADS):
            head = slice(h * HEAD_DIM, (h + 1) * HEAD_DIM)
            total = l_s[h]
            lse[i, h : h + 1, :] = m_s[h] + jnp.log(total)
            acc_s[head, :] = acc_s[head, :] / total
        value = acc_s[...]
        ot[i] = value
        o[i] = value.T.astype(BF)


def moves(sems, pairs):
    copies = [pltpu.make_async_copy(src, dst, sems.at[i]) for i, (src, dst) in enumerate(pairs)]
    for copy in copies:
        copy.start()
    return copies


def wait(copies):
    for copy in copies:
        copy.wait()


def pack_kernel(rs, ids, ins, outs, *refs):
    w_qkv, w_back, w_in, w_out, bias_qv, bias_out, bias_back, bias_in = refs[:8]
    tile, sems = refs[8], refs[9]
    group = ids[4]
    loads = moves(sems, [(ins[i], refs[i]) for i in range(8)])
    rows = moves(
        sems.at[pl.ds(8, 4)],
        [(ins[8 + i].at[which], outs[3 + 2 * i + j]) for i in range(2) for j, which in enumerate((1 - group, group))],
    )
    wait(loads)
    tile[...] = jnp.zeros_like(tile)
    tile[0:2, :rs] = bias_qv[...].astype(F32)
    tile[2:3, :rs] = bias_out[...].astype(F32)
    tile[3:4, :rs] = bias_back[...].astype(F32)
    for i in range(SLABS):
        tile[4 + i : 5 + i, :rs] = bias_in[:, i * rs : (i + 1) * rs].astype(F32)
    turned = tile[...].T[:rs].astype(BF)
    q_keep, f_keep, give = outs[:3]

    def cut(ref, first, core):
        return ref[:, pl.ds(pl.multiple_of(first + core * HALF, HALF), HALF)]

    for i in range(3):
        q_keep[:, i * HALF : (i + 1) * HALF] = cut(w_qkv, i * D, ids[1])
        give[(9 + i) * rs : (10 + i) * rs] = cut(w_qkv, i * D, 1 - ids[1])
    q_keep[:, 3 * HALF :] = turned
    give[12 * rs :, :128] = turned
    give[12 * rs :, 128:] = jnp.zeros((rs, 128), BF)
    for f_out, core in ((f_keep, ids[1]), (give, 1 - ids[1])):
        f_out[: 4 * rs] = cut(w_back, 0, core)
        for i in range(SLABS):
            f_out[(4 + i) * rs : (5 + i) * rs] = cut(w_in, i * D, core)
        f_out[8 * rs : 9 * rs] = cut(w_out, 0, core)
    wait(rows)


def core_kernel(rs, ids, ins, outs):
    q_keep, f_keep, got = ins
    wq, wf = outs
    c = ids[1]
    wq[c] = q_keep[...]
    wf[c] = f_keep[...]
    wf[1 - c] = got[: 9 * rs]
    for i in range(3):
        wq[1 - c, :, i * HALF : (i + 1) * HALF] = got[(9 + i) * rs : (10 + i) * rs]
    wq[1 - c, :, 3 * HALF :] = got[12 * rs :, :128]


def my_bit(ids, where):
    index, bit = where
    return lax.rem(lax.shift_right_logical(ids[index], bit), 2)


def join(ids, own, got, outs, where, post=1):
    mine = my_bit(ids, where)
    pre = own.shape[0] // post
    for p in range(pre):
        out = outs[p * len(outs) // pre]
        at = 2 * p - 2 * pre // len(outs) * (p * len(outs) // pre)
        for q in range(post):
            out[(at + mine) * post + q] = own[p * post + q]
            out[(at + 1 - mine) * post + q] = got[p * post + q]


def first_kernel(nz, ndp, n2, rr, ids, ins, outs, spread, *scratch):
    xo, xs = ins[:2], ins[2:4]
    wq_pieces = ins[4:6]
    xall, wq, kn, vn, kt, vt, q_mine, q_other, ot, lse, o, bo, bb, bi = outs
    z, c = ids[0], ids[1]
    for p in range(nz // 2):
        chip = ids[4] * (nz // 2) + p
        for i, at in enumerate((chip, nz - 1 - chip)):
            xall[2 * at + c] = xo[i][p]
            xall[2 * at + 1 - c] = xs[i][p]
    for far, piece in enumerate(wq_pieces):
        bit = lax.rem(ids[3], 2)
        for j in range(piece.shape[0]):
            wq[(2 * (j // n2) + (1 - bit if far else bit)) * n2 + j % n2] = piece[j]
    bias = wq[:, :, 3 * HALF :].reshape(D, 128).astype(F32)
    turned = bias.T
    bo[...] = turned[2:3]
    bb[...] = turned[3:4]
    lanes = lax.broadcasted_iota(jnp.int32, (D // rr, rr, 128), 2)
    for s in range(SLABS):
        spread[:, s] = jnp.where(lanes == 4 + s, bias.reshape(D // rr, rr, 128), 0.0)
    bi[...] = jnp.sum(spread[...].reshape(FF, 128).T[4:8], axis=0, keepdims=True)
    bias_q = jnp.where(c == 0, turned[0:1, :HALF], turned[0:1, HALF:])
    bias_v = jnp.where(c == 0, turned[1:2, :HALF], turned[1:2, HALF:])
    w_q = wq[:, :, :HALF].reshape(D, HALF)
    w_kv = wq[:, :, HALF : 3 * HALF].reshape(D, 2 * HALF)

    def project(block, unused):
        kv = dot(xall[block], w_kv)
        key = kv[:, :HALF]
        kn[block] = key.astype(BF)
        kt[block] = key.T.astype(BF)
        value = kv[:, HALF:] + bias_v
        vn[block] = value.astype(BF)
        vt[block] = value.T.astype(BF)
        return unused

    lax.fori_loop(0, 2 * nz, project, 0)
    blocks = query_blocks(z, c, nz)
    for i, block in enumerate(blocks):
        q = (dot(xall[block], w_q) + bias_q).astype(BF).astype(F32) * (1.0 / math.sqrt(HEAD_DIM))
        (q_mine if i < 2 else q_other)[i % 2] = q.astype(BF)
    attend_blocks(blocks[2:], kn, vt, q_other, ot, lse, o, scratch)


def place_dp(ids, pieces, ndp, n2, put):
    for i, piece in enumerate(pieces):
        far, half = i // 2, i % 2
        for j in range(ndp // 2):
            if half == 0:
                bit = lax.rem(ids[3], 2)
                dp = (2 * (j // n2) + (1 - bit if far else bit)) * n2 + j % n2
            else:
                bit = lax.rem(ids[5], 2)
                dp = j // (n2 // 2) * n2 + 2 * (j % (n2 // 2)) + (1 - bit if far else bit)
            put(dp, half, piece(j) if callable(piece) else piece[j])


def second_kernel(nz, ids, ins, outs, *scratch):
    kn, vt, qn = ins
    ot, lse, o = outs
    blocks = query_blocks(ids[0], ids[1], nz)
    attend_blocks(blocks[:2], kn, vt, qn, ot, lse, o, scratch)


def ffn_kernel(nz, ndp, n2, parts, ids, ins, outs, *refs):
    alphas, o_mine, got, xall, cot_a, cot_b, bo, bi, bb = ins[:9]
    pieces = ins[9:13]
    rows = pieces[0].shape[1]

    def received(i):
        return lambda j: got[pl.ds(2 * BLOCK + (i * (ndp // 2) + j) * rows, rows)]

    (out_near, out_far, dx1, d_mine, g_keep, give, gb_o, gb_i, gb_b, ga) = outs
    w, wo_s, wi_s, wb_s, mixed, h_s, r_s, dpre_s, dff_s, dattn_s = refs
    c = ids[1]
    for core in range(2):
        own = pieces if core == 0 else [received(i) for i in range(4)]
        which = c if core == 0 else 1 - c

        def put(dp, half, value):
            w[which, 2 * dp + half] = value

        place_dp(ids, own, ndp, n2, put)
    count = ndp * parts
    rd = D // count
    for half in range(2):
        lanes = slice(half * HALF, (half + 1) * HALF)
        whole = w[half].reshape(count, 9 * rd, HALF)
        wo_s[:, lanes] = whole[:, 8 * rd :].reshape(D, HALF)
        for s in range(SLABS):
            wi_s[s, :, lanes] = whole[:, (4 + s) * rd : (5 + s) * rd].reshape(D, HALF)
        wb_s[:, lanes] = whole[:, : 4 * rd].reshape(FF, HALF)
    mixed[c] = o_mine[...]
    mixed[1 - c] = got[: 2 * BLOCK].reshape(2, BLOCK, HALF)
    alpha_attn, alpha_ffn = alphas[0], alphas[1]
    mine = query_blocks(ids[0], c, nz)

    def tile(t, sums):
        rows = pl.ds(pl.multiple_of(t * BLOCK, BLOCK), BLOCK)
        attn = dot(mixed[0, t], wo_s[:HALF, :]) + dot(mixed[1, t], wo_s[HALF:, :]) + bo[...]
        x1 = xall[jnp.where(t == 0, mine[0], mine[1])].astype(F32) + alpha_attn * attn
        hidden = x1.astype(BF)
        h_s[rows, :] = hidden
        dy = jnp.where(t == 0, cot_a[...], cot_b[...]).astype(F32)
        dff = (alpha_ffn * dy).astype(BF)
        dff_s[rows, :] = dff
        ff = jnp.zeros((BLOCK, D), F32) + bb[...]
        dx = dy
        for s in range(SLABS):
            lanes = slice(s * D, (s + 1) * D)
            pre = dot(hidden, wi_s[s]) + bi[:, lanes]
            square = pre * pre
            t_ = jnp.tanh(GELU_C * pre * (1.0 + 0.044715 * square))
            half_up = 0.5 * (1.0 + t_)
            r = (pre * half_up).astype(BF)
            slope = half_up + 0.5 * pre * (1.0 - t_ * t_) * (GELU_C * (1.0 + 3.0 * 0.044715 * square))
            r_s[rows, lanes] = r
            ff = ff + dot(r, wb_s[lanes, :])
            dr = ndot(dff, wb_s[lanes, :]).astype(BF).astype(F32)
            dpre = (dr * slope).astype(BF)
            dpre_s[rows, lanes] = dpre
            dx = dx + ndot(dpre, wi_s[s])
        out = (x1 + alpha_ffn * ff).astype(BF)

        @pl.when(t == 0)
        def _():
            out_near[...] = out

        @pl.when(t == 1)
        def _():
            out_far[...] = out

        dx1[t] = dx
        dattn = (alpha_attn * dx).astype(BF)
        dattn_s[rows, :] = dattn
        d_mine[rows, :] = ndot(dattn, wo_s[pl.ds(pl.multiple_of(c * HALF, HALF), HALF), :]).astype(BF)
        give[rows, :] = ndot(dattn, wo_s[pl.ds(pl.multiple_of((1 - c) * HALF, HALF), HALF), :]).astype(BF)
        return (sums[0] + jnp.sum(dx * attn, axis=0, keepdims=True), sums[1] + jnp.sum(dy * ff, axis=0, keepdims=True))

    zero = jnp.zeros((1, D), F32)
    sum_attn, sum_ffn = lax.fori_loop(0, 2, tile, (zero, zero))
    ga[...] = jnp.concatenate([sum_attn, sum_ffn], axis=0)
    gb_o[...] = jnp.sum(dattn_s[...].astype(F32), axis=0, keepdims=True)
    gb_b[...] = jnp.sum(dff_s[...].astype(F32), axis=0, keepdims=True)
    for s in range(SLABS):
        lanes = slice(s * D, (s + 1) * D)
        gb_i[:, lanes] = jnp.sum(dpre_s[:, lanes].astype(F32), axis=0, keepdims=True)
    both = jnp.concatenate([mixed[0].reshape(2 * BLOCK, HALF), mixed[1].reshape(2 * BLOCK, HALF)], axis=1)
    ht, bt = flip(h_s[...]), flip(both)
    per = count // SLABS

    for core in (c, 1 - c):

        def columns(ref, first):
            return ref[:, pl.ds(pl.multiple_of(first + core * HALF, HALF), HALF)]

        def put(group, first, value):
            if core is c:
                g_keep[group, first : first + value.shape[0], :] = value
            else:
                row = 2 * BLOCK + group * 9 * rd + first
                give[row : row + value.shape[0], :] = value

        dff = columns(dff_s, 0)
        g_out = dot(bt, columns(dattn_s, 0)).astype(BF)
        for i in range(count):
            put(i, 8 * rd, g_out[i * rd : (i + 1) * rd])
        for s in range(SLABS):
            lanes = slice(s * D, (s + 1) * D)
            g_in = dot(ht, columns(dpre_s, s * D)).astype(BF)
            for i in range(count):
                put(i, (4 + s) * rd, g_in[i * rd : (i + 1) * rd])
            g_back = dot(flip(r_s[:, lanes]), dff).astype(BF)
            for i in range(per):
                put(s * per + i, 0, g_back[4 * i * rd : 4 * (i + 1) * rd])


def back_blocks(blocks, kn, vn, kt, q_in, d_in, ot, lse, dk_s, dv_s, dq_out, scratch):
    qz, qzt, oz, ozt, dq_s, p_s, dp_s = scratch
    rows = lax.broadcasted_iota(jnp.int32, (HALF, BLOCK), 0) // HEAD_DIM
    lanes = lax.broadcasted_iota(jnp.int32, (BLOCK, HALF), 1) // HEAD_DIM
    gq = jnp.zeros((1, HALF), F32)
    for i, block in enumerate(blocks):
        q, d_o = q_in[i].astype(F32), d_in[i * BLOCK : (i + 1) * BLOCK].astype(F32)
        qt, dot_ = q.T, d_o.T
        product = dot_ * ot[i]
        deltas = []
        for h in range(CORE_HEADS):
            head = slice(h * HEAD_DIM, (h + 1) * HEAD_DIM)
            deltas.append(jnp.sum(product[head], axis=0, keepdims=True))
            qz[h] = jnp.where(lanes == h, q, 0.0).astype(BF)
            oz[h] = jnp.where(lanes == h, d_o, 0.0).astype(BF)
            qzt[h] = jnp.where(rows == h, qt, 0.0).astype(BF)
            ozt[h] = jnp.where(rows == h, dot_, 0.0).astype(BF)
        dq_s[...] = jnp.zeros_like(dq_s)

        def chunk(first, count):
            size = count * BLOCK
            keys = kn[pl.ds(first, count)].reshape(size, HALF)
            values = vn[pl.ds(first, count)].reshape(size, HALF)
            for h in range(CORE_HEADS):
                p_s[h, :size] = dot(keys, qzt[h])
                dp_s[h, :size] = dot(values, ozt[h])
            dk = dk_s[pl.ds(first, count)].reshape(size, HALF)
            dv = dv_s[pl.ds(first, count)].reshape(size, HALF)
            for h in range(CORE_HEADS):
                head = slice(h * HEAD_DIM, (h + 1) * HEAD_DIM)
                p = jnp.exp(p_s[h, :size] - lse[i, h : h + 1, :])
                ds = (p * (dp_s[h, :size] - deltas[h])).astype(BF)
                dv = dv + dot(p.astype(BF), oz[h])
                dk = dk + dot(ds, qz[h])
                dq = dq_s[head, :]
                for j in range(count):
                    dq = dq + dot(kt[first + j, head, :], ds[j * BLOCK : (j + 1) * BLOCK])
                dq_s[head, :] = dq
            dk_s[pl.ds(first, count)] = dk.reshape(count, BLOCK, HALF)
            dv_s[pl.ds(first, count)] = dv.reshape(count, BLOCK, HALF)

        over_keys(block, chunk)
        dq = (dq_s[...] * (1.0 / math.sqrt(HEAD_DIM))).T.astype(BF)
        gq = gq + jnp.sum(dq.astype(F32), axis=0, keepdims=True)
        dq_out[i] = dq
    return gq


def back_kernel(nz, which, ids, ins, outs, *scratch):
    kn, vn, kt, qn, ot, lse, d_o = ins[:7]
    dk, dv, dq, gq = outs
    if which == 0:
        dk[...] = jnp.zeros_like(dk)
        dv[...] = jnp.zeros_like(dv)
    blocks = query_blocks(ids[0], ids[1], nz)[2 * which : 2 * which + 2]
    gq[...] = back_blocks(blocks, kn, vn, kt, qn, d_o, ot, lse, dk, dv, dq, scratch)


def dx_kernel(nz, ids, ins, outs, dxs):
    wq, dk, dv, dq_mine, dq_other, dx1 = ins
    dx_keep, dqkv, *dx_send = outs
    z, c = ids[0], ids[1]
    dqkv[:, :, :HALF] = jnp.zeros((2 * nz, BLOCK, HALF), BF)
    blocks = query_blocks(z, c, nz)
    for i in range(2):
        dqkv[blocks[i], :, :HALF] = dq_mine[i]
        dqkv[blocks[2 + i], :, :HALF] = dq_other[i]
    w_all = wq[:, :, : 3 * HALF].reshape(D, 3 * HALF)

    def finish(block, unused):
        dqkv[block, :, HALF : 2 * HALF] = dk[block].astype(BF)
        dqkv[block, :, 2 * HALF :] = dv[block].astype(BF)
        dxs[block] = ndot(dqkv[block], w_all)
        return unused

    lax.fori_loop(0, 2 * nz, finish, 0)
    for i in range(2):
        dxs[blocks[i]] = dxs[blocks[i]] + dx1[i]
    half = nz // 2
    for p in range(half):
        chip = ids[4] * half + p
        for i, at in enumerate((chip, nz - 1 - chip)):
            dx_keep[i * half + p] = dxs[2 * at + c].astype(BF)
            dx_send[i][p] = dxs[2 * at + 1 - c].astype(BF)


def dw_kernel(nz, rs, rr, ids, ins, outs, spread):
    xall, dqkv, gq_mine, gq_other, gb_o, gb_i, gb_b, ga = ins
    (dw,) = outs
    c = ids[1]
    gv = jnp.zeros((1, HALF), F32)
    acc = None
    for block in range(2 * nz):
        term = dot(flip(xall[block]), dqkv[block])
        acc = term if block == 0 else acc + term
        gv = gv + jnp.sum(dqkv[block, :, 2 * HALF :].astype(F32), axis=0, keepdims=True)
    gq = gq_mine[...] + gq_other[...]
    nothing = jnp.zeros((1, HALF), F32)
    own = [jnp.concatenate([jnp.where(c == 0, g, nothing), jnp.where(c == 0, nothing, g)], axis=1) for g in (gq, gv)]
    tile = jnp.concatenate(own + [gb_o[...], gb_b[...], jnp.zeros((124, D), F32)], axis=0).T
    spread[...] = jnp.broadcast_to(gb_i[...], (128, FF)).T.reshape(D // rr, SLABS, rr, 128)
    lanes = lax.broadcasted_iota(jnp.int32, (D // rr, rr, 128), 2)
    tile = tile.reshape(D // rr, rr, 128)
    for s in range(SLABS):
        tile = jnp.where(lanes == 4 + s, spread[:, s], tile)
    tile = tile.reshape(D, 128)
    if rs >= 16:
        me = ids[2]
        lane = lax.broadcasted_iota(jnp.int32, (D, 128), 1) - 8 - 6 * (me // rs)
        mine = lax.rem(lax.broadcasted_iota(jnp.int32, (D, 128), 0), rs) == lax.rem(me, rs)
        gates = jnp.sum(ga[...], axis=1, keepdims=True)
        for which in range(2):
            rest = gates[which : which + 1]
            for i in range(3):
                high = rest.astype(BF).astype(F32)
                tile = jnp.where(mine & (lane == 2 * i + which), high, tile)
                rest = rest - high
    rows = dw.shape[1]
    dw[:, :, : 3 * HALF] = acc.astype(BF).reshape(D // rows, rows, 3 * HALF)
    dw[:, :, 3 * HALF :] = tile.astype(BF).reshape(D // rows, rows, 128)


def sum_kernel(plans, ids, ins, outs):
    outs = list(outs)
    for numbers, size, where, pre, post, stride, first, flat in plans:

        def total(static, dynamic):
            source = static * stride // size
            index = (static + dynamic) * stride + first - source * size
            refs = [ins[number] for number in numbers[source]]
            value = refs[0][index]
            if len(refs) == 2 and flat is None:
                value = value.astype(F32) + refs[1][index].astype(F32)
            elif len(refs) == 2:
                rows = value.shape[0]
                start = pl.multiple_of(flat + index * rows, 16)
                value = value.astype(F32) + refs[1][pl.ds(start, rows), :].astype(F32)
            return value

        if where is None:
            out = outs.pop(0)
            for index in range(out.shape[0]):
                out[index] = total(index, 0).astype(out.dtype)
            continue
        keep, send = outs.pop(0), outs.pop(0)
        mine = my_bit(ids, where)
        for p in range(pre):
            for q in range(post):
                keep[p * post + q] = total(2 * p * post + q, mine * post).astype(keep.dtype)
                send[p * post + q] = total(2 * p * post + q, (1 - mine) * post).astype(send.dtype)


def grads_kernel(rs, ids, ins, outs):
    own, other = ins
    w_back, w_in, w_out = outs
    for ref, core in ((own, ids[1]), (other, 1 - ids[1])):

        def lanes(first):
            return pl.ds(pl.multiple_of(first + core * HALF, HALF), HALF)

        value = ref[0].astype(F32)
        w_back[:, lanes(0)] = value[: 4 * rs]
        for s in range(SLABS):
            w_in[:, lanes(s * D)] = value[(4 + s) * rs : (5 + s) * rs]
        w_out[:, lanes(0)] = value[8 * rs :]


def last_kernel(rs, ids, ins, outs):
    own, other = ins
    w_qkv, gb_qv, gb_o, gb_i, gb_b, gates = outs
    for ref, core in ((own, ids[1]), (other, 1 - ids[1])):
        value = ref[0].astype(F32)
        for i in range(3):
            lanes = pl.ds(pl.multiple_of(i * D + core * HALF, HALF), HALF)
            w_qkv[:, lanes] = value[:, i * HALF : (i + 1) * HALF]
    sums = own[0, :, 3 * HALF :] + other[0, :, 3 * HALF :].astype(F32)
    lane = lax.broadcasted_iota(jnp.int32, (1, 128), 1)
    column = jnp.sum(sums, axis=0, keepdims=True)
    for which in range(2):
        used = (lane >= 8) & (lax.rem(lane, 2) == which)
        gates[:, which : which + 1] = jnp.sum(jnp.where(used, column, 0.0), axis=1, keepdims=True)
    by_row = jnp.concatenate([sums, jnp.zeros((128 - rs, 128), F32)], axis=0).T
    gb_qv[...] = by_row[:2, :rs]
    gb_o[...] = by_row[2:3, :rs]
    gb_b[...] = by_row[3:4, :rs]
    for s in range(SLABS):
        gb_i[:, s * rs : (s + 1) * rs] = by_row[4 + s : 5 + s, :rs]


def shape(dims, kind):
    return jax.ShapeDtypeStruct(dims, kind)


def vmem(dims, kind):
    return pltpu.VMEM(dims, kind)


def in_hbm(array):
    return pltpu.with_memory_space_constraint(array, pltpu.HBM)


def cost(megabytes):
    return pl.CostEstimate(flops=0, bytes_accessed=megabytes * 2**20, transcendentals=0)


def call(
    name, kernel, ids, ins, outs, after=(), scratch=(), limit=12, weight=0, where=None, aliases=None, out=VMEM
):
    count, waits = len(ins), len(after)

    def run(*refs):
        given, rest = refs[1 : 1 + count], refs[1 + count + waits :]
        kernel(refs[0], given, rest[: len(outs)], *rest[len(outs) :])

    return pl.pallas_call(
        run,
        out_shape=tuple(outs),
        in_specs=[SMEM] + (where or [VMEM] * count) + [ANY] * waits,
        out_specs=out if isinstance(out, tuple) else (out,) * len(outs),
        scratch_shapes=list(scratch),
        compiler_params=pltpu.CompilerParams(vmem_limit_bytes=limit * 2**20),
        cost_estimate=cost(weight),
        input_output_aliases=aliases or {},
        name=name,
    )(ids, *ins, *after)


def pack_call(ids, rs, ins):
    return call(
        "pack",
        functools.partial(pack_kernel, rs),
        ids,
        [in_hbm(array) for array in ins],
        [vmem((rs, WQ), BF), vmem((9 * rs, HALF), BF), vmem((13 * rs, HALF), BF)] + [vmem((BLOCK, D), BF)] * 4,
        scratch=[pltpu.VMEM(array.shape, BF) for array in ins[:8]]
        + [pltpu.VMEM((128, 128), F32), pltpu.SemaphoreType.DMA((12,))],
        where=[ANY] * 10,
    )


def join_call(name, ids, jobs, after=(), extra=None, extra_ins=(), extra_outs=(), cuts=None):
    ins, outs, spans = [], [], []
    for (own, got, _, _), cut in zip(jobs, cuts or [1] * len(jobs)):
        ins += [own, got]
        spans.append(slice(len(outs), len(outs) + cut))
        outs += [vmem((2 * own.shape[0] // cut,) + own.shape[1:], own.dtype)] * cut
    number = len(outs)

    def kernel(ids_ref, given, results):
        for i, (_, _, where, post) in enumerate(jobs):
            join(ids_ref, given[2 * i], given[2 * i + 1], results[spans[i]], where, post)
        if extra is not None:
            extra(ids_ref, given[2 * len(jobs) :], results[number:])

    return call(name, kernel, ids, ins + list(extra_ins), outs + list(extra_outs), after)


def sum_call(name, ids, jobs, after=(), last=BF, flat=None):
    ins, outs, plans = [], [], []

    def number(array):
        for i, other in enumerate(ins):
            if other is array:
                return i
        ins.append(array)
        return len(ins) - 1

    for sources, where, pre, post, stride, first in jobs:
        numbers = [tuple(number(array) for array in pair if array is not None) for pair in sources]
        tail = sources[0][0].shape[1:]
        size = sources[0][0].shape[0]
        plans.append((numbers, size, where, pre, post, stride, first, flat))
        if where is None:
            outs.append(vmem((size * len(sources) // stride,) + tail, last))
        else:
            outs += [vmem((pre * post,) + tail, last), vmem((pre * post,) + tail, BF)]
    return call(name, functools.partial(sum_kernel, plans), ids, ins, outs, after)


def make_body(n1, n2, nz):
    ndp = n1 * n2
    nsh = ndp * nz * 2
    rs = D // nsh
    rd = D // ndp
    half = nz // 2
    parts = 2 * nz if rs % 16 == 0 else 1
    rr = rd // parts
    nh = 9 * rd // 2
    swap = [(0, 1), (1, 0)]
    bits_a, bits_b, bits_z = (count.bit_length() - 1 for count in (n1, n2, nz))
    counts = {"a": n1, "b": n2, "z": nz}
    slot = {"a": 3, "b": 5, "z": 0}

    def to_mirror(array):
        return lax.ppermute(array, "z", [(s, nz - 1 - s) for s in range(nz)])

    def exchange(array, name, bit):
        return lax.ppermute(array, name, [(s, s ^ (1 << bit)) for s in range(counts[name])])

    def to_other(array):
        return lax.ppermute(array, "c", swap)

    def body(inputs, w_qkv, bias_qv, w_out, bias_out, w_in, bias_in, w_back, bias_back, alphas, cotangent):
        z, c = lax.axis_index("z"), lax.axis_index("c")
        a, b = lax.axis_index("a"), lax.axis_index("b")
        device = ((a * n2 + b) * nz + z) * 2 + c
        ids = jnp.stack([z, c, device, a, z // half, b]).astype(jnp.int32)

        latest = []

        def hand_on(ids_ref, given, results):
            for source, target in zip(given, results):
                target[...] = source[...]

        def step(name, jobs, extra=(), cuts=None, others=()):
            result = join_call(
                name, ids, jobs, latest + list(others), hand_on, extra, [vmem(e.shape, e.dtype) for e in extra], cuts
            )
            latest[:] = [result[0]]
            return result


        q_keep, f_keep, give, x_give, x_keep, cot_give, cot_a = pack_call(
            ids, rs,
            [w_qkv, w_back, w_in, w_out, bias_qv, bias_out[None], bias_back[None], bias_in[None], inputs, cotangent],
        )
        wq, wf = call(
            "core", functools.partial(core_kernel, rs), ids, [q_keep, f_keep, to_other(give)],
            [vmem((2, rs, WQ), BF), vmem((2, 9 * rs, HALF), BF)],
        )
        latest[:] = [wq]
        wq, wf = wq.reshape(1, 2 * rs, WQ), wf.reshape(1, 2 * 9 * rs, HALF)
        wf = wf.reshape(2 * 9 * rs, HALF)
        q_got = exchange(wq, "z", bits_z - 1)
        wf_parts = [(wf, 0)]
        for i in reversed(range(bits_z)):
            wf_parts += [(exchange(part, "z", i), place | (1 << i)) for part, place in wf_parts]
        wf_near = [part for part, place in wf_parts if place == 1]
        for i in reversed(range(1, bits_z)):
            (wq,) = step("q_z", [(wq, q_got, (0, i), 1)])
            q_got = exchange(wq, "z", i - 1)
        wq, x_keep, x_give = step(
            "q_z", [(wq, q_got, (0, 0), 1)], [x_keep, x_give], others=wf_near + [wf_parts[1][0]]
        )
        wq = wq.reshape(rd, WQ)
        if parts == 1:
            hidden_bias = wq[:, 3 * HALF + 4 : 3 * HALF + 8].reshape(2 * nz, rs, SLABS)
            hidden_bias = jnp.transpose(hidden_bias, (0, 2, 1)).reshape(SLABS, rd).T
            wq = jnp.concatenate([wq[:, : 3 * HALF + 4], hidden_bias, wq[:, 3 * HALF + 8 :]], axis=1)
        wq = wq[None]
        x_far = to_mirror(x_give)
        for i in reversed(range(1, bits_b)):
            q_got = exchange(wq, "b", i)
            (wq,) = step("q_b", [(wq, q_got, (5, i), 1)])
        q_got = exchange(wq, "b", 0)
        own = x_keep[None]
        own_got = exchange(own, "z", max(bits_z - 2, 0))

        def in_place(ids_ref, given, results):
            for group in range(2):

                @pl.when(ids_ref[4] == group)
                def _():
                    for ref, (_, place) in zip(given, wf_parts):
                        at = lax.rem(lax.bitwise_xor(ids_ref[0], place), half)
                        results[group ^ (place // half)][at] = ref[...]

        halves = vmem((half, 2 * 9 * rs, HALF), BF)
        first, second = call("f_z", in_place, ids, [part for part, _ in wf_parts], [halves, halves], latest)
        latest[:] = [first]
        if parts == 1:
            wf = jnp.concatenate([first, second], axis=0).reshape(nz, 2, 9 * rs, HALF)
            wf = jnp.concatenate(
                [wf[:, :, : 4 * rs].reshape(4 * rd, HALF)]
                + [wf[:, :, (4 + s) * rs : (5 + s) * rs].reshape(rd, HALF) for s in range(SLABS)]
                + [wf[:, :, 8 * rs :].reshape(rd, HALF)],
                axis=0,
            )
            first, second = wf[:nh], wf[nh:]
        first, second = first.reshape(1, nh, HALF), second.reshape(1, nh, HALF)
        (wq,) = step("q_b", [(wq, q_got, (5, 0), 1)])
        for i in reversed(range(1, bits_a)):
            q_got = exchange(wq, "a", i)
            (wq,) = step("q_a", [(wq, q_got, (3, i), n2)])
        wq_pieces = [wq, exchange(wq, "a", 0)]

        far_rows, cot_give = call(
            "x_far", hand_on, ids, [x_far, cot_give], [vmem((BLOCK, D), BF)] * 2, latest + [own_got]
        )
        latest[:] = [far_rows]
        cot_b = to_mirror(cot_give)
        far_rows = far_rows[None]
        for i in reversed(range(1, bits_z - 1)):
            far_got = exchange(far_rows, "z", i)
            own, far_rows = step("x_z", [(own, own_got, (0, i), 1), (far_rows, far_got, (0, i), 1)])
            own_got = exchange(own, "z", i - 1)
        far_got = exchange(far_rows, "z", 0)

        for i in reversed(range(bits_b)):
            got = exchange(first, "b", i), exchange(second, "a", i)
            first, second = step("f_dp", [(first, got[0], (5, i), 1), (second, got[1], (3, i), 1)])
        for i in reversed(range(1, bits_a)):
            got = exchange(first, "a", i), exchange(second, "b", i)
            first, second = step("f_dp", [(first, got[0], (3, i), n2), (second, got[1], (5, i), 1)])
        wf_pieces = [first, second, exchange(first, "a", 0), exchange(second, "b", 0)]

        def rows_of_all(ids_ref, given, results):
            own_ref, own_got_ref, far_ref, far_got_ref = given
            base, mine = ids_ref[4] * half, my_bit(ids_ref, (0, 0))
            for p in range(half // 2):
                for own_part, far_part, at in (
                    (own_ref, far_ref, base + 2 * p + mine),
                    (own_got_ref, far_got_ref, base + 2 * p + 1 - mine),
                ):
                    results[0][at - base] = own_part[p]
                    results[1][at - base] = far_part[p]

        xo = call(
            "x_all", rows_of_all, ids, [own, own_got, far_rows, far_got], [vmem((half, BLOCK, D), BF)] * 2,
            latest + [wq_pieces[1], cot_b],
        )
        latest[:] = [xo[0]]
        xs = [to_other(part) for part in xo]

        nb = 2 * nz
        heads_t = pltpu.VMEM((CORE_HEADS, HALF, BLOCK), BF)
        scores = pltpu.VMEM((CORE_HEADS, 2 * BLOCK, BLOCK), F32)
        scratch = [
            heads_t,
            scores,
            pltpu.VMEM((CORE_HEADS, 1, BLOCK), F32),
            pltpu.VMEM((CORE_HEADS, 1, BLOCK), F32),
            pltpu.VMEM((HALF, BLOCK), F32),
        ]
        natural, turned = (nb, BLOCK, HALF), (nb, HALF, BLOCK)
        two, two_t = (2, BLOCK, HALF), (2, HALF, BLOCK)
        two_lse = (2, CORE_HEADS, BLOCK)
        spread = pltpu.VMEM((D // rr, SLABS, rr, 128), F32)
        (xall, wq, kn, vn, kt, vt, q_mine, q_other, ot_other, lse_other, o_send, bo, bb, bi) = call(
            "first",
            functools.partial(first_kernel, nz, ndp, n2, rr),
            ids,
            [*xo, *xs, *wq_pieces],
            [
                vmem((nb, BLOCK, D), BF),
                vmem((ndp, rd, WQ), BF),
                vmem(natural, BF),
                vmem(natural, BF),
                vmem(turned, BF),
                vmem(turned, BF),
                vmem(two, BF),
                vmem(two, BF),
                vmem(two_t, F32),
                vmem(two_lse, F32),
                vmem(two, BF),
                vmem((1, D), F32),
                vmem((1, D), F32),
                vmem((1, FF), F32),
            ],
            latest,
            [spread] + scratch,
            limit=16,
        )

        def give_kernel(ids_ref, given, results):
            row = 0
            for part in given:
                for i in range(part.shape[0]):
                    results[0][row : row + part.shape[1]] = part[i]
                    row += part.shape[1]

        (give,) = call(
            "give", give_kernel, ids, [o_send, *wf_pieces], [vmem((2 * BLOCK + 2 * ndp * nh, HALF), BF)],
            limit=16,
        )
        ffn_got = to_other(give)
        ot_mine, lse_mine, o_mine = call(
            "second",
            functools.partial(second_kernel, nz),
            ids,
            [kn, vt, q_mine],
            [vmem(two_t, F32), vmem(two_lse, F32), vmem(two, BF)],
            (),
            scratch,
        )

        grouped = (ndp * parts, 9 * rd // parts, HALF)
        (out_near, out_far, dx1, d_mine, g_keep, give, gb_o, gb_i, gb_b, ga) = call(
            "ffn",
            functools.partial(ffn_kernel, nz, ndp, n2, parts),
            ids,
            [alphas, o_mine, ffn_got, xall, cot_a, cot_b, bo, bi, bb, *wf_pieces],
            [
                vmem((BLOCK, D), BF),
                vmem((BLOCK, D), BF),
                vmem((2, BLOCK, D), F32),
                vmem((2 * BLOCK, HALF), BF),
                vmem(grouped, BF),
                vmem((2 * BLOCK + ndp * 9 * rd, HALF), BF),
                vmem((1, D), F32),
                vmem((1, FF), F32),
                vmem((1, D), F32),
                vmem((2, D), F32),
            ],
            scratch=[
                pltpu.VMEM((2, 2 * ndp, nh, HALF), BF),
                pltpu.VMEM((D, D), BF),
                pltpu.VMEM((SLABS, D, D), BF),
                pltpu.VMEM((FF, D), BF),
                pltpu.VMEM((2, 2, BLOCK, HALF), BF),
                pltpu.VMEM((2 * BLOCK, D), BF),
                pltpu.VMEM((2 * BLOCK, FF), BF),
                pltpu.VMEM((2 * BLOCK, FF), BF),
                pltpu.VMEM((2 * BLOCK, D), BF),
                pltpu.VMEM((2 * BLOCK, D), BF),
            ],
            limit=28,
            where=[SMEM] + [VMEM] * 12,
        )
        back_got = to_other(give)
        back_scratch = [
            pltpu.VMEM((CORE_HEADS, BLOCK, HALF), BF),
            heads_t,
            pltpu.VMEM((CORE_HEADS, BLOCK, HALF), BF),
            heads_t,
            pltpu.VMEM((HALF, BLOCK), F32),
            scores,
            scores,
        ]
        back_out = [vmem(natural, F32), vmem(natural, F32), vmem(two, BF), vmem((1, HALF), F32)]
        dk, dv, dq_mine, gq_mine = call(
            "back_first",
            functools.partial(back_kernel, nz, 0),
            ids,
            [kn, vn, kt, q_mine, ot_mine, lse_mine, d_mine],
            back_out,
            scratch=back_scratch,
            limit=16,
        )

        latest[:] = [gq_mine]
        done = {}

        def along(axis, count, pre, post):
            return [(axis, i, pre * (count >> (i + 1)), post) for i in range(count.bit_length() - 1)]

        def dp_scatter(name, kept, got, rows, columns, flat=None):
            axes = (along("b", n2, n1, 1) + along("a", n1, 1, 1), along("a", n1, 1, n2) + along("b", n2, 1, 1))
            whole = (kept.reshape(2 * ndp, rows, columns), got)
            state = [(whole, 2, 0), (whole, 2, 1)]
            for i in range(len(axes[0])):
                result = sum_call(
                    name,
                    ids,
                    [
                        ([pair], (slot[axis], bit), pre, post, stride, first)
                        for (pair, stride, first), (axis, bit, pre, post) in zip(state, (axes[0][i], axes[1][i]))
                    ],
                    latest,
                    flat=flat if i == 0 else None,
                )
                latest[:] = [result[0]]
                state = [
                    ((result[2 * j], exchange(result[2 * j + 1], axes[j][i][0], axes[j][i][1])), 1, 0)
                    for j in range(2)
                ]
                yield
            return [pair for pair, _, _ in state]

        def z_scatter(name, sources):
            for _, i, pre, _ in along("z", nz, 1, 1):
                kept, send = sum_call(name, ids, [(sources, (slot["z"], i), pre, 1, 1, 0)], latest)
                latest[:] = [kept]
                sources = [(kept, exchange(send, "z", i))]
                yield
            rows, columns = kept.shape[1] // 2, kept.shape[2]
            sources = [tuple(array.reshape(2, rows, columns) for array in sources[0])]
            keep, send = sum_call(name, ids, [(sources, (1, 0), 1, 1, 1, 0)], latest, F32)
            latest[:] = [keep]
            return keep, to_other(send)

        def whole_dp(name, sources):
            return [part[0] for part in sum_call(name, ids, [([pair], None, 0, 0, 1, 0) for pair in sources], latest)]

        def g_chain():
            sources = yield from dp_scatter("g_dp", g_keep, back_got, nh, HALF, 2 * BLOCK)
            if parts == 1:
                g_dp = jnp.concatenate(whole_dp("g_dp", sources), axis=0)
                g_dp = jnp.concatenate(
                    [g_dp[: 4 * rd].reshape(nz, 2, 4 * rs, HALF)]
                    + [g_dp[(4 + s) * rd : (5 + s) * rd].reshape(nz, 2, rs, HALF) for s in range(SLABS)]
                    + [g_dp[8 * rd :].reshape(nz, 2, rs, HALF)],
                    axis=2,
                )
                sources = [(g_dp.reshape(nz, 2 * 9 * rs, HALF), None)]
            else:
                sources = [tuple(array.reshape(half, 2 * 9 * rs, HALF) for array in pair) for pair in sources]
            keep, got = yield from z_scatter("g_z", sources)
            yield
            done["g"] = call(
                "g_last", functools.partial(grads_kernel, rs), ids, [keep, got],
                [shape((4 * rs, D), F32), shape((rs, FF), F32), shape((rs, D), F32)], latest,
            )
            latest[:] = [done["g"][2]]

        g_steps = g_chain()
        next(g_steps)
        dk, dv, dq_other, gq_other = call(
            "back_second",
            functools.partial(back_kernel, nz, 1),
            ids,
            [kn, vn, kt, q_other, ot_other, lse_other, back_got, dk, dv],
            back_out,
            latest,
            back_scratch,
            limit=16,
            aliases={8: 0, 9: 1},
        )
        def out_kernel(ids_ref, given, results, sems):
            group = ids_ref[4]
            copies = moves(sems, [(given[0], results[0].at[group]), (given[1], results[0].at[1 - group])])
            results[1][...] = jnp.zeros_like(results[1])
            wait(copies)

        def to_rows(name, own, got):
            rows, token = call(
                name, out_kernel, ids, [own, got], [pltpu.HBM((2, BLOCK, D), BF), vmem((8, 128), F32)], latest,
                [pltpu.SemaphoreType.DMA((2,))], where=[ANY, ANY],
                out=(pl.BlockSpec(memory_space=pltpu.HBM), VMEM),
            )
            latest[:] = [token]
            return rows

        latest[:] = [gq_other]
        dx_keep, dqkv, *dx_send = call(
            "dx",
            functools.partial(dx_kernel, nz),
            ids,
            [wq, dk, dv, dq_mine, dq_other, dx1],
            [vmem((nz, BLOCK, D), BF), vmem((nb, BLOCK, 3 * HALF), BF)]
            + [vmem((half, BLOCK, D), BF)] * 2,
            latest,
            [pltpu.VMEM((nb, BLOCK, D), F32)],
        )
        dx_got = [to_other(part) for part in dx_send]
        latest[:] = [dx_keep]
        next(g_steps)
        def dx_chain():
            def first_sums(ids_ref, given, results):
                mine = my_bit(ids_ref, (0, 0))
                kept, got = given[0], given[1:]
                for i in range(2):
                    for p in range(half // 2):
                        for bit, target in ((mine, results[0]), (1 - mine, results[1])):
                            received = got[i][2 * p + bit].astype(F32)
                            value = kept[i * half + 2 * p + bit].astype(F32) + received
                            target[i * (half // 2) + p] = value.astype(BF)

            kept, send = call(
                "dx_z", first_sums, ids, [dx_keep, *dx_got], [vmem((half, BLOCK, D), BF)] * 2, latest
            )
            latest[:] = [kept]
            got = exchange(send, "z", 0)
            yield
            for i in range(1, bits_z - 1):
                kept, send = sum_call("dx_z", ids, [([(kept, got)], (0, i), nz >> (i + 1), 1, 1, 0)], latest)
                latest[:] = [kept]
                got = exchange(send, "z", i)
                yield
            near, far = sum_call("dx_z", ids, [([(kept, got)], (0, 30), 1, 1, 1, 0)], latest)
            latest[:] = [near]
            got = to_mirror(far.reshape(BLOCK, D))
            yield
            done["inputs"] = to_rows("dx_last", near.reshape(BLOCK, D), got)

        def dw_chain():
            sources = yield from dp_scatter("w_dp", dw, None, rd // 2, WQ)
            if parts == 1:
                dw_dp = jnp.concatenate(whole_dp("w_dp", sources), axis=0)
                hidden_bias = dw_dp[:, 3 * HALF + 4 : 3 * HALF + 8].T.reshape(2 * nz, SLABS, rs)
                hidden_bias = jnp.transpose(hidden_bias, (0, 2, 1)).reshape(rd, SLABS)
                dw_dp = jnp.concatenate([dw_dp[:, : 3 * HALF + 4], hidden_bias, dw_dp[:, 3 * HALF + 8 :]], axis=1)
                sources = [(dw_dp.reshape(nz, 2 * rs, WQ), None)]
            else:
                sources = [tuple(array.reshape(half, 2 * rs, WQ) for array in pair) for pair in sources]
            keep, got = yield from z_scatter("w_z", sources)
            yield
            done["w"] = call(
                "w_last", functools.partial(last_kernel, rs), ids, [keep, got],
                [shape((rs, 3 * D), F32), shape((2, rs), F32), shape((1, rs), F32), shape((1, SLABS * rs), F32)]
                + [shape((1, rs), F32), shape((1, 2), F32)],
                latest,
            )
            latest[:] = [done["w"][0]]

        dx_steps = dx_chain()
        next(dx_steps)
        (dw,) = call(
            "dw",
            functools.partial(dw_kernel, nz, rs, rr),
            ids,
            [xall, dqkv, gq_mine, gq_other, gb_o, gb_i, gb_b, ga],
            [vmem((2 * ndp, rd // 2, WQ), BF)],
            latest,
            [spread],
        )

        latest[:] = [dw]

        out_b = to_mirror(out_far)
        steps = {"x": dx_steps, "g": g_steps, "w": dw_chain()}
        for name in "wgwxwogwgxwgw" + "xgw" * bits_z:
            if name == "o":
                outputs = to_rows("outputs", out_near, out_b)
            else:
                next(steps[name], 0)
        gb_qv, gb_out, gb_in, gb_back, grad_alphas = done["w"][1:]
        if rs < 16:
            grad_alphas = lax.psum(jnp.sum(ga, axis=1), MESH_AXES)
        return (
            outputs,
            done["inputs"],
            done["w"][0],
            gb_qv,
            done["g"][2],
            gb_out.reshape(rs),
            done["g"][1],
            gb_in.reshape(SLABS * rs),
            done["g"][0],
            gb_back.reshape(rs),
            grad_alphas.reshape(2),
        )

    return body


def solution(mesh):
    ndp, nseq = mesh.devices.shape
    n1 = math.isqrt(ndp)
    n2 = ndp // n1
    nz = nseq // 2
    fine = Mesh(mesh.devices.reshape(n1, n2, nz, 2), MESH_AXES)
    dp, seq = ("a", "b"), ("z", "c")
    rows = P(dp, seq, None)
    both = dp + seq
    return jax.shard_map(
        make_body(n1, n2, nz),
        mesh=fine,
        in_specs=(
            rows,
            P(both, None),
            P(None, both),
            P(both, None),
            P(both),
            P(both, None),
            P(both),
            P(both, None),
            P(both),
            P(),
            rows,
        ),
        out_specs=(
            rows,
            rows,
            P(both, None),
            P(None, both),
            P(both, None),
            P(both),
            P(both, None),
            P(both),
            P(both, None),
            P(both),
            P(),
        ),
        check_vma=False,
    )
```

```python
import functools
import math

import jax
import jax.numpy as jnp
from jax import lax
from jax.experimental import pallas as pl
from jax.experimental.pallas import tpu as pltpu
from jax.sharding import Mesh, PartitionSpec as P

D = 512
HEADS = 8
HEAD_DIM = 64
FF = 2048
BLOCK = 256
HALF = D // 2
CORE_HEADS = HEADS // 2
SLABS = FF // D
BF = jnp.bfloat16
F32 = jnp.float32
MESH_AXES = ("a", "b", "z", "c")
VMEM = pl.BlockSpec(memory_space=pltpu.VMEM)
SMEM = pl.BlockSpec(memory_space=pltpu.SMEM)
ANY = pl.BlockSpec(memory_space=pl.ANY)
WQ = 3 * HALF + 128
GELU_C = math.sqrt(2.0 / math.pi)


def dot(left, right):
    return jnp.dot(left, right, preferred_element_type=F32)


def ndot(left, right):
    return lax.dot_general(left, right, (((1,), (1,)), ((), ())), preferred_element_type=F32)


def flip(block):
    return block.T


def query_blocks(z, c, nz):
    near, far = 2 * z, 2 * (nz - 1 - z)
    return (near + c, far + c, near + 1 - c, far + 1 - c)


def over_keys(block, chunk):
    def step(i, unused):
        chunk(2 * i, 2)
        return unused

    lax.fori_loop(0, (block + 1) // 2, step, 0)

    @pl.when(lax.rem(block, 2) == 0)
    def _():
        chunk(block, 1)


def attend_blocks(blocks, kn, vt, qn, ot, lse, o, scratch):
    qz, s_s, m_s, l_s, acc_s = scratch
    rows = lax.broadcasted_iota(jnp.int32, (HALF, BLOCK), 0) // HEAD_DIM
    for i, block in enumerate(blocks):
        qt = qn[i].astype(F32).T
        for h in range(CORE_HEADS):
            qz[h] = jnp.where(rows == h, qt, 0.0).astype(BF)
        m_s[...] = jnp.full_like(m_s, -1e30)
        l_s[...] = jnp.zeros_like(l_s)
        acc_s[...] = jnp.zeros_like(acc_s)

        def chunk(first, count):
            keys = kn[pl.ds(first, count)].reshape(count * BLOCK, HALF)
            for h in range(CORE_HEADS):
                s_s[h, : count * BLOCK] = dot(keys, qz[h])
            for h in range(CORE_HEADS):
                head = slice(h * HEAD_DIM, (h + 1) * HEAD_DIM)
                s = s_s[h, : count * BLOCK]
                old = m_s[h]
                new = jnp.maximum(old, jnp.max(s, axis=0, keepdims=True))
                p = jnp.exp(s - new)
                shrink = jnp.exp(old - new)
                m_s[h] = new
                l_s[h] = l_s[h] * shrink + jnp.sum(p, axis=0, keepdims=True)
                p = p.astype(BF)
                acc = acc_s[head, :] * shrink
                for j in range(count):
                    acc = acc + dot(vt[first + j, head, :], p[j * BLOCK : (j + 1) * BLOCK])
                acc_s[head, :] = acc

        over_keys(block, chunk)
        for h in range(CORE_HEADS):
            head = slice(h * HEAD_DIM, (h + 1) * HEAD_DIM)
            total = l_s[h]
            lse[i, h : h + 1, :] = m_s[h] + jnp.log(total)
            acc_s[head, :] = acc_s[head, :] / total
        value = acc_s[...]
        ot[i] = value
        o[i] = value.T.astype(BF)


def moves(sems, pairs):
    copies = [pltpu.make_async_copy(src, dst, sems.at[i]) for i, (src, dst) in enumerate(pairs)]
    for copy in copies:
        copy.start()
    return copies


def wait(copies):
    for copy in copies:
        copy.wait()


def pack_kernel(rs, ids, ins, outs, *refs):
    w_qkv, w_back, w_in, w_out, bias_qv, bias_out, bias_back, bias_in = refs[:8]
    tile, sems = refs[8], refs[9]
    group = ids[4]
    loads = moves(sems, [(ins[i], refs[i]) for i in range(8)])
    rows = moves(
        sems.at[pl.ds(8, 4)],
        [(ins[8 + i].at[which], outs[3 + 2 * i + j]) for i in range(2) for j, which in enumerate((1 - group, group))],
    )
    wait(loads)
    tile[...] = jnp.zeros_like(tile)
    tile[0:2, :rs] = bias_qv[...].astype(F32)
    tile[2:3, :rs] = bias_out[...].astype(F32)
    tile[3:4, :rs] = bias_back[...].astype(F32)
    for i in range(SLABS):
        tile[4 + i : 5 + i, :rs] = bias_in[:, i * rs : (i + 1) * rs].astype(F32)
    turned = tile[...].T[:rs].astype(BF)
    q_keep, f_keep, give = outs[:3]

    def cut(ref, first, core):
        return ref[:, pl.ds(pl.multiple_of(first + core * HALF, HALF), HALF)]

    for i in range(3):
        q_keep[:, i * HALF : (i + 1) * HALF] = cut(w_qkv, i * D, ids[1])
        give[(9 + i) * rs : (10 + i) * rs] = cut(w_qkv, i * D, 1 - ids[1])
    q_keep[:, 3 * HALF :] = turned
    give[12 * rs :, :128] = turned
    give[12 * rs :, 128:] = jnp.zeros((rs, 128), BF)
    for f_out, core in ((f_keep, ids[1]), (give, 1 - ids[1])):
        f_out[: 4 * rs] = cut(w_back, 0, core)
        for i in range(SLABS):
            f_out[(4 + i) * rs : (5 + i) * rs] = cut(w_in, i * D, core)
        f_out[8 * rs : 9 * rs] = cut(w_out, 0, core)
    wait(rows)


def core_kernel(rs, ids, ins, outs):
    q_keep, f_keep, got = ins
    wq, wf = outs
    c = ids[1]
    wq[c] = q_keep[...]
    wf[c] = f_keep[...]
    wf[1 - c] = got[: 9 * rs]
    for i in range(3):
        wq[1 - c, :, i * HALF : (i + 1) * HALF] = got[(9 + i) * rs : (10 + i) * rs]
    wq[1 - c, :, 3 * HALF :] = got[12 * rs :, :128]


def my_bit(ids, where):
    index, bit = where
    return lax.rem(lax.shift_right_logical(ids[index], bit), 2)


def join(ids, own, got, outs, where, post=1):
    mine = my_bit(ids, where)
    pre = own.shape[0] // post
    for p in range(pre):
        out = outs[p * len(outs) // pre]
        at = 2 * p - 2 * pre // len(outs) * (p * len(outs) // pre)
        for q in range(post):
            out[(at + mine) * post + q] = own[p * post + q]
            out[(at + 1 - mine) * post + q] = got[p * post + q]


def first_kernel(nz, ndp, n2, rr, ids, ins, outs, spread, *scratch):
    xo, xs = ins[:2], ins[2:4]
    wq_pieces = ins[4:6]
    xall, wq, kn, vn, kt, vt, q_mine, q_other, ot, lse, o, bo, bb, bi = outs
    z, c = ids[0], ids[1]
    for p in range(nz // 2):
        chip = ids[4] * (nz // 2) + p
        for i, at in enumerate((chip, nz - 1 - chip)):
            xall[2 * at + c] = xo[i][p]
            xall[2 * at + 1 - c] = xs[i][p]
    for far, piece in enumerate(wq_pieces):
        bit = lax.rem(ids[3], 2)
        for j in range(piece.shape[0]):
            wq[(2 * (j // n2) + (1 - bit if far else bit)) * n2 + j % n2] = piece[j]
    bias = wq[:, :, 3 * HALF :].reshape(D, 128).astype(F32)
    turned = bias.T
    bo[...] = turned[2:3]
    bb[...] = turned[3:4]
    lanes = lax.broadcasted_iota(jnp.int32, (D // rr, rr, 128), 2)
    for s in range(SLABS):
        spread[:, s] = jnp.where(lanes == 4 + s, bias.reshape(D // rr, rr, 128), 0.0)
    bi[...] = jnp.sum(spread[...].reshape(FF, 128).T[4:8], axis=0, keepdims=True)
    bias_q = jnp.where(c == 0, turned[0:1, :HALF], turned[0:1, HALF:])
    bias_v = jnp.where(c == 0, turned[1:2, :HALF], turned[1:2, HALF:])
    w_q = wq[:, :, :HALF].reshape(D, HALF)
    w_kv = wq[:, :, HALF : 3 * HALF].reshape(D, 2 * HALF)

    def project(block, unused):
        kv = dot(xall[block], w_kv)
        key = kv[:, :HALF]
        kn[block] = key.astype(BF)
        kt[block] = key.astype(BF).T
        value = kv[:, HALF:] + bias_v
        vn[block] = value.astype(BF)
        vt[block] = value.astype(BF).T
        return unused

    lax.fori_loop(0, 2 * nz, project, 0)
    blocks = query_blocks(z, c, nz)
    for i, block in enumerate(blocks):
        q = (dot(xall[block], w_q) + bias_q).astype(BF).astype(F32) * (1.0 / math.sqrt(HEAD_DIM))
        (q_mine if i < 2 else q_other)[i % 2] = q.astype(BF)
    attend_blocks(blocks[2:], kn, vt, q_other, ot, lse, o, scratch)


def place_dp(ids, pieces, ndp, n2, put):
    for i, piece in enumerate(pieces):
        far, half = i // 2, i % 2
        for j in range(ndp // 2):
            if half == 0:
                bit = lax.rem(ids[3], 2)
                dp = (2 * (j // n2) + (1 - bit if far else bit)) * n2 + j % n2
            else:
                bit = lax.rem(ids[5], 2)
                dp = j // (n2 // 2) * n2 + 2 * (j % (n2 // 2)) + (1 - bit if far else bit)
            put(dp, half, piece(j) if callable(piece) else piece[j])


def second_kernel(nz, ids, ins, outs, *scratch):
    kn, vt, qn = ins
    ot, lse, o = outs
    blocks = query_blocks(ids[0], ids[1], nz)
    attend_blocks(blocks[:2], kn, vt, qn, ot, lse, o, scratch)


def ffn_kernel(nz, ndp, n2, parts, ids, ins, outs, *refs):
    alphas, o_mine, got, xall, cot_a, cot_b, bo, bi, bb = ins[:9]
    pieces = ins[9:13]
    rows = pieces[0].shape[1]

    def received(i):
        return lambda j: got[pl.ds(2 * BLOCK + (i * (ndp // 2) + j) * rows, rows)]

    (out_near, out_far, dx1, d_mine, g_keep, give, gb_o, gb_i, gb_b, ga) = outs
    w, wo_s, wi_s, wb_s, mixed, h_s, r_s, dpre_s, dff_s, dattn_s = refs[:10]
    pre_s, dr_s = refs[10:12]
    c = ids[1]
    count = ndp * parts
    rd = D // count
    for core in range(2):
        own = pieces if core == 0 else [received(i) for i in range(4)]
        which = c if core == 0 else 1 - c
        lanes = pl.ds(pl.multiple_of(which * HALF, HALF), HALF)

        def put(dp, half, value):
            if parts == 1:
                w[which, 2 * dp + half] = value
                return
            for g in range(parts // 2):
                at = dp * parts + half * (parts // 2) + g
                part = value[9 * rd * g : 9 * rd * (g + 1)]
                wb_s[pl.ds(pl.multiple_of(at * 4 * rd, 4 * rd), 4 * rd), lanes] = part[: 4 * rd]
                at = pl.multiple_of(at * rd, rd)
                for s in range(SLABS):
                    wi_s[s, pl.ds(at, rd), lanes] = part[(4 + s) * rd : (5 + s) * rd]
                wo_s[pl.ds(at, rd), lanes] = part[8 * rd :]

        place_dp(ids, own, ndp, n2, put)
    if parts == 1:
        for half in range(2):
            lanes = slice(half * HALF, (half + 1) * HALF)
            whole = w[half].reshape(count, 9 * rd, HALF)
            wo_s[:, lanes] = whole[:, 8 * rd :].reshape(D, HALF)
            for s in range(SLABS):
                wi_s[s, :, lanes] = whole[:, (4 + s) * rd : (5 + s) * rd].reshape(D, HALF)
            wb_s[:, lanes] = whole[:, : 4 * rd].reshape(FF, HALF)
    mixed[c] = o_mine[...].reshape(2 * BLOCK, HALF)
    mixed[1 - c] = got[: 2 * BLOCK]
    alpha_attn, alpha_ffn = alphas[0], alphas[1]
    mine = query_blocks(ids[0], c, nz)
    both = 2 * BLOCK
    dy = jnp.concatenate([cot_a[...], cot_b[...]], axis=0).astype(F32)
    dff = (alpha_ffn * dy).astype(BF)
    dff_s[...] = dff
    attn = dot(mixed[0], wo_s[:HALF, :]) + dot(mixed[1], wo_s[HALF:, :]) + bo[...]
    x1 = jnp.concatenate([xall[mine[0]], xall[mine[1]]], axis=0).astype(F32) + alpha_attn * attn
    hidden = x1.astype(BF)
    h_s[...] = hidden
    x1_s = refs[12]
    attn_s = refs[13]
    x1_s[...] = x1
    attn_s[...] = attn
    for s in range(SLABS):
        lanes = slice(s * D, (s + 1) * D)
        pre_s[s] = dot(h_s[...], wi_s[s]) + bi[:, lanes]
        dr_s[s] = ndot(dff_s[...], wb_s[lanes, :])
    ff = None
    dx = None
    for s in range(SLABS):
        lanes = slice(s * D, (s + 1) * D)
        pre = pre_s[s]
        square = pre * pre
        up = 0.5 + 0.5 * jnp.tanh(pre * (GELU_C + (GELU_C * 0.044715) * square))
        r = pre * up
        r_s[:, lanes] = r.astype(BF)
        slope = up + r * (1.0 - up) * (2.0 * GELU_C + (6.0 * GELU_C * 0.044715) * square)
        dpre_s[:, lanes] = (dr_s[s] * slope).astype(BF)
    for s in range(SLABS):
        lanes = slice(s * D, (s + 1) * D)
        t1 = dot(r_s[:, lanes], wb_s[lanes, :])
        t2 = ndot(dpre_s[:, lanes], wi_s[s])
        ff = t1 if ff is None else ff + t1
        dx = t2 if dx is None else dx + t2
    ff = ff + bb[...]
    x1 = x1_s[...]
    out = (x1 + alpha_ffn * ff).astype(BF)
    out_near[...] = out[:BLOCK]
    out_far[...] = out[BLOCK:]
    dy = jnp.concatenate([cot_a[...], cot_b[...]], axis=0).astype(F32)
    dx = dx + dy
    dx1[0] = dx[:BLOCK]
    dx1[1] = dx[BLOCK:]
    dattn = (alpha_attn * dx).astype(BF)
    dattn_s[...] = dattn
    d_mine[...] = ndot(dattn, wo_s[pl.ds(pl.multiple_of(c * HALF, HALF), HALF), :]).astype(BF)
    give[:both, :] = ndot(dattn, wo_s[pl.ds(pl.multiple_of((1 - c) * HALF, HALF), HALF), :]).astype(BF)
    ga[...] = jnp.concatenate(
        [jnp.sum(dx * attn_s[...], axis=0, keepdims=True), jnp.sum(dy * ff, axis=0, keepdims=True)], axis=0
    )
    gb_o[...] = jnp.sum(dattn_s[...].astype(F32), axis=0, keepdims=True)
    gb_b[...] = jnp.sum(dff_s[...].astype(F32), axis=0, keepdims=True)
    for s in range(SLABS):
        lanes = slice(s * D, (s + 1) * D)
        gb_i[:, lanes] = jnp.sum(dpre_s[:, lanes].astype(F32), axis=0, keepdims=True)
    both_t = jnp.concatenate([mixed[0], mixed[1]], axis=1).T
    ht = h_s[...].T
    per = count // SLABS

    def columns(ref, first, core):
        return ref[:, pl.ds(pl.multiple_of(first + core * HALF, HALF), HALF)]

    def put_rows(core, first, value, groups):
        size = value.shape[0] // len(groups)
        for i, group in enumerate(groups):
            part = value[i * size : (i + 1) * size]
            if core == 0:
                g_keep[group, first : first + size, :] = part
            else:
                row = 2 * BLOCK + group * 9 * rd + first
                give[row : row + size, :] = part

    for core, which in enumerate((c, 1 - c)):
        put_rows(core, 8 * rd, dot(both_t, columns(dattn_s, 0, which)).astype(BF), range(count))
    for s in range(SLABS):
        lanes = slice(s * D, (s + 1) * D)
        rt = r_s[:, lanes].T
        for core, which in enumerate((c, 1 - c)):
            put_rows(core, (4 + s) * rd, dot(ht, columns(dpre_s, s * D, which)).astype(BF), range(count))
            put_rows(core, 0, dot(rt, columns(dff_s, 0, which)).astype(BF), range(s * per, (s + 1) * per))


def back_blocks(blocks, kn, vn, kt, q_in, d_in, ot, lse, dk_s, dv_s, dq_out, scratch):
    qz, qzt, oz, ozt, dq_s, p_s, dp_s = scratch
    rows = lax.broadcasted_iota(jnp.int32, (HALF, BLOCK), 0) // HEAD_DIM
    lanes = lax.broadcasted_iota(jnp.int32, (BLOCK, HALF), 1) // HEAD_DIM
    gq = jnp.zeros((1, HALF), F32)
    for i, block in enumerate(blocks):
        q, d_o = q_in[i].astype(F32), d_in[i * BLOCK : (i + 1) * BLOCK].astype(F32)
        qt, dot_ = q.T, d_o.T
        product = dot_ * ot[i]
        deltas = []
        for h in range(CORE_HEADS):
            head = slice(h * HEAD_DIM, (h + 1) * HEAD_DIM)
            deltas.append(jnp.sum(product[head], axis=0, keepdims=True))
            qz[h] = jnp.where(lanes == h, q, 0.0).astype(BF)
            oz[h] = jnp.where(lanes == h, d_o, 0.0).astype(BF)
            qzt[h] = jnp.where(rows == h, qt, 0.0).astype(BF)
            ozt[h] = jnp.where(rows == h, dot_, 0.0).astype(BF)
        dq_s[...] = jnp.zeros_like(dq_s)

        def chunk(first, count):
            size = count * BLOCK
            keys = kn[pl.ds(first, count)].reshape(size, HALF)
            values = vn[pl.ds(first, count)].reshape(size, HALF)
            for h in range(CORE_HEADS):
                p_s[h, :size] = dot(keys, qzt[h])
                dp_s[h, :size] = dot(values, ozt[h])
            dk = dk_s[pl.ds(first, count)].reshape(size, HALF)
            dv = dv_s[pl.ds(first, count)].reshape(size, HALF)
            for h in range(CORE_HEADS):
                head = slice(h * HEAD_DIM, (h + 1) * HEAD_DIM)
                p = jnp.exp(p_s[h, :size] - lse[i, h : h + 1, :])
                ds = (p * (dp_s[h, :size] - deltas[h])).astype(BF)
                dv = dv + dot(p.astype(BF), oz[h])
                dk = dk + dot(ds, qz[h])
                dq = dq_s[head, :]
                for j in range(count):
                    dq = dq + dot(kt[first + j, head, :], ds[j * BLOCK : (j + 1) * BLOCK])
                dq_s[head, :] = dq
            dk_s[pl.ds(first, count)] = dk.reshape(count, BLOCK, HALF)
            dv_s[pl.ds(first, count)] = dv.reshape(count, BLOCK, HALF)

        over_keys(block, chunk)
        dq = (dq_s[...] * (1.0 / math.sqrt(HEAD_DIM))).T.astype(BF)
        gq = gq + jnp.sum(dq.astype(F32), axis=0, keepdims=True)
        dq_out[i] = dq
    return gq


def back_kernel(nz, which, ids, ins, outs, *scratch):
    kn, vn, kt, qn, ot, lse, d_o = ins[:7]
    dk, dv, dq, gq = outs
    if which == 0:
        dk[...] = jnp.zeros_like(dk)
        dv[...] = jnp.zeros_like(dv)
    blocks = query_blocks(ids[0], ids[1], nz)[2 * which : 2 * which + 2]
    gq[...] = back_blocks(blocks, kn, vn, kt, qn, d_o, ot, lse, dk, dv, dq, scratch)


def dx_kernel(nz, which, ids, ins, outs, dxs):
    wq, dk, dv, dq_mine, dq_other, dx1 = ins
    keep, send, dkv = outs
    z, c = ids[0], ids[1]
    half = nz // 2
    place = lax.rem(z, half)
    w_q = wq[:, :, :HALF].reshape(D, HALF)
    w_kv = wq[:, :, HALF : 3 * HALF].reshape(D, 2 * HALF)
    for core, (target, dq) in enumerate(((keep, dq_mine), (send, dq_other))):
        for p in range(half):
            chip = ids[4] * half + p
            block = 2 * (chip if which == 0 else nz - 1 - chip) + (c if core == 0 else 1 - c)
            dkv[core * half + p, :, :HALF] = dk[block].astype(BF)
            dkv[core * half + p, :, HALF:] = dv[block].astype(BF)
        rows = dkv[core * half : (core + 1) * half].reshape(half * BLOCK, 2 * HALF)
        dxs[core] = ndot(rows, w_kv).reshape(half, BLOCK, D)
        value = ndot(dq[which], w_q)
        if core == 0:
            value = value + dx1[which]
        dxs[core, place] = dxs[core, place] + value
        target[...] = dxs[core].astype(BF)


def dw_kernel(nz, rs, rr, ids, ins, outs, spread):
    xall, dkv_near, dkv_far, dq_mine, dq_other, gq_mine, gq_other, gb_o, gb_i, gb_b, ga = ins
    (dw,) = outs
    z, c = ids[0], ids[1]
    half = nz // 2
    rows = []
    for which in range(2):
        for core in range(2):
            for p in range(half):
                chip = ids[4] * half + p
                rows.append(xall[2 * (chip if which == 0 else nz - 1 - chip) + (c if core == 0 else 1 - c)])
    dkv = jnp.concatenate([ref[...].reshape(nz * BLOCK, 2 * HALF) for ref in (dkv_near, dkv_far)], axis=0)
    acc_kv = dot(jnp.concatenate(rows, axis=0).T, dkv)
    gv = jnp.zeros((1, HALF), F32)
    for ref in (dkv_near, dkv_far):
        for i in range(nz):
            gv = gv + jnp.sum(ref[i, :, HALF:].astype(F32), axis=0, keepdims=True)
    queries = jnp.concatenate([xall[block] for block in query_blocks(z, c, nz)], axis=0).T
    dq = jnp.concatenate([dq_mine[...].reshape(2 * BLOCK, HALF), dq_other[...].reshape(2 * BLOCK, HALF)], axis=0)
    acc_q = dot(queries, dq)
    gq = gq_mine[...] + gq_other[...]
    nothing = jnp.zeros((1, HALF), F32)
    own = [jnp.concatenate([jnp.where(c == 0, g, nothing), jnp.where(c == 0, nothing, g)], axis=1) for g in (gq, gv)]
    tile = jnp.concatenate(own + [gb_o[...], gb_b[...], jnp.zeros((124, D), F32)], axis=0).T
    spread[...] = jnp.broadcast_to(gb_i[...], (128, FF)).T.reshape(D // rr, SLABS, rr, 128)
    lanes = lax.broadcasted_iota(jnp.int32, (D // rr, rr, 128), 2)
    tile = tile.reshape(D // rr, rr, 128)
    for s in range(SLABS):
        tile = jnp.where(lanes == 4 + s, spread[:, s], tile)
    tile = tile.reshape(D, 128)
    if rs >= 16:
        me = ids[2]
        lane = lax.broadcasted_iota(jnp.int32, (D, 128), 1) - 8 - 6 * (me // rs)
        mine = lax.rem(lax.broadcasted_iota(jnp.int32, (D, 128), 0), rs) == lax.rem(me, rs)
        gates = jnp.sum(ga[...], axis=1, keepdims=True)
        for which in range(2):
            rest = gates[which : which + 1]
            for i in range(3):
                high = rest.astype(BF).astype(F32)
                tile = jnp.where(mine & (lane == 2 * i + which), high, tile)
                rest = rest - high
    rows = dw.shape[1]
    dw[:, :, :HALF] = acc_q.astype(BF).reshape(D // rows, rows, HALF)
    dw[:, :, HALF : 3 * HALF] = acc_kv.astype(BF).reshape(D // rows, rows, 2 * HALF)
    dw[:, :, 3 * HALF :] = tile.astype(BF).reshape(D // rows, rows, 128)


def sum_kernel(plans, ids, ins, outs):
    outs = list(outs)
    for numbers, size, where, pre, post, stride, first, flat in plans:

        def total(static, dynamic):
            source = static * stride // size
            index = (static + dynamic) * stride + first - source * size
            refs = [ins[number] for number in numbers[source]]
            value = refs[0][index]
            if len(refs) == 2 and flat is None:
                value = value.astype(F32) + refs[1][index].astype(F32)
            elif len(refs) == 2:
                rows = value.shape[0]
                start = pl.multiple_of(flat + index * rows, 16)
                value = value.astype(F32) + refs[1][pl.ds(start, rows), :].astype(F32)
            return value

        if where is None:
            out = outs.pop(0)
            for index in range(out.shape[0]):
                out[index] = total(index, 0).astype(out.dtype)
            continue
        keep, send = outs.pop(0), outs.pop(0)
        mine = my_bit(ids, where)
        for p in range(pre):
            for q in range(post):
                keep[p * post + q] = total(2 * p * post + q, mine * post).astype(keep.dtype)
                send[p * post + q] = total(2 * p * post + q, (1 - mine) * post).astype(send.dtype)


def grads_kernel(rs, ids, ins, outs):
    own, other = ins
    w_back, w_in, w_out = outs
    for ref, core in ((own, ids[1]), (other, 1 - ids[1])):

        def lanes(first):
            return pl.ds(pl.multiple_of(first + core * HALF, HALF), HALF)

        value = ref[0].astype(F32)
        w_back[:, lanes(0)] = value[: 4 * rs]
        for s in range(SLABS):
            w_in[:, lanes(s * D)] = value[(4 + s) * rs : (5 + s) * rs]
        w_out[:, lanes(0)] = value[8 * rs :]


def last_kernel(rs, ids, ins, outs):
    own, other = ins
    w_qkv, gb_qv, gb_o, gb_i, gb_b, gates = outs
    for ref, core in ((own, ids[1]), (other, 1 - ids[1])):
        value = ref[0].astype(F32)
        for i in range(3):
            lanes = pl.ds(pl.multiple_of(i * D + core * HALF, HALF), HALF)
            w_qkv[:, lanes] = value[:, i * HALF : (i + 1) * HALF]
    sums = own[0, :, 3 * HALF :] + other[0, :, 3 * HALF :].astype(F32)
    lane = lax.broadcasted_iota(jnp.int32, (1, 128), 1)
    column = jnp.sum(sums, axis=0, keepdims=True)
    for which in range(2):
        used = (lane >= 8) & (lax.rem(lane, 2) == which)
        gates[:, which : which + 1] = jnp.sum(jnp.where(used, column, 0.0), axis=1, keepdims=True)
    by_row = jnp.concatenate([sums, jnp.zeros((128 - rs, 128), F32)], axis=0).T
    gb_qv[...] = by_row[:2, :rs]
    gb_o[...] = by_row[2:3, :rs]
    gb_b[...] = by_row[3:4, :rs]
    for s in range(SLABS):
        gb_i[:, s * rs : (s + 1) * rs] = by_row[4 + s : 5 + s, :rs]


def shape(dims, kind):
    return jax.ShapeDtypeStruct(dims, kind)


def vmem(dims, kind):
    return pltpu.VMEM(dims, kind)


def in_hbm(array):
    return pltpu.with_memory_space_constraint(array, pltpu.HBM)


def cost(megabytes):
    return pl.CostEstimate(flops=0, bytes_accessed=megabytes * 2**20, transcendentals=0)


def call(
    name, kernel, ids, ins, outs, after=(), scratch=(), limit=12, weight=0, where=None, aliases=None, out=VMEM
):
    count, waits = len(ins), len(after)

    def run(*refs):
        given, rest = refs[:count], refs[count + waits :]
        kernel(ids(), given, rest[: len(outs)], *rest[len(outs) :])

    return pl.pallas_call(
        run,
        out_shape=tuple(outs),
        in_specs=(where or [VMEM] * count) + [ANY] * waits,
        out_specs=out if isinstance(out, tuple) else (out,) * len(outs),
        scratch_shapes=list(scratch),
        compiler_params=pltpu.CompilerParams(vmem_limit_bytes=limit * 2**20),
        cost_estimate=cost(weight),
        input_output_aliases=aliases or {},
        name=name,
    )(*ins, *after)


def pack_call(ids, rs, ins):
    return call(
        "pack",
        functools.partial(pack_kernel, rs),
        ids,
        [in_hbm(array) for array in ins],
        [vmem((rs, WQ), BF), vmem((9 * rs, HALF), BF), vmem((13 * rs, HALF), BF)] + [vmem((BLOCK, D), BF)] * 4,
        scratch=[pltpu.VMEM(array.shape, BF) for array in ins[:8]]
        + [pltpu.VMEM((128, 128), F32), pltpu.SemaphoreType.DMA((12,))],
        where=[ANY] * 10,
    )


def join_call(name, ids, jobs, after=(), extra=None, extra_ins=(), extra_outs=(), cuts=None):
    ins, outs, spans = [], [], []
    for (own, got, _, _), cut in zip(jobs, cuts or [1] * len(jobs)):
        ins += [own, got]
        spans.append(slice(len(outs), len(outs) + cut))
        outs += [vmem((2 * own.shape[0] // cut,) + own.shape[1:], own.dtype)] * cut
    number = len(outs)

    def kernel(ids_ref, given, results):
        for i, (_, _, where, post) in enumerate(jobs):
            join(ids_ref, given[2 * i], given[2 * i + 1], results[spans[i]], where, post)
        if extra is not None:
            extra(ids_ref, given[2 * len(jobs) :], results[number:])

    return call(name, kernel, ids, ins + list(extra_ins), outs + list(extra_outs), after)


def sum_call(name, ids, jobs, after=(), last=BF, flat=None):
    ins, outs, plans = [], [], []

    def number(array):
        for i, other in enumerate(ins):
            if other is array:
                return i
        ins.append(array)
        return len(ins) - 1

    for sources, where, pre, post, stride, first in jobs:
        numbers = [tuple(number(array) for array in pair if array is not None) for pair in sources]
        tail = sources[0][0].shape[1:]
        size = sources[0][0].shape[0]
        plans.append((numbers, size, where, pre, post, stride, first, flat))
        if where is None:
            outs.append(vmem((size * len(sources) // stride,) + tail, last))
        else:
            outs += [vmem((pre * post,) + tail, last), vmem((pre * post,) + tail, BF)]
    return call(name, functools.partial(sum_kernel, plans), ids, ins, outs, after)


def make_body(n1, n2, nz):
    ndp = n1 * n2
    nsh = ndp * nz * 2
    rs = D // nsh
    rd = D // ndp
    half = nz // 2
    parts = 2 * nz if rs % 16 == 0 else 1
    rr = rd // parts
    nh = 9 * rd // 2
    swap = [(0, 1), (1, 0)]
    bits_a, bits_b, bits_z = (count.bit_length() - 1 for count in (n1, n2, nz))
    counts = {"a": n1, "b": n2, "z": nz}
    slot = {"a": 3, "b": 5, "z": 0}

    def to_mirror(array):
        return lax.ppermute(array, "z", [(s, nz - 1 - s) for s in range(nz)])

    def exchange(array, name, bit):
        return lax.ppermute(array, name, [(s, s ^ (1 << bit)) for s in range(counts[name])])

    def to_other(array):
        return lax.ppermute(array, "c", swap)

    def body(inputs, w_qkv, bias_qv, w_out, bias_out, w_in, bias_in, w_back, bias_back, alphas, cotangent):
        z, c = lax.axis_index("z"), lax.axis_index("c")
        a, b = lax.axis_index("a"), lax.axis_index("b")

        def ids():
            z, c = lax.axis_index("z"), lax.axis_index("c")
            a, b = lax.axis_index("a"), lax.axis_index("b")
            return (z, c, ((a * n2 + b) * nz + z) * 2 + c, a, z // half, b)


        latest = []

        def hand_on(ids_ref, given, results):
            for source, target in zip(given, results):
                target[...] = source[...]

        def step(name, jobs, extra=(), cuts=None, others=()):
            result = join_call(
                name, ids, jobs, latest + list(others), hand_on, extra, [vmem(e.shape, e.dtype) for e in extra], cuts
            )
            latest[:] = [result[0]]
            return result


        q_keep, f_keep, give, x_give, x_keep, cot_give, cot_a = pack_call(
            ids, rs,
            [w_qkv, w_back, w_in, w_out, bias_qv, bias_out[None], bias_back[None], bias_in[None], inputs, cotangent],
        )
        wq, wf = call(
            "core", functools.partial(core_kernel, rs), ids, [q_keep, f_keep, to_other(give)],
            [vmem((2, rs, WQ), BF), vmem((2, 9 * rs, HALF), BF)],
        )
        latest[:] = [wq]
        wq, wf = wq.reshape(1, 2 * rs, WQ), wf.reshape(1, 2 * 9 * rs, HALF)
        wf = wf.reshape(2 * 9 * rs, HALF)
        q_got = exchange(wq, "z", bits_z - 1)
        wf_parts = [(wf, 0)]
        for i in reversed(range(bits_z)):
            wf_parts += [(exchange(part, "z", i), place | (1 << i)) for part, place in wf_parts]
        wf_near = [part for part, place in wf_parts if place == 1]
        for i in reversed(range(1, bits_z)):
            (wq,) = step("q_z", [(wq, q_got, (0, i), 1)])
            q_got = exchange(wq, "z", i - 1)
        wq, x_keep, x_give = step(
            "q_z", [(wq, q_got, (0, 0), 1)], [x_keep, x_give], others=wf_near + [wf_parts[1][0]]
        )
        wq = wq.reshape(rd, WQ)
        if parts == 1:
            hidden_bias = wq[:, 3 * HALF + 4 : 3 * HALF + 8].reshape(2 * nz, rs, SLABS)
            hidden_bias = jnp.transpose(hidden_bias, (0, 2, 1)).reshape(SLABS, rd).T
            wq = jnp.concatenate([wq[:, : 3 * HALF + 4], hidden_bias, wq[:, 3 * HALF + 8 :]], axis=1)
        wq = wq[None]
        x_far = to_mirror(x_give)
        for i in reversed(range(1, bits_b)):
            q_got = exchange(wq, "b", i)
            (wq,) = step("q_b", [(wq, q_got, (5, i), 1)])
        q_got = exchange(wq, "b", 0)
        own = x_keep[None]
        own_got = exchange(own, "z", max(bits_z - 2, 0))

        def in_place(ids_ref, given, results):
            for group in range(2):

                @pl.when(ids_ref[4] == group)
                def _():
                    for ref, (_, place) in zip(given, wf_parts):
                        at = lax.rem(lax.bitwise_xor(ids_ref[0], place), half)
                        results[group ^ (place // half)][at] = ref[...]

        halves = vmem((half, 2 * 9 * rs, HALF), BF)
        first, second = call("f_z", in_place, ids, [part for part, _ in wf_parts], [halves, halves], latest)
        latest[:] = [first]
        if parts == 1:
            wf = jnp.concatenate([first, second], axis=0).reshape(nz, 2, 9 * rs, HALF)
            wf = jnp.concatenate(
                [wf[:, :, : 4 * rs].reshape(4 * rd, HALF)]
                + [wf[:, :, (4 + s) * rs : (5 + s) * rs].reshape(rd, HALF) for s in range(SLABS)]
                + [wf[:, :, 8 * rs :].reshape(rd, HALF)],
                axis=0,
            )
            first, second = wf[:nh], wf[nh:]
        first, second = first.reshape(1, nh, HALF), second.reshape(1, nh, HALF)
        (wq,) = step("q_b", [(wq, q_got, (5, 0), 1)])
        for i in reversed(range(1, bits_a)):
            q_got = exchange(wq, "a", i)
            (wq,) = step("q_a", [(wq, q_got, (3, i), n2)])
        wq_pieces = [wq, exchange(wq, "a", 0)]

        far_rows, cot_give = call(
            "x_far", hand_on, ids, [x_far, cot_give], [vmem((BLOCK, D), BF)] * 2, latest + [own_got]
        )
        latest[:] = [far_rows]
        cot_b = to_mirror(cot_give)
        far_rows = far_rows[None]
        for i in reversed(range(1, bits_z - 1)):
            far_got = exchange(far_rows, "z", i)
            own, far_rows = step("x_z", [(own, own_got, (0, i), 1), (far_rows, far_got, (0, i), 1)])
            own_got = exchange(own, "z", i - 1)
        far_got = exchange(far_rows, "z", 0)

        for i in reversed(range(bits_b)):
            got = exchange(first, "b", i), exchange(second, "a", i)
            first, second = step("f_dp", [(first, got[0], (5, i), 1), (second, got[1], (3, i), 1)])
        for i in reversed(range(1, bits_a)):
            got = exchange(first, "a", i), exchange(second, "b", i)
            first, second = step("f_dp", [(first, got[0], (3, i), n2), (second, got[1], (5, i), 1)])
        wf_pieces = [first, second, exchange(first, "a", 0), exchange(second, "b", 0)]

        def rows_of_all(ids_ref, given, results):
            own_ref, own_got_ref, far_ref, far_got_ref = given
            base, mine = ids_ref[4] * half, my_bit(ids_ref, (0, 0))
            for p in range(half // 2):
                for own_part, far_part, at in (
                    (own_ref, far_ref, base + 2 * p + mine),
                    (own_got_ref, far_got_ref, base + 2 * p + 1 - mine),
                ):
                    results[0][at - base] = own_part[p]
                    results[1][at - base] = far_part[p]

        xo = call(
            "x_all", rows_of_all, ids, [own, own_got, far_rows, far_got], [vmem((half, BLOCK, D), BF)] * 2,
            latest + [wq_pieces[1], cot_b],
        )
        latest[:] = [xo[0]]
        xs = [to_other(part) for part in xo]

        nb = 2 * nz
        heads_t = pltpu.VMEM((CORE_HEADS, HALF, BLOCK), BF)
        scores = pltpu.VMEM((CORE_HEADS, 2 * BLOCK, BLOCK), F32)
        scratch = [
            heads_t,
            scores,
            pltpu.VMEM((CORE_HEADS, 1, BLOCK), F32),
            pltpu.VMEM((CORE_HEADS, 1, BLOCK), F32),
            pltpu.VMEM((HALF, BLOCK), F32),
        ]
        natural, turned = (nb, BLOCK, HALF), (nb, HALF, BLOCK)
        two, two_t = (2, BLOCK, HALF), (2, HALF, BLOCK)
        two_lse = (2, CORE_HEADS, BLOCK)
        spread = pltpu.VMEM((D // rr, SLABS, rr, 128), F32)
        (xall, wq, kn, vn, kt, vt, q_mine, q_other, ot_other, lse_other, o_send, bo, bb, bi) = call(
            "first",
            functools.partial(first_kernel, nz, ndp, n2, rr),
            ids,
            [*xo, *xs, *wq_pieces],
            [
                vmem((nb, BLOCK, D), BF),
                vmem((ndp, rd, WQ), BF),
                vmem(natural, BF),
                vmem(natural, BF),
                vmem(turned, BF),
                vmem(turned, BF),
                vmem(two, BF),
                vmem(two, BF),
                vmem(two_t, F32),
                vmem(two_lse, F32),
                vmem(two, BF),
                vmem((1, D), F32),
                vmem((1, D), F32),
                vmem((1, FF), F32),
            ],
            latest,
            [spread] + scratch,
            limit=16,
        )

        def give_kernel(ids_ref, given, results):
            row = 0
            for part in given:
                for i in range(part.shape[0]):
                    results[0][row : row + part.shape[1]] = part[i]
                    row += part.shape[1]

        (give,) = call(
            "give", give_kernel, ids, [o_send, *wf_pieces], [vmem((2 * BLOCK + 2 * ndp * nh, HALF), BF)],
            limit=16,
        )
        ffn_got = to_other(give)
        ot_mine, lse_mine, o_mine = call(
            "second",
            functools.partial(second_kernel, nz),
            ids,
            [kn, vt, q_mine],
            [vmem(two_t, F32), vmem(two_lse, F32), vmem(two, BF)],
            (),
            scratch,
        )

        grouped = (ndp * parts, 9 * rd // parts, HALF)
        (out_near, out_far, dx1, d_mine, g_keep, give, gb_o, gb_i, gb_b, ga) = call(
            "ffn",
            functools.partial(ffn_kernel, nz, ndp, n2, parts),
            ids,
            [alphas, o_mine, ffn_got, xall, cot_a, cot_b, bo, bi, bb, *wf_pieces],
            [
                vmem((BLOCK, D), BF),
                vmem((BLOCK, D), BF),
                vmem((2, BLOCK, D), F32),
                vmem((2 * BLOCK, HALF), BF),
                vmem(grouped, BF),
                vmem((2 * BLOCK + ndp * 9 * rd, HALF), BF),
                vmem((1, D), F32),
                vmem((1, FF), F32),
                vmem((1, D), F32),
                vmem((2, D), F32),
            ],
            scratch=[
                pltpu.VMEM((2, 2 * ndp, nh, HALF) if parts == 1 else (8, 128), BF),
                pltpu.VMEM((D, D), BF),
                pltpu.VMEM((SLABS, D, D), BF),
                pltpu.VMEM((FF, D), BF),
                pltpu.VMEM((2, 2 * BLOCK, HALF), BF),
                pltpu.VMEM((2 * BLOCK, D), BF),
                pltpu.VMEM((2 * BLOCK, FF), BF),
                pltpu.VMEM((2 * BLOCK, FF), BF),
                pltpu.VMEM((2 * BLOCK, D), BF),
                pltpu.VMEM((2 * BLOCK, D), BF),
                pltpu.VMEM((SLABS, 2 * BLOCK, D), F32),
                pltpu.VMEM((SLABS, 2 * BLOCK, D), F32),
                pltpu.VMEM((2 * BLOCK, D), F32),
                pltpu.VMEM((2 * BLOCK, D), F32),
            ],
            limit=36,
            where=[SMEM] + [VMEM] * 12,
        )
        back_got = to_other(give)
        back_scratch = [
            pltpu.VMEM((CORE_HEADS, BLOCK, HALF), BF),
            heads_t,
            pltpu.VMEM((CORE_HEADS, BLOCK, HALF), BF),
            heads_t,
            pltpu.VMEM((HALF, BLOCK), F32),
            scores,
            scores,
        ]
        back_out = [vmem(natural, F32), vmem(natural, F32), vmem(two, BF), vmem((1, HALF), F32)]
        dk, dv, dq_mine, gq_mine = call(
            "back_first",
            functools.partial(back_kernel, nz, 0),
            ids,
            [kn, vn, kt, q_mine, ot_mine, lse_mine, d_mine],
            back_out,
            scratch=back_scratch,
            limit=16,
        )

        latest[:] = [gq_mine]
        done = {}

        def along(axis, count, pre, post):
            return [(axis, i, pre * (count >> (i + 1)), post) for i in range(count.bit_length() - 1)]

        def dp_scatter(name, kept, got, rows, columns, flat=None):
            axes = (along("b", n2, n1, 1) + along("a", n1, 1, 1), along("a", n1, 1, n2) + along("b", n2, 1, 1))
            whole = (kept.reshape(2 * ndp, rows, columns), got)
            state = [(whole, 2, 0), (whole, 2, 1)]
            for i in range(len(axes[0])):
                result = sum_call(
                    name,
                    ids,
                    [
                        ([pair], (slot[axis], bit), pre, post, stride, first)
                        for (pair, stride, first), (axis, bit, pre, post) in zip(state, (axes[0][i], axes[1][i]))
                    ],
                    latest,
                    flat=flat if i == 0 else None,
                )
                latest[:] = [result[0]]
                state = [
                    ((result[2 * j], exchange(result[2 * j + 1], axes[j][i][0], axes[j][i][1])), 1, 0)
                    for j in range(2)
                ]
                yield
            return [pair for pair, _, _ in state]

        def z_scatter(name, sources):
            for _, i, pre, _ in along("z", nz, 1, 1):
                kept, send = sum_call(name, ids, [(sources, (slot["z"], i), pre, 1, 1, 0)], latest)
                latest[:] = [kept]
                sources = [(kept, exchange(send, "z", i))]
                yield
            rows, columns = kept.shape[1] // 2, kept.shape[2]
            sources = [tuple(array.reshape(2, rows, columns) for array in sources[0])]
            keep, send = sum_call(name, ids, [(sources, (1, 0), 1, 1, 1, 0)], latest, F32)
            latest[:] = [keep]
            return keep, to_other(send)

        def whole_dp(name, sources):
            return [part[0] for part in sum_call(name, ids, [([pair], None, 0, 0, 1, 0) for pair in sources], latest)]

        def g_chain():
            sources = yield from dp_scatter("g_dp", g_keep, back_got, nh, HALF, 2 * BLOCK)
            if parts == 1:
                g_dp = jnp.concatenate(whole_dp("g_dp", sources), axis=0)
                g_dp = jnp.concatenate(
                    [g_dp[: 4 * rd].reshape(nz, 2, 4 * rs, HALF)]
                    + [g_dp[(4 + s) * rd : (5 + s) * rd].reshape(nz, 2, rs, HALF) for s in range(SLABS)]
                    + [g_dp[8 * rd :].reshape(nz, 2, rs, HALF)],
                    axis=2,
                )
                sources = [(g_dp.reshape(nz, 2 * 9 * rs, HALF), None)]
            else:
                sources = [tuple(array.reshape(half, 2 * 9 * rs, HALF) for array in pair) for pair in sources]
            keep, got = yield from z_scatter("g_z", sources)
            yield
            done["g"] = call(
                "g_last", functools.partial(grads_kernel, rs), ids, [keep, got],
                [shape((4 * rs, D), F32), shape((rs, FF), F32), shape((rs, D), F32)], latest,
            )
            latest[:] = [done["g"][2]]

        g_steps = g_chain()
        next(g_steps)
        dk, dv, dq_other, gq_other = call(
            "back_second",
            functools.partial(back_kernel, nz, 1),
            ids,
            [kn, vn, kt, q_other, ot_other, lse_other, back_got, dk, dv],
            back_out,
            latest,
            back_scratch,
            limit=16,
            aliases={7: 0, 8: 1},
        )
        def out_kernel(ids_ref, given, results, sems):
            group = ids_ref[4]
            copies = moves(sems, [(given[0], results[0].at[group]), (given[1], results[0].at[1 - group])])
            results[1][...] = jnp.zeros_like(results[1])
            wait(copies)

        def to_rows(name, own, got):
            rows, token = call(
                name, out_kernel, ids, [own, got], [pltpu.HBM((2, BLOCK, D), BF), vmem((8, 128), F32)], latest,
                [pltpu.SemaphoreType.DMA((2,))], where=[ANY, ANY],
                out=(pl.BlockSpec(memory_space=pltpu.HBM), VMEM),
            )
            latest[:] = [token]
            return rows

        latest[:] = [gq_other]
        def dx_call(which):
            keep, send, dkv = call(
                "dx",
                functools.partial(dx_kernel, nz, which),
                ids,
                [wq, dk, dv, dq_mine, dq_other, dx1],
                [vmem((half, BLOCK, D), BF), vmem((half, BLOCK, D), BF), vmem((nz, BLOCK, 2 * HALF), BF)],
                latest,
                [pltpu.VMEM((2, half, BLOCK, D), F32)],
            )
            latest[:] = [keep]
            return (keep, to_other(send)), dkv

        def dx_chain(pair, far):
            for i in range(bits_z - 1):
                kept, send = sum_call("dx_z", ids, [([pair], (0, i), half >> (i + 1), 1, 1, 0)], latest)
                latest[:] = [kept]
                pair = (kept, exchange(send, "z", i))
                yield
            (rows,) = sum_call("dx_z", ids, [([pair], None, 0, 0, 1, 0)], latest)
            latest[:] = [rows]
            rows = rows.reshape(BLOCK, D)
            done["far" if far else "near"] = to_mirror(rows) if far else rows

        far_pair, dkv_far = dx_call(1)
        near_pair, dkv_near = dx_call(0)
        far_steps, near_steps = dx_chain(far_pair, True), dx_chain(near_pair, False)
        next(far_steps)
        next(g_steps)
        next(near_steps)
        (dw,) = call(
            "dw",
            functools.partial(dw_kernel, nz, rs, rr),
            ids,
            [xall, dkv_near, dkv_far, dq_mine, dq_other, gq_mine, gq_other, gb_o, gb_i, gb_b, ga],
            [vmem((2 * ndp, rd // 2, WQ), BF)],
            latest,
            [spread],
            limit=20,
        )
        latest[:] = [dw]

        def dw_chain():
            sources = yield from dp_scatter("w_dp", dw, None, rd // 2, WQ)
            if parts == 1:
                dw_dp = jnp.concatenate(whole_dp("w_dp", sources), axis=0)
                hidden_bias = dw_dp[:, 3 * HALF + 4 : 3 * HALF + 8].T.reshape(2 * nz, SLABS, rs)
                hidden_bias = jnp.transpose(hidden_bias, (0, 2, 1)).reshape(rd, SLABS)
                dw_dp = jnp.concatenate([dw_dp[:, : 3 * HALF + 4], hidden_bias, dw_dp[:, 3 * HALF + 8 :]], axis=1)
                sources = [(dw_dp.reshape(nz, 2 * rs, WQ), None)]
            else:
                sources = [tuple(array.reshape(half, 2 * rs, WQ) for array in pair) for pair in sources]
            keep, got = yield from z_scatter("w_z", sources)
            yield
            done["w"] = call(
                "w_last", functools.partial(last_kernel, rs), ids, [keep, got],
                [shape((rs, 3 * D), F32), shape((2, rs), F32), shape((1, rs), F32), shape((1, SLABS * rs), F32)]
                + [shape((1, rs), F32), shape((1, 2), F32)],
                latest,
            )
            latest[:] = [done["w"][0]]

        out_b = to_mirror(out_far)
        steps = {"f": far_steps, "n": near_steps, "g": g_steps, "w": dw_chain()}
        for name in "fgnwowgwxwgwgw" + "fn" * bits_z + "x" + "gw" * (2 * bits_z):
            if name == "o":
                outputs = to_rows("outputs", out_near, out_b)
            elif name == "x":
                if "inputs" not in done:
                    for chain in (far_steps, near_steps):
                        while next(chain, 0) is None:
                            pass
                    done["inputs"] = to_rows("dx_last", done["near"], done["far"])
            else:
                next(steps[name], 0)
        gb_qv, gb_out, gb_in, gb_back, grad_alphas = done["w"][1:]
        if rs < 16:
            grad_alphas = lax.psum(jnp.sum(ga, axis=1), MESH_AXES)
        return (
            outputs,
            done["inputs"],
            done["w"][0],
            gb_qv,
            done["g"][2],
            gb_out.reshape(rs),
            done["g"][1],
            gb_in.reshape(SLABS * rs),
            done["g"][0],
            gb_back.reshape(rs),
            grad_alphas.reshape(2),
        )

    return body


def solution(mesh):
    ndp, nseq = mesh.devices.shape
    n1 = math.isqrt(ndp)
    n2 = ndp // n1
    nz = nseq // 2
    fine = Mesh(mesh.devices.reshape(n1, n2, nz, 2), MESH_AXES)
    dp, seq = ("a", "b"), ("z", "c")
    rows = P(dp, seq, None)
    both = dp + seq
    return jax.shard_map(
        make_body(n1, n2, nz),
        mesh=fine,
        in_specs=(
            rows,
            P(both, None),
            P(None, both),
            P(both, None),
            P(both),
            P(both, None),
            P(both),
            P(both, None),
            P(both),
            P(),
            rows,
        ),
        out_specs=(
            rows,
            rows,
            P(both, None),
            P(None, both),
            P(both, None),
            P(both),
            P(both, None),
            P(both),
            P(both, None),
            P(both),
            P(),
        ),
        check_vma=False,
    )
```

```python
import functools
import math

import jax
import jax.numpy as jnp
from jax import lax
from jax.experimental import pallas as pl
from jax.experimental.pallas import tpu as pltpu
from jax.sharding import Mesh, PartitionSpec as P

D = 512
HEADS = 8
HEAD_DIM = 64
FF = 2048
BLOCK = 256
HALF = D // 2
CORE_HEADS = HEADS // 2
SLABS = FF // D
BF = jnp.bfloat16
F32 = jnp.float32
MESH_AXES = ("a", "b", "z", "c")
VMEM = pl.BlockSpec(memory_space=pltpu.VMEM)
SMEM = pl.BlockSpec(memory_space=pltpu.SMEM)
ANY = pl.BlockSpec(memory_space=pl.ANY)
WQ = 3 * HALF + 128
GELU_C = math.sqrt(2.0 / math.pi)


def dot(left, right):
    return jnp.dot(left, right, preferred_element_type=F32)


def ndot(left, right):
    return lax.dot_general(left, right, (((1,), (1,)), ((), ())), preferred_element_type=F32)


def flip(block):
    return block.T


def query_blocks(z, c, nz):
    near, far = 2 * z, 2 * (nz - 1 - z)
    return (near + c, far + c, near + 1 - c, far + 1 - c)


def over_keys(block, chunk):
    count = block + 1

    def step(i, unused):
        chunk(4 * i, 4)
        return unused

    lax.fori_loop(0, count // 4, step, 0)

    @pl.when(lax.rem(count, 4) >= 2)
    def _():
        chunk(count // 4 * 4, 2)

    @pl.when(lax.rem(count, 2) == 1)
    def _():
        chunk(block, 1)


def attend_blocks(blocks, kn, vt, qn, ot, lse, o, scratch):
    qz, s_s, m_s, l_s, acc_s = scratch
    rows = lax.broadcasted_iota(jnp.int32, (HALF, BLOCK), 0) // HEAD_DIM
    for i, block in enumerate(blocks):
        qt = qn[i].astype(F32).T
        for h in range(CORE_HEADS):
            qz[h] = jnp.where(rows == h, qt, 0.0).astype(BF)
        m_s[...] = jnp.full_like(m_s, -1e30)
        l_s[...] = jnp.zeros_like(l_s)
        acc_s[...] = jnp.zeros_like(acc_s)

        def chunk(first, count):
            keys = kn[pl.ds(first, count)].reshape(count * BLOCK, HALF)
            for h in range(CORE_HEADS):
                s_s[h, : count * BLOCK] = dot(keys, qz[h])
            for h in range(CORE_HEADS):
                head = slice(h * HEAD_DIM, (h + 1) * HEAD_DIM)
                s = s_s[h, : count * BLOCK]
                old = m_s[h]
                new = jnp.maximum(old, jnp.max(s, axis=0, keepdims=True))
                p = jnp.exp(s - new)
                shrink = jnp.exp(old - new)
                m_s[h] = new
                l_s[h] = l_s[h] * shrink + jnp.sum(p, axis=0, keepdims=True)
                p = p.astype(BF)
                acc = acc_s[head, :] * shrink
                for j in range(count):
                    acc = acc + dot(vt[first + j, head, :], p[j * BLOCK : (j + 1) * BLOCK])
                acc_s[head, :] = acc

        over_keys(block, chunk)
        for h in range(CORE_HEADS):
            head = slice(h * HEAD_DIM, (h + 1) * HEAD_DIM)
            total = l_s[h]
            lse[i, h : h + 1, :] = m_s[h] + jnp.log(total)
            acc_s[head, :] = acc_s[head, :] / total
        value = acc_s[...]
        ot[i] = value
        o[i] = value.T.astype(BF)


def moves(sems, pairs):
    copies = [pltpu.make_async_copy(src, dst, sems.at[i]) for i, (src, dst) in enumerate(pairs)]
    for copy in copies:
        copy.start()
    return copies


def wait(copies):
    for copy in copies:
        copy.wait()


def pack_kernel(rs, ids, ins, outs, *refs):
    w_qkv, w_back, w_in, w_out, bias_qv, bias_out, bias_back, bias_in = refs[:8]
    gates, tile, sems = refs[8:]
    group = ids[4]
    loads = moves(sems, [(ins[i], refs[i]) for i in range(8)] + [(ins[10], gates)])
    rows = moves(
        sems.at[pl.ds(9, 4)],
        [(ins[8 + i].at[which], outs[3 + 2 * i + j]) for i in range(2) for j, which in enumerate((1 - group, group))],
    )
    wait(loads)
    tile[...] = jnp.zeros_like(tile)
    tile[0:2, :rs] = bias_qv[...].astype(F32)
    tile[2:3, :rs] = bias_out[...].astype(F32)
    tile[3:4, :rs] = bias_back[...].astype(F32)
    for i in range(SLABS):
        tile[4 + i : 5 + i, :rs] = bias_in[:, i * rs : (i + 1) * rs].astype(F32)
    outs[7][0:1, 0:2] = gates[...]
    turned = tile[...].T[:rs].astype(BF)
    q_keep, f_keep, give = outs[:3]

    def cut(ref, first, core):
        return ref[:, pl.ds(pl.multiple_of(first + core * HALF, HALF), HALF)]

    for i in range(3):
        q_keep[:, i * HALF : (i + 1) * HALF] = cut(w_qkv, i * D, ids[1])
        give[(9 + i) * rs : (10 + i) * rs] = cut(w_qkv, i * D, 1 - ids[1])
    q_keep[:, 3 * HALF :] = turned
    give[12 * rs :, :128] = turned
    give[12 * rs :, 128:] = jnp.zeros((rs, 128), BF)
    for f_out, core in ((f_keep, ids[1]), (give, 1 - ids[1])):
        f_out[: 4 * rs] = cut(w_back, 0, core)
        for i in range(SLABS):
            f_out[(4 + i) * rs : (5 + i) * rs] = cut(w_in, i * D, core)
        f_out[8 * rs : 9 * rs] = cut(w_out, 0, core)
    wait(rows)


def core_kernel(rs, ids, ins, outs):
    q_keep, f_keep, got = ins
    wq, wf = outs
    c = ids[1]
    wq[c] = q_keep[...]
    wf[c] = f_keep[...]
    wf[1 - c] = got[: 9 * rs]
    for i in range(3):
        wq[1 - c, :, i * HALF : (i + 1) * HALF] = got[(9 + i) * rs : (10 + i) * rs]
    wq[1 - c, :, 3 * HALF :] = got[12 * rs :, :128]


def my_bit(ids, where):
    index, bit = where
    return lax.rem(lax.shift_right_logical(ids[index], bit), 2)


def join(ids, own, got, outs, where, post=1):
    mine = my_bit(ids, where)
    pre = own.shape[0] // post
    for p in range(pre):
        out = outs[p * len(outs) // pre]
        at = 2 * p - 2 * pre // len(outs) * (p * len(outs) // pre)
        for q in range(post):
            out[(at + mine) * post + q] = own[p * post + q]
            out[(at + 1 - mine) * post + q] = got[p * post + q]


def first_kernel(nz, ndp, n2, rr, ids, ins, outs, spread, *scratch):
    xo, xs = ins[:2], ins[2:4]
    wq_pieces = ins[4:6]
    xall, wq, kn, vn, kt, vt, q_mine, q_other, ot, lse, o, bo, bb, bi = outs
    z, c = ids[0], ids[1]
    for p in range(nz // 2):
        chip = ids[4] * (nz // 2) + p
        for i, at in enumerate((chip, nz - 1 - chip)):
            xall[2 * at + c] = xo[i][p]
            xall[2 * at + 1 - c] = xs[i][p]
    for far, piece in enumerate(wq_pieces):
        bit = lax.rem(ids[3], 2)
        for j in range(piece.shape[0]):
            wq[(2 * (j // n2) + (1 - bit if far else bit)) * n2 + j % n2] = piece[j]
    bias = wq[:, :, 3 * HALF :].reshape(D, 128).astype(F32)
    turned = bias.T
    bo[...] = turned[2:3]
    bb[...] = turned[3:4]
    lanes = lax.broadcasted_iota(jnp.int32, (D // rr, rr, 128), 2)
    for s in range(SLABS):
        spread[:, s] = jnp.where(lanes == 4 + s, bias.reshape(D // rr, rr, 128), 0.0)
    bi[...] = jnp.sum(spread[...].reshape(FF, 128).T[4:8], axis=0, keepdims=True)
    bias_q = jnp.where(c == 0, turned[0:1, :HALF], turned[0:1, HALF:])
    bias_v = jnp.where(c == 0, turned[1:2, :HALF], turned[1:2, HALF:])
    w_q = wq[:, :, :HALF].reshape(D, HALF)
    w_kv = wq[:, :, HALF : 3 * HALF].reshape(D, 2 * HALF)

    def project(i, unused):
        blocks = pl.ds(4 * i, 4)
        kv = dot(xall[blocks].reshape(4 * BLOCK, D), w_kv)
        key = kv[:, :HALF].astype(BF).reshape(4, BLOCK, HALF)
        value = (kv[:, HALF:] + bias_v).astype(BF).reshape(4, BLOCK, HALF)
        kn[blocks] = key
        vn[blocks] = value
        for j in range(4):
            kt[4 * i + j] = key[j].T
            vt[4 * i + j] = value[j].T
        return unused

    lax.fori_loop(0, nz // 2, project, 0)
    blocks = query_blocks(z, c, nz)
    q = dot(jnp.concatenate([xall[block] for block in blocks], axis=0), w_q) + bias_q
    q = (q.astype(BF).astype(F32) * (1.0 / math.sqrt(HEAD_DIM))).astype(BF)
    for i in range(4):
        (q_mine if i < 2 else q_other)[i % 2] = q[i * BLOCK : (i + 1) * BLOCK]
    attend_blocks(blocks[2:], kn, vt, q_other, ot, lse, o, scratch)


def place_dp(ids, pieces, ndp, n2, put):
    for i, piece in enumerate(pieces):
        far, half = i // 2, i % 2
        for j in range(ndp // 2):
            if half == 0:
                bit = lax.rem(ids[3], 2)
                dp = (2 * (j // n2) + (1 - bit if far else bit)) * n2 + j % n2
            else:
                bit = lax.rem(ids[5], 2)
                dp = j // (n2 // 2) * n2 + 2 * (j % (n2 // 2)) + (1 - bit if far else bit)
            put(dp, half, piece(j) if callable(piece) else piece[j])


def second_kernel(nz, ids, ins, outs, *scratch):
    kn, vt, qn = ins
    ot, lse, o = outs
    blocks = query_blocks(ids[0], ids[1], nz)
    attend_blocks(blocks[:2], kn, vt, qn, ot, lse, o, scratch)


def ffn_kernel(nz, ndp, n2, parts, ids, ins, outs, *refs):
    alphas, o_mine, got, xall, cot_a, cot_b, bo, bi, bb = ins[:9]
    pieces = ins[9:13]
    rows = pieces[0].shape[1]

    def received(i):
        return lambda j: got[pl.ds(2 * BLOCK + (i * (ndp // 2) + j) * rows, rows)]

    (out_near, out_far, dx1, d_mine, g_keep, give, gb_o, gb_i, gb_b, ga) = outs
    w, wo_s, wi_s, wb_s, mixed, h_s, r_s, dpre_s, dff_s, dattn_s = refs[:10]
    pre_s, dr_s = refs[10:12]
    c = ids[1]
    count = ndp * parts
    rd = D // count
    for core in range(2):
        own = pieces if core == 0 else [received(i) for i in range(4)]
        which = c if core == 0 else 1 - c
        lanes = pl.ds(pl.multiple_of(which * HALF, HALF), HALF)

        def put(dp, half, value):
            if parts == 1:
                w[which, 2 * dp + half] = value
                return
            for g in range(parts // 2):
                at = dp * parts + half * (parts // 2) + g
                part = value[9 * rd * g : 9 * rd * (g + 1)]
                wb_s[pl.ds(pl.multiple_of(at * 4 * rd, 4 * rd), 4 * rd), lanes] = part[: 4 * rd]
                at = pl.multiple_of(at * rd, rd)
                for s in range(SLABS):
                    wi_s[s, pl.ds(at, rd), lanes] = part[(4 + s) * rd : (5 + s) * rd]
                wo_s[pl.ds(at, rd), lanes] = part[8 * rd :]

        place_dp(ids, own, ndp, n2, put)
    if parts == 1:
        for half in range(2):
            lanes = slice(half * HALF, (half + 1) * HALF)
            whole = w[half].reshape(count, 9 * rd, HALF)
            wo_s[:, lanes] = whole[:, 8 * rd :].reshape(D, HALF)
            for s in range(SLABS):
                wi_s[s, :, lanes] = whole[:, (4 + s) * rd : (5 + s) * rd].reshape(D, HALF)
            wb_s[:, lanes] = whole[:, : 4 * rd].reshape(FF, HALF)
    mixed[c] = o_mine[...].reshape(2 * BLOCK, HALF)
    mixed[1 - c] = got[: 2 * BLOCK]
    alpha_attn, alpha_ffn = alphas[0:1, 0:1], alphas[0:1, 1:2]
    mine = query_blocks(ids[0], c, nz)
    both = 2 * BLOCK
    dy = jnp.concatenate([cot_a[...], cot_b[...]], axis=0).astype(F32)
    dff = (alpha_ffn * dy).astype(BF)
    dff_s[...] = dff
    attn = dot(mixed[0], wo_s[:HALF, :]) + dot(mixed[1], wo_s[HALF:, :]) + bo[...]
    x1 = jnp.concatenate([xall[mine[0]], xall[mine[1]]], axis=0).astype(F32) + alpha_attn * attn
    hidden = x1.astype(BF)
    h_s[...] = hidden
    x1_s = refs[12]
    attn_s = refs[13]
    x1_s[...] = x1
    attn_s[...] = attn
    for s in range(SLABS):
        lanes = slice(s * D, (s + 1) * D)
        pre_s[s] = dot(h_s[...], wi_s[s]) + bi[:, lanes]
        dr_s[s] = ndot(dff_s[...], wb_s[lanes, :])
    ff = None
    dx = None
    for s in range(SLABS):
        lanes = slice(s * D, (s + 1) * D)
        pre = pre_s[s]
        square = pre * pre
        up = 0.5 + 0.5 * jnp.tanh(pre * (GELU_C + (GELU_C * 0.044715) * square))
        r = pre * up
        r_s[:, lanes] = r.astype(BF)
        slope = up + r * (1.0 - up) * (2.0 * GELU_C + (6.0 * GELU_C * 0.044715) * square)
        dpre_s[:, lanes] = (dr_s[s] * slope).astype(BF)
    for s in range(SLABS):
        lanes = slice(s * D, (s + 1) * D)
        t1 = dot(r_s[:, lanes], wb_s[lanes, :])
        t2 = ndot(dpre_s[:, lanes], wi_s[s])
        ff = t1 if ff is None else ff + t1
        dx = t2 if dx is None else dx + t2
    ff = ff + bb[...]
    x1 = x1_s[...]
    out = (x1 + alpha_ffn * ff).astype(BF)
    out_near[...] = out[:BLOCK]
    out_far[...] = out[BLOCK:]
    dy = jnp.concatenate([cot_a[...], cot_b[...]], axis=0).astype(F32)
    dx = dx + dy
    dx1[0] = dx[:BLOCK]
    dx1[1] = dx[BLOCK:]
    dattn = (alpha_attn * dx).astype(BF)
    dattn_s[...] = dattn
    d_mine[...] = ndot(dattn, wo_s[pl.ds(pl.multiple_of(c * HALF, HALF), HALF), :]).astype(BF)
    give[:both, :] = ndot(dattn, wo_s[pl.ds(pl.multiple_of((1 - c) * HALF, HALF), HALF), :]).astype(BF)
    ga[...] = jnp.concatenate(
        [jnp.sum(dx * attn_s[...], axis=0, keepdims=True), jnp.sum(dy * ff, axis=0, keepdims=True)], axis=0
    )
    gb_o[...] = jnp.sum(dattn_s[...].astype(F32), axis=0, keepdims=True)
    gb_b[...] = jnp.sum(dff_s[...].astype(F32), axis=0, keepdims=True)
    for s in range(SLABS):
        lanes = slice(s * D, (s + 1) * D)
        gb_i[:, lanes] = jnp.sum(dpre_s[:, lanes].astype(F32), axis=0, keepdims=True)
    both_t = jnp.concatenate([mixed[0], mixed[1]], axis=1).T
    ht = h_s[...].T
    per = count // SLABS

    def columns(ref, first, core):
        return ref[:, pl.ds(pl.multiple_of(first + core * HALF, HALF), HALF)]

    def put_rows(core, first, value, groups):
        size = value.shape[0] // len(groups)
        for i, group in enumerate(groups):
            part = value[i * size : (i + 1) * size]
            if core == 0:
                g_keep[group, first : first + size, :] = part
            else:
                row = 2 * BLOCK + group * 9 * rd + first
                give[row : row + size, :] = part

    for core, which in enumerate((c, 1 - c)):
        put_rows(core, 8 * rd, dot(both_t, columns(dattn_s, 0, which)).astype(BF), range(count))
    for s in range(SLABS):
        lanes = slice(s * D, (s + 1) * D)
        rt = r_s[:, lanes].T
        for core, which in enumerate((c, 1 - c)):
            put_rows(core, (4 + s) * rd, dot(ht, columns(dpre_s, s * D, which)).astype(BF), range(count))
            put_rows(core, 0, dot(rt, columns(dff_s, 0, which)).astype(BF), range(s * per, (s + 1) * per))


def back_blocks(blocks, kn, vn, kt, q_in, d_in, ot, lse, dk_s, dv_s, dq_out, scratch):
    qz, qzt, oz, ozt, dq_s, p_s, dp_s = scratch
    rows = lax.broadcasted_iota(jnp.int32, (HALF, BLOCK), 0) // HEAD_DIM
    lanes = lax.broadcasted_iota(jnp.int32, (BLOCK, HALF), 1) // HEAD_DIM
    gq = jnp.zeros((1, HALF), F32)
    for i, block in enumerate(blocks):
        q, d_o = q_in[i].astype(F32), d_in[i * BLOCK : (i + 1) * BLOCK].astype(F32)
        qt, dot_ = q.T, d_o.T
        product = dot_ * ot[i]
        deltas = []
        for h in range(CORE_HEADS):
            head = slice(h * HEAD_DIM, (h + 1) * HEAD_DIM)
            deltas.append(jnp.sum(product[head], axis=0, keepdims=True))
            qz[h] = jnp.where(lanes == h, q, 0.0).astype(BF)
            oz[h] = jnp.where(lanes == h, d_o, 0.0).astype(BF)
            qzt[h] = jnp.where(rows == h, qt, 0.0).astype(BF)
            ozt[h] = jnp.where(rows == h, dot_, 0.0).astype(BF)
        dq_s[...] = jnp.zeros_like(dq_s)

        def chunk(first, count):
            size = count * BLOCK
            keys = kn[pl.ds(first, count)].reshape(size, HALF)
            values = vn[pl.ds(first, count)].reshape(size, HALF)
            for h in range(CORE_HEADS):
                p_s[h, :size] = dot(keys, qzt[h])
                dp_s[h, :size] = dot(values, ozt[h])
            dk = dk_s[pl.ds(first, count)].reshape(size, HALF)
            dv = dv_s[pl.ds(first, count)].reshape(size, HALF)
            for h in range(CORE_HEADS):
                head = slice(h * HEAD_DIM, (h + 1) * HEAD_DIM)
                p = jnp.exp(p_s[h, :size] - lse[i, h : h + 1, :])
                ds = (p * (dp_s[h, :size] - deltas[h])).astype(BF)
                dv = dv + dot(p.astype(BF), oz[h])
                dk = dk + dot(ds, qz[h])
                dq = dq_s[head, :]
                for j in range(count):
                    dq = dq + dot(kt[first + j, head, :], ds[j * BLOCK : (j + 1) * BLOCK])
                dq_s[head, :] = dq
            dk_s[pl.ds(first, count)] = dk.reshape(count, BLOCK, HALF)
            dv_s[pl.ds(first, count)] = dv.reshape(count, BLOCK, HALF)

        over_keys(block, chunk)
        dq = (dq_s[...] * (1.0 / math.sqrt(HEAD_DIM))).T.astype(BF)
        gq = gq + jnp.sum(dq.astype(F32), axis=0, keepdims=True)
        dq_out[i] = dq
    return gq


def back_kernel(nz, which, ids, ins, outs, *scratch):
    kn, vn, kt, qn, ot, lse, d_o = ins[:7]
    dk, dv, dq, gq = outs
    if which == 0:
        dk[...] = jnp.zeros_like(dk)
        dv[...] = jnp.zeros_like(dv)
    blocks = query_blocks(ids[0], ids[1], nz)[2 * which : 2 * which + 2]
    gq[...] = back_blocks(blocks, kn, vn, kt, qn, d_o, ot, lse, dk, dv, dq, scratch)


def dx_kernel(nz, which, ids, ins, outs, dxs):
    wq, dk, dv, dq_mine, dq_other, dx1 = ins
    keep, send, dkv = outs
    z, c = ids[0], ids[1]
    half = nz // 2
    place = lax.rem(z, half)
    w_q = wq[:, :, :HALF].reshape(D, HALF)
    w_kv = wq[:, :, HALF : 3 * HALF].reshape(D, 2 * HALF)
    for core, (target, dq) in enumerate(((keep, dq_mine), (send, dq_other))):
        for p in range(half):
            chip = ids[4] * half + p
            block = 2 * (chip if which == 0 else nz - 1 - chip) + (c if core == 0 else 1 - c)
            dkv[core * half + p, :, :HALF] = dk[block].astype(BF)
            dkv[core * half + p, :, HALF:] = dv[block].astype(BF)
        rows = dkv[core * half : (core + 1) * half].reshape(half * BLOCK, 2 * HALF)
        dxs[core] = ndot(rows, w_kv).reshape(half, BLOCK, D)
        value = ndot(dq[which], w_q)
        if core == 0:
            value = value + dx1[which]
        dxs[core, place] = dxs[core, place] + value
        target[...] = dxs[core].astype(BF)


def dw_kernel(nz, rs, rr, ids, ins, outs, spread):
    xall, dkv_near, dkv_far, dq_mine, dq_other, gq_mine, gq_other, gb_o, gb_i, gb_b, ga = ins
    (dw,) = outs
    z, c = ids[0], ids[1]
    half = nz // 2
    rows = []
    for which in range(2):
        for core in range(2):
            for p in range(half):
                chip = ids[4] * half + p
                rows.append(xall[2 * (chip if which == 0 else nz - 1 - chip) + (c if core == 0 else 1 - c)])
    dkv = jnp.concatenate([ref[...].reshape(nz * BLOCK, 2 * HALF) for ref in (dkv_near, dkv_far)], axis=0)
    acc_kv = dot(jnp.concatenate(rows, axis=0).T, dkv)
    gv = jnp.zeros((1, HALF), F32)
    for ref in (dkv_near, dkv_far):
        for i in range(nz):
            gv = gv + jnp.sum(ref[i, :, HALF:].astype(F32), axis=0, keepdims=True)
    queries = jnp.concatenate([xall[block] for block in query_blocks(z, c, nz)], axis=0).T
    dq = jnp.concatenate([dq_mine[...].reshape(2 * BLOCK, HALF), dq_other[...].reshape(2 * BLOCK, HALF)], axis=0)
    acc_q = dot(queries, dq)
    gq = gq_mine[...] + gq_other[...]
    nothing = jnp.zeros((1, HALF), F32)
    own = [jnp.concatenate([jnp.where(c == 0, g, nothing), jnp.where(c == 0, nothing, g)], axis=1) for g in (gq, gv)]
    tile = jnp.concatenate(own + [gb_o[...], gb_b[...], jnp.zeros((124, D), F32)], axis=0).T
    spread[...] = jnp.broadcast_to(gb_i[...], (128, FF)).T.reshape(D // rr, SLABS, rr, 128)
    lanes = lax.broadcasted_iota(jnp.int32, (D // rr, rr, 128), 2)
    tile = tile.reshape(D // rr, rr, 128)
    for s in range(SLABS):
        tile = jnp.where(lanes == 4 + s, spread[:, s], tile)
    tile = tile.reshape(D, 128)
    if rs >= 16:
        me = ids[2]
        lane = lax.broadcasted_iota(jnp.int32, (D, 128), 1) - 8 - 6 * (me // rs)
        mine = lax.rem(lax.broadcasted_iota(jnp.int32, (D, 128), 0), rs) == lax.rem(me, rs)
        gates = jnp.sum(ga[...], axis=1, keepdims=True)
        for which in range(2):
            rest = gates[which : which + 1]
            for i in range(3):
                high = rest.astype(BF).astype(F32)
                tile = jnp.where(mine & (lane == 2 * i + which), high, tile)
                rest = rest - high
    rows = dw.shape[1]
    dw[:, :, :HALF] = acc_q.astype(BF).reshape(D // rows, rows, HALF)
    dw[:, :, HALF : 3 * HALF] = acc_kv.astype(BF).reshape(D // rows, rows, 2 * HALF)
    dw[:, :, 3 * HALF :] = tile.astype(BF).reshape(D // rows, rows, 128)


def sum_kernel(plans, ids, ins, outs):
    outs = list(outs)
    for numbers, size, where, pre, post, stride, first, flat in plans:

        def total(static, dynamic):
            source = static * stride // size
            index = (static + dynamic) * stride + first - source * size
            refs = [ins[number] for number in numbers[source]]
            value = refs[0][index]
            if len(refs) == 2 and flat is None:
                value = value.astype(F32) + refs[1][index].astype(F32)
            elif len(refs) == 2:
                rows = value.shape[0]
                start = pl.multiple_of(flat + index * rows, 16)
                value = value.astype(F32) + refs[1][pl.ds(start, rows), :].astype(F32)
            return value

        if where is None:
            out = outs.pop(0)
            for index in range(out.shape[0]):
                out[index] = total(index, 0).astype(out.dtype)
            continue
        keep, send = outs.pop(0), outs.pop(0)
        mine = my_bit(ids, where)
        for p in range(pre):
            for q in range(post):
                keep[p * post + q] = total(2 * p * post + q, mine * post).astype(keep.dtype)
                send[p * post + q] = total(2 * p * post + q, (1 - mine) * post).astype(send.dtype)


def grads_kernel(rs, ids, ins, outs):
    own, other = ins
    w_back, w_in, w_out = outs
    for ref, core in ((own, ids[1]), (other, 1 - ids[1])):

        def lanes(first):
            return pl.ds(pl.multiple_of(first + core * HALF, HALF), HALF)

        value = ref[0].astype(F32)
        w_back[:, lanes(0)] = value[: 4 * rs]
        for s in range(SLABS):
            w_in[:, lanes(s * D)] = value[(4 + s) * rs : (5 + s) * rs]
        w_out[:, lanes(0)] = value[8 * rs :]


def last_kernel(rs, ids, ins, outs):
    own, other = ins
    w_qkv, gb_qv, gb_o, gb_i, gb_b, gates = outs
    for ref, core in ((own, ids[1]), (other, 1 - ids[1])):
        value = ref[0].astype(F32)
        for i in range(3):
            lanes = pl.ds(pl.multiple_of(i * D + core * HALF, HALF), HALF)
            w_qkv[:, lanes] = value[:, i * HALF : (i + 1) * HALF]
    sums = own[0, :, 3 * HALF :] + other[0, :, 3 * HALF :].astype(F32)
    lane = lax.broadcasted_iota(jnp.int32, (1, 128), 1)
    column = jnp.sum(sums, axis=0, keepdims=True)
    for which in range(2):
        used = (lane >= 8) & (lax.rem(lane, 2) == which)
        gates[:, which : which + 1] = jnp.sum(jnp.where(used, column, 0.0), axis=1, keepdims=True)
    by_row = jnp.concatenate([sums, jnp.zeros((128 - rs, 128), F32)], axis=0).T
    gb_qv[...] = by_row[:2, :rs]
    gb_o[...] = by_row[2:3, :rs]
    gb_b[...] = by_row[3:4, :rs]
    for s in range(SLABS):
        gb_i[:, s * rs : (s + 1) * rs] = by_row[4 + s : 5 + s, :rs]


def shape(dims, kind):
    return jax.ShapeDtypeStruct(dims, kind)


def vmem(dims, kind):
    return pltpu.VMEM(dims, kind)


def in_hbm(array):
    return pltpu.with_memory_space_constraint(array, pltpu.HBM)


def cost(megabytes):
    return pl.CostEstimate(flops=0, bytes_accessed=megabytes * 2**20, transcendentals=0)


def call(
    name, kernel, ids, ins, outs, after=(), scratch=(), limit=12, weight=0, where=None, aliases=None, out=VMEM
):
    count, waits = len(ins), len(after)

    def run(*refs):
        given, rest = refs[:count], refs[count + waits :]
        kernel(ids(), given, rest[: len(outs)], *rest[len(outs) :])

    return pl.pallas_call(
        run,
        out_shape=tuple(outs),
        in_specs=(where or [VMEM] * count) + [ANY] * waits,
        out_specs=out if isinstance(out, tuple) else (out,) * len(outs),
        scratch_shapes=list(scratch),
        compiler_params=pltpu.CompilerParams(vmem_limit_bytes=limit * 2**20),
        cost_estimate=cost(weight),
        input_output_aliases=aliases or {},
        name=name,
    )(*ins, *after)


def pack_call(ids, rs, ins):
    return call(
        "pack",
        functools.partial(pack_kernel, rs),
        ids,
        [in_hbm(array) for array in ins],
        [vmem((rs, WQ), BF), vmem((9 * rs, HALF), BF), vmem((13 * rs, HALF), BF)] + [vmem((BLOCK, D), BF)] * 4
        + [vmem((8, 128), F32)],
        scratch=[pltpu.VMEM(array.shape, BF) for array in ins[:8]]
        + [pltpu.VMEM((1, 2), F32), pltpu.VMEM((128, 128), F32), pltpu.SemaphoreType.DMA((13,))],
        where=[ANY] * 11,
    )


def join_call(name, ids, jobs, after=(), extra=None, extra_ins=(), extra_outs=(), cuts=None):
    ins, outs, spans = [], [], []
    for (own, got, _, _), cut in zip(jobs, cuts or [1] * len(jobs)):
        ins += [own, got]
        spans.append(slice(len(outs), len(outs) + cut))
        outs += [vmem((2 * own.shape[0] // cut,) + own.shape[1:], own.dtype)] * cut
    number = len(outs)

    def kernel(ids_ref, given, results):
        for i, (_, _, where, post) in enumerate(jobs):
            join(ids_ref, given[2 * i], given[2 * i + 1], results[spans[i]], where, post)
        if extra is not None:
            extra(ids_ref, given[2 * len(jobs) :], results[number:])

    return call(name, kernel, ids, ins + list(extra_ins), outs + list(extra_outs), after)


def sum_call(name, ids, jobs, after=(), last=BF, flat=None):
    ins, outs, plans = [], [], []

    def number(array):
        for i, other in enumerate(ins):
            if other is array:
                return i
        ins.append(array)
        return len(ins) - 1

    for sources, where, pre, post, stride, first in jobs:
        numbers = [tuple(number(array) for array in pair if array is not None) for pair in sources]
        tail = sources[0][0].shape[1:]
        size = sources[0][0].shape[0]
        plans.append((numbers, size, where, pre, post, stride, first, flat))
        if where is None:
            outs.append(vmem((size * len(sources) // stride,) + tail, last))
        else:
            outs += [vmem((pre * post,) + tail, last), vmem((pre * post,) + tail, BF)]
    return call(name, functools.partial(sum_kernel, plans), ids, ins, outs, after)


def make_body(n1, n2, nz):
    ndp = n1 * n2
    nsh = ndp * nz * 2
    rs = D // nsh
    rd = D // ndp
    half = nz // 2
    parts = 2 * nz if rs % 16 == 0 else 1
    rr = rd // parts
    nh = 9 * rd // 2
    swap = [(0, 1), (1, 0)]
    bits_a, bits_b, bits_z = (count.bit_length() - 1 for count in (n1, n2, nz))
    counts = {"a": n1, "b": n2, "z": nz}
    slot = {"a": 3, "b": 5, "z": 0}

    def to_mirror(array):
        return lax.ppermute(array, "z", [(s, nz - 1 - s) for s in range(nz)])

    def exchange(array, name, bit):
        return lax.ppermute(array, name, [(s, s ^ (1 << bit)) for s in range(counts[name])])

    def to_other(array):
        return lax.ppermute(array, "c", swap)

    def body(inputs, w_qkv, bias_qv, w_out, bias_out, w_in, bias_in, w_back, bias_back, alphas, cotangent):
        z, c = lax.axis_index("z"), lax.axis_index("c")
        a, b = lax.axis_index("a"), lax.axis_index("b")

        def ids():
            z, c = lax.axis_index("z"), lax.axis_index("c")
            a, b = lax.axis_index("a"), lax.axis_index("b")
            return (z, c, ((a * n2 + b) * nz + z) * 2 + c, a, z // half, b)


        latest = []

        def hand_on(ids_ref, given, results):
            for source, target in zip(given, results):
                target[...] = source[...]

        def step(name, jobs, extra=(), cuts=None, others=()):
            result = join_call(
                name, ids, jobs, latest + list(others), hand_on, extra, [vmem(e.shape, e.dtype) for e in extra], cuts
            )
            latest[:] = [result[0]]
            return result


        q_keep, f_keep, give, x_give, x_keep, cot_give, cot_a, gates = pack_call(
            ids, rs,
            [w_qkv, w_back, w_in, w_out, bias_qv, bias_out[None], bias_back[None], bias_in[None], inputs, cotangent,
             alphas[None]],
        )
        wq, wf = call(
            "core", functools.partial(core_kernel, rs), ids, [q_keep, f_keep, to_other(give)],
            [vmem((2, rs, WQ), BF), vmem((2, 9 * rs, HALF), BF)],
        )
        latest[:] = [wq]
        wq, wf = wq.reshape(1, 2 * rs, WQ), wf.reshape(1, 2 * 9 * rs, HALF)
        wf = wf.reshape(2 * 9 * rs, HALF)
        q_got = exchange(wq, "z", bits_z - 1)
        wf_parts = [(wf, 0)]
        for i in reversed(range(bits_z)):
            wf_parts += [(exchange(part, "z", i), place | (1 << i)) for part, place in wf_parts]
        wf_near = [part for part, place in wf_parts if place == 1]
        for i in reversed(range(1, bits_z)):
            (wq,) = step("q_z", [(wq, q_got, (0, i), 1)])
            q_got = exchange(wq, "z", i - 1)
        wq, x_keep, x_give = step(
            "q_z", [(wq, q_got, (0, 0), 1)], [x_keep, x_give], others=wf_near + [wf_parts[1][0]]
        )
        wq = wq.reshape(rd, WQ)
        if parts == 1:
            hidden_bias = wq[:, 3 * HALF + 4 : 3 * HALF + 8].reshape(2 * nz, rs, SLABS)
            hidden_bias = jnp.transpose(hidden_bias, (0, 2, 1)).reshape(SLABS, rd).T
            wq = jnp.concatenate([wq[:, : 3 * HALF + 4], hidden_bias, wq[:, 3 * HALF + 8 :]], axis=1)
        wq = wq[None]
        x_far = to_mirror(x_give)
        for i in reversed(range(1, bits_b)):
            q_got = exchange(wq, "b", i)
            (wq,) = step("q_b", [(wq, q_got, (5, i), 1)])
        q_got = exchange(wq, "b", 0)
        own = x_keep[None]
        own_got = exchange(own, "z", max(bits_z - 2, 0))

        def in_place(ids_ref, given, results):
            for group in range(2):

                @pl.when(ids_ref[4] == group)
                def _():
                    for ref, (_, place) in zip(given, wf_parts):
                        at = lax.rem(lax.bitwise_xor(ids_ref[0], place), half)
                        results[group ^ (place // half)][at] = ref[...]

        halves = vmem((half, 2 * 9 * rs, HALF), BF)
        first, second = call("f_z", in_place, ids, [part for part, _ in wf_parts], [halves, halves], latest)
        latest[:] = [first]
        if parts == 1:
            wf = jnp.concatenate([first, second], axis=0).reshape(nz, 2, 9 * rs, HALF)
            wf = jnp.concatenate(
                [wf[:, :, : 4 * rs].reshape(4 * rd, HALF)]
                + [wf[:, :, (4 + s) * rs : (5 + s) * rs].reshape(rd, HALF) for s in range(SLABS)]
                + [wf[:, :, 8 * rs :].reshape(rd, HALF)],
                axis=0,
            )
            first, second = wf[:nh], wf[nh:]
        first, second = first.reshape(1, nh, HALF), second.reshape(1, nh, HALF)
        (wq,) = step("q_b", [(wq, q_got, (5, 0), 1)])
        for i in reversed(range(1, bits_a)):
            q_got = exchange(wq, "a", i)
            (wq,) = step("q_a", [(wq, q_got, (3, i), n2)])
        wq_pieces = [wq, exchange(wq, "a", 0)]

        far_rows, cot_give = call(
            "x_far", hand_on, ids, [x_far, cot_give], [vmem((BLOCK, D), BF)] * 2, latest + [own_got]
        )
        latest[:] = [far_rows]
        cot_b = to_mirror(cot_give)
        far_rows = far_rows[None]
        for i in reversed(range(1, bits_z - 1)):
            far_got = exchange(far_rows, "z", i)
            own, far_rows = step("x_z", [(own, own_got, (0, i), 1), (far_rows, far_got, (0, i), 1)])
            own_got = exchange(own, "z", i - 1)
        far_got = exchange(far_rows, "z", 0)

        for i in reversed(range(bits_b)):
            got = exchange(first, "b", i), exchange(second, "a", i)
            first, second = step("f_dp", [(first, got[0], (5, i), 1), (second, got[1], (3, i), 1)])
        for i in reversed(range(1, bits_a)):
            got = exchange(first, "a", i), exchange(second, "b", i)
            first, second = step("f_dp", [(first, got[0], (3, i), n2), (second, got[1], (5, i), 1)])
        wf_pieces = [first, second, exchange(first, "a", 0), exchange(second, "b", 0)]

        def rows_of_all(ids_ref, given, results):
            own_ref, own_got_ref, far_ref, far_got_ref = given
            base, mine = ids_ref[4] * half, my_bit(ids_ref, (0, 0))
            for p in range(half // 2):
                for own_part, far_part, at in (
                    (own_ref, far_ref, base + 2 * p + mine),
                    (own_got_ref, far_got_ref, base + 2 * p + 1 - mine),
                ):
                    results[0][at - base] = own_part[p]
                    results[1][at - base] = far_part[p]

        xo = call(
            "x_all", rows_of_all, ids, [own, own_got, far_rows, far_got], [vmem((half, BLOCK, D), BF)] * 2,
            latest + [wq_pieces[1], cot_b],
        )
        latest[:] = [xo[0]]
        xs = [to_other(part) for part in xo]

        nb = 2 * nz
        heads_t = pltpu.VMEM((CORE_HEADS, HALF, BLOCK), BF)
        scores = pltpu.VMEM((CORE_HEADS, 4 * BLOCK, BLOCK), F32)
        scratch = [
            heads_t,
            scores,
            pltpu.VMEM((CORE_HEADS, 1, BLOCK), F32),
            pltpu.VMEM((CORE_HEADS, 1, BLOCK), F32),
            pltpu.VMEM((HALF, BLOCK), F32),
        ]
        natural, turned = (nb, BLOCK, HALF), (nb, HALF, BLOCK)
        two, two_t = (2, BLOCK, HALF), (2, HALF, BLOCK)
        two_lse = (2, CORE_HEADS, BLOCK)
        spread = pltpu.VMEM((D // rr, SLABS, rr, 128), F32)
        (xall, wq, kn, vn, kt, vt, q_mine, q_other, ot_other, lse_other, o_send, bo, bb, bi) = call(
            "first",
            functools.partial(first_kernel, nz, ndp, n2, rr),
            ids,
            [*xo, *xs, *wq_pieces],
            [
                vmem((nb, BLOCK, D), BF),
                vmem((ndp, rd, WQ), BF),
                vmem(natural, BF),
                vmem(natural, BF),
                vmem(turned, BF),
                vmem(turned, BF),
                vmem(two, BF),
                vmem(two, BF),
                vmem(two_t, F32),
                vmem(two_lse, F32),
                vmem(two, BF),
                vmem((1, D), F32),
                vmem((1, D), F32),
                vmem((1, FF), F32),
            ],
            latest,
            [spread] + scratch,
            limit=24,
        )

        def give_kernel(ids_ref, given, results):
            row = 0
            for part in given:
                for i in range(part.shape[0]):
                    results[0][row : row + part.shape[1]] = part[i]
                    row += part.shape[1]

        (give,) = call(
            "give", give_kernel, ids, [o_send, *wf_pieces], [vmem((2 * BLOCK + 2 * ndp * nh, HALF), BF)],
            limit=24,
        )
        ffn_got = to_other(give)
        ot_mine, lse_mine, o_mine = call(
            "second",
            functools.partial(second_kernel, nz),
            ids,
            [kn, vt, q_mine],
            [vmem(two_t, F32), vmem(two_lse, F32), vmem(two, BF)],
            (),
            scratch,
            limit=24,
        )

        grouped = (ndp * parts, 9 * rd // parts, HALF)
        (out_near, out_far, dx1, d_mine, g_keep, give, gb_o, gb_i, gb_b, ga) = call(
            "ffn",
            functools.partial(ffn_kernel, nz, ndp, n2, parts),
            ids,
            [gates, o_mine, ffn_got, xall, cot_a, cot_b, bo, bi, bb, *wf_pieces],
            [
                vmem((BLOCK, D), BF),
                vmem((BLOCK, D), BF),
                vmem((2, BLOCK, D), F32),
                vmem((2 * BLOCK, HALF), BF),
                vmem(grouped, BF),
                vmem((2 * BLOCK + ndp * 9 * rd, HALF), BF),
                vmem((1, D), F32),
                vmem((1, FF), F32),
                vmem((1, D), F32),
                vmem((2, D), F32),
            ],
            scratch=[
                pltpu.VMEM((2, 2 * ndp, nh, HALF) if parts == 1 else (8, 128), BF),
                pltpu.VMEM((D, D), BF),
                pltpu.VMEM((SLABS, D, D), BF),
                pltpu.VMEM((FF, D), BF),
                pltpu.VMEM((2, 2 * BLOCK, HALF), BF),
                pltpu.VMEM((2 * BLOCK, D), BF),
                pltpu.VMEM((2 * BLOCK, FF), BF),
                pltpu.VMEM((2 * BLOCK, FF), BF),
                pltpu.VMEM((2 * BLOCK, D), BF),
                pltpu.VMEM((2 * BLOCK, D), BF),
                pltpu.VMEM((SLABS, 2 * BLOCK, D), F32),
                pltpu.VMEM((SLABS, 2 * BLOCK, D), F32),
                pltpu.VMEM((2 * BLOCK, D), F32),
                pltpu.VMEM((2 * BLOCK, D), F32),
            ],
            limit=36,
        )
        back_got = to_other(give)
        back_scratch = [
            pltpu.VMEM((CORE_HEADS, BLOCK, HALF), BF),
            heads_t,
            pltpu.VMEM((CORE_HEADS, BLOCK, HALF), BF),
            heads_t,
            pltpu.VMEM((HALF, BLOCK), F32),
            scores,
            scores,
        ]
        back_out = [vmem(natural, F32), vmem(natural, F32), vmem(two, BF), vmem((1, HALF), F32)]
        dk, dv, dq_mine, gq_mine = call(
            "back_first",
            functools.partial(back_kernel, nz, 0),
            ids,
            [kn, vn, kt, q_mine, ot_mine, lse_mine, d_mine],
            back_out,
            scratch=back_scratch,
            limit=24,
        )

        latest[:] = [gq_mine]
        done = {}

        def along(axis, count, pre, post):
            return [(axis, i, pre * (count >> (i + 1)), post) for i in range(count.bit_length() - 1)]

        def dp_scatter(name, kept, got, rows, columns, flat=None):
            axes = (along("b", n2, n1, 1) + along("a", n1, 1, 1), along("a", n1, 1, n2) + along("b", n2, 1, 1))
            whole = (kept.reshape(2 * ndp, rows, columns), got)
            state = [(whole, 2, 0), (whole, 2, 1)]
            for i in range(len(axes[0])):
                result = sum_call(
                    name,
                    ids,
                    [
                        ([pair], (slot[axis], bit), pre, post, stride, first)
                        for (pair, stride, first), (axis, bit, pre, post) in zip(state, (axes[0][i], axes[1][i]))
                    ],
                    latest,
                    flat=flat if i == 0 else None,
                )
                latest[:] = [result[0]]
                state = [
                    ((result[2 * j], exchange(result[2 * j + 1], axes[j][i][0], axes[j][i][1])), 1, 0)
                    for j in range(2)
                ]
                yield
            return [pair for pair, _, _ in state]

        def z_scatter(name, sources):
            for _, i, pre, _ in along("z", nz, 1, 1):
                kept, send = sum_call(name, ids, [(sources, (slot["z"], i), pre, 1, 1, 0)], latest)
                latest[:] = [kept]
                sources = [(kept, exchange(send, "z", i))]
                yield
            rows, columns = kept.shape[1] // 2, kept.shape[2]
            sources = [tuple(array.reshape(2, rows, columns) for array in sources[0])]
            keep, send = sum_call(name, ids, [(sources, (1, 0), 1, 1, 1, 0)], latest, F32)
            latest[:] = [keep]
            return keep, to_other(send)

        def whole_dp(name, sources):
            return [part[0] for part in sum_call(name, ids, [([pair], None, 0, 0, 1, 0) for pair in sources], latest)]

        def g_chain():
            sources = yield from dp_scatter("g_dp", g_keep, back_got, nh, HALF, 2 * BLOCK)
            if parts == 1:
                g_dp = jnp.concatenate(whole_dp("g_dp", sources), axis=0)
                g_dp = jnp.concatenate(
                    [g_dp[: 4 * rd].reshape(nz, 2, 4 * rs, HALF)]
                    + [g_dp[(4 + s) * rd : (5 + s) * rd].reshape(nz, 2, rs, HALF) for s in range(SLABS)]
                    + [g_dp[8 * rd :].reshape(nz, 2, rs, HALF)],
                    axis=2,
                )
                sources = [(g_dp.reshape(nz, 2 * 9 * rs, HALF), None)]
            else:
                sources = [tuple(array.reshape(half, 2 * 9 * rs, HALF) for array in pair) for pair in sources]
            keep, got = yield from z_scatter("g_z", sources)
            yield
            done["g"] = call(
                "g_last", functools.partial(grads_kernel, rs), ids, [keep, got],
                [pltpu.HBM((4 * rs, D), F32), pltpu.HBM((rs, FF), F32), pltpu.HBM((rs, D), F32)], latest,
            )

        g_steps = g_chain()
        next(g_steps)
        dk, dv, dq_other, gq_other = call(
            "back_second",
            functools.partial(back_kernel, nz, 1),
            ids,
            [kn, vn, kt, q_other, ot_other, lse_other, back_got, dk, dv],
            back_out,
            latest,
            back_scratch,
            limit=24,
            aliases={7: 0, 8: 1},
        )
        def out_kernel(ids_ref, given, results, sems):
            group = ids_ref[4]
            copies = moves(sems, [(given[0], results[0].at[group]), (given[1], results[0].at[1 - group])])
            results[1][...] = jnp.zeros_like(results[1])
            wait(copies)

        def to_rows(name, own, got):
            rows, token = call(
                name, out_kernel, ids, [own, got], [pltpu.HBM((2, BLOCK, D), BF), vmem((8, 128), F32)], latest,
                [pltpu.SemaphoreType.DMA((2,))], where=[ANY, ANY],
                out=(pl.BlockSpec(memory_space=pltpu.HBM), VMEM),
            )
            latest[:] = [token]
            return rows

        latest[:] = [gq_other]
        out_b = to_mirror(out_far)
        latest.append(out_b)

        def dx_call(which):
            keep, send, dkv = call(
                "dx",
                functools.partial(dx_kernel, nz, which),
                ids,
                [wq, dk, dv, dq_mine, dq_other, dx1],
                [vmem((half, BLOCK, D), BF), vmem((half, BLOCK, D), BF), vmem((nz, BLOCK, 2 * HALF), BF)],
                latest,
                [pltpu.VMEM((2, half, BLOCK, D), F32)],
            )
            latest[:] = [keep]
            return (keep, to_other(send)), dkv

        def dx_chain(pair, far):
            for i in range(bits_z - 1):
                kept, send = sum_call("dx_z", ids, [([pair], (0, i), half >> (i + 1), 1, 1, 0)], latest)
                latest[:] = [kept]
                pair = (kept, exchange(send, "z", i))
                yield
            (rows,) = sum_call("dx_z", ids, [([pair], None, 0, 0, 1, 0)], latest)
            latest[:] = [rows]
            rows = rows.reshape(BLOCK, D)
            done["far" if far else "near"] = to_mirror(rows) if far else rows

        far_pair, dkv_far = dx_call(1)
        near_pair, dkv_near = dx_call(0)
        far_steps, near_steps = dx_chain(far_pair, True), dx_chain(near_pair, False)
        next(far_steps)
        next(g_steps)
        next(near_steps)
        (dw,) = call(
            "dw",
            functools.partial(dw_kernel, nz, rs, rr),
            ids,
            [xall, dkv_near, dkv_far, dq_mine, dq_other, gq_mine, gq_other, gb_o, gb_i, gb_b, ga],
            [vmem((2 * ndp, rd // 2, WQ), BF)],
            latest,
            [spread],
            limit=20,
        )
        latest[:] = [dw]

        def dw_chain():
            sources = yield from dp_scatter("w_dp", dw, None, rd // 2, WQ)
            if parts == 1:
                dw_dp = jnp.concatenate(whole_dp("w_dp", sources), axis=0)
                hidden_bias = dw_dp[:, 3 * HALF + 4 : 3 * HALF + 8].T.reshape(2 * nz, SLABS, rs)
                hidden_bias = jnp.transpose(hidden_bias, (0, 2, 1)).reshape(rd, SLABS)
                dw_dp = jnp.concatenate([dw_dp[:, : 3 * HALF + 4], hidden_bias, dw_dp[:, 3 * HALF + 8 :]], axis=1)
                sources = [(dw_dp.reshape(nz, 2 * rs, WQ), None)]
            else:
                sources = [tuple(array.reshape(half, 2 * rs, WQ) for array in pair) for pair in sources]
            keep, got = yield from z_scatter("w_z", sources)
            yield
            done["w"] = call(
                "w_last", functools.partial(last_kernel, rs), ids, [keep, got],
                [shape((rs, 3 * D), F32), shape((2, rs), F32), shape((1, rs), F32), shape((1, SLABS * rs), F32)]
                + [shape((1, rs), F32), shape((1, 2), F32)],
                latest,
            )
            latest[:] = [done["w"][0]]

        steps = {"f": far_steps, "n": near_steps, "g": g_steps, "w": dw_chain()}
        for name in "fgwnowgwxwgwgw" + "fn" * bits_z + "x" + "gw" * (2 * bits_z):
            if name == "o":
                outputs = to_rows("outputs", out_near, out_b)
            elif name == "x":
                if "inputs" not in done:
                    for chain in (far_steps, near_steps):
                        while next(chain, 0) is None:
                            pass
                    done["inputs"] = to_rows("dx_last", done["near"], done["far"])
            else:
                next(steps[name], 0)
        gb_qv, gb_out, gb_in, gb_back, grad_alphas = done["w"][1:]
        if rs < 16:
            grad_alphas = lax.psum(jnp.sum(ga, axis=1), MESH_AXES)
        return (
            outputs,
            done["inputs"],
            done["w"][0],
            gb_qv,
            done["g"][2],
            gb_out.reshape(rs),
            done["g"][1],
            gb_in.reshape(SLABS * rs),
            done["g"][0],
            gb_back.reshape(rs),
            grad_alphas.reshape(2),
        )

    return body


def solution(mesh):
    ndp, nseq = mesh.devices.shape
    n1 = math.isqrt(ndp)
    n2 = ndp // n1
    nz = nseq // 2
    fine = Mesh(mesh.devices.reshape(n1, n2, nz, 2), MESH_AXES)
    dp, seq = ("a", "b"), ("z", "c")
    rows = P(dp, seq, None)
    both = dp + seq
    return jax.shard_map(
        make_body(n1, n2, nz),
        mesh=fine,
        in_specs=(
            rows,
            P(both, None),
            P(None, both),
            P(both, None),
            P(both),
            P(both, None),
            P(both),
            P(both, None),
            P(both),
            P(),
            rows,
        ),
        out_specs=(
            rows,
            rows,
            P(both, None),
            P(None, both),
            P(both, None),
            P(both),
            P(both, None),
            P(both),
            P(both, None),
            P(both),
            P(),
        ),
        check_vma=False,
    )
```

```python
import functools
import math

import jax
import jax.numpy as jnp
from jax import lax
from jax.experimental import pallas as pl
from jax.experimental.pallas import tpu as pltpu
from jax.sharding import Mesh, PartitionSpec as P

D = 512
HEADS = 8
HEAD_DIM = 64
FF = 2048
BLOCK = 256
HALF = D // 2
CORE_HEADS = HEADS // 2
SLABS = FF // D
BF = jnp.bfloat16
F32 = jnp.float32
MESH_AXES = ("a", "b", "z", "c")
VMEM = pl.BlockSpec(memory_space=pltpu.VMEM)
SMEM = pl.BlockSpec(memory_space=pltpu.SMEM)
ANY = pl.BlockSpec(memory_space=pl.ANY)
WQ = 3 * HALF + 128
GELU_C = math.sqrt(2.0 / math.pi)


def dot(left, right):
    return jnp.dot(left, right, preferred_element_type=F32)


def ndot(left, right):
    return lax.dot_general(left, right, (((1,), (1,)), ((), ())), preferred_element_type=F32)


def flip(block):
    return block.T


def query_blocks(z, c, nz):
    near, far = 2 * z, 2 * (nz - 1 - z)
    return (near + c, far + c, near + 1 - c, far + 1 - c)


def over_keys(block, chunk):
    count = block + 1

    def step(i, unused):
        chunk(4 * i, 4)
        return unused

    lax.fori_loop(0, count // 4, step, 0)

    @pl.when(lax.rem(count, 4) >= 2)
    def _():
        chunk(count // 4 * 4, 2)

    @pl.when(lax.rem(count, 2) == 1)
    def _():
        chunk(block, 1)


def attend_blocks(blocks, kn, vt, qn, ot, lse, o, scratch):
    qz, s_s, m_s, l_s, acc_s = scratch
    rows = lax.broadcasted_iota(jnp.int32, (HALF, BLOCK), 0) // HEAD_DIM
    def one(i, unused):
        block = jnp.where(i == 0, blocks[0], blocks[1])
        qt = qn[i].astype(F32).T
        for h in range(CORE_HEADS):
            qz[h] = jnp.where(rows == h, qt, 0.0).astype(BF)
        m_s[...] = jnp.full_like(m_s, -1e30)
        l_s[...] = jnp.zeros_like(l_s)
        acc_s[...] = jnp.zeros_like(acc_s)

        def chunk(first, count):
            keys = kn[pl.ds(first, count)].reshape(count * BLOCK, HALF)
            for h in range(CORE_HEADS):
                s_s[h, : count * BLOCK] = dot(keys, qz[h])
            for h in range(CORE_HEADS):
                head = slice(h * HEAD_DIM, (h + 1) * HEAD_DIM)
                s = s_s[h, : count * BLOCK]
                old = m_s[h]
                new = jnp.maximum(old, jnp.max(s, axis=0, keepdims=True))
                p = jnp.exp(s - new)
                shrink = jnp.exp(old - new)
                m_s[h] = new
                l_s[h] = l_s[h] * shrink + jnp.sum(p, axis=0, keepdims=True)
                p = p.astype(BF)
                acc = acc_s[head, :] * shrink
                for j in range(count):
                    acc = acc + dot(vt[first + j, head, :], p[j * BLOCK : (j + 1) * BLOCK])
                acc_s[head, :] = acc

        over_keys(block, chunk)
        for h in range(CORE_HEADS):
            head = slice(h * HEAD_DIM, (h + 1) * HEAD_DIM)
            total = l_s[h]
            lse[i, h : h + 1, :] = m_s[h] + jnp.log(total)
            acc_s[head, :] = acc_s[head, :] / total
        value = acc_s[...]
        ot[i] = value
        o[i] = value.T.astype(BF)
        return unused

    lax.fori_loop(0, 2, one, 0)


def moves(sems, pairs):
    copies = [pltpu.make_async_copy(src, dst, sems.at[i]) for i, (src, dst) in enumerate(pairs)]
    for copy in copies:
        copy.start()
    return copies


def wait(copies):
    for copy in copies:
        copy.wait()


def pack_kernel(rs, ids, ins, outs, *refs):
    w_qkv, w_back, w_in, w_out, bias_qv, bias_out, bias_back, bias_in = refs[:8]
    gates, tile, sems = refs[8:]
    group = ids[4]
    loads = moves(sems, [(ins[i], refs[i]) for i in range(8)] + [(ins[10], gates)])
    rows = moves(
        sems.at[pl.ds(9, 4)],
        [(ins[8 + i].at[which], outs[3 + 2 * i + j]) for i in range(2) for j, which in enumerate((1 - group, group))],
    )
    wait(loads)
    tile[...] = jnp.zeros_like(tile)
    tile[0:2, :rs] = bias_qv[...].astype(F32)
    tile[2:3, :rs] = bias_out[...].astype(F32)
    tile[3:4, :rs] = bias_back[...].astype(F32)
    for i in range(SLABS):
        tile[4 + i : 5 + i, :rs] = bias_in[:, i * rs : (i + 1) * rs].astype(F32)
    outs[7][0:1, 0:2] = gates[...]
    turned = tile[...].T[:rs].astype(BF)
    q_keep, f_keep, give = outs[:3]

    def cut(ref, first, core):
        return ref[:, pl.ds(pl.multiple_of(first + core * HALF, HALF), HALF)]

    for i in range(3):
        q_keep[:, i * HALF : (i + 1) * HALF] = cut(w_qkv, i * D, ids[1])
        give[(9 + i) * rs : (10 + i) * rs] = cut(w_qkv, i * D, 1 - ids[1])
    q_keep[:, 3 * HALF :] = turned
    give[12 * rs :, :128] = turned
    give[12 * rs :, 128:] = jnp.zeros((rs, 128), BF)
    for f_out, core in ((f_keep, ids[1]), (give, 1 - ids[1])):
        f_out[: 4 * rs] = cut(w_back, 0, core)
        for i in range(SLABS):
            f_out[(4 + i) * rs : (5 + i) * rs] = cut(w_in, i * D, core)
        f_out[8 * rs : 9 * rs] = cut(w_out, 0, core)
    wait(rows)


def core_kernel(rs, ids, ins, outs):
    q_keep, f_keep, got = ins
    wq, wf = outs
    c = ids[1]
    wq[c] = q_keep[...]
    wf[c] = f_keep[...]
    wf[1 - c] = got[: 9 * rs]
    for i in range(3):
        wq[1 - c, :, i * HALF : (i + 1) * HALF] = got[(9 + i) * rs : (10 + i) * rs]
    wq[1 - c, :, 3 * HALF :] = got[12 * rs :, :128]


def my_bit(ids, where):
    index, bit = where
    return lax.rem(lax.shift_right_logical(ids[index], bit), 2)


def join(ids, own, got, outs, where, post=1):
    mine = my_bit(ids, where)
    pre = own.shape[0] // post
    for p in range(pre):
        out = outs[p * len(outs) // pre]
        at = 2 * p - 2 * pre // len(outs) * (p * len(outs) // pre)
        for q in range(post):
            out[(at + mine) * post + q] = own[p * post + q]
            out[(at + 1 - mine) * post + q] = got[p * post + q]


def first_kernel(nz, ndp, n2, rr, ids, ins, outs, spread, *scratch):
    xo, xs = ins[:2], ins[2:4]
    wq_pieces = ins[4:6]
    xall, wq, kn, vn, kt, vt, q_mine, q_other, ot, lse, o, bo, bb, bi = outs
    z, c = ids[0], ids[1]
    for p in range(nz // 2):
        chip = ids[4] * (nz // 2) + p
        for i, at in enumerate((chip, nz - 1 - chip)):
            xall[2 * at + c] = xo[i][p]
            xall[2 * at + 1 - c] = xs[i][p]
    for far, piece in enumerate(wq_pieces):
        bit = lax.rem(ids[3], 2)
        for j in range(piece.shape[0]):
            wq[(2 * (j // n2) + (1 - bit if far else bit)) * n2 + j % n2] = piece[j]
    bias = wq[:, :, 3 * HALF :].reshape(D, 128).astype(F32)
    turned = bias.T
    bo[...] = turned[2:3]
    bb[...] = turned[3:4]
    lanes = lax.broadcasted_iota(jnp.int32, (D // rr, rr, 128), 2)
    for s in range(SLABS):
        spread[:, s] = jnp.where(lanes == 4 + s, bias.reshape(D // rr, rr, 128), 0.0)
    bi[...] = jnp.sum(spread[...].reshape(FF, 128).T[4:8], axis=0, keepdims=True)
    bias_q = jnp.where(c == 0, turned[0:1, :HALF], turned[0:1, HALF:])
    bias_v = jnp.where(c == 0, turned[1:2, :HALF], turned[1:2, HALF:])
    w_q = wq[:, :, :HALF].reshape(D, HALF)
    w_kv = wq[:, :, HALF : 3 * HALF].reshape(D, 2 * HALF)

    def project(i, unused):
        blocks = pl.ds(4 * i, 4)
        kv = dot(xall[blocks].reshape(4 * BLOCK, D), w_kv)
        key = kv[:, :HALF].astype(BF).reshape(4, BLOCK, HALF)
        value = (kv[:, HALF:] + bias_v).astype(BF).reshape(4, BLOCK, HALF)
        kn[blocks] = key
        vn[blocks] = value
        for j in range(4):
            kt[4 * i + j] = key[j].T
            vt[4 * i + j] = value[j].T
        return unused

    lax.fori_loop(0, nz // 2, project, 0)
    blocks = query_blocks(z, c, nz)
    q = dot(jnp.concatenate([xall[block] for block in blocks], axis=0), w_q) + bias_q
    q = (q.astype(BF).astype(F32) * (1.0 / math.sqrt(HEAD_DIM))).astype(BF)
    for i in range(4):
        (q_mine if i < 2 else q_other)[i % 2] = q[i * BLOCK : (i + 1) * BLOCK]
    attend_blocks(blocks[2:], kn, vt, q_other, ot, lse, o, scratch)


def place_dp(ids, pieces, ndp, n2, put):
    for i, piece in enumerate(pieces):
        far, half = i // 2, i % 2
        for j in range(ndp // 2):
            if half == 0:
                bit = lax.rem(ids[3], 2)
                dp = (2 * (j // n2) + (1 - bit if far else bit)) * n2 + j % n2
            else:
                bit = lax.rem(ids[5], 2)
                dp = j // (n2 // 2) * n2 + 2 * (j % (n2 // 2)) + (1 - bit if far else bit)
            put(dp, half, piece(j) if callable(piece) else piece[j])


def second_kernel(nz, ids, ins, outs, *scratch):
    kn, vt, qn = ins
    ot, lse, o = outs
    blocks = query_blocks(ids[0], ids[1], nz)
    attend_blocks(blocks[:2], kn, vt, qn, ot, lse, o, scratch)


def ffn_kernel(nz, ndp, n2, parts, ids, ins, outs, *refs):
    alphas, o_mine, got, xall, cot_a, cot_b, bo, bi, bb = ins[:9]
    pieces = ins[9:13]
    rows = pieces[0].shape[1]

    def received(i):
        return lambda j: got[pl.ds(2 * BLOCK + (i * (ndp // 2) + j) * rows, rows)]

    (out_near, out_far, dx1, d_mine, g_keep, give, gb_o, gb_i, gb_b, ga) = outs
    w, wo_s, wi_s, wb_s, mixed, h_s, r_s, dpre_s, dff_s, dattn_s = refs[:10]
    pre_s, dr_s = refs[10:12]
    c = ids[1]
    count = ndp * parts
    rd = D // count
    for core in range(2):
        own = pieces if core == 0 else [received(i) for i in range(4)]
        which = c if core == 0 else 1 - c
        lanes = pl.ds(pl.multiple_of(which * HALF, HALF), HALF)

        def put(dp, half, value):
            if parts == 1:
                w[which, 2 * dp + half] = value
                return
            for g in range(parts // 2):
                at = dp * parts + half * (parts // 2) + g
                part = value[9 * rd * g : 9 * rd * (g + 1)]
                wb_s[pl.ds(pl.multiple_of(at * 4 * rd, 4 * rd), 4 * rd), lanes] = part[: 4 * rd]
                at = pl.multiple_of(at * rd, rd)
                for s in range(SLABS):
                    wi_s[s, pl.ds(at, rd), lanes] = part[(4 + s) * rd : (5 + s) * rd]
                wo_s[pl.ds(at, rd), lanes] = part[8 * rd :]

        place_dp(ids, own, ndp, n2, put)
    if parts == 1:
        for half in range(2):
            lanes = slice(half * HALF, (half + 1) * HALF)
            whole = w[half].reshape(count, 9 * rd, HALF)
            wo_s[:, lanes] = whole[:, 8 * rd :].reshape(D, HALF)
            for s in range(SLABS):
                wi_s[s, :, lanes] = whole[:, (4 + s) * rd : (5 + s) * rd].reshape(D, HALF)
            wb_s[:, lanes] = whole[:, : 4 * rd].reshape(FF, HALF)
    mixed[c] = o_mine[...].reshape(2 * BLOCK, HALF)
    mixed[1 - c] = got[: 2 * BLOCK]
    alpha_attn, alpha_ffn = alphas[0:1, 0:1], alphas[0:1, 1:2]
    mine = query_blocks(ids[0], c, nz)
    both = 2 * BLOCK
    dy = jnp.concatenate([cot_a[...], cot_b[...]], axis=0).astype(F32)
    dff = (alpha_ffn * dy).astype(BF)
    dff_s[...] = dff
    attn = dot(mixed[0], wo_s[:HALF, :]) + dot(mixed[1], wo_s[HALF:, :]) + bo[...]
    x1 = jnp.concatenate([xall[mine[0]], xall[mine[1]]], axis=0).astype(F32) + alpha_attn * attn
    hidden = x1.astype(BF)
    h_s[...] = hidden
    x1_s = refs[12]
    attn_s = refs[13]
    x1_s[...] = x1
    attn_s[...] = attn
    for s in range(SLABS):
        lanes = slice(s * D, (s + 1) * D)
        pre_s[s] = dot(h_s[...], wi_s[s]) + bi[:, lanes]
        dr_s[s] = ndot(dff_s[...], wb_s[lanes, :])
    ff = None
    dx = None
    for s in range(SLABS):
        lanes = slice(s * D, (s + 1) * D)
        pre = pre_s[s]
        square = pre * pre
        up = 0.5 + 0.5 * jnp.tanh(pre * (GELU_C + (GELU_C * 0.044715) * square))
        r = pre * up
        r_s[:, lanes] = r.astype(BF)
        slope = up + r * (1.0 - up) * (2.0 * GELU_C + (6.0 * GELU_C * 0.044715) * square)
        dpre_s[:, lanes] = (dr_s[s] * slope).astype(BF)
    for s in range(SLABS):
        lanes = slice(s * D, (s + 1) * D)
        t1 = dot(r_s[:, lanes], wb_s[lanes, :])
        t2 = ndot(dpre_s[:, lanes], wi_s[s])
        ff = t1 if ff is None else ff + t1
        dx = t2 if dx is None else dx + t2
    ff = ff + bb[...]
    x1 = x1_s[...]
    out = (x1 + alpha_ffn * ff).astype(BF)
    out_near[...] = out[:BLOCK]
    out_far[...] = out[BLOCK:]
    dy = jnp.concatenate([cot_a[...], cot_b[...]], axis=0).astype(F32)
    dx = dx + dy
    dx1[0] = dx[:BLOCK]
    dx1[1] = dx[BLOCK:]
    dattn = (alpha_attn * dx).astype(BF)
    dattn_s[...] = dattn
    d_mine[...] = ndot(dattn, wo_s[pl.ds(pl.multiple_of(c * HALF, HALF), HALF), :]).astype(BF)
    give[:both, :] = ndot(dattn, wo_s[pl.ds(pl.multiple_of((1 - c) * HALF, HALF), HALF), :]).astype(BF)
    ga[...] = jnp.concatenate(
        [jnp.sum(dx * attn_s[...], axis=0, keepdims=True), jnp.sum(dy * ff, axis=0, keepdims=True)], axis=0
    )
    gb_o[...] = jnp.sum(dattn_s[...].astype(F32), axis=0, keepdims=True)
    gb_b[...] = jnp.sum(dff_s[...].astype(F32), axis=0, keepdims=True)
    for s in range(SLABS):
        lanes = slice(s * D, (s + 1) * D)
        gb_i[:, lanes] = jnp.sum(dpre_s[:, lanes].astype(F32), axis=0, keepdims=True)
    both_t = jnp.concatenate([mixed[0], mixed[1]], axis=1).T
    ht = h_s[...].T
    per = count // SLABS

    def columns(ref, first, core):
        return ref[:, pl.ds(pl.multiple_of(first + core * HALF, HALF), HALF)]

    def put_rows(core, first, value, groups):
        size = value.shape[0] // len(groups)
        for i, group in enumerate(groups):
            part = value[i * size : (i + 1) * size]
            if core == 0:
                g_keep[group, first : first + size, :] = part
            else:
                row = 2 * BLOCK + group * 9 * rd + first
                give[row : row + size, :] = part

    for core, which in enumerate((c, 1 - c)):
        put_rows(core, 8 * rd, dot(both_t, columns(dattn_s, 0, which)).astype(BF), range(count))
    for s in range(SLABS):
        lanes = slice(s * D, (s + 1) * D)
        rt = r_s[:, lanes].T
        for core, which in enumerate((c, 1 - c)):
            put_rows(core, (4 + s) * rd, dot(ht, columns(dpre_s, s * D, which)).astype(BF), range(count))
            put_rows(core, 0, dot(rt, columns(dff_s, 0, which)).astype(BF), range(s * per, (s + 1) * per))


def back_blocks(blocks, kn, vn, kt, q_in, d_in, ot, lse, dk_s, dv_s, dq_out, scratch):
    qz, qzt, oz, ozt, dq_s, p_s, dp_s = scratch
    rows = lax.broadcasted_iota(jnp.int32, (HALF, BLOCK), 0) // HEAD_DIM
    lanes = lax.broadcasted_iota(jnp.int32, (BLOCK, HALF), 1) // HEAD_DIM
    def one(i, gq):
        block = jnp.where(i == 0, blocks[0], blocks[1])
        q = q_in[i].astype(F32)
        d_o = d_in[pl.ds(pl.multiple_of(i * BLOCK, BLOCK), BLOCK), :].astype(F32)
        qt, dot_ = q.T, d_o.T
        product = dot_ * ot[i]
        deltas = []
        for h in range(CORE_HEADS):
            head = slice(h * HEAD_DIM, (h + 1) * HEAD_DIM)
            deltas.append(jnp.sum(product[head], axis=0, keepdims=True))
            qz[h] = jnp.where(lanes == h, q, 0.0).astype(BF)
            oz[h] = jnp.where(lanes == h, d_o, 0.0).astype(BF)
            qzt[h] = jnp.where(rows == h, qt, 0.0).astype(BF)
            ozt[h] = jnp.where(rows == h, dot_, 0.0).astype(BF)
        dq_s[...] = jnp.zeros_like(dq_s)

        def chunk(first, count):
            size = count * BLOCK
            keys = kn[pl.ds(first, count)].reshape(size, HALF)
            values = vn[pl.ds(first, count)].reshape(size, HALF)
            for h in range(CORE_HEADS):
                p_s[h, :size] = dot(keys, qzt[h])
                dp_s[h, :size] = dot(values, ozt[h])
            dk = dk_s[pl.ds(first, count)].reshape(size, HALF)
            dv = dv_s[pl.ds(first, count)].reshape(size, HALF)
            for h in range(CORE_HEADS):
                head = slice(h * HEAD_DIM, (h + 1) * HEAD_DIM)
                p = jnp.exp(p_s[h, :size] - lse[i, h : h + 1, :])
                ds = (p * (dp_s[h, :size] - deltas[h])).astype(BF)
                dv = dv + dot(p.astype(BF), oz[h])
                dk = dk + dot(ds, qz[h])
                dq = dq_s[head, :]
                for j in range(count):
                    dq = dq + dot(kt[first + j, head, :], ds[j * BLOCK : (j + 1) * BLOCK])
                dq_s[head, :] = dq
            dk_s[pl.ds(first, count)] = dk.reshape(count, BLOCK, HALF)
            dv_s[pl.ds(first, count)] = dv.reshape(count, BLOCK, HALF)

        over_keys(block, chunk)
        dq = (dq_s[...] * (1.0 / math.sqrt(HEAD_DIM))).T.astype(BF)
        dq_out[i] = dq
        return gq + jnp.sum(dq.astype(F32), axis=0, keepdims=True)

    return lax.fori_loop(0, 2, one, jnp.zeros((1, HALF), F32))


def back_kernel(nz, which, ids, ins, outs, *scratch):
    kn, vn, kt, qn, ot, lse, d_o = ins[:7]
    dk, dv, dq, gq = outs
    if which == 0:
        dk[...] = jnp.zeros_like(dk)
        dv[...] = jnp.zeros_like(dv)
    blocks = query_blocks(ids[0], ids[1], nz)[2 * which : 2 * which + 2]
    gq[...] = back_blocks(blocks, kn, vn, kt, qn, d_o, ot, lse, dk, dv, dq, scratch)


def dx_kernel(nz, which, ids, ins, outs, dxs):
    wq, dk, dv, dq_mine, dq_other, dx1 = ins
    keep, send, dkv = outs
    z, c = ids[0], ids[1]
    half = nz // 2
    place = lax.rem(z, half)
    w_q = wq[:, :, :HALF].reshape(D, HALF)
    w_kv = wq[:, :, HALF : 3 * HALF].reshape(D, 2 * HALF)
    for core, (target, dq) in enumerate(((keep, dq_mine), (send, dq_other))):
        for p in range(half):
            chip = ids[4] * half + p
            block = 2 * (chip if which == 0 else nz - 1 - chip) + (c if core == 0 else 1 - c)
            dkv[core * half + p, :, :HALF] = dk[block].astype(BF)
            dkv[core * half + p, :, HALF:] = dv[block].astype(BF)
        rows = dkv[core * half : (core + 1) * half].reshape(half * BLOCK, 2 * HALF)
        dxs[core] = ndot(rows, w_kv).reshape(half, BLOCK, D)
        value = ndot(dq[which], w_q)
        if core == 0:
            value = value + dx1[which]
        dxs[core, place] = dxs[core, place] + value
        target[...] = dxs[core].astype(BF)


def dw_kernel(nz, rs, rr, ids, ins, outs, spread):
    xall, dkv_near, dkv_far, dq_mine, dq_other, gq_mine, gq_other, gb_o, gb_i, gb_b, ga = ins
    (dw,) = outs
    z, c = ids[0], ids[1]
    half = nz // 2
    rows = []
    for which in range(2):
        for core in range(2):
            for p in range(half):
                chip = ids[4] * half + p
                rows.append(xall[2 * (chip if which == 0 else nz - 1 - chip) + (c if core == 0 else 1 - c)])
    dkv = jnp.concatenate([ref[...].reshape(nz * BLOCK, 2 * HALF) for ref in (dkv_near, dkv_far)], axis=0)
    acc_kv = dot(jnp.concatenate(rows, axis=0).T, dkv)
    gv = jnp.zeros((1, HALF), F32)
    for ref in (dkv_near, dkv_far):
        for i in range(nz):
            gv = gv + jnp.sum(ref[i, :, HALF:].astype(F32), axis=0, keepdims=True)
    queries = jnp.concatenate([xall[block] for block in query_blocks(z, c, nz)], axis=0).T
    dq = jnp.concatenate([dq_mine[...].reshape(2 * BLOCK, HALF), dq_other[...].reshape(2 * BLOCK, HALF)], axis=0)
    acc_q = dot(queries, dq)
    gq = gq_mine[...] + gq_other[...]
    nothing = jnp.zeros((1, HALF), F32)
    own = [jnp.concatenate([jnp.where(c == 0, g, nothing), jnp.where(c == 0, nothing, g)], axis=1) for g in (gq, gv)]
    tile = jnp.concatenate(own + [gb_o[...], gb_b[...], jnp.zeros((124, D), F32)], axis=0).T
    spread[...] = jnp.broadcast_to(gb_i[...], (128, FF)).T.reshape(D // rr, SLABS, rr, 128)
    lanes = lax.broadcasted_iota(jnp.int32, (D // rr, rr, 128), 2)
    tile = tile.reshape(D // rr, rr, 128)
    for s in range(SLABS):
        tile = jnp.where(lanes == 4 + s, spread[:, s], tile)
    tile = tile.reshape(D, 128)
    if rs >= 16:
        me = ids[2]
        lane = lax.broadcasted_iota(jnp.int32, (D, 128), 1) - 8 - 6 * (me // rs)
        mine = lax.rem(lax.broadcasted_iota(jnp.int32, (D, 128), 0), rs) == lax.rem(me, rs)
        gates = jnp.sum(ga[...], axis=1, keepdims=True)
        for which in range(2):
            rest = gates[which : which + 1]
            for i in range(3):
                high = rest.astype(BF).astype(F32)
                tile = jnp.where(mine & (lane == 2 * i + which), high, tile)
                rest = rest - high
    rows = dw.shape[1]
    dw[:, :, :HALF] = acc_q.astype(BF).reshape(D // rows, rows, HALF)
    dw[:, :, HALF : 3 * HALF] = acc_kv.astype(BF).reshape(D // rows, rows, 2 * HALF)
    dw[:, :, 3 * HALF :] = tile.astype(BF).reshape(D // rows, rows, 128)


def sum_kernel(plans, ids, ins, outs):
    outs = list(outs)
    for numbers, size, where, pre, post, stride, first, flat in plans:

        def total(static, dynamic):
            source = static * stride // size
            index = (static + dynamic) * stride + first - source * size
            refs = [ins[number] for number in numbers[source]]
            value = refs[0][index]
            if len(refs) == 2 and flat is None:
                value = value.astype(F32) + refs[1][index].astype(F32)
            elif len(refs) == 2:
                rows = value.shape[0]
                start = pl.multiple_of(flat + index * rows, 16)
                value = value.astype(F32) + refs[1][pl.ds(start, rows), :].astype(F32)
            return value

        if where is None:
            out = outs.pop(0)
            for index in range(out.shape[0]):
                out[index] = total(index, 0).astype(out.dtype)
            continue
        keep, send = outs.pop(0), outs.pop(0)
        mine = my_bit(ids, where)
        for p in range(pre):
            for q in range(post):
                keep[p * post + q] = total(2 * p * post + q, mine * post).astype(keep.dtype)
                send[p * post + q] = total(2 * p * post + q, (1 - mine) * post).astype(send.dtype)


def grads_kernel(rs, ids, ins, outs):
    own, other = ins
    w_back, w_in, w_out = outs
    for ref, core in ((own, ids[1]), (other, 1 - ids[1])):

        def lanes(first):
            return pl.ds(pl.multiple_of(first + core * HALF, HALF), HALF)

        value = ref[0].astype(F32)
        w_back[:, lanes(0)] = value[: 4 * rs]
        for s in range(SLABS):
            w_in[:, lanes(s * D)] = value[(4 + s) * rs : (5 + s) * rs]
        w_out[:, lanes(0)] = value[8 * rs :]


def last_kernel(rs, ids, ins, outs):
    own, other = ins
    w_qkv, gb_qv, gb_o, gb_i, gb_b, gates = outs
    for ref, core in ((own, ids[1]), (other, 1 - ids[1])):
        value = ref[0].astype(F32)
        for i in range(3):
            lanes = pl.ds(pl.multiple_of(i * D + core * HALF, HALF), HALF)
            w_qkv[:, lanes] = value[:, i * HALF : (i + 1) * HALF]
    sums = own[0, :, 3 * HALF :] + other[0, :, 3 * HALF :].astype(F32)
    lane = lax.broadcasted_iota(jnp.int32, (1, 128), 1)
    column = jnp.sum(sums, axis=0, keepdims=True)
    for which in range(2):
        used = (lane >= 8) & (lax.rem(lane, 2) == which)
        gates[:, which : which + 1] = jnp.sum(jnp.where(used, column, 0.0), axis=1, keepdims=True)
    by_row = jnp.concatenate([sums, jnp.zeros((128 - rs, 128), F32)], axis=0).T
    gb_qv[...] = by_row[:2, :rs]
    gb_o[...] = by_row[2:3, :rs]
    gb_b[...] = by_row[3:4, :rs]
    for s in range(SLABS):
        gb_i[:, s * rs : (s + 1) * rs] = by_row[4 + s : 5 + s, :rs]


def shape(dims, kind):
    return jax.ShapeDtypeStruct(dims, kind)


def vmem(dims, kind):
    return pltpu.VMEM(dims, kind)


def in_hbm(array):
    return pltpu.with_memory_space_constraint(array, pltpu.HBM)


def cost(megabytes):
    return pl.CostEstimate(flops=0, bytes_accessed=megabytes * 2**20, transcendentals=0)


def call(
    name, kernel, ids, ins, outs, after=(), scratch=(), limit=12, weight=0, where=None, aliases=None, out=VMEM
):
    count, waits = len(ins), len(after)

    def run(*refs):
        given, rest = refs[:count], refs[count + waits :]
        kernel(ids(), given, rest[: len(outs)], *rest[len(outs) :])

    return pl.pallas_call(
        run,
        out_shape=tuple(outs),
        in_specs=(where or [VMEM] * count) + [ANY] * waits,
        out_specs=out if isinstance(out, tuple) else (out,) * len(outs),
        scratch_shapes=list(scratch),
        compiler_params=pltpu.CompilerParams(vmem_limit_bytes=limit * 2**20),
        cost_estimate=cost(weight),
        input_output_aliases=aliases or {},
        name=name,
    )(*ins, *after)


def pack_call(ids, rs, ins):
    return call(
        "pack",
        functools.partial(pack_kernel, rs),
        ids,
        [in_hbm(array) for array in ins],
        [vmem((rs, WQ), BF), vmem((9 * rs, HALF), BF), vmem((13 * rs, HALF), BF)] + [vmem((BLOCK, D), BF)] * 4
        + [vmem((8, 128), F32)],
        scratch=[pltpu.VMEM(array.shape, BF) for array in ins[:8]]
        + [pltpu.VMEM((1, 2), F32), pltpu.VMEM((128, 128), F32), pltpu.SemaphoreType.DMA((13,))],
        where=[ANY] * 11,
    )


def join_call(name, ids, jobs, after=(), extra=None, extra_ins=(), extra_outs=(), cuts=None):
    ins, outs, spans = [], [], []
    for (own, got, _, _), cut in zip(jobs, cuts or [1] * len(jobs)):
        ins += [own, got]
        spans.append(slice(len(outs), len(outs) + cut))
        outs += [vmem((2 * own.shape[0] // cut,) + own.shape[1:], own.dtype)] * cut
    number = len(outs)

    def kernel(ids_ref, given, results):
        for i, (_, _, where, post) in enumerate(jobs):
            join(ids_ref, given[2 * i], given[2 * i + 1], results[spans[i]], where, post)
        if extra is not None:
            extra(ids_ref, given[2 * len(jobs) :], results[number:])

    return call(name, kernel, ids, ins + list(extra_ins), outs + list(extra_outs), after)


def sum_call(name, ids, jobs, after=(), last=BF, flat=None):
    ins, outs, plans = [], [], []

    def number(array):
        for i, other in enumerate(ins):
            if other is array:
                return i
        ins.append(array)
        return len(ins) - 1

    for sources, where, pre, post, stride, first in jobs:
        numbers = [tuple(number(array) for array in pair if array is not None) for pair in sources]
        tail = sources[0][0].shape[1:]
        size = sources[0][0].shape[0]
        plans.append((numbers, size, where, pre, post, stride, first, flat))
        if where is None:
            outs.append(vmem((size * len(sources) // stride,) + tail, last))
        else:
            outs += [vmem((pre * post,) + tail, last), vmem((pre * post,) + tail, BF)]
    return call(name, functools.partial(sum_kernel, plans), ids, ins, outs, after)


def make_body(n1, n2, nz):
    ndp = n1 * n2
    nsh = ndp * nz * 2
    rs = D // nsh
    rd = D // ndp
    half = nz // 2
    parts = 2 * nz if rs % 16 == 0 else 1
    rr = rd // parts
    nh = 9 * rd // 2
    swap = [(0, 1), (1, 0)]
    bits_a, bits_b, bits_z = (count.bit_length() - 1 for count in (n1, n2, nz))
    counts = {"a": n1, "b": n2, "z": nz}
    slot = {"a": 3, "b": 5, "z": 0}

    def to_mirror(array):
        return lax.ppermute(array, "z", [(s, nz - 1 - s) for s in range(nz)])

    def exchange(array, name, bit):
        return lax.ppermute(array, name, [(s, s ^ (1 << bit)) for s in range(counts[name])])

    def to_other(array):
        return lax.ppermute(array, "c", swap)

    def body(inputs, w_qkv, bias_qv, w_out, bias_out, w_in, bias_in, w_back, bias_back, alphas, cotangent):
        z, c = lax.axis_index("z"), lax.axis_index("c")
        a, b = lax.axis_index("a"), lax.axis_index("b")

        def ids():
            z, c = lax.axis_index("z"), lax.axis_index("c")
            a, b = lax.axis_index("a"), lax.axis_index("b")
            return (z, c, ((a * n2 + b) * nz + z) * 2 + c, a, z // half, b)


        latest = []

        def hand_on(ids_ref, given, results):
            for source, target in zip(given, results):
                target[...] = source[...]

        def step(name, jobs, extra=(), cuts=None, others=()):
            result = join_call(
                name, ids, jobs, latest + list(others), hand_on, extra, [vmem(e.shape, e.dtype) for e in extra], cuts
            )
            latest[:] = [result[0]]
            return result


        q_keep, f_keep, give, x_give, x_keep, cot_give, cot_a, gates = pack_call(
            ids, rs,
            [w_qkv, w_back, w_in, w_out, bias_qv, bias_out[None], bias_back[None], bias_in[None], inputs, cotangent,
             alphas[None]],
        )
        wq, wf = call(
            "core", functools.partial(core_kernel, rs), ids, [q_keep, f_keep, to_other(give)],
            [vmem((2, rs, WQ), BF), vmem((2, 9 * rs, HALF), BF)],
        )
        latest[:] = [wq]
        wq, wf = wq.reshape(1, 2 * rs, WQ), wf.reshape(1, 2 * 9 * rs, HALF)
        wf = wf.reshape(2 * 9 * rs, HALF)
        q_got = exchange(wq, "z", bits_z - 1)
        wf_parts = [(wf, 0)]
        for i in reversed(range(bits_z)):
            wf_parts += [(exchange(part, "z", i), place | (1 << i)) for part, place in wf_parts]
        wf_near = [part for part, place in wf_parts if place == 1]
        for i in reversed(range(1, bits_z)):
            (wq,) = step("q_z", [(wq, q_got, (0, i), 1)])
            q_got = exchange(wq, "z", i - 1)
        wq, x_keep, x_give = step(
            "q_z", [(wq, q_got, (0, 0), 1)], [x_keep, x_give], others=wf_near + [wf_parts[1][0]]
        )
        wq = wq.reshape(rd, WQ)
        if parts == 1:
            hidden_bias = wq[:, 3 * HALF + 4 : 3 * HALF + 8].reshape(2 * nz, rs, SLABS)
            hidden_bias = jnp.transpose(hidden_bias, (0, 2, 1)).reshape(SLABS, rd).T
            wq = jnp.concatenate([wq[:, : 3 * HALF + 4], hidden_bias, wq[:, 3 * HALF + 8 :]], axis=1)
        wq = wq[None]
        x_far = to_mirror(x_give)
        for i in reversed(range(1, bits_b)):
            q_got = exchange(wq, "b", i)
            (wq,) = step("q_b", [(wq, q_got, (5, i), 1)])
        q_got = exchange(wq, "b", 0)
        own = x_keep[None]
        own_got = exchange(own, "z", max(bits_z - 2, 0))

        def in_place(ids_ref, given, results):
            for group in range(2):

                @pl.when(ids_ref[4] == group)
                def _():
                    for ref, (_, place) in zip(given, wf_parts):
                        at = lax.rem(lax.bitwise_xor(ids_ref[0], place), half)
                        results[group ^ (place // half)][at] = ref[...]

        halves = vmem((half, 2 * 9 * rs, HALF), BF)
        first, second = call("f_z", in_place, ids, [part for part, _ in wf_parts], [halves, halves], latest)
        latest[:] = [first]
        if parts == 1:
            wf = jnp.concatenate([first, second], axis=0).reshape(nz, 2, 9 * rs, HALF)
            wf = jnp.concatenate(
                [wf[:, :, : 4 * rs].reshape(4 * rd, HALF)]
                + [wf[:, :, (4 + s) * rs : (5 + s) * rs].reshape(rd, HALF) for s in range(SLABS)]
                + [wf[:, :, 8 * rs :].reshape(rd, HALF)],
                axis=0,
            )
            first, second = wf[:nh], wf[nh:]
        first, second = first.reshape(1, nh, HALF), second.reshape(1, nh, HALF)
        (wq,) = step("q_b", [(wq, q_got, (5, 0), 1)])
        for i in reversed(range(1, bits_a)):
            q_got = exchange(wq, "a", i)
            (wq,) = step("q_a", [(wq, q_got, (3, i), n2)])
        wq_pieces = [wq, exchange(wq, "a", 0)]

        far_rows, cot_give = call(
            "x_far", hand_on, ids, [x_far, cot_give], [vmem((BLOCK, D), BF)] * 2, latest + [own_got]
        )
        latest[:] = [far_rows]
        cot_b = to_mirror(cot_give)
        far_rows = far_rows[None]
        for i in reversed(range(1, bits_z - 1)):
            far_got = exchange(far_rows, "z", i)
            own, far_rows = step("x_z", [(own, own_got, (0, i), 1), (far_rows, far_got, (0, i), 1)])
            own_got = exchange(own, "z", i - 1)
        far_got = exchange(far_rows, "z", 0)

        for i in reversed(range(bits_b)):
            got = exchange(first, "b", i), exchange(second, "a", i)
            first, second = step("f_dp", [(first, got[0], (5, i), 1), (second, got[1], (3, i), 1)])
        for i in reversed(range(1, bits_a)):
            got = exchange(first, "a", i), exchange(second, "b", i)
            first, second = step("f_dp", [(first, got[0], (3, i), n2), (second, got[1], (5, i), 1)])
        wf_pieces = [first, second, exchange(first, "a", 0), exchange(second, "b", 0)]

        def rows_of_all(ids_ref, given, results):
            own_ref, own_got_ref, far_ref, far_got_ref = given
            base, mine = ids_ref[4] * half, my_bit(ids_ref, (0, 0))
            for p in range(half // 2):
                for own_part, far_part, at in (
                    (own_ref, far_ref, base + 2 * p + mine),
                    (own_got_ref, far_got_ref, base + 2 * p + 1 - mine),
                ):
                    results[0][at - base] = own_part[p]
                    results[1][at - base] = far_part[p]

        xo = call(
            "x_all", rows_of_all, ids, [own, own_got, far_rows, far_got], [vmem((half, BLOCK, D), BF)] * 2,
            latest + [wq_pieces[1], cot_b],
        )
        latest[:] = [xo[0]]
        xs = [to_other(part) for part in xo]

        nb = 2 * nz
        heads_t = pltpu.VMEM((CORE_HEADS, HALF, BLOCK), BF)
        scores = pltpu.VMEM((CORE_HEADS, 4 * BLOCK, BLOCK), F32)
        scratch = [
            heads_t,
            scores,
            pltpu.VMEM((CORE_HEADS, 1, BLOCK), F32),
            pltpu.VMEM((CORE_HEADS, 1, BLOCK), F32),
            pltpu.VMEM((HALF, BLOCK), F32),
        ]
        natural, turned = (nb, BLOCK, HALF), (nb, HALF, BLOCK)
        two, two_t = (2, BLOCK, HALF), (2, HALF, BLOCK)
        two_lse = (2, CORE_HEADS, BLOCK)
        spread = pltpu.VMEM((D // rr, SLABS, rr, 128), F32)
        (xall, wq, kn, vn, kt, vt, q_mine, q_other, ot_other, lse_other, o_send, bo, bb, bi) = call(
            "first",
            functools.partial(first_kernel, nz, ndp, n2, rr),
            ids,
            [*xo, *xs, *wq_pieces],
            [
                vmem((nb, BLOCK, D), BF),
                vmem((ndp, rd, WQ), BF),
                vmem(natural, BF),
                vmem(natural, BF),
                vmem(turned, BF),
                vmem(turned, BF),
                vmem(two, BF),
                vmem(two, BF),
                vmem(two_t, F32),
                vmem(two_lse, F32),
                vmem(two, BF),
                vmem((1, D), F32),
                vmem((1, D), F32),
                vmem((1, FF), F32),
            ],
            latest,
            [spread] + scratch,
            limit=24,
        )

        def give_kernel(ids_ref, given, results):
            row = 0
            for part in given:
                for i in range(part.shape[0]):
                    results[0][row : row + part.shape[1]] = part[i]
                    row += part.shape[1]

        (give,) = call(
            "give", give_kernel, ids, [o_send, *wf_pieces], [vmem((2 * BLOCK + 2 * ndp * nh, HALF), BF)],
            limit=24,
        )
        ffn_got = to_other(give)
        ot_mine, lse_mine, o_mine = call(
            "second",
            functools.partial(second_kernel, nz),
            ids,
            [kn, vt, q_mine],
            [vmem(two_t, F32), vmem(two_lse, F32), vmem(two, BF)],
            (),
            scratch,
            limit=24,
        )

        grouped = (ndp * parts, 9 * rd // parts, HALF)
        (out_near, out_far, dx1, d_mine, g_keep, give, gb_o, gb_i, gb_b, ga) = call(
            "ffn",
            functools.partial(ffn_kernel, nz, ndp, n2, parts),
            ids,
            [gates, o_mine, ffn_got, xall, cot_a, cot_b, bo, bi, bb, *wf_pieces],
            [
                vmem((BLOCK, D), BF),
                vmem((BLOCK, D), BF),
                vmem((2, BLOCK, D), F32),
                vmem((2 * BLOCK, HALF), BF),
                vmem(grouped, BF),
                vmem((2 * BLOCK + ndp * 9 * rd, HALF), BF),
                vmem((1, D), F32),
                vmem((1, FF), F32),
                vmem((1, D), F32),
                vmem((2, D), F32),
            ],
            scratch=[
                pltpu.VMEM((2, 2 * ndp, nh, HALF) if parts == 1 else (8, 128), BF),
                pltpu.VMEM((D, D), BF),
                pltpu.VMEM((SLABS, D, D), BF),
                pltpu.VMEM((FF, D), BF),
                pltpu.VMEM((2, 2 * BLOCK, HALF), BF),
                pltpu.VMEM((2 * BLOCK, D), BF),
                pltpu.VMEM((2 * BLOCK, FF), BF),
                pltpu.VMEM((2 * BLOCK, FF), BF),
                pltpu.VMEM((2 * BLOCK, D), BF),
                pltpu.VMEM((2 * BLOCK, D), BF),
                pltpu.VMEM((SLABS, 2 * BLOCK, D), F32),
                pltpu.VMEM((SLABS, 2 * BLOCK, D), F32),
                pltpu.VMEM((2 * BLOCK, D), F32),
                pltpu.VMEM((2 * BLOCK, D), F32),
            ],
            limit=36,
        )
        back_got = to_other(give)
        back_scratch = [
            pltpu.VMEM((CORE_HEADS, BLOCK, HALF), BF),
            heads_t,
            pltpu.VMEM((CORE_HEADS, BLOCK, HALF), BF),
            heads_t,
            pltpu.VMEM((HALF, BLOCK), F32),
            scores,
            scores,
        ]
        back_out = [vmem(natural, F32), vmem(natural, F32), vmem(two, BF), vmem((1, HALF), F32)]
        dk, dv, dq_mine, gq_mine = call(
            "back_first",
            functools.partial(back_kernel, nz, 0),
            ids,
            [kn, vn, kt, q_mine, ot_mine, lse_mine, d_mine],
            back_out,
            scratch=back_scratch,
            limit=24,
        )

        latest[:] = [gq_mine]
        done = {}

        def along(axis, count, pre, post):
            return [(axis, i, pre * (count >> (i + 1)), post) for i in range(count.bit_length() - 1)]

        def dp_scatter(name, kept, got, rows, columns, flat=None):
            axes = (along("b", n2, n1, 1) + along("a", n1, 1, 1), along("a", n1, 1, n2) + along("b", n2, 1, 1))
            whole = (kept.reshape(2 * ndp, rows, columns), got)
            state = [(whole, 2, 0), (whole, 2, 1)]
            for i in range(len(axes[0])):
                result = sum_call(
                    name,
                    ids,
                    [
                        ([pair], (slot[axis], bit), pre, post, stride, first)
                        for (pair, stride, first), (axis, bit, pre, post) in zip(state, (axes[0][i], axes[1][i]))
                    ],
                    latest,
                    flat=flat if i == 0 else None,
                )
                latest[:] = [result[0]]
                state = [
                    ((result[2 * j], exchange(result[2 * j + 1], axes[j][i][0], axes[j][i][1])), 1, 0)
                    for j in range(2)
                ]
                yield
            return [pair for pair, _, _ in state]

        def z_scatter(name, sources):
            for _, i, pre, _ in along("z", nz, 1, 1):
                kept, send = sum_call(name, ids, [(sources, (slot["z"], i), pre, 1, 1, 0)], latest)
                latest[:] = [kept]
                sources = [(kept, exchange(send, "z", i))]
                yield
            rows, columns = kept.shape[1] // 2, kept.shape[2]
            sources = [tuple(array.reshape(2, rows, columns) for array in sources[0])]
            keep, send = sum_call(name, ids, [(sources, (1, 0), 1, 1, 1, 0)], latest, F32)
            latest[:] = [keep]
            return keep, to_other(send)

        def whole_dp(name, sources):
            return [part[0] for part in sum_call(name, ids, [([pair], None, 0, 0, 1, 0) for pair in sources], latest)]

        def g_chain():
            sources = yield from dp_scatter("g_dp", g_keep, back_got, nh, HALF, 2 * BLOCK)
            if parts == 1:
                g_dp = jnp.concatenate(whole_dp("g_dp", sources), axis=0)
                g_dp = jnp.concatenate(
                    [g_dp[: 4 * rd].reshape(nz, 2, 4 * rs, HALF)]
                    + [g_dp[(4 + s) * rd : (5 + s) * rd].reshape(nz, 2, rs, HALF) for s in range(SLABS)]
                    + [g_dp[8 * rd :].reshape(nz, 2, rs, HALF)],
                    axis=2,
                )
                sources = [(g_dp.reshape(nz, 2 * 9 * rs, HALF), None)]
            else:
                sources = [tuple(array.reshape(half, 2 * 9 * rs, HALF) for array in pair) for pair in sources]
            keep, got = yield from z_scatter("g_z", sources)
            yield
            done["g"] = call(
                "g_last", functools.partial(grads_kernel, rs), ids, [keep, got],
                [pltpu.HBM((4 * rs, D), F32), pltpu.HBM((rs, FF), F32), pltpu.HBM((rs, D), F32)], latest,
            )

        g_steps = g_chain()
        next(g_steps)
        dk, dv, dq_other, gq_other = call(
            "back_second",
            functools.partial(back_kernel, nz, 1),
            ids,
            [kn, vn, kt, q_other, ot_other, lse_other, back_got, dk, dv],
            back_out,
            latest,
            back_scratch,
            limit=24,
            aliases={7: 0, 8: 1},
        )
        def out_kernel(ids_ref, given, results, sems):
            group = ids_ref[4]
            copies = moves(sems, [(given[0], results[0].at[group]), (given[1], results[0].at[1 - group])])
            results[1][...] = jnp.zeros_like(results[1])
            wait(copies)

        def to_rows(name, own, got):
            rows, token = call(
                name, out_kernel, ids, [own, got], [pltpu.HBM((2, BLOCK, D), BF), vmem((8, 128), F32)], latest,
                [pltpu.SemaphoreType.DMA((2,))], where=[ANY, ANY],
                out=(pl.BlockSpec(memory_space=pltpu.HBM), VMEM),
            )
            latest[:] = [token]
            return rows

        latest[:] = [gq_other]
        out_b = to_mirror(out_far)
        latest.append(out_b)

        def dx_call(which):
            keep, send, dkv = call(
                "dx",
                functools.partial(dx_kernel, nz, which),
                ids,
                [wq, dk, dv, dq_mine, dq_other, dx1],
                [vmem((half, BLOCK, D), BF), vmem((half, BLOCK, D), BF), vmem((nz, BLOCK, 2 * HALF), BF)],
                latest,
                [pltpu.VMEM((2, half, BLOCK, D), F32)],
            )
            latest[:] = [keep]
            return (keep, to_other(send)), dkv

        def dx_chain(pair, far):
            for i in range(bits_z - 1):
                kept, send = sum_call("dx_z", ids, [([pair], (0, i), half >> (i + 1), 1, 1, 0)], latest)
                latest[:] = [kept]
                pair = (kept, exchange(send, "z", i))
                yield
            (rows,) = sum_call("dx_z", ids, [([pair], None, 0, 0, 1, 0)], latest)
            latest[:] = [rows]
            rows = rows.reshape(BLOCK, D)
            done["far" if far else "near"] = to_mirror(rows) if far else rows

        far_pair, dkv_far = dx_call(1)
        near_pair, dkv_near = dx_call(0)
        far_steps, near_steps = dx_chain(far_pair, True), dx_chain(near_pair, False)
        next(far_steps)
        next(g_steps)
        next(near_steps)
        (dw,) = call(
            "dw",
            functools.partial(dw_kernel, nz, rs, rr),
            ids,
            [xall, dkv_near, dkv_far, dq_mine, dq_other, gq_mine, gq_other, gb_o, gb_i, gb_b, ga],
            [vmem((2 * ndp, rd // 2, WQ), BF)],
            latest,
            [spread],
            limit=20,
        )
        latest[:] = [dw]

        def dw_chain():
            sources = yield from dp_scatter("w_dp", dw, None, rd // 2, WQ)
            if parts == 1:
                dw_dp = jnp.concatenate(whole_dp("w_dp", sources), axis=0)
                hidden_bias = dw_dp[:, 3 * HALF + 4 : 3 * HALF + 8].T.reshape(2 * nz, SLABS, rs)
                hidden_bias = jnp.transpose(hidden_bias, (0, 2, 1)).reshape(rd, SLABS)
                dw_dp = jnp.concatenate([dw_dp[:, : 3 * HALF + 4], hidden_bias, dw_dp[:, 3 * HALF + 8 :]], axis=1)
                sources = [(dw_dp.reshape(nz, 2 * rs, WQ), None)]
            else:
                sources = [tuple(array.reshape(half, 2 * rs, WQ) for array in pair) for pair in sources]
            keep, got = yield from z_scatter("w_z", sources)
            yield
            done["w"] = call(
                "w_last", functools.partial(last_kernel, rs), ids, [keep, got],
                [shape((rs, 3 * D), F32), shape((2, rs), F32), shape((1, rs), F32), shape((1, SLABS * rs), F32)]
                + [shape((1, rs), F32), shape((1, 2), F32)],
                latest,
            )
            latest[:] = [done["w"][0]]

        steps = {"f": far_steps, "n": near_steps, "g": g_steps, "w": dw_chain()}
        for name in "fgwnowgwxwgwgw" + "fn" * bits_z + "x" + "gw" * (2 * bits_z):
            if name == "o":
                outputs = to_rows("outputs", out_near, out_b)
            elif name == "x":
                if "inputs" not in done:
                    for chain in (far_steps, near_steps):
                        while next(chain, 0) is None:
                            pass
                    done["inputs"] = to_rows("dx_last", done["near"], done["far"])
            else:
                next(steps[name], 0)
        gb_qv, gb_out, gb_in, gb_back, grad_alphas = done["w"][1:]
        if rs < 16:
            grad_alphas = lax.psum(jnp.sum(ga, axis=1), MESH_AXES)
        return (
            outputs,
            done["inputs"],
            done["w"][0],
            gb_qv,
            done["g"][2],
            gb_out.reshape(rs),
            done["g"][1],
            gb_in.reshape(SLABS * rs),
            done["g"][0],
            gb_back.reshape(rs),
            grad_alphas.reshape(2),
        )

    return body


def solution(mesh):
    ndp, nseq = mesh.devices.shape
    n1 = math.isqrt(ndp)
    n2 = ndp // n1
    nz = nseq // 2
    fine = Mesh(mesh.devices.reshape(n1, n2, nz, 2), MESH_AXES)
    dp, seq = ("a", "b"), ("z", "c")
    rows = P(dp, seq, None)
    both = dp + seq
    return jax.shard_map(
        make_body(n1, n2, nz),
        mesh=fine,
        in_specs=(
            rows,
            P(both, None),
            P(None, both),
            P(both, None),
            P(both),
            P(both, None),
            P(both),
            P(both, None),
            P(both),
            P(),
            rows,
        ),
        out_specs=(
            rows,
            rows,
            P(both, None),
            P(None, both),
            P(both, None),
            P(both),
            P(both, None),
            P(both),
            P(both, None),
            P(both),
            P(),
        ),
        check_vma=False,
    )
```

```python
import functools
import math

import jax
import jax.numpy as jnp
from jax import lax
from jax.experimental import pallas as pl
from jax.experimental.pallas import tpu as pltpu
from jax.sharding import Mesh, PartitionSpec as P

D = 512
HEADS = 8
HEAD_DIM = 64
FF = 2048
BLOCK = 256
HALF = D // 2
CORE_HEADS = HEADS // 2
SLABS = FF // D
BF = jnp.bfloat16
F32 = jnp.float32
MESH_AXES = ("a", "b", "z", "c")
VMEM = pl.BlockSpec(memory_space=pltpu.VMEM)
SMEM = pl.BlockSpec(memory_space=pltpu.SMEM)
ANY = pl.BlockSpec(memory_space=pl.ANY)
WQ = 3 * HALF + 128
GELU_C = math.sqrt(2.0 / math.pi)


def dot(left, right):
    return jnp.dot(left, right, preferred_element_type=F32)


def ndot(left, right):
    return lax.dot_general(left, right, (((1,), (1,)), ((), ())), preferred_element_type=F32)


def flip(block):
    return block.T


def query_blocks(z, c, nz):
    near, far = 2 * z, 2 * (nz - 1 - z)
    return (near + c, far + c, near + 1 - c, far + 1 - c)


def over_keys(block, chunk):
    count = block + 1

    def step(i, unused):
        chunk(4 * i, 4)
        return unused

    lax.fori_loop(0, count // 4, step, 0)

    @pl.when(lax.rem(count, 4) >= 2)
    def _():
        chunk(count // 4 * 4, 2)

    @pl.when(lax.rem(count, 2) == 1)
    def _():
        chunk(block, 1)


def attend_blocks(blocks, kn, vt, qn, ot, lse, o, scratch):
    qz, s_s, m_s, l_s, acc_s = scratch
    rows = lax.broadcasted_iota(jnp.int32, (HALF, BLOCK), 0) // HEAD_DIM
    def one(i, unused):
        block = jnp.where(i == 0, blocks[0], blocks[1])
        qt = qn[i].astype(F32).T
        for h in range(CORE_HEADS):
            qz[h] = jnp.where(rows == h, qt, 0.0).astype(BF)
        m_s[...] = jnp.full_like(m_s, -1e30)
        l_s[...] = jnp.zeros_like(l_s)
        acc_s[...] = jnp.zeros_like(acc_s)

        def chunk(first, count):
            keys = kn[pl.ds(first, count)].reshape(count * BLOCK, HALF)
            for h in range(CORE_HEADS):
                s_s[h, : count * BLOCK] = dot(keys, qz[h])
            for h in range(CORE_HEADS):
                head = slice(h * HEAD_DIM, (h + 1) * HEAD_DIM)
                s = s_s[h, : count * BLOCK]
                old = m_s[h]
                new = jnp.maximum(old, jnp.max(s, axis=0, keepdims=True))
                p = jnp.exp(s - new)
                shrink = jnp.exp(old - new)
                m_s[h] = new
                l_s[h] = l_s[h] * shrink + jnp.sum(p, axis=0, keepdims=True)
                p = p.astype(BF)
                acc = acc_s[head, :] * shrink
                for j in range(count):
                    acc = acc + dot(vt[first + j, head, :], p[j * BLOCK : (j + 1) * BLOCK])
                acc_s[head, :] = acc

        over_keys(block, chunk)
        for h in range(CORE_HEADS):
            head = slice(h * HEAD_DIM, (h + 1) * HEAD_DIM)
            total = l_s[h]
            lse[i, h : h + 1, :] = m_s[h] + jnp.log(total)
            acc_s[head, :] = acc_s[head, :] / total
        value = acc_s[...]
        ot[i] = value
        o[i] = value.T.astype(BF)
        return unused

    lax.fori_loop(0, 2, one, 0)


def moves(sems, pairs):
    copies = [pltpu.make_async_copy(src, dst, sems.at[i]) for i, (src, dst) in enumerate(pairs)]
    for copy in copies:
        copy.start()
    return copies


def wait(copies):
    for copy in copies:
        copy.wait()


def pack_kernel(rs, ids, ins, outs, *refs):
    w_qkv, w_back, w_in, w_out, bias_qv, bias_out, bias_back, bias_in = refs[:8]
    gates, tile, sems = refs[8:]
    group = ids[4]
    loads = moves(sems, [(ins[i], refs[i]) for i in range(8)] + [(ins[10], gates)])
    rows = moves(
        sems.at[pl.ds(9, 4)],
        [(ins[8 + i].at[which], outs[3 + 2 * i + j]) for i in range(2) for j, which in enumerate((1 - group, group))],
    )
    wait(loads)
    tile[...] = jnp.zeros_like(tile)
    tile[0:2, :rs] = bias_qv[...].astype(F32)
    tile[2:3, :rs] = bias_out[...].astype(F32)
    tile[3:4, :rs] = bias_back[...].astype(F32)
    for i in range(SLABS):
        tile[4 + i : 5 + i, :rs] = bias_in[:, i * rs : (i + 1) * rs].astype(F32)
    outs[7][0:1, 0:2] = gates[...]
    turned = tile[...].T[:rs].astype(BF)
    q_keep, f_keep, give = outs[:3]

    def cut(ref, first, core):
        return ref[:, pl.ds(pl.multiple_of(first + core * HALF, HALF), HALF)]

    for i in range(3):
        q_keep[:, i * HALF : (i + 1) * HALF] = cut(w_qkv, i * D, ids[1])
        give[(9 + i) * rs : (10 + i) * rs] = cut(w_qkv, i * D, 1 - ids[1])
    q_keep[:, 3 * HALF :] = turned
    give[12 * rs :, :128] = turned
    give[12 * rs :, 128:] = jnp.zeros((rs, 128), BF)
    for f_out, core in ((f_keep, ids[1]), (give, 1 - ids[1])):
        f_out[: 4 * rs] = cut(w_back, 0, core)
        for i in range(SLABS):
            f_out[(4 + i) * rs : (5 + i) * rs] = cut(w_in, i * D, core)
        f_out[8 * rs : 9 * rs] = cut(w_out, 0, core)
    wait(rows)


def core_kernel(rs, ids, ins, outs):
    q_keep, f_keep, got = ins
    wq, wf = outs
    c = ids[1]
    wq[c] = q_keep[...]
    wf[c] = f_keep[...]
    wf[1 - c] = got[: 9 * rs]
    for i in range(3):
        wq[1 - c, :, i * HALF : (i + 1) * HALF] = got[(9 + i) * rs : (10 + i) * rs]
    wq[1 - c, :, 3 * HALF :] = got[12 * rs :, :128]


def my_bit(ids, where):
    index, bit = where
    return lax.rem(lax.shift_right_logical(ids[index], bit), 2)


def join(ids, own, got, outs, where, post=1):
    mine = my_bit(ids, where)
    pre = own.shape[0] // post
    for p in range(pre):
        out = outs[p * len(outs) // pre]
        at = 2 * p - 2 * pre // len(outs) * (p * len(outs) // pre)
        for q in range(post):
            out[(at + mine) * post + q] = own[p * post + q]
            out[(at + 1 - mine) * post + q] = got[p * post + q]


def first_kernel(nz, ndp, n2, rr, ids, ins, outs, spread, *scratch):
    xo, xs = ins[:2], ins[2:4]
    wq_pieces = ins[4:8]
    xall, wq, kn, vn, kt, vt, q_mine, q_other, ot, lse, o, bo, bb, bi = outs
    z, c = ids[0], ids[1]
    for p in range(nz // 2):
        chip = ids[4] * (nz // 2) + p
        for i, at in enumerate((chip, nz - 1 - chip)):
            xall[2 * at + c] = xo[i][p]
            xall[2 * at + 1 - c] = xs[i][p]

    def put(dp, half, value):
        wq[2 * dp + half] = value

    place_dp(ids, wq_pieces, ndp, n2, put)
    bias = wq[:, :, 3 * HALF :].reshape(D, 128).astype(F32)
    turned = bias.T
    bo[...] = turned[2:3]
    bb[...] = turned[3:4]
    lanes = lax.broadcasted_iota(jnp.int32, (D // rr, rr, 128), 2)
    for s in range(SLABS):
        spread[:, s] = jnp.where(lanes == 4 + s, bias.reshape(D // rr, rr, 128), 0.0)
    bi[...] = jnp.sum(spread[...].reshape(FF, 128).T[4:8], axis=0, keepdims=True)
    bias_q = jnp.where(c == 0, turned[0:1, :HALF], turned[0:1, HALF:])
    bias_v = jnp.where(c == 0, turned[1:2, :HALF], turned[1:2, HALF:])
    w_q = wq[:, :, :HALF].reshape(D, HALF)
    w_kv = wq[:, :, HALF : 3 * HALF].reshape(D, 2 * HALF)

    def project(i, unused):
        blocks = pl.ds(4 * i, 4)
        kv = dot(xall[blocks].reshape(4 * BLOCK, D), w_kv)
        key = kv[:, :HALF].astype(BF).reshape(4, BLOCK, HALF)
        value = (kv[:, HALF:] + bias_v).astype(BF).reshape(4, BLOCK, HALF)
        kn[blocks] = key
        vn[blocks] = value
        for j in range(4):
            kt[4 * i + j] = key[j].T
            vt[4 * i + j] = value[j].T
        return unused

    lax.fori_loop(0, nz // 2, project, 0)
    blocks = query_blocks(z, c, nz)
    q = dot(jnp.concatenate([xall[block] for block in blocks], axis=0), w_q) + bias_q
    q = (q.astype(BF).astype(F32) * (1.0 / math.sqrt(HEAD_DIM))).astype(BF)
    for i in range(4):
        (q_mine if i < 2 else q_other)[i % 2] = q[i * BLOCK : (i + 1) * BLOCK]
    attend_blocks(blocks[2:], kn, vt, q_other, ot, lse, o, scratch)


def place_dp(ids, pieces, ndp, n2, put):
    for i, piece in enumerate(pieces):
        far, half = i // 2, i % 2
        for j in range(ndp // 2):
            if half == 0:
                bit = lax.rem(ids[3], 2)
                dp = (2 * (j // n2) + (1 - bit if far else bit)) * n2 + j % n2
            else:
                bit = lax.rem(ids[5], 2)
                dp = j // (n2 // 2) * n2 + 2 * (j % (n2 // 2)) + (1 - bit if far else bit)
            put(dp, half, piece(j) if callable(piece) else piece[j])


def second_kernel(nz, ids, ins, outs, *scratch):
    kn, vt, qn = ins
    ot, lse, o = outs
    blocks = query_blocks(ids[0], ids[1], nz)
    attend_blocks(blocks[:2], kn, vt, qn, ot, lse, o, scratch)


def ffn_kernel(nz, ndp, n2, parts, ids, ins, outs, *refs):
    alphas, o_mine, got, xall, cot_a, cot_b, bo, bi, bb = ins[:9]
    pieces = ins[9:13]
    rows = pieces[0].shape[1]

    def received(i):
        return lambda j: got[pl.ds(2 * BLOCK + (i * (ndp // 2) + j) * rows, rows)]

    (out_near, out_far, dx1, d_mine, g_keep, give, gb_o, gb_i, gb_b, ga) = outs
    w, wo_s, wi_s, wb_s, mixed, h_s, r_s, dpre_s, dff_s, dattn_s = refs[:10]
    pre_s, dr_s = refs[10:12]
    c = ids[1]
    count = ndp * parts
    rd = D // count
    for core in range(2):
        own = pieces if core == 0 else [received(i) for i in range(4)]
        which = c if core == 0 else 1 - c
        lanes = pl.ds(pl.multiple_of(which * HALF, HALF), HALF)

        def put(dp, half, value):
            if parts == 1:
                w[which, 2 * dp + half] = value
                return
            for g in range(parts // 2):
                at = dp * parts + half * (parts // 2) + g
                part = value[9 * rd * g : 9 * rd * (g + 1)]
                wb_s[pl.ds(pl.multiple_of(at * 4 * rd, 4 * rd), 4 * rd), lanes] = part[: 4 * rd]
                at = pl.multiple_of(at * rd, rd)
                for s in range(SLABS):
                    wi_s[s, pl.ds(at, rd), lanes] = part[(4 + s) * rd : (5 + s) * rd]
                wo_s[pl.ds(at, rd), lanes] = part[8 * rd :]

        place_dp(ids, own, ndp, n2, put)
    if parts == 1:
        for half in range(2):
            lanes = slice(half * HALF, (half + 1) * HALF)
            whole = w[half].reshape(count, 9 * rd, HALF)
            wo_s[:, lanes] = whole[:, 8 * rd :].reshape(D, HALF)
            for s in range(SLABS):
                wi_s[s, :, lanes] = whole[:, (4 + s) * rd : (5 + s) * rd].reshape(D, HALF)
            wb_s[:, lanes] = whole[:, : 4 * rd].reshape(FF, HALF)
    mixed[c] = o_mine[...].reshape(2 * BLOCK, HALF)
    mixed[1 - c] = got[: 2 * BLOCK]
    alpha_attn, alpha_ffn = alphas[0:1, 0:1], alphas[0:1, 1:2]
    mine = query_blocks(ids[0], c, nz)
    both = 2 * BLOCK
    dy = jnp.concatenate([cot_a[...], cot_b[...]], axis=0).astype(F32)
    dff = (alpha_ffn * dy).astype(BF)
    dff_s[...] = dff
    attn = dot(mixed[0], wo_s[:HALF, :]) + dot(mixed[1], wo_s[HALF:, :]) + bo[...]
    x1 = jnp.concatenate([xall[mine[0]], xall[mine[1]]], axis=0).astype(F32) + alpha_attn * attn
    hidden = x1.astype(BF)
    h_s[...] = hidden
    x1_s = refs[12]
    attn_s = refs[13]
    x1_s[...] = x1
    attn_s[...] = attn
    for s in range(SLABS):
        lanes = slice(s * D, (s + 1) * D)
        pre_s[s] = dot(h_s[...], wi_s[s]) + bi[:, lanes]
        dr_s[s] = ndot(dff_s[...], wb_s[lanes, :])
    ff = None
    dx = None
    for s in range(SLABS):
        lanes = slice(s * D, (s + 1) * D)
        pre = pre_s[s]
        square = pre * pre
        up = 0.5 + 0.5 * jnp.tanh(pre * (GELU_C + (GELU_C * 0.044715) * square))
        r = pre * up
        r_s[:, lanes] = r.astype(BF)
        slope = up + r * (1.0 - up) * (2.0 * GELU_C + (6.0 * GELU_C * 0.044715) * square)
        dpre_s[:, lanes] = (dr_s[s] * slope).astype(BF)
    for s in range(SLABS):
        lanes = slice(s * D, (s + 1) * D)
        t1 = dot(r_s[:, lanes], wb_s[lanes, :])
        t2 = ndot(dpre_s[:, lanes], wi_s[s])
        ff = t1 if ff is None else ff + t1
        dx = t2 if dx is None else dx + t2
    ff = ff + bb[...]
    x1 = x1_s[...]
    out = (x1 + alpha_ffn * ff).astype(BF)
    out_near[...] = out[:BLOCK]
    out_far[...] = out[BLOCK:]
    dy = jnp.concatenate([cot_a[...], cot_b[...]], axis=0).astype(F32)
    dx = dx + dy
    dx1[0] = dx[:BLOCK]
    dx1[1] = dx[BLOCK:]
    dattn = (alpha_attn * dx).astype(BF)
    dattn_s[...] = dattn
    d_mine[...] = ndot(dattn, wo_s[pl.ds(pl.multiple_of(c * HALF, HALF), HALF), :]).astype(BF)
    give[:both, :] = ndot(dattn, wo_s[pl.ds(pl.multiple_of((1 - c) * HALF, HALF), HALF), :]).astype(BF)
    ga[...] = jnp.concatenate(
        [jnp.sum(dx * attn_s[...], axis=0, keepdims=True), jnp.sum(dy * ff, axis=0, keepdims=True)], axis=0
    )
    gb_o[...] = jnp.sum(dattn_s[...].astype(F32), axis=0, keepdims=True)
    gb_b[...] = jnp.sum(dff_s[...].astype(F32), axis=0, keepdims=True)
    for s in range(SLABS):
        lanes = slice(s * D, (s + 1) * D)
        gb_i[:, lanes] = jnp.sum(dpre_s[:, lanes].astype(F32), axis=0, keepdims=True)
    both_t = jnp.concatenate([mixed[0], mixed[1]], axis=1).T
    ht = h_s[...].T
    per = count // SLABS

    def columns(ref, first, core):
        return ref[:, pl.ds(pl.multiple_of(first + core * HALF, HALF), HALF)]

    def put_rows(core, first, value, groups):
        size = value.shape[0] // len(groups)
        for i, group in enumerate(groups):
            part = value[i * size : (i + 1) * size]
            if core == 0:
                g_keep[group, first : first + size, :] = part
            else:
                row = 2 * BLOCK + group * 9 * rd + first
                give[row : row + size, :] = part

    for core, which in enumerate((c, 1 - c)):
        put_rows(core, 8 * rd, dot(both_t, columns(dattn_s, 0, which)).astype(BF), range(count))
    for s in range(SLABS):
        lanes = slice(s * D, (s + 1) * D)
        rt = r_s[:, lanes].T
        for core, which in enumerate((c, 1 - c)):
            put_rows(core, (4 + s) * rd, dot(ht, columns(dpre_s, s * D, which)).astype(BF), range(count))
            put_rows(core, 0, dot(rt, columns(dff_s, 0, which)).astype(BF), range(s * per, (s + 1) * per))


def back_blocks(blocks, kn, vn, kt, q_in, d_in, ot, lse, dk_s, dv_s, dq_out, scratch):
    qz, qzt, oz, ozt, dq_s, p_s, dp_s = scratch
    rows = lax.broadcasted_iota(jnp.int32, (HALF, BLOCK), 0) // HEAD_DIM
    lanes = lax.broadcasted_iota(jnp.int32, (BLOCK, HALF), 1) // HEAD_DIM
    def one(i, gq):
        block = jnp.where(i == 0, blocks[0], blocks[1])
        q = q_in[i].astype(F32)
        d_o = d_in[pl.ds(pl.multiple_of(i * BLOCK, BLOCK), BLOCK), :].astype(F32)
        qt, dot_ = q.T, d_o.T
        product = dot_ * ot[i]
        deltas = []
        for h in range(CORE_HEADS):
            head = slice(h * HEAD_DIM, (h + 1) * HEAD_DIM)
            deltas.append(jnp.sum(product[head], axis=0, keepdims=True))
            qz[h] = jnp.where(lanes == h, q, 0.0).astype(BF)
            oz[h] = jnp.where(lanes == h, d_o, 0.0).astype(BF)
            qzt[h] = jnp.where(rows == h, qt, 0.0).astype(BF)
            ozt[h] = jnp.where(rows == h, dot_, 0.0).astype(BF)
        dq_s[...] = jnp.zeros_like(dq_s)

        def chunk(first, count):
            size = count * BLOCK
            keys = kn[pl.ds(first, count)].reshape(size, HALF)
            values = vn[pl.ds(first, count)].reshape(size, HALF)
            for h in range(CORE_HEADS):
                p_s[h, :size] = dot(keys, qzt[h])
                dp_s[h, :size] = dot(values, ozt[h])
            dk = dk_s[pl.ds(first, count)].reshape(size, HALF)
            dv = dv_s[pl.ds(first, count)].reshape(size, HALF)
            for h in range(CORE_HEADS):
                head = slice(h * HEAD_DIM, (h + 1) * HEAD_DIM)
                p = jnp.exp(p_s[h, :size] - lse[i, h : h + 1, :])
                ds = (p * (dp_s[h, :size] - deltas[h])).astype(BF)
                dv = dv + dot(p.astype(BF), oz[h])
                dk = dk + dot(ds, qz[h])
                dq = dq_s[head, :]
                for j in range(count):
                    dq = dq + dot(kt[first + j, head, :], ds[j * BLOCK : (j + 1) * BLOCK])
                dq_s[head, :] = dq
            dk_s[pl.ds(first, count)] = dk.reshape(count, BLOCK, HALF)
            dv_s[pl.ds(first, count)] = dv.reshape(count, BLOCK, HALF)

        over_keys(block, chunk)
        dq = (dq_s[...] * (1.0 / math.sqrt(HEAD_DIM))).T.astype(BF)
        dq_out[i] = dq
        return gq + jnp.sum(dq.astype(F32), axis=0, keepdims=True)

    return lax.fori_loop(0, 2, one, jnp.zeros((1, HALF), F32))


def back_kernel(nz, which, ids, ins, outs, *scratch):
    kn, vn, kt, qn, ot, lse, d_o = ins[:7]
    dk, dv, dq, gq = outs
    if which == 0:
        dk[...] = jnp.zeros_like(dk)
        dv[...] = jnp.zeros_like(dv)
    blocks = query_blocks(ids[0], ids[1], nz)[2 * which : 2 * which + 2]
    gq[...] = back_blocks(blocks, kn, vn, kt, qn, d_o, ot, lse, dk, dv, dq, scratch)


def dx_kernel(nz, which, ids, ins, outs, dxs):
    wq, dk, dv, dq_mine, dq_other, dx1 = ins
    keep, send, dkv = outs
    z, c = ids[0], ids[1]
    half = nz // 2
    place = lax.rem(z, half)
    w_q = wq[:, :, :HALF].reshape(D, HALF)
    w_kv = wq[:, :, HALF : 3 * HALF].reshape(D, 2 * HALF)
    for core, (target, dq) in enumerate(((keep, dq_mine), (send, dq_other))):
        for p in range(half):
            chip = ids[4] * half + p
            block = 2 * (chip if which == 0 else nz - 1 - chip) + (c if core == 0 else 1 - c)
            dkv[core * half + p, :, :HALF] = dk[block].astype(BF)
            dkv[core * half + p, :, HALF:] = dv[block].astype(BF)
        rows = dkv[core * half : (core + 1) * half].reshape(half * BLOCK, 2 * HALF)
        dxs[core] = ndot(rows, w_kv).reshape(half, BLOCK, D)
        value = ndot(dq[which], w_q)
        if core == 0:
            value = value + dx1[which]
        dxs[core, place] = dxs[core, place] + value
        target[...] = dxs[core].astype(BF)


def dw_kernel(nz, rs, rr, ids, ins, outs, spread):
    xall, dkv_near, dkv_far, dq_mine, dq_other, gq_mine, gq_other, gb_o, gb_i, gb_b, ga = ins
    (dw,) = outs
    z, c = ids[0], ids[1]
    half = nz // 2
    rows = []
    for which in range(2):
        for core in range(2):
            for p in range(half):
                chip = ids[4] * half + p
                rows.append(xall[2 * (chip if which == 0 else nz - 1 - chip) + (c if core == 0 else 1 - c)])
    dkv = jnp.concatenate([ref[...].reshape(nz * BLOCK, 2 * HALF) for ref in (dkv_near, dkv_far)], axis=0)
    acc_kv = dot(jnp.concatenate(rows, axis=0).T, dkv)
    gv = jnp.zeros((1, HALF), F32)
    for ref in (dkv_near, dkv_far):
        for i in range(nz):
            gv = gv + jnp.sum(ref[i, :, HALF:].astype(F32), axis=0, keepdims=True)
    queries = jnp.concatenate([xall[block] for block in query_blocks(z, c, nz)], axis=0).T
    dq = jnp.concatenate([dq_mine[...].reshape(2 * BLOCK, HALF), dq_other[...].reshape(2 * BLOCK, HALF)], axis=0)
    acc_q = dot(queries, dq)
    gq = gq_mine[...] + gq_other[...]
    nothing = jnp.zeros((1, HALF), F32)
    own = [jnp.concatenate([jnp.where(c == 0, g, nothing), jnp.where(c == 0, nothing, g)], axis=1) for g in (gq, gv)]
    tile = jnp.concatenate(own + [gb_o[...], gb_b[...], jnp.zeros((124, D), F32)], axis=0).T
    spread[...] = jnp.broadcast_to(gb_i[...], (128, FF)).T.reshape(D // rr, SLABS, rr, 128)
    lanes = lax.broadcasted_iota(jnp.int32, (D // rr, rr, 128), 2)
    tile = tile.reshape(D // rr, rr, 128)
    for s in range(SLABS):
        tile = jnp.where(lanes == 4 + s, spread[:, s], tile)
    tile = tile.reshape(D, 128)
    if rs >= 16:
        me = ids[2]
        lane = lax.broadcasted_iota(jnp.int32, (D, 128), 1) - 8 - 6 * (me // rs)
        mine = lax.rem(lax.broadcasted_iota(jnp.int32, (D, 128), 0), rs) == lax.rem(me, rs)
        gates = jnp.sum(ga[...], axis=1, keepdims=True)
        for which in range(2):
            rest = gates[which : which + 1]
            for i in range(3):
                high = rest.astype(BF).astype(F32)
                tile = jnp.where(mine & (lane == 2 * i + which), high, tile)
                rest = rest - high
    rows = dw.shape[1]
    dw[:, :, :HALF] = acc_q.astype(BF).reshape(D // rows, rows, HALF)
    dw[:, :, HALF : 3 * HALF] = acc_kv.astype(BF).reshape(D // rows, rows, 2 * HALF)
    dw[:, :, 3 * HALF :] = tile.astype(BF).reshape(D // rows, rows, 128)


def sum_kernel(plans, ids, ins, outs):
    outs = list(outs)
    for numbers, size, where, pre, post, stride, first, flat in plans:

        def total(static, dynamic):
            source = static * stride // size
            index = (static + dynamic) * stride + first - source * size
            refs = [ins[number] for number in numbers[source]]
            value = refs[0][index]
            if len(refs) == 2 and flat is None:
                value = value.astype(F32) + refs[1][index].astype(F32)
            elif len(refs) == 2:
                rows = value.shape[0]
                start = pl.multiple_of(flat + index * rows, 16)
                value = value.astype(F32) + refs[1][pl.ds(start, rows), :].astype(F32)
            return value

        if where is None:
            out = outs.pop(0)
            for index in range(out.shape[0]):
                out[index] = total(index, 0).astype(out.dtype)
            continue
        keep, send = outs.pop(0), outs.pop(0)
        mine = my_bit(ids, where)
        for p in range(pre):
            for q in range(post):
                keep[p * post + q] = total(2 * p * post + q, mine * post).astype(keep.dtype)
                send[p * post + q] = total(2 * p * post + q, (1 - mine) * post).astype(send.dtype)


def grads_kernel(rs, ids, ins, outs):
    own, other = ins
    w_back, w_in, w_out = outs
    for ref, core in ((own, ids[1]), (other, 1 - ids[1])):

        def lanes(first):
            return pl.ds(pl.multiple_of(first + core * HALF, HALF), HALF)

        value = ref[0].astype(F32)
        w_back[:, lanes(0)] = value[: 4 * rs]
        for s in range(SLABS):
            w_in[:, lanes(s * D)] = value[(4 + s) * rs : (5 + s) * rs]
        w_out[:, lanes(0)] = value[8 * rs :]


def last_kernel(rs, ids, ins, outs):
    own, other = ins
    w_qkv, gb_qv, gb_o, gb_i, gb_b, gates = outs
    for ref, core in ((own, ids[1]), (other, 1 - ids[1])):
        value = ref[0].astype(F32)
        for i in range(3):
            lanes = pl.ds(pl.multiple_of(i * D + core * HALF, HALF), HALF)
            w_qkv[:, lanes] = value[:, i * HALF : (i + 1) * HALF]
    sums = own[0, :, 3 * HALF :] + other[0, :, 3 * HALF :].astype(F32)
    lane = lax.broadcasted_iota(jnp.int32, (1, 128), 1)
    column = jnp.sum(sums, axis=0, keepdims=True)
    for which in range(2):
        used = (lane >= 8) & (lax.rem(lane, 2) == which)
        gates[:, which : which + 1] = jnp.sum(jnp.where(used, column, 0.0), axis=1, keepdims=True)
    by_row = jnp.concatenate([sums, jnp.zeros((128 - rs, 128), F32)], axis=0).T
    gb_qv[...] = by_row[:2, :rs]
    gb_o[...] = by_row[2:3, :rs]
    gb_b[...] = by_row[3:4, :rs]
    for s in range(SLABS):
        gb_i[:, s * rs : (s + 1) * rs] = by_row[4 + s : 5 + s, :rs]


def shape(dims, kind):
    return jax.ShapeDtypeStruct(dims, kind)


def vmem(dims, kind):
    return pltpu.VMEM(dims, kind)


def in_hbm(array):
    return pltpu.with_memory_space_constraint(array, pltpu.HBM)


def cost(megabytes):
    return pl.CostEstimate(flops=0, bytes_accessed=megabytes * 2**20, transcendentals=0)


def call(
    name, kernel, ids, ins, outs, after=(), scratch=(), limit=12, weight=0, where=None, aliases=None, out=VMEM
):
    count, waits = len(ins), len(after)

    def run(*refs):
        given, rest = refs[:count], refs[count + waits :]
        kernel(ids(), given, rest[: len(outs)], *rest[len(outs) :])

    return pl.pallas_call(
        run,
        out_shape=tuple(outs),
        in_specs=(where or [VMEM] * count) + [ANY] * waits,
        out_specs=out if isinstance(out, tuple) else (out,) * len(outs),
        scratch_shapes=list(scratch),
        compiler_params=pltpu.CompilerParams(vmem_limit_bytes=limit * 2**20),
        cost_estimate=cost(weight),
        input_output_aliases=aliases or {},
        name=name,
    )(*ins, *after)


def pack_call(ids, rs, ins):
    return call(
        "pack",
        functools.partial(pack_kernel, rs),
        ids,
        [in_hbm(array) for array in ins],
        [vmem((rs, WQ), BF), vmem((9 * rs, HALF), BF), vmem((13 * rs, HALF), BF)] + [vmem((BLOCK, D), BF)] * 4
        + [vmem((8, 128), F32)],
        scratch=[pltpu.VMEM(array.shape, BF) for array in ins[:8]]
        + [pltpu.VMEM((1, 2), F32), pltpu.VMEM((128, 128), F32), pltpu.SemaphoreType.DMA((13,))],
        where=[ANY] * 11,
    )


def join_call(name, ids, jobs, after=(), extra=None, extra_ins=(), extra_outs=(), cuts=None):
    ins, outs, spans = [], [], []
    for (own, got, _, _), cut in zip(jobs, cuts or [1] * len(jobs)):
        ins += [own, got]
        spans.append(slice(len(outs), len(outs) + cut))
        outs += [vmem((2 * own.shape[0] // cut,) + own.shape[1:], own.dtype)] * cut
    number = len(outs)

    def kernel(ids_ref, given, results):
        for i, (_, _, where, post) in enumerate(jobs):
            join(ids_ref, given[2 * i], given[2 * i + 1], results[spans[i]], where, post)
        if extra is not None:
            extra(ids_ref, given[2 * len(jobs) :], results[number:])

    return call(name, kernel, ids, ins + list(extra_ins), outs + list(extra_outs), after)


def sum_call(name, ids, jobs, after=(), last=BF, flat=None):
    ins, outs, plans = [], [], []

    def number(array):
        for i, other in enumerate(ins):
            if other is array:
                return i
        ins.append(array)
        return len(ins) - 1

    for sources, where, pre, post, stride, first in jobs:
        numbers = [tuple(number(array) for array in pair if array is not None) for pair in sources]
        tail = sources[0][0].shape[1:]
        size = sources[0][0].shape[0]
        plans.append((numbers, size, where, pre, post, stride, first, flat))
        if where is None:
            outs.append(vmem((size * len(sources) // stride,) + tail, last))
        else:
            outs += [vmem((pre * post,) + tail, last), vmem((pre * post,) + tail, BF)]
    return call(name, functools.partial(sum_kernel, plans), ids, ins, outs, after)


def make_body(n1, n2, nz):
    ndp = n1 * n2
    nsh = ndp * nz * 2
    rs = D // nsh
    rd = D // ndp
    half = nz // 2
    parts = 2 * nz if rs % 16 == 0 else 1
    rr = rd // parts
    nh = 9 * rd // 2
    swap = [(0, 1), (1, 0)]
    bits_a, bits_b, bits_z = (count.bit_length() - 1 for count in (n1, n2, nz))
    counts = {"a": n1, "b": n2, "z": nz}
    slot = {"a": 3, "b": 5, "z": 0}

    def to_mirror(array):
        return lax.ppermute(array, "z", [(s, nz - 1 - s) for s in range(nz)])

    def exchange(array, name, bit):
        return lax.ppermute(array, name, [(s, s ^ (1 << bit)) for s in range(counts[name])])

    def to_other(array):
        return lax.ppermute(array, "c", swap)

    def body(inputs, w_qkv, bias_qv, w_out, bias_out, w_in, bias_in, w_back, bias_back, alphas, cotangent):
        z, c = lax.axis_index("z"), lax.axis_index("c")
        a, b = lax.axis_index("a"), lax.axis_index("b")

        def ids():
            z, c = lax.axis_index("z"), lax.axis_index("c")
            a, b = lax.axis_index("a"), lax.axis_index("b")
            return (z, c, ((a * n2 + b) * nz + z) * 2 + c, a, z // half, b)


        latest = []

        def hand_on(ids_ref, given, results):
            for source, target in zip(given, results):
                target[...] = source[...]

        def step(name, jobs, extra=(), cuts=None, others=()):
            result = join_call(
                name, ids, jobs, latest + list(others), hand_on, extra, [vmem(e.shape, e.dtype) for e in extra], cuts
            )
            latest[:] = [result[0]]
            return result


        q_keep, f_keep, give, x_give, x_keep, cot_give, cot_a, gates = pack_call(
            ids, rs,
            [w_qkv, w_back, w_in, w_out, bias_qv, bias_out[None], bias_back[None], bias_in[None], inputs, cotangent,
             alphas[None]],
        )
        wq, wf = call(
            "core", functools.partial(core_kernel, rs), ids, [q_keep, f_keep, to_other(give)],
            [vmem((2, rs, WQ), BF), vmem((2, 9 * rs, HALF), BF)],
        )
        latest[:] = [wq]
        wq, wf = wq.reshape(1, 2 * rs, WQ), wf.reshape(1, 2 * 9 * rs, HALF)
        wf = wf.reshape(2 * 9 * rs, HALF)
        q_got = exchange(wq, "z", bits_z - 1)
        wf_parts = [(wf, 0)]
        for i in reversed(range(bits_z)):
            wf_parts += [(exchange(part, "z", i), place | (1 << i)) for part, place in wf_parts]
        wf_near = [part for part, place in wf_parts if place == 1]
        for i in reversed(range(1, bits_z)):
            (wq,) = step("q_z", [(wq, q_got, (0, i), 1)])
            q_got = exchange(wq, "z", i - 1)
        q_first, q_second, x_keep, x_give = step(
            "q_z", [(wq, q_got, (0, 0), 1)], [x_keep, x_give], [2], wf_near + [wf_parts[1][0]]
        )
        if parts == 1:
            wq = jnp.concatenate([q_first, q_second], axis=0).reshape(rd, WQ)
            hidden_bias = wq[:, 3 * HALF + 4 : 3 * HALF + 8].reshape(2 * nz, rs, SLABS)
            hidden_bias = jnp.transpose(hidden_bias, (0, 2, 1)).reshape(SLABS, rd).T
            wq = jnp.concatenate([wq[:, : 3 * HALF + 4], hidden_bias, wq[:, 3 * HALF + 8 :]], axis=1)
            q_first, q_second = wq[: rd // 2], wq[rd // 2 :]
        q_first, q_second = q_first.reshape(1, rd // 2, WQ), q_second.reshape(1, rd // 2, WQ)
        x_far = to_mirror(x_give)
        for i in reversed(range(1, bits_b)):
            got = exchange(q_first, "b", i), exchange(q_second, "a", i)
            q_first, q_second = step("q_dp", [(q_first, got[0], (5, i), 1), (q_second, got[1], (3, i), 1)])
        q_got = exchange(q_first, "b", 0), exchange(q_second, "a", 0)
        own = x_keep[None]
        own_got = exchange(own, "z", max(bits_z - 2, 0))

        q_first, q_second = step("q_dp", [(q_first, q_got[0], (5, 0), 1), (q_second, q_got[1], (3, 0), 1)])
        for i in reversed(range(1, bits_a)):
            got = exchange(q_first, "a", i), exchange(q_second, "b", i)
            q_first, q_second = step("q_dp", [(q_first, got[0], (3, i), n2), (q_second, got[1], (5, i), 1)])
        wq_pieces = [q_first, q_second, exchange(q_first, "a", 0), exchange(q_second, "b", 0)]

        def in_place(ids_ref, given, results):
            for group in range(2):

                @pl.when(ids_ref[4] == group)
                def _():
                    for ref, (_, place) in zip(given, wf_parts):
                        at = lax.rem(lax.bitwise_xor(ids_ref[0], place), half)
                        results[group ^ (place // half)][at] = ref[...]

        halves = vmem((half, 2 * 9 * rs, HALF), BF)
        first, second = call("f_z", in_place, ids, [part for part, _ in wf_parts], [halves, halves], latest)
        latest[:] = [first]
        if parts == 1:
            wf = jnp.concatenate([first, second], axis=0).reshape(nz, 2, 9 * rs, HALF)
            wf = jnp.concatenate(
                [wf[:, :, : 4 * rs].reshape(4 * rd, HALF)]
                + [wf[:, :, (4 + s) * rs : (5 + s) * rs].reshape(rd, HALF) for s in range(SLABS)]
                + [wf[:, :, 8 * rs :].reshape(rd, HALF)],
                axis=0,
            )
            first, second = wf[:nh], wf[nh:]
        first, second = first.reshape(1, nh, HALF), second.reshape(1, nh, HALF)
        far_rows, cot_give = call(
            "x_far", hand_on, ids, [x_far, cot_give], [vmem((BLOCK, D), BF)] * 2, latest + [own_got]
        )
        latest[:] = [far_rows]
        cot_b = to_mirror(cot_give)
        far_rows = far_rows[None]
        for i in reversed(range(1, bits_z - 1)):
            far_got = exchange(far_rows, "z", i)
            own, far_rows = step("x_z", [(own, own_got, (0, i), 1), (far_rows, far_got, (0, i), 1)])
            own_got = exchange(own, "z", i - 1)
        far_got = exchange(far_rows, "z", 0)

        for i in reversed(range(bits_b)):
            got = exchange(first, "b", i), exchange(second, "a", i)
            first, second = step("f_dp", [(first, got[0], (5, i), 1), (second, got[1], (3, i), 1)])
        for i in reversed(range(1, bits_a)):
            got = exchange(first, "a", i), exchange(second, "b", i)
            first, second = step("f_dp", [(first, got[0], (3, i), n2), (second, got[1], (5, i), 1)])
        wf_pieces = [first, second, exchange(first, "a", 0), exchange(second, "b", 0)]

        def rows_of_all(ids_ref, given, results):
            own_ref, own_got_ref, far_ref, far_got_ref = given
            base, mine = ids_ref[4] * half, my_bit(ids_ref, (0, 0))
            for p in range(half // 2):
                for own_part, far_part, at in (
                    (own_ref, far_ref, base + 2 * p + mine),
                    (own_got_ref, far_got_ref, base + 2 * p + 1 - mine),
                ):
                    results[0][at - base] = own_part[p]
                    results[1][at - base] = far_part[p]

        xo = call(
            "x_all", rows_of_all, ids, [own, own_got, far_rows, far_got], [vmem((half, BLOCK, D), BF)] * 2,
            latest + wq_pieces[2:] + [cot_b],
        )
        latest[:] = [xo[0]]
        xs = [to_other(part) for part in xo]

        nb = 2 * nz
        heads_t = pltpu.VMEM((CORE_HEADS, HALF, BLOCK), BF)
        scores = pltpu.VMEM((CORE_HEADS, 4 * BLOCK, BLOCK), F32)
        scratch = [
            heads_t,
            scores,
            pltpu.VMEM((CORE_HEADS, 1, BLOCK), F32),
            pltpu.VMEM((CORE_HEADS, 1, BLOCK), F32),
            pltpu.VMEM((HALF, BLOCK), F32),
        ]
        natural, turned = (nb, BLOCK, HALF), (nb, HALF, BLOCK)
        two, two_t = (2, BLOCK, HALF), (2, HALF, BLOCK)
        two_lse = (2, CORE_HEADS, BLOCK)
        spread = pltpu.VMEM((D // rr, SLABS, rr, 128), F32)
        (xall, wq, kn, vn, kt, vt, q_mine, q_other, ot_other, lse_other, o_send, bo, bb, bi) = call(
            "first",
            functools.partial(first_kernel, nz, ndp, n2, rr),
            ids,
            [*xo, *xs, *wq_pieces],
            [
                vmem((nb, BLOCK, D), BF),
                vmem((2 * ndp, rd // 2, WQ), BF),
                vmem(natural, BF),
                vmem(natural, BF),
                vmem(turned, BF),
                vmem(turned, BF),
                vmem(two, BF),
                vmem(two, BF),
                vmem(two_t, F32),
                vmem(two_lse, F32),
                vmem(two, BF),
                vmem((1, D), F32),
                vmem((1, D), F32),
                vmem((1, FF), F32),
            ],
            latest,
            [spread] + scratch,
            limit=24,
        )

        def give_kernel(ids_ref, given, results):
            row = 0
            for part in given:
                for i in range(part.shape[0]):
                    results[0][row : row + part.shape[1]] = part[i]
                    row += part.shape[1]

        (give,) = call(
            "give", give_kernel, ids, [o_send, *wf_pieces], [vmem((2 * BLOCK + 2 * ndp * nh, HALF), BF)],
            limit=24,
        )
        ffn_got = to_other(give)
        ot_mine, lse_mine, o_mine = call(
            "second",
            functools.partial(second_kernel, nz),
            ids,
            [kn, vt, q_mine],
            [vmem(two_t, F32), vmem(two_lse, F32), vmem(two, BF)],
            (),
            scratch,
            limit=24,
        )

        grouped = (ndp * parts, 9 * rd // parts, HALF)
        (out_near, out_far, dx1, d_mine, g_keep, give, gb_o, gb_i, gb_b, ga) = call(
            "ffn",
            functools.partial(ffn_kernel, nz, ndp, n2, parts),
            ids,
            [gates, o_mine, ffn_got, xall, cot_a, cot_b, bo, bi, bb, *wf_pieces],
            [
                vmem((BLOCK, D), BF),
                vmem((BLOCK, D), BF),
                vmem((2, BLOCK, D), F32),
                vmem((2 * BLOCK, HALF), BF),
                vmem(grouped, BF),
                vmem((2 * BLOCK + ndp * 9 * rd, HALF), BF),
                vmem((1, D), F32),
                vmem((1, FF), F32),
                vmem((1, D), F32),
                vmem((2, D), F32),
            ],
            scratch=[
                pltpu.VMEM((2, 2 * ndp, nh, HALF) if parts == 1 else (8, 128), BF),
                pltpu.VMEM((D, D), BF),
                pltpu.VMEM((SLABS, D, D), BF),
                pltpu.VMEM((FF, D), BF),
                pltpu.VMEM((2, 2 * BLOCK, HALF), BF),
                pltpu.VMEM((2 * BLOCK, D), BF),
                pltpu.VMEM((2 * BLOCK, FF), BF),
                pltpu.VMEM((2 * BLOCK, FF), BF),
                pltpu.VMEM((2 * BLOCK, D), BF),
                pltpu.VMEM((2 * BLOCK, D), BF),
                pltpu.VMEM((SLABS, 2 * BLOCK, D), F32),
                pltpu.VMEM((SLABS, 2 * BLOCK, D), F32),
                pltpu.VMEM((2 * BLOCK, D), F32),
                pltpu.VMEM((2 * BLOCK, D), F32),
            ],
            limit=36,
        )
        back_got = to_other(give)
        back_scratch = [
            pltpu.VMEM((CORE_HEADS, BLOCK, HALF), BF),
            heads_t,
            pltpu.VMEM((CORE_HEADS, BLOCK, HALF), BF),
            heads_t,
            pltpu.VMEM((HALF, BLOCK), F32),
            scores,
            scores,
        ]
        back_out = [vmem(natural, F32), vmem(natural, F32), vmem(two, BF), vmem((1, HALF), F32)]
        dk, dv, dq_mine, gq_mine = call(
            "back_first",
            functools.partial(back_kernel, nz, 0),
            ids,
            [kn, vn, kt, q_mine, ot_mine, lse_mine, d_mine],
            back_out,
            scratch=back_scratch,
            limit=24,
        )

        latest[:] = [gq_mine]
        done = {}

        def along(axis, count, pre, post):
            return [(axis, i, pre * (count >> (i + 1)), post) for i in range(count.bit_length() - 1)]

        def dp_scatter(name, kept, got, rows, columns, flat=None):
            axes = (along("b", n2, n1, 1) + along("a", n1, 1, 1), along("a", n1, 1, n2) + along("b", n2, 1, 1))
            whole = (kept.reshape(2 * ndp, rows, columns), got)
            state = [(whole, 2, 0), (whole, 2, 1)]
            for i in range(len(axes[0])):
                result = sum_call(
                    name,
                    ids,
                    [
                        ([pair], (slot[axis], bit), pre, post, stride, first)
                        for (pair, stride, first), (axis, bit, pre, post) in zip(state, (axes[0][i], axes[1][i]))
                    ],
                    latest,
                    flat=flat if i == 0 else None,
                )
                latest[:] = [result[0]]
                state = [
                    ((result[2 * j], exchange(result[2 * j + 1], axes[j][i][0], axes[j][i][1])), 1, 0)
                    for j in range(2)
                ]
                yield
            return [pair for pair, _, _ in state]

        def z_scatter(name, sources):
            for _, i, pre, _ in along("z", nz, 1, 1):
                kept, send = sum_call(name, ids, [(sources, (slot["z"], i), pre, 1, 1, 0)], latest)
                latest[:] = [kept]
                sources = [(kept, exchange(send, "z", i))]
                yield
            rows, columns = kept.shape[1] // 2, kept.shape[2]
            sources = [tuple(array.reshape(2, rows, columns) for array in sources[0])]
            keep, send = sum_call(name, ids, [(sources, (1, 0), 1, 1, 1, 0)], latest, F32)
            latest[:] = [keep]
            return keep, to_other(send)

        def whole_dp(name, sources):
            return [part[0] for part in sum_call(name, ids, [([pair], None, 0, 0, 1, 0) for pair in sources], latest)]

        def g_chain():
            sources = yield from dp_scatter("g_dp", g_keep, back_got, nh, HALF, 2 * BLOCK)
            if parts == 1:
                g_dp = jnp.concatenate(whole_dp("g_dp", sources), axis=0)
                g_dp = jnp.concatenate(
                    [g_dp[: 4 * rd].reshape(nz, 2, 4 * rs, HALF)]
                    + [g_dp[(4 + s) * rd : (5 + s) * rd].reshape(nz, 2, rs, HALF) for s in range(SLABS)]
                    + [g_dp[8 * rd :].reshape(nz, 2, rs, HALF)],
                    axis=2,
                )
                sources = [(g_dp.reshape(nz, 2 * 9 * rs, HALF), None)]
            else:
                sources = [tuple(array.reshape(half, 2 * 9 * rs, HALF) for array in pair) for pair in sources]
            keep, got = yield from z_scatter("g_z", sources)
            yield
            done["g"] = call(
                "g_last", functools.partial(grads_kernel, rs), ids, [keep, got],
                [pltpu.HBM((4 * rs, D), F32), pltpu.HBM((rs, FF), F32), pltpu.HBM((rs, D), F32)], latest,
            )

        g_steps = g_chain()
        next(g_steps)
        dk, dv, dq_other, gq_other = call(
            "back_second",
            functools.partial(back_kernel, nz, 1),
            ids,
            [kn, vn, kt, q_other, ot_other, lse_other, back_got, dk, dv],
            back_out,
            latest,
            back_scratch,
            limit=24,
            aliases={7: 0, 8: 1},
        )
        def out_kernel(ids_ref, given, results, sems):
            group = ids_ref[4]
            copies = moves(sems, [(given[0], results[0].at[group]), (given[1], results[0].at[1 - group])])
            results[1][...] = jnp.zeros_like(results[1])
            wait(copies)

        def to_rows(name, own, got):
            rows, token = call(
                name, out_kernel, ids, [own, got], [pltpu.HBM((2, BLOCK, D), BF), vmem((8, 128), F32)], latest,
                [pltpu.SemaphoreType.DMA((2,))], where=[ANY, ANY],
                out=(pl.BlockSpec(memory_space=pltpu.HBM), VMEM),
            )
            latest[:] = [token]
            return rows

        latest[:] = [gq_other]
        out_b = to_mirror(out_far)
        latest.append(out_b)

        def dx_call(which):
            keep, send, dkv = call(
                "dx",
                functools.partial(dx_kernel, nz, which),
                ids,
                [wq, dk, dv, dq_mine, dq_other, dx1],
                [vmem((half, BLOCK, D), BF), vmem((half, BLOCK, D), BF), vmem((nz, BLOCK, 2 * HALF), BF)],
                latest,
                [pltpu.VMEM((2, half, BLOCK, D), F32)],
            )
            latest[:] = [keep]
            return (keep, to_other(send)), dkv

        def dx_chain(near, far):
            def first_sums(ids_ref, given, results):
                mine = my_bit(ids_ref, (0, 0))
                for i in range(2):
                    for p in range(half // 2):
                        for bit, target in ((mine, results[0]), (1 - mine, results[1])):
                            value = given[i][2 * p + bit].astype(F32) + given[2 + i][2 * p + bit].astype(F32)
                            target[i * (half // 2) + p] = value.astype(BF)

            kept, send = call(
                "dx_z", first_sums, ids, [near[0], far[0], near[1], far[1]], [vmem((half, BLOCK, D), BF)] * 2, latest
            )
            latest[:] = [kept]
            got = exchange(send, "z", 0)
            yield
            for i in range(1, bits_z - 1):
                kept, send = sum_call("dx_z", ids, [([(kept, got)], (0, i), nz >> (i + 1), 1, 1, 0)], latest)
                latest[:] = [kept]
                got = exchange(send, "z", i)
                yield
            rows, send = sum_call("dx_z", ids, [([(kept, got)], (0, 30), 1, 1, 1, 0)], latest)
            latest[:] = [rows]
            done["near"], done["far"] = rows.reshape(BLOCK, D), to_mirror(send.reshape(BLOCK, D))

        far_pair, dkv_far = dx_call(1)
        near_pair, dkv_near = dx_call(0)
        dx_steps = dx_chain(near_pair, far_pair)
        next(dx_steps)
        next(g_steps)
        (dw,) = call(
            "dw",
            functools.partial(dw_kernel, nz, rs, rr),
            ids,
            [xall, dkv_near, dkv_far, dq_mine, dq_other, gq_mine, gq_other, gb_o, gb_i, gb_b, ga],
            [vmem((2 * ndp, rd // 2, WQ), BF)],
            latest,
            [spread],
            limit=20,
        )
        latest[:] = [dw]

        def dw_chain():
            sources = yield from dp_scatter("w_dp", dw, None, rd // 2, WQ)
            if parts == 1:
                dw_dp = jnp.concatenate(whole_dp("w_dp", sources), axis=0)
                hidden_bias = dw_dp[:, 3 * HALF + 4 : 3 * HALF + 8].T.reshape(2 * nz, SLABS, rs)
                hidden_bias = jnp.transpose(hidden_bias, (0, 2, 1)).reshape(rd, SLABS)
                dw_dp = jnp.concatenate([dw_dp[:, : 3 * HALF + 4], hidden_bias, dw_dp[:, 3 * HALF + 8 :]], axis=1)
                sources = [(dw_dp.reshape(nz, 2 * rs, WQ), None)]
            else:
                sources = [tuple(array.reshape(half, 2 * rs, WQ) for array in pair) for pair in sources]
            keep, got = yield from z_scatter("w_z", sources)
            yield
            done["w"] = call(
                "w_last", functools.partial(last_kernel, rs), ids, [keep, got],
                [shape((rs, 3 * D), F32), shape((2, rs), F32), shape((1, rs), F32), shape((1, SLABS * rs), F32)]
                + [shape((1, rs), F32), shape((1, 2), F32)],
                latest,
            )
            latest[:] = [done["w"][0]]

        steps = {"x": dx_steps, "g": g_steps, "w": dw_chain()}
        for name in "gwxowgwXwgwgw" + "x" * bits_z + "X" + "gw" * (2 * bits_z):
            if name == "o":
                outputs = to_rows("outputs", out_near, out_b)
            elif name == "X":
                if "inputs" not in done:
                    while next(dx_steps, 0) is None:
                        pass
                    done["inputs"] = to_rows("dx_last", done["near"], done["far"])
            else:
                next(steps[name], 0)
        gb_qv, gb_out, gb_in, gb_back, grad_alphas = done["w"][1:]
        if rs < 16:
            grad_alphas = lax.psum(jnp.sum(ga, axis=1), MESH_AXES)
        return (
            outputs,
            done["inputs"],
            done["w"][0],
            gb_qv,
            done["g"][2],
            gb_out.reshape(rs),
            done["g"][1],
            gb_in.reshape(SLABS * rs),
            done["g"][0],
            gb_back.reshape(rs),
            grad_alphas.reshape(2),
        )

    return body


def solution(mesh):
    ndp, nseq = mesh.devices.shape
    n1 = math.isqrt(ndp)
    n2 = ndp // n1
    nz = nseq // 2
    fine = Mesh(mesh.devices.reshape(n1, n2, nz, 2), MESH_AXES)
    dp, seq = ("a", "b"), ("z", "c")
    rows = P(dp, seq, None)
    both = dp + seq
    return jax.shard_map(
        make_body(n1, n2, nz),
        mesh=fine,
        in_specs=(
            rows,
            P(both, None),
            P(None, both),
            P(both, None),
            P(both),
            P(both, None),
            P(both),
            P(both, None),
            P(both),
            P(),
            rows,
        ),
        out_specs=(
            rows,
            rows,
            P(both, None),
            P(None, both),
            P(both, None),
            P(both),
            P(both, None),
            P(both),
            P(both, None),
            P(both),
            P(),
        ),
        check_vma=False,
    )
```

```python
import functools
import math

import jax
import jax.numpy as jnp
from jax import lax
from jax.experimental import pallas as pl
from jax.experimental.pallas import tpu as pltpu
from jax.sharding import Mesh, PartitionSpec as P

D = 512
HEADS = 8
HEAD_DIM = 64
FF = 2048
BLOCK = 256
HALF = D // 2
CORE_HEADS = HEADS // 2
SLABS = FF // D
BF = jnp.bfloat16
F32 = jnp.float32
MESH_AXES = ("a", "b", "z", "c")
VMEM = pl.BlockSpec(memory_space=pltpu.VMEM)
SMEM = pl.BlockSpec(memory_space=pltpu.SMEM)
ANY = pl.BlockSpec(memory_space=pl.ANY)
WQ = 3 * HALF + 128
GELU_C = math.sqrt(2.0 / math.pi)


def dot(left, right):
    return jnp.dot(left, right, preferred_element_type=F32)


def ndot(left, right):
    return lax.dot_general(left, right, (((1,), (1,)), ((), ())), preferred_element_type=F32)


def flip(block):
    return block.T


def query_blocks(z, c, nz):
    near, far = 2 * z, 2 * (nz - 1 - z)
    return (near + c, far + c, near + 1 - c, far + 1 - c)


def over_keys(block, chunk):
    count = block + 1

    def step(i, unused):
        chunk(4 * i, 4)
        return unused

    lax.fori_loop(0, count // 4, step, 0)

    @pl.when(lax.rem(count, 4) >= 2)
    def _():
        chunk(count // 4 * 4, 2)

    @pl.when(lax.rem(count, 2) == 1)
    def _():
        chunk(block, 1)


def attend_blocks(blocks, kn, vt, qn, ot, lse, o, scratch):
    qz, s_s, m_s, l_s, acc_s = scratch
    rows = lax.broadcasted_iota(jnp.int32, (HALF, BLOCK), 0) // HEAD_DIM
    def one(i, unused):
        block = jnp.where(i == 0, blocks[0], blocks[1])
        qt = qn[i].astype(F32).T
        for h in range(CORE_HEADS):
            qz[h] = jnp.where(rows == h, qt, 0.0).astype(BF)
        m_s[...] = jnp.full_like(m_s, -1e30)
        l_s[...] = jnp.zeros_like(l_s)
        acc_s[...] = jnp.zeros_like(acc_s)

        def chunk(first, count):
            keys = kn[pl.ds(first, count)].reshape(count * BLOCK, HALF)
            for h in range(CORE_HEADS):
                s_s[h, : count * BLOCK] = dot(keys, qz[h])
            for h in range(CORE_HEADS):
                head = slice(h * HEAD_DIM, (h + 1) * HEAD_DIM)
                s = s_s[h, : count * BLOCK]
                old = m_s[h]
                new = jnp.maximum(old, jnp.max(s, axis=0, keepdims=True))
                p = jnp.exp(s - new)
                shrink = jnp.exp(old - new)
                m_s[h] = new
                l_s[h] = l_s[h] * shrink + jnp.sum(p, axis=0, keepdims=True)
                p = p.astype(BF)
                acc = acc_s[head, :] * shrink
                for j in range(count):
                    acc = acc + dot(vt[first + j, head, :], p[j * BLOCK : (j + 1) * BLOCK])
                acc_s[head, :] = acc

        over_keys(block, chunk)
        for h in range(CORE_HEADS):
            head = slice(h * HEAD_DIM, (h + 1) * HEAD_DIM)
            total = l_s[h]
            lse[i, h : h + 1, :] = m_s[h] + jnp.log(total)
            acc_s[head, :] = acc_s[head, :] / total
        value = acc_s[...]
        ot[i] = value
        o[i] = value.T.astype(BF)
        return unused

    lax.fori_loop(0, 2, one, 0)


def moves(sems, pairs):
    copies = [pltpu.make_async_copy(src, dst, sems.at[i]) for i, (src, dst) in enumerate(pairs)]
    for copy in copies:
        copy.start()
    return copies


def wait(copies):
    for copy in copies:
        copy.wait()


def pack_kernel(rs, ids, ins, outs, *refs):
    w_qkv, w_back, w_in, w_out, bias_qv, bias_out, bias_back, bias_in = refs[:8]
    gates, tile, sems = refs[8:]
    group = ids[4]
    loads = moves(sems, [(ins[i], refs[i]) for i in range(8)] + [(ins[10], gates)])
    rows = moves(
        sems.at[pl.ds(9, 4)],
        [(ins[8 + i].at[which], outs[3 + 2 * i + j]) for i in range(2) for j, which in enumerate((1 - group, group))],
    )
    wait(loads)
    tile[...] = jnp.zeros_like(tile)
    tile[0:2, :rs] = bias_qv[...].astype(F32)
    tile[2:3, :rs] = bias_out[...].astype(F32)
    tile[3:4, :rs] = bias_back[...].astype(F32)
    for i in range(SLABS):
        tile[4 + i : 5 + i, :rs] = bias_in[:, i * rs : (i + 1) * rs].astype(F32)
    outs[7][0:1, 0:2] = gates[...]
    turned = tile[...].T[:rs].astype(BF)
    q_keep, f_keep, give = outs[:3]

    def cut(ref, first, core):
        return ref[:, pl.ds(pl.multiple_of(first + core * HALF, HALF), HALF)]

    for i in range(3):
        q_keep[:, i * HALF : (i + 1) * HALF] = cut(w_qkv, i * D, ids[1])
        give[(9 + i) * rs : (10 + i) * rs] = cut(w_qkv, i * D, 1 - ids[1])
    q_keep[:, 3 * HALF :] = turned
    give[12 * rs :, :128] = turned
    give[12 * rs :, 128:] = jnp.zeros((rs, 128), BF)
    for f_out, core in ((f_keep, ids[1]), (give, 1 - ids[1])):
        f_out[: 4 * rs] = cut(w_back, 0, core)
        for i in range(SLABS):
            f_out[(4 + i) * rs : (5 + i) * rs] = cut(w_in, i * D, core)
        f_out[8 * rs : 9 * rs] = cut(w_out, 0, core)
    wait(rows)


def core_kernel(rs, ids, ins, outs):
    q_keep, f_keep, got = ins
    wq, wf = outs
    c = ids[1]
    wq[c] = q_keep[...]
    wf[c] = f_keep[...]
    wf[1 - c] = got[: 9 * rs]
    for i in range(3):
        wq[1 - c, :, i * HALF : (i + 1) * HALF] = got[(9 + i) * rs : (10 + i) * rs]
    wq[1 - c, :, 3 * HALF :] = got[12 * rs :, :128]


def my_bit(ids, where):
    index, bit = where
    return lax.rem(lax.shift_right_logical(ids[index], bit), 2)


def join(ids, own, got, outs, where, post=1):
    mine = my_bit(ids, where)
    pre = own.shape[0] // post
    for p in range(pre):
        out = outs[p * len(outs) // pre]
        at = 2 * p - 2 * pre // len(outs) * (p * len(outs) // pre)
        for q in range(post):
            out[(at + mine) * post + q] = own[p * post + q]
            out[(at + 1 - mine) * post + q] = got[p * post + q]


def first_kernel(nz, ndp, n2, rr, ids, ins, outs, spread, *scratch):
    xo, xs = ins[:2], ins[2:4]
    wq_pieces = ins[4:8]
    xall, wq, kn, vn, kt, vt, q_mine, q_other, ot, lse, o, bo, bb, bi = outs
    z, c = ids[0], ids[1]
    for p in range(nz // 2):
        chip = ids[4] * (nz // 2) + p
        for i, at in enumerate((chip, nz - 1 - chip)):
            xall[2 * at + c] = xo[i][p]
            xall[2 * at + 1 - c] = xs[i][p]

    def put(dp, half, value):
        wq[2 * dp + half] = value

    place_dp(ids, wq_pieces, ndp, n2, put)
    bias = wq[:, :, 3 * HALF :].reshape(D, 128).astype(F32)
    turned = bias.T
    bo[...] = turned[2:3]
    bb[...] = turned[3:4]
    lanes = lax.broadcasted_iota(jnp.int32, (D // rr, rr, 128), 2)
    for s in range(SLABS):
        spread[:, s] = jnp.where(lanes == 4 + s, bias.reshape(D // rr, rr, 128), 0.0)
    bi[...] = jnp.sum(spread[...].reshape(FF, 128).T[4:8], axis=0, keepdims=True)
    bias_q = jnp.where(c == 0, turned[0:1, :HALF], turned[0:1, HALF:])
    bias_v = jnp.where(c == 0, turned[1:2, :HALF], turned[1:2, HALF:])
    w_q = wq[:, :, :HALF].reshape(D, HALF)
    w_kv = wq[:, :, HALF : 3 * HALF].reshape(D, 2 * HALF)

    def project(i, unused):
        blocks = pl.ds(4 * i, 4)
        kv = dot(xall[blocks].reshape(4 * BLOCK, D), w_kv)
        key = kv[:, :HALF].astype(BF).reshape(4, BLOCK, HALF)
        value = (kv[:, HALF:] + bias_v).astype(BF).reshape(4, BLOCK, HALF)
        kn[blocks] = key
        vn[blocks] = value
        for j in range(4):
            kt[4 * i + j] = key[j].T
            vt[4 * i + j] = value[j].T
        return unused

    lax.fori_loop(0, nz // 2, project, 0)
    blocks = query_blocks(z, c, nz)
    q = dot(jnp.concatenate([xall[block] for block in blocks], axis=0), w_q) + bias_q
    q = (q.astype(BF).astype(F32) * (1.0 / math.sqrt(HEAD_DIM))).astype(BF)
    for i in range(4):
        (q_mine if i < 2 else q_other)[i % 2] = q[i * BLOCK : (i + 1) * BLOCK]
    attend_blocks(blocks[2:], kn, vt, q_other, ot, lse, o, scratch)


def place_dp(ids, pieces, ndp, n2, put):
    for i, piece in enumerate(pieces):
        far, half = i // 2, i % 2
        for j in range(ndp // 2):
            if half == 0:
                bit = lax.rem(ids[3], 2)
                dp = (2 * (j // n2) + (1 - bit if far else bit)) * n2 + j % n2
            else:
                bit = lax.rem(ids[5], 2)
                dp = j // (n2 // 2) * n2 + 2 * (j % (n2 // 2)) + (1 - bit if far else bit)
            put(dp, half, piece(j) if callable(piece) else piece[j])


def second_kernel(nz, ids, ins, outs, *scratch):
    kn, vt, qn = ins
    ot, lse, o = outs
    blocks = query_blocks(ids[0], ids[1], nz)
    attend_blocks(blocks[:2], kn, vt, qn, ot, lse, o, scratch)


def ffn_kernel(nz, ndp, n2, parts, ids, ins, outs, *refs):
    alphas, o_mine, got, xall, cot_a, cot_b, bo, bi, bb = ins[:9]
    pieces = ins[9:13]
    rows = pieces[0].shape[1]

    def received(i):
        return lambda j: got[pl.ds(2 * BLOCK + (i * (ndp // 2) + j) * rows, rows)]

    (out_near, out_far, dx1, d_mine, g_keep, give, gb_o, gb_i, gb_b, ga) = outs
    w, wo_s, wi_s, wb_s, mixed, h_s, r_s, dpre_s, dff_s, dattn_s = refs[:10]
    pre_s, dr_s = refs[10:12]
    c = ids[1]
    count = ndp * parts
    rd = D // count
    for core in range(2):
        own = pieces if core == 0 else [received(i) for i in range(4)]
        which = c if core == 0 else 1 - c
        lanes = pl.ds(pl.multiple_of(which * HALF, HALF), HALF)

        def put(dp, half, value):
            if parts == 1:
                w[which, 2 * dp + half] = value
                return
            for g in range(parts // 2):
                at = dp * parts + half * (parts // 2) + g
                part = value[9 * rd * g : 9 * rd * (g + 1)]
                wb_s[pl.ds(pl.multiple_of(at * 4 * rd, 4 * rd), 4 * rd), lanes] = part[: 4 * rd]
                at = pl.multiple_of(at * rd, rd)
                for s in range(SLABS):
                    wi_s[s, pl.ds(at, rd), lanes] = part[(4 + s) * rd : (5 + s) * rd]
                wo_s[pl.ds(at, rd), lanes] = part[8 * rd :]

        place_dp(ids, own, ndp, n2, put)
    if parts == 1:
        for half in range(2):
            lanes = slice(half * HALF, (half + 1) * HALF)
            whole = w[half].reshape(count, 9 * rd, HALF)
            wo_s[:, lanes] = whole[:, 8 * rd :].reshape(D, HALF)
            for s in range(SLABS):
                wi_s[s, :, lanes] = whole[:, (4 + s) * rd : (5 + s) * rd].reshape(D, HALF)
            wb_s[:, lanes] = whole[:, : 4 * rd].reshape(FF, HALF)
    mixed[c] = o_mine[...].reshape(2 * BLOCK, HALF)
    mixed[1 - c] = got[: 2 * BLOCK]
    alpha_attn, alpha_ffn = alphas[0:1, 0:1], alphas[0:1, 1:2]
    mine = query_blocks(ids[0], c, nz)
    both = 2 * BLOCK
    dy = jnp.concatenate([cot_a[...], cot_b[...]], axis=0).astype(F32)
    dff = (alpha_ffn * dy).astype(BF)
    dff_s[...] = dff
    attn = dot(mixed[0], wo_s[:HALF, :]) + dot(mixed[1], wo_s[HALF:, :]) + bo[...]
    x1 = jnp.concatenate([xall[mine[0]], xall[mine[1]]], axis=0).astype(F32) + alpha_attn * attn
    hidden = x1.astype(BF)
    h_s[...] = hidden
    x1_s = refs[12]
    attn_s = refs[13]
    x1_s[...] = x1
    attn_s[...] = attn
    for s in range(SLABS):
        lanes = slice(s * D, (s + 1) * D)
        pre_s[s] = dot(h_s[...], wi_s[s]) + bi[:, lanes]
        dr_s[s] = ndot(dff_s[...], wb_s[lanes, :])
    ff = None
    dx = None
    for s in range(SLABS):
        lanes = slice(s * D, (s + 1) * D)
        pre = pre_s[s]
        square = pre * pre
        up = 0.5 + 0.5 * jnp.tanh(pre * (GELU_C + (GELU_C * 0.044715) * square))
        r = pre * up
        r_s[:, lanes] = r.astype(BF)
        slope = up + r * (1.0 - up) * (2.0 * GELU_C + (6.0 * GELU_C * 0.044715) * square)
        dpre_s[:, lanes] = (dr_s[s] * slope).astype(BF)
    for s in range(SLABS):
        lanes = slice(s * D, (s + 1) * D)
        t2 = ndot(dpre_s[:, lanes], wi_s[s])
        dx = t2 if dx is None else dx + t2
    ff = dot(r_s[...], wb_s[...])
    ff = ff + bb[...]
    x1 = x1_s[...]
    out = (x1 + alpha_ffn * ff).astype(BF)
    out_near[...] = out[:BLOCK]
    out_far[...] = out[BLOCK:]
    dy = jnp.concatenate([cot_a[...], cot_b[...]], axis=0).astype(F32)
    dx = dx + dy
    dx1[0] = dx[:BLOCK]
    dx1[1] = dx[BLOCK:]
    dattn = (alpha_attn * dx).astype(BF)
    dattn_s[...] = dattn
    d_mine[...] = ndot(dattn, wo_s[pl.ds(pl.multiple_of(c * HALF, HALF), HALF), :]).astype(BF)
    give[:both, :] = ndot(dattn, wo_s[pl.ds(pl.multiple_of((1 - c) * HALF, HALF), HALF), :]).astype(BF)
    ga[...] = jnp.concatenate(
        [jnp.sum(dx * attn_s[...], axis=0, keepdims=True), jnp.sum(dy * ff, axis=0, keepdims=True)], axis=0
    )
    gb_o[...] = jnp.sum(dattn_s[...].astype(F32), axis=0, keepdims=True)
    gb_b[...] = jnp.sum(dff_s[...].astype(F32), axis=0, keepdims=True)
    for s in range(SLABS):
        lanes = slice(s * D, (s + 1) * D)
        gb_i[:, lanes] = jnp.sum(dpre_s[:, lanes].astype(F32), axis=0, keepdims=True)
    both_t = jnp.concatenate([mixed[0], mixed[1]], axis=1).T
    ht = h_s[...].T
    per = count // SLABS

    def columns(ref, first, core):
        return ref[:, pl.ds(pl.multiple_of(first + core * HALF, HALF), HALF)]

    def put_rows(core, first, value, groups):
        size = value.shape[0] // len(groups)
        for i, group in enumerate(groups):
            part = value[i * size : (i + 1) * size]
            if core == 0:
                g_keep[group, first : first + size, :] = part
            else:
                row = 2 * BLOCK + group * 9 * rd + first
                give[row : row + size, :] = part

    for core, which in enumerate((c, 1 - c)):
        put_rows(core, 8 * rd, dot(both_t, columns(dattn_s, 0, which)).astype(BF), range(count))
    for s in range(SLABS):
        lanes = slice(s * D, (s + 1) * D)
        rt = r_s[:, lanes].T
        for core, which in enumerate((c, 1 - c)):
            put_rows(core, (4 + s) * rd, dot(ht, columns(dpre_s, s * D, which)).astype(BF), range(count))
            put_rows(core, 0, dot(rt, columns(dff_s, 0, which)).astype(BF), range(s * per, (s + 1) * per))


def back_blocks(blocks, kn, vn, kt, q_in, d_in, ot, lse, dk_s, dv_s, dq_out, scratch):
    qz, qzt, oz, ozt, dq_s, p_s, dp_s = scratch
    rows = lax.broadcasted_iota(jnp.int32, (HALF, BLOCK), 0) // HEAD_DIM
    lanes = lax.broadcasted_iota(jnp.int32, (BLOCK, HALF), 1) // HEAD_DIM
    def one(i, gq):
        block = jnp.where(i == 0, blocks[0], blocks[1])
        q = q_in[i].astype(F32)
        d_o = d_in[pl.ds(pl.multiple_of(i * BLOCK, BLOCK), BLOCK), :].astype(F32)
        qt, dot_ = q.T, d_o.T
        product = dot_ * ot[i]
        deltas = []
        for h in range(CORE_HEADS):
            head = slice(h * HEAD_DIM, (h + 1) * HEAD_DIM)
            deltas.append(jnp.sum(product[head], axis=0, keepdims=True))
            qz[h] = jnp.where(lanes == h, q, 0.0).astype(BF)
            oz[h] = jnp.where(lanes == h, d_o, 0.0).astype(BF)
            qzt[h] = jnp.where(rows == h, qt, 0.0).astype(BF)
            ozt[h] = jnp.where(rows == h, dot_, 0.0).astype(BF)
        dq_s[...] = jnp.zeros_like(dq_s)

        def chunk(first, count):
            size = count * BLOCK
            keys = kn[pl.ds(first, count)].reshape(size, HALF)
            values = vn[pl.ds(first, count)].reshape(size, HALF)
            for h in range(CORE_HEADS):
                p_s[h, :size] = dot(keys, qzt[h])
                dp_s[h, :size] = dot(values, ozt[h])
            dk = dk_s[pl.ds(first, count)].reshape(size, HALF)
            dv = dv_s[pl.ds(first, count)].reshape(size, HALF)
            for h in range(CORE_HEADS):
                head = slice(h * HEAD_DIM, (h + 1) * HEAD_DIM)
                p = jnp.exp(p_s[h, :size] - lse[i, h : h + 1, :])
                ds = (p * (dp_s[h, :size] - deltas[h])).astype(BF)
                dv = dv + dot(p.astype(BF), oz[h])
                dk = dk + dot(ds, qz[h])
                dq = dq_s[head, :]
                for j in range(count):
                    dq = dq + dot(kt[first + j, head, :], ds[j * BLOCK : (j + 1) * BLOCK])
                dq_s[head, :] = dq
            dk_s[pl.ds(first, count)] = dk.reshape(count, BLOCK, HALF)
            dv_s[pl.ds(first, count)] = dv.reshape(count, BLOCK, HALF)

        over_keys(block, chunk)
        dq = (dq_s[...] * (1.0 / math.sqrt(HEAD_DIM))).T.astype(BF)
        dq_out[i] = dq
        return gq + jnp.sum(dq.astype(F32), axis=0, keepdims=True)

    return lax.fori_loop(0, 2, one, jnp.zeros((1, HALF), F32))


def back_kernel(nz, which, ids, ins, outs, *scratch):
    kn, vn, kt, qn, ot, lse, d_o = ins[:7]
    dk, dv, dq, gq = outs
    if which == 0:
        dk[...] = jnp.zeros_like(dk)
        dv[...] = jnp.zeros_like(dv)
    blocks = query_blocks(ids[0], ids[1], nz)[2 * which : 2 * which + 2]
    gq[...] = back_blocks(blocks, kn, vn, kt, qn, d_o, ot, lse, dk, dv, dq, scratch)


def dx_kernel(nz, which, ids, ins, outs, dxs):
    wq, dk, dv, dq_mine, dq_other, dx1 = ins
    keep, send, dkv = outs
    z, c = ids[0], ids[1]
    half = nz // 2
    place = lax.rem(z, half)
    w_q = wq[:, :, :HALF].reshape(D, HALF)
    w_kv = wq[:, :, HALF : 3 * HALF].reshape(D, 2 * HALF)
    for core, (target, dq) in enumerate(((keep, dq_mine), (send, dq_other))):
        for p in range(half):
            chip = ids[4] * half + p
            block = 2 * (chip if which == 0 else nz - 1 - chip) + (c if core == 0 else 1 - c)
            dkv[core * half + p, :, :HALF] = dk[block].astype(BF)
            dkv[core * half + p, :, HALF:] = dv[block].astype(BF)
        rows = dkv[core * half : (core + 1) * half].reshape(half * BLOCK, 2 * HALF)
        dxs[core] = ndot(rows, w_kv).reshape(half, BLOCK, D)
        value = ndot(dq[which], w_q)
        if core == 0:
            value = value + dx1[which]
        dxs[core, place] = dxs[core, place] + value
        target[...] = dxs[core].astype(BF)


def dw_kernel(nz, rs, rr, ids, ins, outs, spread):
    xall, dkv_near, dkv_far, dq_mine, dq_other, gq_mine, gq_other, gb_o, gb_i, gb_b, ga = ins
    (dw,) = outs
    z, c = ids[0], ids[1]
    half = nz // 2
    rows = []
    for which in range(2):
        for core in range(2):
            for p in range(half):
                chip = ids[4] * half + p
                rows.append(xall[2 * (chip if which == 0 else nz - 1 - chip) + (c if core == 0 else 1 - c)])
    dkv = jnp.concatenate([ref[...].reshape(nz * BLOCK, 2 * HALF) for ref in (dkv_near, dkv_far)], axis=0)
    acc_kv = dot(jnp.concatenate(rows, axis=0).T, dkv)
    gv = jnp.zeros((1, HALF), F32)
    for ref in (dkv_near, dkv_far):
        for i in range(nz):
            gv = gv + jnp.sum(ref[i, :, HALF:].astype(F32), axis=0, keepdims=True)
    queries = jnp.concatenate([xall[block] for block in query_blocks(z, c, nz)], axis=0).T
    dq = jnp.concatenate([dq_mine[...].reshape(2 * BLOCK, HALF), dq_other[...].reshape(2 * BLOCK, HALF)], axis=0)
    acc_q = dot(queries, dq)
    gq = gq_mine[...] + gq_other[...]
    nothing = jnp.zeros((1, HALF), F32)
    own = [jnp.concatenate([jnp.where(c == 0, g, nothing), jnp.where(c == 0, nothing, g)], axis=1) for g in (gq, gv)]
    tile = jnp.concatenate(own + [gb_o[...], gb_b[...], jnp.zeros((124, D), F32)], axis=0).T
    spread[...] = jnp.broadcast_to(gb_i[...], (128, FF)).T.reshape(D // rr, SLABS, rr, 128)
    lanes = lax.broadcasted_iota(jnp.int32, (D // rr, rr, 128), 2)
    tile = tile.reshape(D // rr, rr, 128)
    for s in range(SLABS):
        tile = jnp.where(lanes == 4 + s, spread[:, s], tile)
    tile = tile.reshape(D, 128)
    if rs >= 16:
        me = ids[2]
        lane = lax.broadcasted_iota(jnp.int32, (D, 128), 1) - 8 - 6 * (me // rs)
        mine = lax.rem(lax.broadcasted_iota(jnp.int32, (D, 128), 0), rs) == lax.rem(me, rs)
        gates = jnp.sum(ga[...], axis=1, keepdims=True)
        for which in range(2):
            rest = gates[which : which + 1]
            for i in range(3):
                high = rest.astype(BF).astype(F32)
                tile = jnp.where(mine & (lane == 2 * i + which), high, tile)
                rest = rest - high
    rows = dw.shape[1]
    dw[:, :, :HALF] = acc_q.astype(BF).reshape(D // rows, rows, HALF)
    dw[:, :, HALF : 3 * HALF] = acc_kv.astype(BF).reshape(D // rows, rows, 2 * HALF)
    dw[:, :, 3 * HALF :] = tile.astype(BF).reshape(D // rows, rows, 128)


def sum_kernel(plans, ids, ins, outs):
    outs = list(outs)
    for numbers, size, where, pre, post, stride, first, flat in plans:

        def total(static, dynamic):
            source = static * stride // size
            index = (static + dynamic) * stride + first - source * size
            refs = [ins[number] for number in numbers[source]]
            value = refs[0][index]
            if len(refs) == 2 and flat is None:
                value = value.astype(F32) + refs[1][index].astype(F32)
            elif len(refs) == 2:
                rows = value.shape[0]
                start = pl.multiple_of(flat + index * rows, 16)
                value = value.astype(F32) + refs[1][pl.ds(start, rows), :].astype(F32)
            return value

        if where is None:
            out = outs.pop(0)
            for index in range(out.shape[0]):
                out[index] = total(index, 0).astype(out.dtype)
            continue
        keep, send = outs.pop(0), outs.pop(0)
        mine = my_bit(ids, where)
        for p in range(pre):
            for q in range(post):
                keep[p * post + q] = total(2 * p * post + q, mine * post).astype(keep.dtype)
                send[p * post + q] = total(2 * p * post + q, (1 - mine) * post).astype(send.dtype)


def grads_kernel(rs, ids, ins, outs):
    own, other = ins
    w_back, w_in, w_out, token = outs
    token[...] = jnp.zeros_like(token)
    for ref, core in ((own, ids[1]), (other, 1 - ids[1])):

        def lanes(first):
            return pl.ds(pl.multiple_of(first + core * HALF, HALF), HALF)

        value = ref[0].astype(F32)
        w_back[:, lanes(0)] = value[: 4 * rs]
        for s in range(SLABS):
            w_in[:, lanes(s * D)] = value[(4 + s) * rs : (5 + s) * rs]
        w_out[:, lanes(0)] = value[8 * rs :]


def last_kernel(rs, ids, ins, outs):
    own, other = ins
    w_qkv, gb_qv, gb_o, gb_i, gb_b, gates = outs
    for ref, core in ((own, ids[1]), (other, 1 - ids[1])):
        value = ref[0].astype(F32)
        for i in range(3):
            lanes = pl.ds(pl.multiple_of(i * D + core * HALF, HALF), HALF)
            w_qkv[:, lanes] = value[:, i * HALF : (i + 1) * HALF]
    sums = own[0, :, 3 * HALF :] + other[0, :, 3 * HALF :].astype(F32)
    lane = lax.broadcasted_iota(jnp.int32, (1, 128), 1)
    column = jnp.sum(sums, axis=0, keepdims=True)
    for which in range(2):
        used = (lane >= 8) & (lax.rem(lane, 2) == which)
        gates[:, which : which + 1] = jnp.sum(jnp.where(used, column, 0.0), axis=1, keepdims=True)
    by_row = jnp.concatenate([sums, jnp.zeros((128 - rs, 128), F32)], axis=0).T
    gb_qv[...] = by_row[:2, :rs]
    gb_o[...] = by_row[2:3, :rs]
    gb_b[...] = by_row[3:4, :rs]
    for s in range(SLABS):
        gb_i[:, s * rs : (s + 1) * rs] = by_row[4 + s : 5 + s, :rs]


def shape(dims, kind):
    return jax.ShapeDtypeStruct(dims, kind)


def vmem(dims, kind):
    return pltpu.VMEM(dims, kind)


def in_hbm(array):
    return pltpu.with_memory_space_constraint(array, pltpu.HBM)


def cost(megabytes):
    return pl.CostEstimate(flops=0, bytes_accessed=megabytes * 2**20, transcendentals=0)


def call(
    name, kernel, ids, ins, outs, after=(), scratch=(), limit=12, weight=0, where=None, aliases=None, out=VMEM
):
    count, waits = len(ins), len(after)

    def run(*refs):
        given, rest = refs[:count], refs[count + waits :]
        kernel(ids(), given, rest[: len(outs)], *rest[len(outs) :])

    return pl.pallas_call(
        run,
        out_shape=tuple(outs),
        in_specs=(where or [VMEM] * count) + [ANY] * waits,
        out_specs=out if isinstance(out, tuple) else (out,) * len(outs),
        scratch_shapes=list(scratch),
        compiler_params=pltpu.CompilerParams(vmem_limit_bytes=limit * 2**20),
        cost_estimate=cost(weight),
        input_output_aliases=aliases or {},
        name=name,
    )(*ins, *after)


def pack_call(ids, rs, ins):
    return call(
        "pack",
        functools.partial(pack_kernel, rs),
        ids,
        [in_hbm(array) for array in ins],
        [vmem((rs, WQ), BF), vmem((9 * rs, HALF), BF), vmem((13 * rs, HALF), BF)] + [vmem((BLOCK, D), BF)] * 4
        + [vmem((8, 128), F32)],
        scratch=[pltpu.VMEM(array.shape, BF) for array in ins[:8]]
        + [pltpu.VMEM((1, 2), F32), pltpu.VMEM((128, 128), F32), pltpu.SemaphoreType.DMA((13,))],
        where=[ANY] * 11,
    )


def join_call(name, ids, jobs, after=(), extra=None, extra_ins=(), extra_outs=(), cuts=None):
    ins, outs, spans = [], [], []
    for (own, got, _, _), cut in zip(jobs, cuts or [1] * len(jobs)):
        ins += [own, got]
        spans.append(slice(len(outs), len(outs) + cut))
        outs += [vmem((2 * own.shape[0] // cut,) + own.shape[1:], own.dtype)] * cut
    number = len(outs)

    def kernel(ids_ref, given, results):
        for i, (_, _, where, post) in enumerate(jobs):
            join(ids_ref, given[2 * i], given[2 * i + 1], results[spans[i]], where, post)
        if extra is not None:
            extra(ids_ref, given[2 * len(jobs) :], results[number:])

    return call(name, kernel, ids, ins + list(extra_ins), outs + list(extra_outs), after)


def sum_call(name, ids, jobs, after=(), last=BF, flat=None):
    ins, outs, plans = [], [], []

    def number(array):
        for i, other in enumerate(ins):
            if other is array:
                return i
        ins.append(array)
        return len(ins) - 1

    for sources, where, pre, post, stride, first in jobs:
        numbers = [tuple(number(array) for array in pair if array is not None) for pair in sources]
        tail = sources[0][0].shape[1:]
        size = sources[0][0].shape[0]
        plans.append((numbers, size, where, pre, post, stride, first, flat))
        if where is None:
            outs.append(vmem((size * len(sources) // stride,) + tail, last))
        else:
            outs += [vmem((pre * post,) + tail, last), vmem((pre * post,) + tail, BF)]
    return call(name, functools.partial(sum_kernel, plans), ids, ins, outs, after)


def make_body(n1, n2, nz):
    ndp = n1 * n2
    nsh = ndp * nz * 2
    rs = D // nsh
    rd = D // ndp
    half = nz // 2
    parts = 2 * nz if rs % 16 == 0 else 1
    rr = rd // parts
    nh = 9 * rd // 2
    swap = [(0, 1), (1, 0)]
    bits_a, bits_b, bits_z = (count.bit_length() - 1 for count in (n1, n2, nz))
    counts = {"a": n1, "b": n2, "z": nz}
    slot = {"a": 3, "b": 5, "z": 0}

    def to_mirror(array):
        return lax.ppermute(array, "z", [(s, nz - 1 - s) for s in range(nz)])

    def exchange(array, name, bit):
        return lax.ppermute(array, name, [(s, s ^ (1 << bit)) for s in range(counts[name])])

    def to_other(array):
        return lax.ppermute(array, "c", swap)

    def body(inputs, w_qkv, bias_qv, w_out, bias_out, w_in, bias_in, w_back, bias_back, alphas, cotangent):
        z, c = lax.axis_index("z"), lax.axis_index("c")
        a, b = lax.axis_index("a"), lax.axis_index("b")

        def ids():
            z, c = lax.axis_index("z"), lax.axis_index("c")
            a, b = lax.axis_index("a"), lax.axis_index("b")
            return (z, c, ((a * n2 + b) * nz + z) * 2 + c, a, z // half, b)


        latest = []

        def hand_on(ids_ref, given, results):
            for source, target in zip(given, results):
                target[...] = source[...]

        def step(name, jobs, extra=(), cuts=None, others=()):
            result = join_call(
                name, ids, jobs, latest + list(others), hand_on, extra, [vmem(e.shape, e.dtype) for e in extra], cuts
            )
            latest[:] = [result[0]]
            return result


        q_keep, f_keep, give, x_give, x_keep, cot_give, cot_a, gates = pack_call(
            ids, rs,
            [w_qkv, w_back, w_in, w_out, bias_qv, bias_out[None], bias_back[None], bias_in[None], inputs, cotangent,
             alphas[None]],
        )
        wq, wf = call(
            "core", functools.partial(core_kernel, rs), ids, [q_keep, f_keep, to_other(give)],
            [vmem((2, rs, WQ), BF), vmem((2, 9 * rs, HALF), BF)],
        )
        latest[:] = [wq]
        wq, wf = wq.reshape(1, 2 * rs, WQ), wf.reshape(1, 2 * 9 * rs, HALF)
        wf = wf.reshape(2 * 9 * rs, HALF)
        q_got = exchange(wq, "z", bits_z - 1)
        wf_parts = [(wf, 0)]
        for i in reversed(range(bits_z)):
            wf_parts += [(exchange(part, "z", i), place | (1 << i)) for part, place in wf_parts]
        wf_near = [part for part, place in wf_parts if place == 1]
        for i in reversed(range(1, bits_z)):
            (wq,) = step("q_z", [(wq, q_got, (0, i), 1)])
            q_got = exchange(wq, "z", i - 1)
        q_first, q_second, x_keep, x_give = step(
            "q_z", [(wq, q_got, (0, 0), 1)], [x_keep, x_give], [2], wf_near
        )
        if parts == 1:
            wq = jnp.concatenate([q_first, q_second], axis=0).reshape(rd, WQ)
            hidden_bias = wq[:, 3 * HALF + 4 : 3 * HALF + 8].reshape(2 * nz, rs, SLABS)
            hidden_bias = jnp.transpose(hidden_bias, (0, 2, 1)).reshape(SLABS, rd).T
            wq = jnp.concatenate([wq[:, : 3 * HALF + 4], hidden_bias, wq[:, 3 * HALF + 8 :]], axis=1)
            q_first, q_second = wq[: rd // 2], wq[rd // 2 :]
        q_first, q_second = q_first.reshape(1, rd // 2, WQ), q_second.reshape(1, rd // 2, WQ)
        x_far = to_mirror(x_give)
        for i in reversed(range(1, bits_b)):
            got = exchange(q_first, "b", i), exchange(q_second, "a", i)
            q_first, q_second = step("q_dp", [(q_first, got[0], (5, i), 1), (q_second, got[1], (3, i), 1)])
        q_got = exchange(q_first, "b", 0), exchange(q_second, "a", 0)
        own = x_keep[None]
        own_got = exchange(own, "z", max(bits_z - 2, 0))

        q_first, q_second = step("q_dp", [(q_first, q_got[0], (5, 0), 1), (q_second, q_got[1], (3, 0), 1)])
        for i in reversed(range(1, bits_a)):
            got = exchange(q_first, "a", i), exchange(q_second, "b", i)
            q_first, q_second = step("q_dp", [(q_first, got[0], (3, i), n2), (q_second, got[1], (5, i), 1)])
        wq_pieces = [q_first, q_second, exchange(q_first, "a", 0), exchange(q_second, "b", 0)]

        def in_place(ids_ref, given, results):
            for group in range(2):

                @pl.when(ids_ref[4] == group)
                def _():
                    for ref, (_, place) in zip(given, wf_parts):
                        at = lax.rem(lax.bitwise_xor(ids_ref[0], place), half)
                        results[group ^ (place // half)][at] = ref[...]

        halves = vmem((half, 2 * 9 * rs, HALF), BF)
        first, second = call("f_z", in_place, ids, [part for part, _ in wf_parts], [halves, halves], latest)
        latest[:] = [first]
        if parts == 1:
            wf = jnp.concatenate([first, second], axis=0).reshape(nz, 2, 9 * rs, HALF)
            wf = jnp.concatenate(
                [wf[:, :, : 4 * rs].reshape(4 * rd, HALF)]
                + [wf[:, :, (4 + s) * rs : (5 + s) * rs].reshape(rd, HALF) for s in range(SLABS)]
                + [wf[:, :, 8 * rs :].reshape(rd, HALF)],
                axis=0,
            )
            first, second = wf[:nh], wf[nh:]
        first, second = first.reshape(1, nh, HALF), second.reshape(1, nh, HALF)
        far_rows, cot_give = call(
            "x_far", hand_on, ids, [x_far, cot_give], [vmem((BLOCK, D), BF)] * 2, latest + [own_got]
        )
        latest[:] = [far_rows]
        cot_b = to_mirror(cot_give)
        far_rows = far_rows[None]
        for i in reversed(range(1, bits_z - 1)):
            far_got = exchange(far_rows, "z", i)
            own, far_rows = step("x_z", [(own, own_got, (0, i), 1), (far_rows, far_got, (0, i), 1)])
            own_got = exchange(own, "z", i - 1)
        far_got = exchange(far_rows, "z", 0)

        for i in reversed(range(bits_b)):
            got = exchange(first, "b", i), exchange(second, "a", i)
            first, second = step("f_dp", [(first, got[0], (5, i), 1), (second, got[1], (3, i), 1)])
        for i in reversed(range(1, bits_a)):
            got = exchange(first, "a", i), exchange(second, "b", i)
            first, second = step("f_dp", [(first, got[0], (3, i), n2), (second, got[1], (5, i), 1)])
        wf_pieces = [first, second, exchange(first, "a", 0), exchange(second, "b", 0)]

        def rows_of_all(ids_ref, given, results):
            own_ref, own_got_ref, far_ref, far_got_ref = given
            base, mine = ids_ref[4] * half, my_bit(ids_ref, (0, 0))
            for p in range(half // 2):
                for own_part, far_part, at in (
                    (own_ref, far_ref, base + 2 * p + mine),
                    (own_got_ref, far_got_ref, base + 2 * p + 1 - mine),
                ):
                    results[0][at - base] = own_part[p]
                    results[1][at - base] = far_part[p]

        xo = call(
            "x_all", rows_of_all, ids, [own, own_got, far_rows, far_got], [vmem((half, BLOCK, D), BF)] * 2,
            latest + wq_pieces[2:] + [cot_b],
        )
        latest[:] = [xo[0]]
        xs = [to_other(part) for part in xo]

        nb = 2 * nz
        heads_t = pltpu.VMEM((CORE_HEADS, HALF, BLOCK), BF)
        scores = pltpu.VMEM((CORE_HEADS, 4 * BLOCK, BLOCK), F32)
        scratch = [
            heads_t,
            scores,
            pltpu.VMEM((CORE_HEADS, 1, BLOCK), F32),
            pltpu.VMEM((CORE_HEADS, 1, BLOCK), F32),
            pltpu.VMEM((HALF, BLOCK), F32),
        ]
        natural, turned = (nb, BLOCK, HALF), (nb, HALF, BLOCK)
        two, two_t = (2, BLOCK, HALF), (2, HALF, BLOCK)
        two_lse = (2, CORE_HEADS, BLOCK)
        spread = pltpu.VMEM((D // rr, SLABS, rr, 128), F32)
        (xall, wq, kn, vn, kt, vt, q_mine, q_other, ot_other, lse_other, o_send, bo, bb, bi) = call(
            "first",
            functools.partial(first_kernel, nz, ndp, n2, rr),
            ids,
            [*xo, *xs, *wq_pieces],
            [
                vmem((nb, BLOCK, D), BF),
                vmem((2 * ndp, rd // 2, WQ), BF),
                vmem(natural, BF),
                vmem(natural, BF),
                vmem(turned, BF),
                vmem(turned, BF),
                vmem(two, BF),
                vmem(two, BF),
                vmem(two_t, F32),
                vmem(two_lse, F32),
                vmem(two, BF),
                vmem((1, D), F32),
                vmem((1, D), F32),
                vmem((1, FF), F32),
            ],
            latest,
            [spread] + scratch,
            limit=24,
        )

        def give_kernel(ids_ref, given, results):
            row = 0
            for part in given:
                for i in range(part.shape[0]):
                    results[0][row : row + part.shape[1]] = part[i]
                    row += part.shape[1]

        (give,) = call(
            "give", give_kernel, ids, [o_send, *wf_pieces], [vmem((2 * BLOCK + 2 * ndp * nh, HALF), BF)],
            limit=24,
        )
        ffn_got = to_other(give)
        ot_mine, lse_mine, o_mine = call(
            "second",
            functools.partial(second_kernel, nz),
            ids,
            [kn, vt, q_mine],
            [vmem(two_t, F32), vmem(two_lse, F32), vmem(two, BF)],
            (),
            scratch,
            limit=24,
        )

        grouped = (ndp * parts, 9 * rd // parts, HALF)
        (out_near, out_far, dx1, d_mine, g_keep, give, gb_o, gb_i, gb_b, ga) = call(
            "ffn",
            functools.partial(ffn_kernel, nz, ndp, n2, parts),
            ids,
            [gates, o_mine, ffn_got, xall, cot_a, cot_b, bo, bi, bb, *wf_pieces],
            [
                vmem((BLOCK, D), BF),
                vmem((BLOCK, D), BF),
                vmem((2, BLOCK, D), F32),
                vmem((2 * BLOCK, HALF), BF),
                vmem(grouped, BF),
                vmem((2 * BLOCK + ndp * 9 * rd, HALF), BF),
                vmem((1, D), F32),
                vmem((1, FF), F32),
                vmem((1, D), F32),
                vmem((2, D), F32),
            ],
            scratch=[
                pltpu.VMEM((2, 2 * ndp, nh, HALF) if parts == 1 else (8, 128), BF),
                pltpu.VMEM((D, D), BF),
                pltpu.VMEM((SLABS, D, D), BF),
                pltpu.VMEM((FF, D), BF),
                pltpu.VMEM((2, 2 * BLOCK, HALF), BF),
                pltpu.VMEM((2 * BLOCK, D), BF),
                pltpu.VMEM((2 * BLOCK, FF), BF),
                pltpu.VMEM((2 * BLOCK, FF), BF),
                pltpu.VMEM((2 * BLOCK, D), BF),
                pltpu.VMEM((2 * BLOCK, D), BF),
                pltpu.VMEM((SLABS, 2 * BLOCK, D), F32),
                pltpu.VMEM((SLABS, 2 * BLOCK, D), F32),
                pltpu.VMEM((2 * BLOCK, D), F32),
                pltpu.VMEM((2 * BLOCK, D), F32),
            ],
            limit=36,
        )
        back_got = to_other(give)
        back_scratch = [
            pltpu.VMEM((CORE_HEADS, BLOCK, HALF), BF),
            heads_t,
            pltpu.VMEM((CORE_HEADS, BLOCK, HALF), BF),
            heads_t,
            pltpu.VMEM((HALF, BLOCK), F32),
            scores,
            scores,
        ]
        back_out = [vmem(natural, F32), vmem(natural, F32), vmem(two, BF), vmem((1, HALF), F32)]
        dk, dv, dq_mine, gq_mine = call(
            "back_first",
            functools.partial(back_kernel, nz, 0),
            ids,
            [kn, vn, kt, q_mine, ot_mine, lse_mine, d_mine],
            back_out,
            scratch=back_scratch,
            limit=24,
        )

        latest[:] = [gq_mine]
        done = {}

        def along(axis, count, pre, post):
            return [(axis, i, pre * (count >> (i + 1)), post) for i in range(count.bit_length() - 1)]

        def dp_scatter(name, kept, got, rows, columns, flat=None):
            axes = (along("b", n2, n1, 1) + along("a", n1, 1, 1), along("a", n1, 1, n2) + along("b", n2, 1, 1))
            whole = (kept.reshape(2 * ndp, rows, columns), got)
            state = [(whole, 2, 0), (whole, 2, 1)]
            for i in range(len(axes[0])):
                result = sum_call(
                    name,
                    ids,
                    [
                        ([pair], (slot[axis], bit), pre, post, stride, first)
                        for (pair, stride, first), (axis, bit, pre, post) in zip(state, (axes[0][i], axes[1][i]))
                    ],
                    latest,
                    flat=flat if i == 0 else None,
                )
                latest[:] = [result[0]]
                state = [
                    ((result[2 * j], exchange(result[2 * j + 1], axes[j][i][0], axes[j][i][1])), 1, 0)
                    for j in range(2)
                ]
                yield
            return [pair for pair, _, _ in state]

        def z_scatter(name, sources):
            for _, i, pre, _ in along("z", nz, 1, 1):
                kept, send = sum_call(name, ids, [(sources, (slot["z"], i), pre, 1, 1, 0)], latest)
                latest[:] = [kept]
                sources = [(kept, exchange(send, "z", i))]
                yield
            rows, columns = kept.shape[1] // 2, kept.shape[2]
            sources = [tuple(array.reshape(2, rows, columns) for array in sources[0])]
            keep, send = sum_call(name, ids, [(sources, (1, 0), 1, 1, 1, 0)], latest, F32)
            latest[:] = [keep]
            return keep, to_other(send)

        def whole_dp(name, sources):
            return [part[0] for part in sum_call(name, ids, [([pair], None, 0, 0, 1, 0) for pair in sources], latest)]

        def g_chain():
            sources = yield from dp_scatter("g_dp", g_keep, back_got, nh, HALF, 2 * BLOCK)
            if parts == 1:
                g_dp = jnp.concatenate(whole_dp("g_dp", sources), axis=0)
                g_dp = jnp.concatenate(
                    [g_dp[: 4 * rd].reshape(nz, 2, 4 * rs, HALF)]
                    + [g_dp[(4 + s) * rd : (5 + s) * rd].reshape(nz, 2, rs, HALF) for s in range(SLABS)]
                    + [g_dp[8 * rd :].reshape(nz, 2, rs, HALF)],
                    axis=2,
                )
                sources = [(g_dp.reshape(nz, 2 * 9 * rs, HALF), None)]
            else:
                sources = [tuple(array.reshape(half, 2 * 9 * rs, HALF) for array in pair) for pair in sources]
            keep, got = yield from z_scatter("g_z", sources)
            yield
            done["g"] = call(
                "g_last", functools.partial(grads_kernel, rs), ids, [keep, got],
                [pltpu.HBM((4 * rs, D), F32), pltpu.HBM((rs, FF), F32), pltpu.HBM((rs, D), F32),
                 vmem((8, 128), F32)],
                latest,
            )
            latest[:] = [done["g"][3]]

        g_steps = g_chain()
        next(g_steps)
        dk, dv, dq_other, gq_other = call(
            "back_second",
            functools.partial(back_kernel, nz, 1),
            ids,
            [kn, vn, kt, q_other, ot_other, lse_other, back_got, dk, dv],
            back_out,
            latest,
            back_scratch,
            limit=24,
            aliases={7: 0, 8: 1},
        )
        def out_kernel(ids_ref, given, results, sems):
            group = ids_ref[4]
            copies = moves(sems, [(given[0], results[0].at[group]), (given[1], results[0].at[1 - group])])
            results[1][...] = jnp.zeros_like(results[1])
            wait(copies)

        def to_rows(name, own, got):
            rows, token = call(
                name, out_kernel, ids, [own, got], [pltpu.HBM((2, BLOCK, D), BF), vmem((8, 128), F32)], latest,
                [pltpu.SemaphoreType.DMA((2,))], where=[ANY, ANY],
                out=(pl.BlockSpec(memory_space=pltpu.HBM), VMEM),
            )
            latest[:] = [token]
            return rows

        latest[:] = [gq_other]
        out_b = to_mirror(out_far)
        latest.append(out_b)

        def dx_call(which):
            keep, send, dkv = call(
                "dx",
                functools.partial(dx_kernel, nz, which),
                ids,
                [wq, dk, dv, dq_mine, dq_other, dx1],
                [vmem((half, BLOCK, D), BF), vmem((half, BLOCK, D), BF), vmem((nz, BLOCK, 2 * HALF), BF)],
                latest,
                [pltpu.VMEM((2, half, BLOCK, D), F32)],
            )
            latest[:] = [keep]
            return (keep, to_other(send)), dkv

        def dx_chain(near, far):
            def first_sums(ids_ref, given, results):
                mine = my_bit(ids_ref, (0, 0))
                for i in range(2):
                    for p in range(half // 2):
                        for bit, target in ((mine, results[0]), (1 - mine, results[1])):
                            value = given[i][2 * p + bit].astype(F32) + given[2 + i][2 * p + bit].astype(F32)
                            target[i * (half // 2) + p] = value.astype(BF)

            kept, send = call(
                "dx_z", first_sums, ids, [near[0], far[0], near[1], far[1]], [vmem((half, BLOCK, D), BF)] * 2, latest
            )
            latest[:] = [kept]
            got = exchange(send, "z", 0)
            yield
            for i in range(1, bits_z - 1):
                kept, send = sum_call("dx_z", ids, [([(kept, got)], (0, i), nz >> (i + 1), 1, 1, 0)], latest)
                latest[:] = [kept]
                got = exchange(send, "z", i)
                yield
            rows, send = sum_call("dx_z", ids, [([(kept, got)], (0, 30), 1, 1, 1, 0)], latest)
            latest[:] = [rows]
            done["near"], done["far"] = rows.reshape(BLOCK, D), to_mirror(send.reshape(BLOCK, D))

        far_pair, dkv_far = dx_call(1)
        near_pair, dkv_near = dx_call(0)
        dx_steps = dx_chain(near_pair, far_pair)
        next(dx_steps)
        next(g_steps)
        (dw,) = call(
            "dw",
            functools.partial(dw_kernel, nz, rs, rr),
            ids,
            [xall, dkv_near, dkv_far, dq_mine, dq_other, gq_mine, gq_other, gb_o, gb_i, gb_b, ga],
            [vmem((2 * ndp, rd // 2, WQ), BF)],
            latest,
            [spread],
            limit=20,
        )
        latest[:] = [dw]

        def dw_chain():
            sources = yield from dp_scatter("w_dp", dw, None, rd // 2, WQ)
            if parts == 1:
                dw_dp = jnp.concatenate(whole_dp("w_dp", sources), axis=0)
                hidden_bias = dw_dp[:, 3 * HALF + 4 : 3 * HALF + 8].T.reshape(2 * nz, SLABS, rs)
                hidden_bias = jnp.transpose(hidden_bias, (0, 2, 1)).reshape(rd, SLABS)
                dw_dp = jnp.concatenate([dw_dp[:, : 3 * HALF + 4], hidden_bias, dw_dp[:, 3 * HALF + 8 :]], axis=1)
                sources = [(dw_dp.reshape(nz, 2 * rs, WQ), None)]
            else:
                sources = [tuple(array.reshape(half, 2 * rs, WQ) for array in pair) for pair in sources]
            keep, got = yield from z_scatter("w_z", sources)
            yield
            done["w"] = call(
                "w_last", functools.partial(last_kernel, rs), ids, [keep, got],
                [shape((rs, 3 * D), F32), shape((2, rs), F32), shape((1, rs), F32), shape((1, SLABS * rs), F32)]
                + [shape((1, rs), F32), shape((1, 2), F32)],
                latest,
            )
            latest[:] = [done["w"][0]]

        steps = {"x": dx_steps, "g": g_steps, "w": dw_chain()}
        for name in "gwxowgwXwgwgw" + "x" * bits_z + "X" + "gw" * (2 * bits_z):
            if name == "o":
                outputs = to_rows("outputs", out_near, out_b)
            elif name == "X":
                if "inputs" not in done:
                    while next(dx_steps, 0) is None:
                        pass
                    done["inputs"] = to_rows("dx_last", done["near"], done["far"])
            else:
                next(steps[name], 0)
        gb_qv, gb_out, gb_in, gb_back, grad_alphas = done["w"][1:]
        if rs < 16:
            grad_alphas = lax.psum(jnp.sum(ga, axis=1), MESH_AXES)
        return (
            outputs,
            done["inputs"],
            done["w"][0],
            gb_qv,
            done["g"][2],
            gb_out.reshape(rs),
            done["g"][1],
            gb_in.reshape(SLABS * rs),
            done["g"][0],
            gb_back.reshape(rs),
            grad_alphas.reshape(2),
        )

    return body


def solution(mesh):
    ndp, nseq = mesh.devices.shape
    n1 = math.isqrt(ndp)
    n2 = ndp // n1
    nz = nseq // 2
    fine = Mesh(mesh.devices.reshape(n1, n2, nz, 2), MESH_AXES)
    dp, seq = ("a", "b"), ("z", "c")
    rows = P(dp, seq, None)
    both = dp + seq
    return jax.shard_map(
        make_body(n1, n2, nz),
        mesh=fine,
        in_specs=(
            rows,
            P(both, None),
            P(None, both),
            P(both, None),
            P(both),
            P(both, None),
            P(both),
            P(both, None),
            P(both),
            P(),
            rows,
        ),
        out_specs=(
            rows,
            rows,
            P(both, None),
            P(None, both),
            P(both, None),
            P(both),
            P(both, None),
            P(both),
            P(both, None),
            P(both),
            P(),
        ),
        check_vma=False,
    )
```
